32 devices in a mesh: dp: 8 (over z, core), tensor: 4 (over y, x).
Axes of the slice: x: 2, y: 2, z: 4, core: 2. Of those that a mesh axis runs over, the one named last changes fastest.
Arguments:
- x_in: bfloat16 [8192, 1536], P(('dp', 'tensor')), may hold values from -6 to 6
- segments: int32 [8192], P('dp'), may hold values from 0 to 4, as said below
- pre_gain: float32 [1536], replicated, may hold values from 0.25 to 1.75
- w_z: bfloat16 [1536, 3072], P('dp', 'tensor'), may hold values from -0.15625 to 0.15625
- w_x: bfloat16 [1536, 3072], P('dp', 'tensor'), may hold values from -0.15625 to 0.15625
- w_bc: bfloat16 [1536, 256], P('dp'), may hold values from -0.15625 to 0.15625
- w_dt: bfloat16 [1536, 48], P('dp', 'tensor'), may hold values from -0.078125 to 0.078125
- conv_x_w: float32 [4, 3072], P(None, 'tensor'), may hold values from -3 to 3
- conv_x_b: float32 [3072], P('tensor'), may hold values from -3 to 3
- conv_bc_w: float32 [4, 256], replicated, may hold values from -3 to 3
- conv_bc_b: float32 [256], replicated, may hold values from -3 to 3
- a_log: float32 [48], P('tensor'), may hold values from 0 to 2
- dt_bias: float32 [48], P('tensor'), may hold values from -7.5 to -2.5
- d_skip: float32 [48], P('tensor'), may hold values from 0.5 to 1.5
- gate_gain: float32 [3072], P('tensor'), may hold values from 0.25 to 1.75
- w_out: bfloat16 [3072, 1536], P('tensor', 'dp'), may hold values from -0.109375 to 0.109375
- cotangent: bfloat16 [8192, 1536], P(('dp', 'tensor')), may hold values from -6 to 6
Outputs:
- block_out: bfloat16 [8192, 1536], P(('dp', 'tensor'))
- grad_x: bfloat16 [8192, 1536], P(('dp', 'tensor'))
- grad_pre_gain: float32 [1536], replicated
- grad_w_z: float32 [1536, 3072], P('dp', 'tensor')
- grad_w_x: float32 [1536, 3072], P('dp', 'tensor')
- grad_w_bc: float32 [1536, 256], P('dp')
- grad_w_dt: float32 [1536, 48], P('dp', 'tensor')
- grad_conv_x_w: float32 [4, 3072], P(None, 'tensor')
- grad_conv_x_b: float32 [3072], P('tensor')
- grad_conv_bc_w: float32 [4, 256], replicated
- grad_conv_bc_b: float32 [256], replicated
- grad_a_log: float32 [48], P('tensor')
- grad_dt_bias: float32 [48], P('tensor')
- grad_d_skip: float32 [48], P('tensor')
- grad_gate_gain: float32 [3072], P('tensor')
- grad_w_out: float32 [3072, 1536], P('tensor', 'dp')
The draws below stay inside these ranges and needn't reach their ends.
Inputs may be any that keep to these rules, and one draw needn't show every extreme that they name: `segments`: within each packed row of 1024 tokens (those of one index of dp) the numbers start at 0, never fall and rise by at most one from a token to the next; equal numbers mark one document; every row holds exactly five documents.
All inputs are finite; a program needn't handle non-finite values.
Results may differ from the reference program's by a relative error of at most 0.02.
Values may be sent and summed in bfloat16 or wider, within the bound.
A program may use at most 128 MiB of HBM per device.

```python
import jax
import jax.numpy as jnp
from jax import lax

D = 1536
NHEADS = 48
HEADDIM = 64
NSTATE = 128
KCONV = 4
GROUP = 256
TOK_DEV = 256
INNER = 3072
ROW = 1024
TOKENS = 8192
N_TENSOR = 4


def draw_segments(key, part):
    key = jax.random.fold_in(key, 7)
    key_begin, key_end, key_noise = jax.random.split(key, 3)
    row_total = TOKENS // ROW
    long_begin = jax.random.randint(key_begin, (row_total, 1), 3, TOK_DEV)
    long_end = jax.random.randint(key_end, (row_total, 1), ROW - TOK_DEV + 1, ROW)
    positions = jnp.arange(ROW, dtype=jnp.int32)[None, :]
    outside = ((positions < long_begin) | (positions > long_end)) & (positions > 0)
    ranks = jax.random.randint(key_noise, (row_total, ROW), 0, 65536) * ROW + positions
    scores = jnp.where(outside, ranks, 1073741824)
    order = jnp.argsort(scores, axis=1, stable=True).astype(jnp.int32)
    chosen = order[:, :2]
    extra = jnp.any(positions[:, :, None] == chosen[:, None, :], axis=2)
    flags = (positions == long_begin) | (positions == long_end) | extra
    numbers = jnp.cumsum(flags.astype(jnp.int32), axis=1)
    return numbers.reshape(-1).astype(jnp.int32)


def steps_of(key, extent, shards, smallest, largest):
    def one(axis_at, shards_of):
        draws = jax.random.uniform(jax.random.fold_in(jax.random.fold_in(key, 6), axis_at), (shards_of,), jnp.float32, smallest / len(shards), largest / len(shards))
        return jnp.repeat(jnp.exp(draws), extent[axis_at] // shards_of).reshape((-1,) + (1,) * (len(extent) - axis_at - 1))

    level = one(*shards[0])
    for cut in shards[1:]:
        level = level * one(*cut)
    return level


def bell_draw(stream_key, dims, spread, most, cuts=(), held_as=jnp.bfloat16):
    values = jax.random.normal(stream_key, dims, jnp.float32) * spread
    if len(cuts) > 0:
        values = steps_of(stream_key, dims, cuts, -0.22, 0.18) * values
    return jnp.clip(values, min=-most, max=most).astype(held_as)


def setup_inputs(seed: int = 0) -> dict:
    seeds = jax.random.split(jax.random.key(seed), 18)
    return {
        "x_in": bell_draw(seeds[0], (TOKENS, D), 1.0, 6.0, ((0, 32),)),
        "segments": draw_segments(jax.random.fold_in(seeds[17], 71), 0),
        "pre_gain": jnp.clip(1.0 + 0.15 * jax.random.normal(seeds[2], (D,), jnp.float32), 0.25, 1.75),
        "w_z": bell_draw(seeds[3], (D, INNER), D ** -0.5, 0.15625, ((0, 8), (1, 4))),
        "w_x": bell_draw(seeds[4], (D, INNER), D ** -0.5, 0.15625, ((0, 8), (1, 4))),
        "w_bc": bell_draw(seeds[5], (D, 2 * NSTATE), D ** -0.5, 0.15625, ((0, 8),)),
        "w_dt": bell_draw(seeds[6], (D, NHEADS), (4 * D) ** -0.5, 0.078125, ((0, 8), (1, 4))),
        "conv_x_w": bell_draw(seeds[7], (KCONV, INNER), KCONV ** -0.5, 3.0, ((1, 4),), jnp.float32),
        "conv_x_b": bell_draw(seeds[8], (INNER,), 0.5, 3.0, ((0, 4),), jnp.float32),
        "conv_bc_w": bell_draw(seeds[9], (KCONV, 2 * NSTATE), KCONV ** -0.5, 3.0, (), jnp.float32),
        "conv_bc_b": bell_draw(seeds[10], (2 * NSTATE,), 0.5, 3.0, (), jnp.float32),
        "a_log": jnp.clip(2.0 * jax.random.uniform(seeds[11], (NHEADS,), jnp.float32) ** steps_of(seeds[11], (NHEADS,), ((0, 4),), -0.2, 0.2), 0.0, 2.0),
        "dt_bias": jnp.clip(-7.5 + 5.0 * jax.random.uniform(seeds[12], (NHEADS,), jnp.float32) ** steps_of(seeds[12], (NHEADS,), ((0, 4),), -0.2, 0.2), -7.5, -2.5),
        "d_skip": jnp.clip(0.5 + 1.0 * jax.random.uniform(seeds[13], (NHEADS,), jnp.float32) ** steps_of(seeds[13], (NHEADS,), ((0, 4),), -0.2, 0.2), 0.5, 1.5),
        "gate_gain": jnp.clip(1.0 + 0.15 * jax.random.normal(seeds[14], (INNER,), jnp.float32), 0.25, 1.75),
        "w_out": bell_draw(seeds[15], (INNER, D), INNER ** -0.5, 0.109375, ((0, 4), (1, 8))),
        "cotangent": bell_draw(seeds[16], (TOKENS, D), 1.0, 6.0, ((0, 32),)),
    }


highest = lax.Precision.HIGHEST

@jax.custom_vjp
def low(v):
    return lax.optimization_barrier(v.astype(jnp.bfloat16)).astype(jnp.float32)

@jax.custom_vjp
def low_back(v):
    return v

def low_keep(v):
    return (low(v), None)

def low_pass(kept, grad):
    return (grad,)

def back_keep(v):
    return (v, None)

def back_low(kept, grad):
    return (low(grad),)
low.defvjp(low_keep, low_pass)
low_back.defvjp(back_keep, back_low)

def conv_causal(values, weight, bias_vec, segment):
    length = values.shape[0]
    tap_count = weight.shape[0]
    padded = jnp.concatenate([jnp.zeros((tap_count - 1, values.shape[1]), values.dtype), values], axis=0)
    seg_pad = jnp.concatenate([jnp.full((tap_count - 1,), -1, jnp.int32), segment.astype(jnp.int32)], axis=0)
    summed = jnp.zeros_like(values) + bias_vec[None, :]
    for offset in range(tap_count):
        matching = (seg_pad[offset:offset + length] == segment).astype(values.dtype)
        summed = summed + weight[offset][None, :] * padded[offset:offset + length] * matching[:, None]
    return summed

def scan_heads(x_chan, b_mat, c_mat, step_size, a_neg, d_skip, segment):
    length = x_chan.shape[0]
    heads = step_size.shape[1]
    blocks = length // GROUP
    x_blocks = x_chan.reshape(blocks, GROUP, heads, HEADDIM)
    b_blocks = b_mat.reshape(blocks, GROUP, NSTATE)
    c_blocks = c_mat.reshape(blocks, GROUP, NSTATE)
    dt_blocks = step_size.reshape(blocks, GROUP, heads)
    seg_blocks = segment.reshape(blocks, GROUP)
    positions = jnp.arange(GROUP)

    def block_step(carried, inputs_now):
        hidden_state, seg_prev = carried
        x_blk, b_blk, c_blk, dt_blk, seg_blk = inputs_now
        log_step = dt_blk * a_neg[None, :]
        cumulative = jnp.cumsum(log_step, axis=0)
        visible = (seg_blk[:, None] == seg_blk[None, :]) & (positions[:, None] >= positions[None, :])
        log_gap = cumulative[:, None, :] - cumulative[None, :, :]
        decays = jnp.where(visible[:, :, None], jnp.exp(jnp.where(visible[:, :, None], log_gap, 0.0)), 0.0)
        scores = jnp.dot(c_blk, b_blk.T, precision=highest)
        mixing = scores[:, :, None] * decays * dt_blk[None, :, :]
        within = jnp.einsum('tsh,shp->thp', mixing, x_blk, precision=highest)
        carried_in = (seg_blk == seg_prev).astype(x_blk.dtype)
        from_state = jnp.einsum('tn,hpn->thp', c_blk, hidden_state, precision=highest)
        from_state = from_state * (jnp.exp(cumulative) * carried_in[:, None])[:, :, None]
        output = within + from_state + d_skip[None, :, None] * x_blk
        final_seg = seg_blk[GROUP - 1]
        to_end = (seg_blk == final_seg).astype(x_blk.dtype)
        end_weights = jnp.exp(cumulative[GROUP - 1][None, :] - cumulative) * to_end[:, None] * dt_blk
        carry_on = (final_seg == seg_prev).astype(x_blk.dtype)
        updated = hidden_state * (jnp.exp(cumulative[GROUP - 1]) * carry_on)[:, None, None]
        updated = updated + jnp.einsum('shp,sn->hpn', x_blk * end_weights[:, :, None], b_blk, precision=highest)
        return ((updated, final_seg), output)
    start_state = (jnp.zeros((heads, HEADDIM, NSTATE), x_chan.dtype), jnp.array(-1, dtype=jnp.int32))
    ignored, outputs = lax.scan(jax.checkpoint(block_step), start_state, (x_blocks, b_blocks, c_blocks, dt_blocks, seg_blocks))
    return outputs.reshape(length, heads * HEADDIM)

def mixer_block(z_raw, x_raw, bc_raw, dt_raw, conv_x_w, conv_x_b, conv_bc_w, conv_bc_b, a_log, dt_bias, d_skip, segment):
    x_chan = jax.nn.silu(conv_causal(x_raw, conv_x_w, conv_x_b, segment))
    bc_chan = jax.nn.silu(conv_causal(bc_raw, conv_bc_w, conv_bc_b, segment))
    b_mat = bc_chan[:, :NSTATE]
    c_mat = bc_chan[:, NSTATE:]
    step_size = jax.nn.softplus(dt_raw + dt_bias[None, :])
    a_neg = -jnp.exp(a_log)
    scanned = scan_heads(x_chan, b_mat, c_mat, step_size, a_neg, d_skip, segment)
    return scanned * jax.nn.silu(z_raw)

def row_forward(row_x, segment, weights):
    pre_gain, w_z, w_x, w_bc, w_dt, conv_x_w, conv_x_b, conv_bc_w, conv_bc_b, a_log, dt_bias, d_skip, gate_gain, w_out = weights
    scale = lax.rsqrt(lax.optimization_barrier(jnp.mean(row_x * row_x, axis=1)) + 1e-05)
    normed = low(row_x * scale[:, None] * pre_gain[None, :])
    inner_blk = INNER // N_TENSOR
    head_blk = NHEADS // N_TENSOR
    pieces = []
    for split_index in range(N_TENSOR):
        chan_begin = split_index * inner_blk
        chan_end = chan_begin + inner_blk
        head_begin = split_index * head_blk
        head_end = head_begin + head_blk
        shared = low_back(normed)
        z_raw = low_back(jnp.dot(shared, w_z[:, chan_begin:chan_end], precision=highest))
        x_raw = low_back(jnp.dot(shared, w_x[:, chan_begin:chan_end], precision=highest))
        bc_raw = low_back(jnp.dot(shared, w_bc, precision=highest))
        dt_raw = low_back(jnp.dot(shared, w_dt[:, head_begin:head_end], precision=highest))
        pieces.append(mixer_block(z_raw, x_raw, bc_raw, dt_raw, conv_x_w[:, chan_begin:chan_end], conv_x_b[chan_begin:chan_end], conv_bc_w, conv_bc_b, a_log[head_begin:head_end], dt_bias[head_begin:head_end], d_skip[head_begin:head_end], segment))
    gated = jnp.concatenate(pieces, axis=1)
    scale_two = lax.rsqrt(lax.optimization_barrier(jnp.mean(gated * gated, axis=1)) + 1e-05)
    mixed = low(gated * scale_two[:, None] * gate_gain[None, :])
    branch = jnp.zeros_like(row_x)
    for split_index in range(N_TENSOR):
        chan_begin = split_index * inner_blk
        chan_end = chan_begin + inner_blk
        branch = branch + low(jnp.dot(mixed[:, chan_begin:chan_end], w_out[chan_begin:chan_end], precision=highest))
    return row_x + branch

def reference(x_in, segments, pre_gain, w_z, w_x, w_bc, w_dt, conv_x_w, conv_x_b, conv_bc_w, conv_bc_b, a_log, dt_bias, d_skip, gate_gain, w_out, cotangent):
    weights = tuple((item.astype(jnp.float32) for item in (pre_gain, w_z, w_x, w_bc, w_dt, conv_x_w, conv_x_b, conv_bc_w, conv_bc_b, a_log, dt_bias, d_skip, gate_gain, w_out)))
    row_total = TOKENS // ROW
    rows_x = x_in.astype(jnp.float32).reshape(row_total, ROW, D)
    rows_seg = segments.astype(jnp.int32).reshape(row_total, ROW)
    rows_cot = cotangent.astype(jnp.float32).reshape(row_total, ROW, D)
    zero_grads = tuple((jnp.zeros_like(item) for item in weights))

    def one_row(totals, inputs_now):
        row_x, row_seg, row_cot = inputs_now

        def forward(values, *params):
            return row_forward(values, row_seg, params)
        result, pullback = jax.vjp(forward, row_x, *weights)
        grads = pullback(row_cot)
        totals = tuple((summed + fresh for summed, fresh in zip(totals, grads[1:])))
        return (totals, (result.astype(jnp.bfloat16), grads[0].astype(jnp.bfloat16)))
    totals, (outputs, input_grads) = lax.scan(one_row, zero_grads, (rows_x, rows_seg, rows_cot))
    return (outputs.reshape(TOKENS, D), input_grads.reshape(TOKENS, D), totals[0], totals[1], totals[2], totals[3], totals[4], totals[5], totals[6], totals[7], totals[8], totals[9], totals[10], totals[11], totals[12], totals[13])
```

```python
import functools
import types

import jax
import jax.numpy as jnp
from jax import lax
from jax.experimental import pallas as pl
from jax.experimental.pallas import tpu as pltpu
from jax.sharding import PartitionSpec as P

HEADDIM = 64
NSTATE = 128
CHUNK = 128
LANES = 128
EPS = 1e-05
LOG2E = 1.4426950408889634
F32 = jnp.float32
BF16 = jnp.bfloat16
VMEM_LIMIT = 62 * 1024 * 1024
exact = lax.Precision.HIGHEST


def dot_nn(a, b):
    return lax.dot_general(a, b, (((1,), (0,)), ((), ())), preferred_element_type=F32)


def dot_nt(a, b):
    return lax.dot_general(a, b, (((1,), (1,)), ((), ())), preferred_element_type=F32)


def dot_tn(a, b):
    return lax.dot_general(a, b, (((0,), (0,)), ((), ())), preferred_element_type=F32)


def sigmoid(v):
    return 1.0 / (1.0 + jnp.exp(-v))


def softplus(v):
    return jnp.maximum(v, 0.0) + jnp.log1p(jnp.exp(-jnp.abs(v)))


def fold_rows(v):
    return jnp.sum(v.reshape(v.shape[0] // 8, 8, v.shape[1]), axis=0)


def split_two(v):
    high = v.astype(BF16)
    return high, (v - high.astype(F32)).astype(BF16)


def tile_iotas():
    shape = (CHUNK, LANES)
    return lax.broadcasted_iota(jnp.int32, shape, 0), lax.broadcasted_iota(jnp.int32, shape, 1)


def chunk_rows(c, pad=0, extra=0):
    return pl.ds(pl.multiple_of(c * CHUNK + pad, 8), CHUNK + extra)


def prepare_steps(c, r):
    row, col = tile_iotas()
    rows = chunk_rows(c)
    lower = (row >= col).astype(F32)
    step = softplus(r.dtr[rows, r.dtr_at : r.dtr_at + LANES] + r.dt_bias[...])
    log_step = step * (-jnp.exp(r.a_log[...]) * LOG2E)
    total = jnp.dot(lower, log_step, precision=exact, preferred_element_type=F32)
    r.step[rows, :] = step
    r.total[rows, :] = total
    r.total_t[pl.ds(pl.multiple_of(c * 16, 16), 16), :] = total.T[:16]


def segment_parts(c, r):
    down = r.seg_down[chunk_rows(c, 8), :]
    across = r.seg_across[pl.ds(c, 1), :]
    before = r.seg_down[pl.ds(pl.multiple_of(c * CHUNK, 8), 8), :][7:8, :]
    last = down[CHUNK - 1 : CHUNK, :]
    carried = (down == before).astype(F32)
    to_end = (down == last).astype(F32)
    carry_on = (last == before).astype(F32)
    return down, across, carried, to_end, carry_on


def masks_back(c, r, down):
    window = r.seg_down[chunk_rows(c, 0, 8), :]
    return [
        (pltpu.roll(window, j, 0)[8 : 8 + CHUNK] == down).astype(F32) for j in range(1, 4)
    ]


def masks_ahead(c, r, down):
    window = r.seg_down[chunk_rows(c, 8, 8), :]
    full = CHUNK + 8
    return [(pltpu.roll(window, full - j, 0)[:CHUNK] == down).astype(F32) for j in range(1, 4)]


def conv_tile(c, ref, at, weight, bias, w_at, masks):
    lanes = slice(at, at + LANES)
    w_lanes = slice(w_at, w_at + LANES)
    here = ref[chunk_rows(c), lanes]
    ahead = ref[pl.ds(pl.multiple_of(jnp.maximum(c * CHUNK - 8, 0), 8), 8), lanes]
    window = jnp.concatenate([ahead, here], axis=0)
    out = here * weight[3:4, w_lanes] + bias[0:1, w_lanes]
    for j in range(1, 4):
        shifted = pltpu.roll(window, j, 0)[8 : 8 + CHUNK]
        out = out + (shifted * masks[j - 1]) * weight[3 - j : 4 - j, w_lanes]
    return out


def pair_columns(tile, p, first):
    left = jnp.broadcast_to(tile[:, 2 * p : 2 * p + 1], (CHUNK, LANES))
    right = jnp.broadcast_to(tile[:, 2 * p + 1 : 2 * p + 2], (CHUNK, LANES))
    return left, right, jnp.where(first, left, right)


def stack_heads(tile, first):
    zero = jnp.zeros_like(tile)
    return jnp.concatenate([jnp.where(first, tile, zero), jnp.where(first, zero, tile)], axis=0)


def scan_chunk(c, r):
    rows = chunk_rows(c)
    row, col = tile_iotas()
    down, across, carried, to_end, carry_on = segment_parts(c, r)
    masks = masks_back(c, r, down)
    maps = []
    for half in range(2):
        pre = conv_tile(c, r.bc, r.bc_at + half * LANES, r.cbw, r.cbb, half * LANES, masks)
        r.pre_bc[rows, half * LANES : (half + 1) * LANES] = pre
        maps.append((pre * sigmoid(pre)).astype(BF16))
    b_map, c_map = maps
    r.maps[rows, :LANES] = b_map
    r.maps[rows, LANES:] = c_map
    scores = jnp.where((down == across) & (row >= col), dot_nt(c_map, b_map), 0.0)
    b_turned = b_map.T
    total = r.total[rows, :]
    step = r.step[rows, :]
    first = col < HEADDIM
    for p in range(r.pairs):
        lanes = slice(p * LANES, (p + 1) * LANES)
        pre = conv_tile(c, r.xr, r.xr_at + p * LANES, r.cxw, r.cxb, p * LANES, masks)
        r.pre_x[rows, lanes] = pre
        chan = pre * sigmoid(pre)
        left, right, both = pair_columns(total, p, first)
        _, _, step_pair = pair_columns(step, p, first)
        fed = step_pair * chan
        stacked = stack_heads(fed.astype(BF16), first)
        mixing = []
        for k, mine in enumerate((left, right)):
            other = r.total_t[pl.ds(c * 16 + 2 * p + k, 1), :]
            mixing.append((scores * jnp.exp2(jnp.minimum(mine - other, 0.0))).astype(BF16))
        within = dot_nn(jnp.concatenate(mixing, axis=1), stacked)
        state = r.state[:, lanes]
        state_low = state.astype(BF16)
        r.states[rows, lanes] = state_low
        decay_in = jnp.exp2(both) * carried
        r.y[rows, lanes] = (
            within + decay_in * dot_nn(c_map, state_low) + r.skip[0:1, lanes] * chan
        )
        last = both[CHUNK - 1 : CHUNK, :]
        decay_out = jnp.exp2(last - both) * to_end
        r.state[:, lanes] = (jnp.exp2(last) * carry_on) * state + dot_nn(
            b_turned, (decay_out * fed).astype(BF16)
        )


def scan_chunk_back(c, r):
    rows = chunk_rows(c)
    row, col = tile_iotas()
    down, across, carried, to_end, carry_on = segment_parts(c, r)
    ahead = masks_ahead(c, r, down)
    b_map = r.maps[rows, :LANES]
    c_map = r.maps[rows, LANES:]
    visible = (down == across) & (row <= col)
    scores = jnp.where(visible, dot_nt(b_map, c_map), 0.0)
    c_turned = c_map.T
    total = r.total[rows, :]
    step = r.step[rows, :]
    first = col < HEADDIM
    d_scores = jnp.zeros((CHUNK, LANES), F32)
    width = r.pairs * LANES
    for p in range(r.pairs):
        lanes = slice(p * LANES, (p + 1) * LANES)
        lows = slice(width + p * LANES, width + (p + 1) * LANES)
        gy_low = r.gy[rows, lanes]
        gy = gy_low.astype(F32)
        pre = r.pre_x[rows, lanes]
        gate = sigmoid(pre)
        chan = pre * gate
        left, right, both = pair_columns(total, p, first)
        _, _, step_pair = pair_columns(step, p, first)
        fed = step_pair * chan
        fed_low = fed.astype(BF16)
        d_mixing = dot_nt(stack_heads(fed_low, first), gy_low)
        mixing = []
        for k, mine in enumerate((left, right)):
            other = r.total_t[pl.ds(c * 16 + 2 * p + k, 1), :]
            decay = jnp.exp2(jnp.minimum(other - mine, 0.0))
            mixing.append((scores * decay).astype(BF16))
            d_scores = d_scores + d_mixing[k * CHUNK : (k + 1) * CHUNK] * decay
        d_state = r.d_state[:, lanes]
        d_state_low = d_state.astype(BF16)
        last = both[CHUNK - 1 : CHUNK, :]
        decay_out = jnp.exp2(last - both) * to_end
        from_state = decay_out * dot_nn(b_map, d_state_low)
        d_fed = dot_nn(jnp.concatenate(mixing, axis=1), stack_heads(gy_low, first)) + from_state
        fed_held = fed_low.astype(F32)
        skip = r.skip[0:1, lanes]
        flow = gy * (r.y[rows, lanes] - skip * chan) - fed_held * d_fed
        direct = chan * d_fed
        for k, part in enumerate((flow, direct)):
            spot = slice(k * CHUNK, (k + 1) * CHUNK)
            r.sums[spot, lanes], r.sums[spot, lows] = split_two(part)
        keep = jnp.exp2(last) * carry_on
        through = jnp.sum(fed_held * from_state, axis=0, keepdims=True) + keep * jnp.sum(
            r.states[rows, lanes].astype(F32) * d_state, axis=0, keepdims=True
        )
        spot = slice(2 * CHUNK, 2 * CHUNK + 16)
        r.sums[spot, lanes], r.sums[spot, lows] = split_two(
            jnp.broadcast_to(through, (16, LANES))
        )
        grad_in = (jnp.exp2(both) * carried * gy).astype(BF16)
        r.grad_in[:, lanes] = grad_in
        r.fed_out[:, lanes] = (decay_out * fed).astype(BF16)
        r.d_state_low[:, lanes] = d_state_low
        r.d_state[:, lanes] = keep * d_state + dot_nn(c_turned, grad_in)
        d_chan = skip * gy + step_pair * d_fed
        r.g_skip[:, lanes] += fold_rows(gy * chan)
        d_pre = d_chan * (gate * (1.0 + pre * (1.0 - gate)))
        conv_back(c, r, d_pre, r.d_pre_x, r.xr, r.xr_at, r.cxw, p * LANES, ahead, r.dx_at, r.g_cxw, r.g_cxb)
    d_scores_low = jnp.where(visible, d_scores, 0.0).astype(BF16)
    d_b = dot_nn(d_scores_low, c_map) + dot_nt(r.fed_out[...], r.d_state_low[...])
    d_c = dot_tn(d_scores_low, b_map) + dot_nt(r.grad_in[...], r.states[rows, :])
    for half, d_map in enumerate((d_b, d_c)):
        pre = r.pre_bc[rows, half * LANES : (half + 1) * LANES]
        gate = sigmoid(pre)
        d_pre = d_map * (gate * (1.0 + pre * (1.0 - gate)))
        conv_back(
            c, r, d_pre, r.d_pre_bc, r.bc, r.bc_at, r.cbw, half * LANES, ahead, r.dbc_at, r.g_cbw, r.g_cbb
        )
    reduced = dot_nn(r.sums[...], r.head_sum[...])
    d_total = jnp.dot(
        (row <= col).astype(F32), reduced[:CHUNK], precision=exact, preferred_element_type=F32
    ) + reduced[2 * CHUNK : 2 * CHUNK + 1]
    a_neg = -jnp.exp(r.a_log[...])
    d_step = reduced[CHUNK : 2 * CHUNK] + a_neg * d_total
    r.g_alog[...] += fold_rows(step * d_total) * a_neg
    d_raw = d_step * sigmoid(r.dtr[rows, r.dtr_at : r.dtr_at + LANES] + r.dt_bias[...])
    r.g_dtb[...] += fold_rows(d_raw)
    r.d_proj[rows, r.ddt_at : r.ddt_at + LANES] = d_raw.astype(BF16)


def conv_back(c, r, d_pre, held, raw, raw_at, weight, at, ahead, out_at, g_w, g_b):
    lanes = slice(at, at + LANES)
    rows = chunk_rows(c)
    held[CHUNK : CHUNK + 8, lanes] = held[0:8, lanes]
    held[0:CHUNK, lanes] = d_pre
    window = held[:, lanes]
    values = raw[rows, raw_at + at : raw_at + at + LANES]
    g_b[:, lanes] += fold_rows(d_pre)
    g_w[24:32, lanes] += fold_rows(d_pre * values)
    d_raw = d_pre * weight[3:4, lanes]
    for j in range(1, 4):
        shifted = pltpu.roll(window, CHUNK + 8 - j, 0)[:CHUNK] * ahead[j - 1]
        d_raw = d_raw + shifted * weight[3 - j : 4 - j, lanes]
        g_w[(3 - j) * 8 : (4 - j) * 8, lanes] += fold_rows(shifted * values)
    r.d_proj[rows, out_at + at : out_at + at + LANES] = d_raw.astype(BF16)


def head_sum_matrix(width):
    shape = (2 * width, LANES)
    lane = lax.broadcasted_iota(jnp.int32, shape, 0)
    lane = jnp.where(lane >= width, lane - width, lane)
    return (lane // HEADDIM == lax.broadcasted_iota(jnp.int32, shape, 1)).astype(BF16)


def layout_of(width):
    return types.SimpleNamespace(
        x=width, bc=2 * width, dt=2 * width + 2 * NSTATE, all=2 * width + 2 * NSTATE + LANES
    )


SMALL_IN = ("seg_down", "seg_across", "cxw", "cxb", "cbw", "cbb", "a_log", "dt_bias", "skip")


def small_inputs(segments, cxw, cxb, cbw, cbb, a_log, dt_bias, d_skip):
    tokens = segments.shape[0]
    seg = segments.astype(F32)
    edge = jnp.full((8,), -1.0, F32)
    down = jnp.broadcast_to(jnp.concatenate([edge, seg, edge])[:, None], (tokens + 16, LANES))
    heads = a_log.shape[0]
    pad = lambda v: jnp.pad(v, (0, LANES - heads))[None, :]
    return (
        down,
        seg.reshape(tokens // CHUNK, CHUNK),
        cxw,
        cxb[None, :],
        cbw,
        cbb[None, :],
        pad(a_log),
        pad(dt_bias),
        jnp.repeat(d_skip, HEADDIM)[None, :],
    )


def forward_kernel(*refs, names, width):
    r = types.SimpleNamespace(**dict(zip(names, refs)))
    at = layout_of(width)
    r.pairs = width // LANES
    r.xr = r.bc = r.dtr = r.proj
    r.xr_at, r.bc_at, r.dtr_at = at.x, at.bc, at.dt
    chunks = r.proj.shape[0] // CHUNK
    r.state[...] = jnp.zeros_like(r.state)

    def body(c, carry):
        prepare_steps(c, r)
        scan_chunk(c, r)
        return carry

    lax.fori_loop(0, chunks, body, 0)


def backward_kernel(*refs, names, width):
    r = types.SimpleNamespace(**dict(zip(names, refs)))
    at = layout_of(width)
    r.pairs = width // LANES
    r.xr = r.bc = r.dtr = r.proj
    r.xr_at, r.bc_at, r.dtr_at = at.x, at.bc, at.dt
    r.dx_at, r.dbc_at, r.ddt_at = 0, width, width + 2 * NSTATE
    start_back(r)
    chunks = r.proj.shape[0] // CHUNK

    def body(i, carry):
        scan_chunk_back(chunks - 1 - i, r)
        return carry

    lax.fori_loop(0, chunks, body, 0)


def start_back(r):
    for ref in (r.d_state, r.d_pre_x, r.d_pre_bc, r.g_cxw, r.g_cxb, r.g_cbw, r.g_cbb):
        ref[...] = jnp.zeros_like(ref)
    for ref in (r.g_skip, r.g_alog, r.g_dtb):
        ref[...] = jnp.zeros_like(ref)
    r.head_sum[...] = head_sum_matrix(r.pairs * LANES)


def call_local(kernel, width, ins, outs, scratch, values, flops):
    names = tuple(ins) + tuple(outs) + tuple(scratch)
    whole = pl.BlockSpec(memory_space=pltpu.VMEM)
    return pl.pallas_call(
        functools.partial(kernel, names=names, width=width),
        out_shape=tuple(jax.ShapeDtypeStruct(*spec) for spec in outs.values()),
        in_specs=[whole] * len(ins),
        out_specs=tuple([whole] * len(outs)),
        scratch_shapes=[pltpu.VMEM(*spec) for spec in scratch.values()],
        compiler_params=pltpu.CompilerParams(vmem_limit_bytes=VMEM_LIMIT),
        cost_estimate=pl.CostEstimate(flops=flops, bytes_accessed=1 << 24, transcendentals=0),
    )(*values)


def mixer_forward(projected, small, width):
    tokens = projected.shape[0]
    outs = dict(
        y=((tokens, width), F32),
        pre_x=((tokens, width), F32),
        pre_bc=((tokens, 2 * NSTATE), F32),
        maps=((tokens, 2 * NSTATE), BF16),
        states=((tokens, width), BF16),
        step=((tokens, LANES), F32),
        total=((tokens, LANES), F32),
        total_t=((tokens // CHUNK * 16, LANES), F32),
    )
    scratch = dict(state=((NSTATE, width), F32))
    return call_local(
        forward_kernel, width, ("proj",) + SMALL_IN, outs, scratch, (projected,) + small, 10**10
    )


BACK_SCRATCH = lambda width: dict(
    d_state=((NSTATE, width), F32),
    d_state_low=((NSTATE, width), BF16),
    grad_in=((CHUNK, width), BF16),
    fed_out=((CHUNK, width), BF16),
    sums=((2 * CHUNK + 16, 2 * width), BF16),
    head_sum=((2 * width, LANES), BF16),
    d_pre_x=((CHUNK + 8, width), F32),
    d_pre_bc=((CHUNK + 8, 2 * NSTATE), F32),
)
GRAD_OUT = lambda width: dict(
    g_cxw=((32, width), F32),
    g_cxb=((8, width), F32),
    g_cbw=((32, 2 * NSTATE), F32),
    g_cbb=((8, 2 * NSTATE), F32),
    g_skip=((8, width), F32),
    g_alog=((8, LANES), F32),
    g_dtb=((8, LANES), F32),
)


def mixer_backward(projected, small, saved, gy, width):
    tokens = projected.shape[0]
    outs = dict(d_proj=((tokens, width + 2 * NSTATE + LANES), BF16), **GRAD_OUT(width))
    ins = ("proj",) + SMALL_IN
    ins = ins + ("y", "pre_x", "pre_bc", "maps", "states", "step", "total", "total_t", "gy")
    return call_local(
        backward_kernel,
        width,
        ins,
        outs,
        BACK_SCRATCH(width),
        (projected,) + small + tuple(saved) + (gy,),
        3 * 10**10,
    )


def on_device(
    x_in,
    segments,
    pre_gain,
    w_z,
    w_x,
    w_bc,
    w_dt,
    conv_x_w,
    conv_x_b,
    conv_bc_w,
    conv_bc_b,
    a_log,
    dt_bias,
    d_skip,
    gate_gain,
    w_out,
    cotangent,
):
    width = w_z.shape[1]
    heads = a_log.shape[0]
    at = layout_of(width)
    values = x_in.astype(F32)
    scale = lax.rsqrt(jnp.mean(values * values, axis=1) + EPS)
    normed = (values * scale[:, None] * pre_gain[None, :]).astype(BF16)
    row_normed = lax.all_gather(normed, "tensor", axis=0, tiled=True)
    mine = jnp.concatenate(
        (w_z, w_x, w_bc, jnp.pad(w_dt, ((0, 0), (0, LANES - heads)))), axis=1
    )
    stacked = lax.all_gather(mine, "dp", axis=0, tiled=True)
    full_out = lax.all_gather(w_out.T, "dp", axis=0, tiled=True)
    projected = jnp.dot(row_normed, stacked, preferred_element_type=F32)
    small = small_inputs(
        segments, conv_x_w, conv_x_b, conv_bc_w, conv_bc_b, a_log, dt_bias, d_skip
    )
    saved = mixer_forward(projected, small, width)
    y = saved[0]
    z_raw = projected[:, :width]
    gate = sigmoid(z_raw)
    gated = y * (z_raw * gate)
    inner_total = width * lax.axis_size("tensor")
    row_cot = lax.all_gather(cotangent, "tensor", axis=0, tiled=True)
    d_mixed = dot_nn(row_cot, full_out)
    weighted = d_mixed * gate_gain[None, :]
    squares, cross = lax.psum(
        (jnp.sum(gated * gated, axis=1), jnp.sum(weighted * gated, axis=1)), "tensor"
    )
    scale_two = lax.rsqrt(squares / inner_total + EPS)
    mixed = (gated * scale_two[:, None] * gate_gain[None, :]).astype(BF16)
    branch = lax.psum_scatter(
        dot_nt(mixed, full_out).astype(BF16), "tensor", scatter_dimension=0, tiled=True
    ).astype(F32)
    block_out = (values + branch).astype(BF16)
    grad_gate_part = jnp.sum(d_mixed * gated * scale_two[:, None], axis=0)
    d_gated = (
        scale_two[:, None] * weighted
        - gated * (scale_two * scale_two * scale_two * cross / inner_total)[:, None]
    )
    gy = (d_gated * (z_raw * gate)).astype(BF16)
    d_z = (d_gated * y * (gate * (1.0 + z_raw * (1.0 - gate)))).astype(BF16)
    d_rest, g_cxw, g_cxb, g_cbw, g_cbb, g_skip, g_alog, g_dtb = mixer_backward(
        projected, small, saved, gy, width
    )
    d_proj = jnp.concatenate((d_z, d_rest), axis=1)
    d_normed = lax.psum_scatter(
        dot_nt(d_proj, stacked).astype(BF16), "tensor", scatter_dimension=0, tiled=True
    ).astype(F32)
    proj_part = dot_tn(row_normed, d_proj)
    out_part = dot_tn(row_cot, mixed)
    owned = lax.psum_scatter(
        jnp.concatenate((proj_part, out_part), axis=1).astype(BF16),
        "dp",
        scatter_dimension=0,
        tiled=True,
    ).astype(F32)
    grad_w_bc = lax.psum(owned[:, at.bc : at.dt].astype(BF16), "tensor").astype(F32)
    pre_weighted = d_normed * pre_gain[None, :]
    grad_pre_part = jnp.sum(d_normed * values * scale[:, None], axis=0)
    feature_sum = jnp.sum(pre_weighted * values, axis=1)
    grad_x = (
        cotangent.astype(F32)
        + scale[:, None] * pre_weighted
        - values * (scale * scale * scale * feature_sum / values.shape[1])[:, None]
    ).astype(BF16)
    over_taps = lambda v: jnp.sum(v.reshape(4, 8, v.shape[1]), axis=1)
    over_rows = lambda v: jnp.sum(v, axis=0)
    grad_gate_gain, grad_cxw, grad_cxb, grad_alog, grad_dtb, grad_skip = lax.psum(
        (
            grad_gate_part,
            over_taps(g_cxw),
            over_rows(g_cxb),
            over_rows(g_alog)[:heads],
            over_rows(g_dtb)[:heads],
            jnp.sum(over_rows(g_skip).reshape(heads, HEADDIM), axis=1),
        ),
        "dp",
    )
    grad_pre_gain, grad_cbw, grad_cbb = lax.psum(
        (grad_pre_part, over_taps(g_cbw), over_rows(g_cbb)), ("dp", "tensor")
    )
    return (
        block_out,
        grad_x,
        grad_pre_gain,
        owned[:, :width],
        owned[:, width : at.bc],
        grad_w_bc,
        owned[:, at.dt : at.dt + heads],
        grad_cxw,
        grad_cxb,
        grad_cbw,
        grad_cbb,
        grad_alog,
        grad_dtb,
        grad_skip,
        grad_gate_gain,
        owned[:, at.all :].T,
    )


def solution(mesh):
    tokens = P(("dp", "tensor"), None)
    both = P("dp", "tensor")
    heads = P("tensor")
    return jax.shard_map(
        on_device,
        mesh=mesh,
        in_specs=(
            tokens,
            P("dp"),
            P(),
            both,
            both,
            P("dp", None),
            both,
            P(None, "tensor"),
            heads,
            P(),
            P(),
            heads,
            heads,
            heads,
            heads,
            P("tensor", "dp"),
            tokens,
        ),
        out_specs=(
            tokens,
            tokens,
            P(),
            both,
            both,
            P("dp", None),
            both,
            P(None, "tensor"),
            heads,
            P(),
            P(),
            heads,
            heads,
            heads,
            heads,
            P("tensor", "dp"),
        ),
        check_vma=False,
    )
```

```python
import functools
import types

import jax
import jax.numpy as jnp
from jax import lax
from jax.experimental import pallas as pl
from jax.experimental.pallas import tpu as pltpu
from jax.sharding import PartitionSpec as P

HEADDIM = 64
NSTATE = 128
CHUNK = 128
LANES = 128
EPS = 1e-05
LOG2E = 1.4426950408889634
F32 = jnp.float32
BF16 = jnp.bfloat16
VMEM_LIMIT = 62 * 1024 * 1024
exact = lax.Precision.HIGHEST


def dot_nn(a, b):
    return lax.dot_general(a, b, (((1,), (0,)), ((), ())), preferred_element_type=F32)


def dot_nt(a, b):
    return lax.dot_general(a, b, (((1,), (1,)), ((), ())), preferred_element_type=F32)


def dot_tn(a, b):
    return lax.dot_general(a, b, (((0,), (0,)), ((), ())), preferred_element_type=F32)


def sigmoid(v):
    return 1.0 / (1.0 + jnp.exp(-v))


def softplus(v):
    return jnp.maximum(v, 0.0) + jnp.log1p(jnp.exp(-jnp.abs(v)))


def fold_rows(v):
    return jnp.sum(v.reshape(v.shape[0] // 8, 8, v.shape[1]), axis=0)


def split_two(v):
    high = v.astype(BF16)
    return high, (v - high.astype(F32)).astype(BF16)


def tile_iotas():
    shape = (CHUNK, LANES)
    return lax.broadcasted_iota(jnp.int32, shape, 0), lax.broadcasted_iota(jnp.int32, shape, 1)


def chunk_rows(c, pad=0, extra=0):
    return pl.ds(pl.multiple_of(c * CHUNK + pad, 8), CHUNK + extra)


def prepare_steps(c, r):
    row, col = tile_iotas()
    rows = chunk_rows(c)
    lower = (row >= col).astype(F32)
    step = softplus(r.dtr[rows, r.dtr_at : r.dtr_at + LANES] + r.dt_bias[...])
    log_step = step * (-jnp.exp(r.a_log[...]) * LOG2E)
    total = jnp.dot(lower, log_step, precision=exact, preferred_element_type=F32)
    r.step[rows, :] = step
    r.total[rows, :] = total
    r.total_t[pl.ds(pl.multiple_of(c * 16, 16), 16), :] = total.T[:16]


def segment_parts(c, r):
    down = r.seg_down[chunk_rows(c, 8), :]
    across = r.seg_across[pl.ds(c, 1), :]
    before = r.seg_down[pl.ds(pl.multiple_of(c * CHUNK, 8), 8), :][7:8, :]
    last = down[CHUNK - 1 : CHUNK, :]
    carried = (down == before).astype(F32)
    to_end = (down == last).astype(F32)
    carry_on = (last == before).astype(F32)
    return down, across, carried, to_end, carry_on


def masks_back(c, r, down):
    window = r.seg_down[chunk_rows(c, 0, 8), :]
    return [
        (pltpu.roll(window, j, 0)[8 : 8 + CHUNK] == down).astype(F32) for j in range(1, 4)
    ]


def masks_ahead(c, r, down):
    window = r.seg_down[chunk_rows(c, 8, 8), :]
    full = CHUNK + 8
    return [(pltpu.roll(window, full - j, 0)[:CHUNK] == down).astype(F32) for j in range(1, 4)]


def conv_tile(c, ref, at, weight, bias, w_at, masks):
    lanes = slice(at, at + LANES)
    w_lanes = slice(w_at, w_at + LANES)
    here = ref[chunk_rows(c), lanes]
    ahead = ref[pl.ds(pl.multiple_of(jnp.maximum(c * CHUNK - 8, 0), 8), 8), lanes]
    window = jnp.concatenate([ahead, here], axis=0)
    out = here * weight[3:4, w_lanes] + bias[0:1, w_lanes]
    for j in range(1, 4):
        shifted = pltpu.roll(window, j, 0)[8 : 8 + CHUNK]
        out = out + (shifted * masks[j - 1]) * weight[3 - j : 4 - j, w_lanes]
    return out


def pair_columns(tile, p, first):
    left = jnp.broadcast_to(tile[:, 2 * p : 2 * p + 1], (CHUNK, LANES))
    right = jnp.broadcast_to(tile[:, 2 * p + 1 : 2 * p + 2], (CHUNK, LANES))
    return left, right, jnp.where(first, left, right)


def stack_heads(tile, first):
    zero = jnp.zeros_like(tile)
    return jnp.concatenate([jnp.where(first, tile, zero), jnp.where(first, zero, tile)], axis=0)


def scan_chunk(c, r):
    rows = chunk_rows(c)
    row, col = tile_iotas()
    down, across, carried, to_end, carry_on = segment_parts(c, r)
    masks = masks_back(c, r, down)
    maps = []
    for half in range(2):
        pre = conv_tile(c, r.bc, r.bc_at + half * LANES, r.cbw, r.cbb, half * LANES, masks)
        r.pre_bc[rows, half * LANES : (half + 1) * LANES] = pre
        maps.append((pre * sigmoid(pre)).astype(BF16))
    b_map, c_map = maps
    r.maps[rows, :LANES] = b_map
    r.maps[rows, LANES:] = c_map
    scores = jnp.where((down == across) & (row >= col), dot_nt(c_map, b_map), 0.0)
    b_turned = b_map.T
    total = r.total[rows, :]
    step = r.step[rows, :]
    first = col < HEADDIM
    for p in range(r.pairs):
        lanes = slice(p * LANES, (p + 1) * LANES)
        pre = conv_tile(c, r.xr, r.xr_at + p * LANES, r.cxw, r.cxb, p * LANES, masks)
        r.pre_x[rows, lanes] = pre
        chan = pre * sigmoid(pre)
        left, right, both = pair_columns(total, p, first)
        _, _, step_pair = pair_columns(step, p, first)
        fed = step_pair * chan
        stacked = stack_heads(fed.astype(BF16), first)
        mixing = []
        for k, mine in enumerate((left, right)):
            other = r.total_t[pl.ds(c * 16 + 2 * p + k, 1), :]
            mixing.append((scores * jnp.exp2(jnp.minimum(mine - other, 0.0))).astype(BF16))
        within = dot_nn(jnp.concatenate(mixing, axis=1), stacked)
        state = r.state[:, lanes]
        state_low = state.astype(BF16)
        r.states[rows, lanes] = state_low
        decay_in = jnp.exp2(both) * carried
        r.y[rows, lanes] = (
            within + decay_in * dot_nn(c_map, state_low) + r.skip[0:1, lanes] * chan
        )
        last = both[CHUNK - 1 : CHUNK, :]
        decay_out = jnp.exp2(last - both) * to_end
        r.state[:, lanes] = (jnp.exp2(last) * carry_on) * state + dot_nn(
            b_turned, (decay_out * fed).astype(BF16)
        )


def scan_chunk_back(c, r):
    rows = chunk_rows(c)
    row, col = tile_iotas()
    down, across, carried, to_end, carry_on = segment_parts(c, r)
    ahead = masks_ahead(c, r, down)
    b_map = r.maps[rows, :LANES]
    c_map = r.maps[rows, LANES:]
    visible = (down == across) & (row <= col)
    scores = jnp.where(visible, dot_nt(b_map, c_map), 0.0)
    c_turned = c_map.T
    total = r.total[rows, :]
    step = r.step[rows, :]
    first = col < HEADDIM
    d_scores = jnp.zeros((CHUNK, LANES), F32)
    width = r.pairs * LANES
    for p in range(r.pairs):
        lanes = slice(p * LANES, (p + 1) * LANES)
        lows = slice(width + p * LANES, width + (p + 1) * LANES)
        gy_low = r.gy[rows, lanes]
        gy = gy_low.astype(F32)
        pre = r.pre_x[rows, lanes]
        gate = sigmoid(pre)
        chan = pre * gate
        left, right, both = pair_columns(total, p, first)
        _, _, step_pair = pair_columns(step, p, first)
        fed = step_pair * chan
        fed_low = fed.astype(BF16)
        d_mixing = dot_nt(stack_heads(fed_low, first), gy_low)
        mixing = []
        for k, mine in enumerate((left, right)):
            other = r.total_t[pl.ds(c * 16 + 2 * p + k, 1), :]
            decay = jnp.exp2(jnp.minimum(other - mine, 0.0))
            mixing.append((scores * decay).astype(BF16))
            d_scores = d_scores + d_mixing[k * CHUNK : (k + 1) * CHUNK] * decay
        d_state = r.d_state[:, lanes]
        d_state_low = d_state.astype(BF16)
        last = both[CHUNK - 1 : CHUNK, :]
        decay_out = jnp.exp2(last - both) * to_end
        from_state = decay_out * dot_nn(b_map, d_state_low)
        d_fed = dot_nn(jnp.concatenate(mixing, axis=1), stack_heads(gy_low, first)) + from_state
        fed_held = fed_low.astype(F32)
        skip = r.skip[0:1, lanes]
        flow = gy * (r.y[rows, lanes] - skip * chan) - fed_held * d_fed
        direct = chan * d_fed
        for k, part in enumerate((flow, direct)):
            spot = slice(k * CHUNK, (k + 1) * CHUNK)
            r.sums[spot, lanes], r.sums[spot, lows] = split_two(part)
        keep = jnp.exp2(last) * carry_on
        through = jnp.sum(fed_held * from_state, axis=0, keepdims=True) + keep * jnp.sum(
            r.states[rows, lanes].astype(F32) * d_state, axis=0, keepdims=True
        )
        spot = slice(2 * CHUNK, 2 * CHUNK + 16)
        r.sums[spot, lanes], r.sums[spot, lows] = split_two(
            jnp.broadcast_to(through, (16, LANES))
        )
        grad_in = (jnp.exp2(both) * carried * gy).astype(BF16)
        r.grad_in[:, lanes] = grad_in
        r.fed_out[:, lanes] = (decay_out * fed).astype(BF16)
        r.d_state_low[:, lanes] = d_state_low
        r.d_state[:, lanes] = keep * d_state + dot_nn(c_turned, grad_in)
        d_chan = skip * gy + step_pair * d_fed
        r.g_skip[:, lanes] += fold_rows(gy * chan)
        d_pre = d_chan * (gate * (1.0 + pre * (1.0 - gate)))
        conv_back(c, r, d_pre, r.d_pre_x, r.xr, r.xr_at, r.cxw, p * LANES, ahead, r.dx_at, r.g_cxw, r.g_cxb)
    d_scores_low = jnp.where(visible, d_scores, 0.0).astype(BF16)
    d_b = dot_nn(d_scores_low, c_map) + dot_nt(r.fed_out[...], r.d_state_low[...])
    d_c = dot_tn(d_scores_low, b_map) + dot_nt(r.grad_in[...], r.states[rows, :])
    for half, d_map in enumerate((d_b, d_c)):
        pre = r.pre_bc[rows, half * LANES : (half + 1) * LANES]
        gate = sigmoid(pre)
        d_pre = d_map * (gate * (1.0 + pre * (1.0 - gate)))
        conv_back(
            c, r, d_pre, r.d_pre_bc, r.bc, r.bc_at, r.cbw, half * LANES, ahead, r.dbc_at, r.g_cbw, r.g_cbb
        )
    reduced = dot_nn(r.sums[...], r.head_sum[...])
    d_total = jnp.dot(
        (row <= col).astype(F32), reduced[:CHUNK], precision=exact, preferred_element_type=F32
    ) + reduced[2 * CHUNK : 2 * CHUNK + 1]
    a_neg = -jnp.exp(r.a_log[...])
    d_step = reduced[CHUNK : 2 * CHUNK] + a_neg * d_total
    r.g_alog[...] += fold_rows(step * d_total) * a_neg
    d_raw = d_step * sigmoid(r.dtr[rows, r.dtr_at : r.dtr_at + LANES] + r.dt_bias[...])
    r.g_dtb[...] += fold_rows(d_raw)
    r.d_proj[rows, r.ddt_at : r.ddt_at + LANES] = d_raw.astype(BF16)


def conv_back(c, r, d_pre, held, raw, raw_at, weight, at, ahead, out_at, g_w, g_b):
    lanes = slice(at, at + LANES)
    rows = chunk_rows(c)
    held[CHUNK : CHUNK + 8, lanes] = held[0:8, lanes]
    held[0:CHUNK, lanes] = d_pre
    window = held[:, lanes]
    values = raw[rows, raw_at + at : raw_at + at + LANES]
    g_b[:, lanes] += fold_rows(d_pre)
    g_w[24:32, lanes] += fold_rows(d_pre * values)
    d_raw = d_pre * weight[3:4, lanes]
    for j in range(1, 4):
        shifted = pltpu.roll(window, CHUNK + 8 - j, 0)[:CHUNK] * ahead[j - 1]
        d_raw = d_raw + shifted * weight[3 - j : 4 - j, lanes]
        g_w[(3 - j) * 8 : (4 - j) * 8, lanes] += fold_rows(shifted * values)
    r.d_proj[rows, out_at + at : out_at + at + LANES] = d_raw.astype(BF16)


def head_sum_matrix(width):
    shape = (2 * width, LANES)
    lane = lax.broadcasted_iota(jnp.int32, shape, 0)
    lane = jnp.where(lane >= width, lane - width, lane)
    return (lane // HEADDIM == lax.broadcasted_iota(jnp.int32, shape, 1)).astype(BF16)


def layout_of(width):
    return types.SimpleNamespace(
        x=width, bc=2 * width, dt=2 * width + 2 * NSTATE, all=2 * width + 2 * NSTATE + LANES
    )


SMALL_IN = ("seg_down", "seg_across", "cxw", "cxb", "cbw", "cbb", "a_log", "dt_bias", "skip")


def small_inputs(segments, cxw, cxb, cbw, cbb, a_log, dt_bias, d_skip):
    tokens = segments.shape[0]
    seg = segments.astype(F32)
    edge = jnp.full((8,), -1.0, F32)
    down = jnp.broadcast_to(jnp.concatenate([edge, seg, edge])[:, None], (tokens + 16, LANES))
    heads = a_log.shape[0]
    pad = lambda v: jnp.pad(v, (0, LANES - heads))[None, :]
    return (
        down,
        seg.reshape(tokens // CHUNK, CHUNK),
        cxw,
        cxb[None, :],
        cbw,
        cbb[None, :],
        pad(a_log),
        pad(dt_bias),
        jnp.repeat(d_skip, HEADDIM)[None, :],
    )


def take_projections(r, width):
    r.pairs = width // LANES
    if hasattr(r, "proj"):
        at = layout_of(width)
        r.xr = r.bc = r.dtr = r.proj
        r.xr_at, r.bc_at, r.dtr_at = at.x, at.bc, at.dt
    else:
        r.xr_at = r.bc_at = r.dtr_at = 0


def forward_kernel(*refs, names, width):
    r = types.SimpleNamespace(**dict(zip(names, refs)))
    take_projections(r, width)
    chunks = r.dtr.shape[0] // CHUNK
    r.state[...] = jnp.zeros_like(r.state)

    def body(c, carry):
        prepare_steps(c, r)
        scan_chunk(c, r)
        return carry

    lax.fori_loop(0, chunks, body, 0)


def backward_kernel(*refs, names, width):
    r = types.SimpleNamespace(**dict(zip(names, refs)))
    take_projections(r, width)
    r.dx_at, r.dbc_at, r.ddt_at = 0, width, width + 2 * NSTATE
    start_back(r)
    chunks = r.dtr.shape[0] // CHUNK

    def body(i, carry):
        scan_chunk_back(chunks - 1 - i, r)
        return carry

    lax.fori_loop(0, chunks, body, 0)


def start_back(r):
    for ref in (r.d_state, r.d_pre_x, r.d_pre_bc, r.g_cxw, r.g_cxb, r.g_cbw, r.g_cbb):
        ref[...] = jnp.zeros_like(ref)
    for ref in (r.g_skip, r.g_alog, r.g_dtb):
        ref[...] = jnp.zeros_like(ref)
    r.head_sum[...] = head_sum_matrix(r.pairs * LANES)


def call_local(kernel, width, ins, outs, scratch, values, flops):
    names = tuple(ins) + tuple(outs) + tuple(scratch)
    whole = pl.BlockSpec(memory_space=pltpu.VMEM)
    return pl.pallas_call(
        functools.partial(kernel, names=names, width=width),
        out_shape=tuple(jax.ShapeDtypeStruct(*spec) for spec in outs.values()),
        in_specs=[whole] * len(ins),
        out_specs=tuple([whole] * len(outs)),
        scratch_shapes=[pltpu.VMEM(*spec) for spec in scratch.values()],
        compiler_params=pltpu.CompilerParams(vmem_limit_bytes=VMEM_LIMIT),
        cost_estimate=pl.CostEstimate(flops=flops, bytes_accessed=1 << 24, transcendentals=0),
    )(*values)


def mixer_forward(projected, small, width):
    tokens = projected.shape[0]
    outs = dict(
        y=((tokens, width), F32),
        pre_x=((tokens, width), F32),
        pre_bc=((tokens, 2 * NSTATE), F32),
        maps=((tokens, 2 * NSTATE), BF16),
        states=((tokens, width), BF16),
        step=((tokens, LANES), F32),
        total=((tokens, LANES), F32),
        total_t=((tokens // CHUNK * 16, LANES), F32),
    )
    scratch = dict(state=((NSTATE, width), F32))
    return call_local(
        forward_kernel, width, ("proj",) + SMALL_IN, outs, scratch, (projected,) + small, 10**10
    )


BACK_SCRATCH = lambda width: dict(
    d_state=((NSTATE, width), F32),
    d_state_low=((NSTATE, width), BF16),
    grad_in=((CHUNK, width), BF16),
    fed_out=((CHUNK, width), BF16),
    sums=((2 * CHUNK + 16, 2 * width), BF16),
    head_sum=((2 * width, LANES), BF16),
    d_pre_x=((CHUNK + 8, width), F32),
    d_pre_bc=((CHUNK + 8, 2 * NSTATE), F32),
)
GRAD_OUT = lambda width: dict(
    g_cxw=((32, width), F32),
    g_cxb=((8, width), F32),
    g_cbw=((32, 2 * NSTATE), F32),
    g_cbb=((8, 2 * NSTATE), F32),
    g_skip=((8, width), F32),
    g_alog=((8, LANES), F32),
    g_dtb=((8, LANES), F32),
)


SAVED = ("y", "pre_x", "pre_bc", "maps", "states", "step", "total", "total_t")


def mixer_backward(projected, small, saved, gy, width):
    tokens = gy.shape[0]
    outs = dict(d_proj=((tokens, width + 2 * NSTATE + LANES), BF16), **GRAD_OUT(width))
    ins = (("proj",) if len(projected) == 1 else ("xr", "bc", "dtr")) + SMALL_IN
    ins = ins + SAVED + ("gy",)
    return call_local(
        backward_kernel,
        width,
        ins,
        outs,
        BACK_SCRATCH(width),
        tuple(projected) + small + tuple(saved) + (gy,),
        3 * 10**10,
    )


LAST_Z = 3
UP, DOWN, PAIR_LOW, PAIR_HIGH = range(4)


def place():
    dp = lax.axis_index("dp")
    tp = lax.axis_index("tensor")
    z = dp // 2
    core = dp - 2 * z
    x = lax.rem(tp, 2)
    y = tp // 2
    near_x = y * 2 + (1 - x)
    near_y = (1 - y) * 2 + x
    across = (1 - y) * 2 + (1 - x)
    return types.SimpleNamespace(
        dp=dp,
        tp=tp,
        z=z,
        core=core,
        mate=dp + 1 - 2 * core,
        near_x=near_x,
        near_y=near_y,
        across=across,
    )


def device(w, dp=None, tp=None):
    return {"dp": w.dp if dp is None else dp, "tensor": w.tp if tp is None else tp}


def greet(w):
    barrier = pltpu.get_barrier_semaphore()

    def tell(**where):
        pl.semaphore_signal(
            barrier, inc=1, device_id=device(w, **where), device_id_type=pl.DeviceIdType.MESH
        )

    tell(dp=w.mate)
    tell(tp=w.near_x)
    tell(tp=w.near_y)
    tell(tp=w.across)
    pl.when(w.z < LAST_Z)(lambda: tell(dp=w.dp + 2))
    pl.when(w.z > 0)(lambda: tell(dp=w.dp - 2))
    below = (w.z + LAST_Z - 1) // LAST_Z
    above = (2 * LAST_Z - 1 - w.z) // LAST_Z
    pl.semaphore_wait(barrier, 4 + below + above)


def remote(src, dst, send, recv, where):
    return pltpu.make_async_remote_copy(
        src_ref=src,
        dst_ref=dst,
        send_sem=send,
        recv_sem=recv,
        device_id=where,
        device_id_type=pl.DeviceIdType.MESH,
    )


class LineGather:
    def __init__(self, w, ref, send, recv):
        self.w, self.ref, self.send, self.recv = w, ref, send, recv
        self.rows = ref.shape[0] // (2 * (LAST_Z + 1))

    def shard(self, z, core):
        start = pl.multiple_of((z * 2 + core) * self.rows, 16)
        return self.ref.at[pl.ds(start, self.rows)]

    def copy(self, z, step, kind):
        w = self.w
        part = self.shard(z, w.core)
        to = {UP: w.dp + 2, DOWN: w.dp - 2}.get(kind, w.mate)
        return remote(
            part,
            part,
            self.send.at[step, kind],
            self.recv.at[z * 2 + w.core],
            device(w, dp=to),
        )

    def arrived(self, z, core):
        part = self.shard(z, core)
        remote(
            part, part, self.send.at[0, 0], self.recv.at[z * 2 + core], device(self.w)
        ).wait_recv()

    def relay(self, step, act=None):
        w = self.w

        def low():
            z = w.z - step
            if act is None and step > 0:
                self.arrived(z, w.core)
            do = act or (lambda copy: copy.start())
            pl.when(w.z < LAST_Z)(lambda: do(self.copy(z, step, UP)))
            do(self.copy(z, step, PAIR_LOW))
            if step == 0:
                pl.when(w.z > 0)(lambda: do(self.copy(z, step, DOWN)))

        def high():
            z = w.z + step
            if act is None:
                self.arrived(z, w.core)
            do = act or (lambda copy: copy.start())
            pl.when(w.z > 0)(lambda: do(self.copy(z, step, DOWN)))
            do(self.copy(z, step, PAIR_HIGH))

        if step == 0:
            low()
        else:
            pl.when(w.z >= step)(low)
            pl.when(w.z <= LAST_Z - step)(high)

    def finish(self):
        for z in range(LAST_Z + 1):
            self.arrived(z, 1 - self.w.core)

    def drain(self):
        for step in range(LAST_Z + 1):
            self.relay(step, lambda copy: copy.wait_send())


class RowGather:
    def __init__(self, w, ref, send, recv):
        self.w, self.ref, self.send, self.recv = w, ref, send, recv
        self.rows = ref.shape[0] // 4

    def block(self, slot, half=None):
        rows = self.rows if half is None else self.rows // 2
        start = slot * self.rows + (0 if half is None else half * rows)
        return self.ref.at[pl.ds(pl.multiple_of(start, 16), rows)]

    def copy(self, i):
        w = self.w
        part, to = (
            (self.block(w.tp), w.near_x),
            (self.block(w.tp), w.near_y),
            (self.block(w.near_x, 0), w.near_y),
            (self.block(w.near_y, 1), w.near_x),
        )[i]
        return remote(part, part, self.send.at[i], self.recv.at[i], device(w, tp=to))

    def start(self):
        for i in range(2):
            self.copy(i).start()

    def hand_on(self):
        for i in range(2):
            self.copy(i).wait_recv()
            self.copy(i + 2).start()

    def finish(self):
        for i in range(2, 4):
            self.copy(i).wait_recv()

    def drain(self):
        for i in range(4):
            self.copy(i).wait_send()


def norm_rows(x_ref, gain_ref, out_ref, start):
    rows = 64

    def body(i, carry):
        here = pl.ds(pl.multiple_of(i * rows, rows), rows)
        values = x_ref[here, :].astype(F32)
        scale = lax.rsqrt(jnp.mean(values * values, axis=1, keepdims=True) + EPS)
        there = pl.ds(pl.multiple_of(start + i * rows, 16), rows)
        out_ref[there, :] = (values * scale * gain_ref[...]).astype(BF16)
        return carry

    lax.fori_loop(0, x_ref.shape[0] // rows, body, 0)


def by_rows(total, rows, body):
    def step(i, carry):
        body(pl.ds(pl.multiple_of(i * rows, rows), rows))
        return carry

    lax.fori_loop(0, total // rows, step, 0)


def gate_chunk(c, r):
    rows = chunk_rows(c)
    square = jnp.zeros((CHUNK, LANES), F32)
    cross = jnp.zeros((CHUNK, LANES), F32)
    for p in range(r.pairs):
        lanes = slice(p * LANES, (p + 1) * LANES)
        z = r.z[rows, lanes]
        gated = r.y[rows, lanes] * (z * sigmoid(z))
        square = square + gated * gated
        cross = cross + r.d_mixed[rows, lanes] * r.gain[0:1, lanes] * gated
    half = r.parts.shape[1] // 2
    mine = r.parts.at[r.w.tp]
    mine[pl.ds(c, 1), :] = jnp.sum(square.T, axis=0, keepdims=True)
    mine[pl.ds(half + c, 1), :] = jnp.sum(cross.T, axis=0, keepdims=True)


class SumExchange:
    def __init__(self, w, ref, send, recv):
        self.w, self.ref, self.send, self.recv = w, ref, send, recv

    def copies(self):
        w = self.w
        mine = self.ref.at[w.tp]
        return [
            remote(mine, mine, self.send.at[i], self.recv.at[i], device(w, tp=to))
            for i, to in enumerate((w.near_x, w.near_y, w.across))
        ]

    def start(self):
        for copy in self.copies():
            copy.start()

    def finish(self):
        for copy in self.copies():
            copy.wait()


def phase_one(r):
    w = r.w
    width = r.pairs * LANES
    tokens = r.row_normed.shape[0]
    chunks = tokens // CHUNK
    own = pl.ds(pl.multiple_of(w.dp * r.w_x.shape[0], 16), r.w_x.shape[0])
    r.full_x[own, :width] = r.w_x[...]
    r.full_x[own, width : width + 2 * NSTATE] = r.w_bc[...]
    r.full_x[own, width + 2 * NSTATE :] = r.w_dt[...]
    r.full_out[own, :] = r.w_out[...]
    r.full_z[own, :] = r.w_z[...]
    shard_x = LineGather(w, r.full_x, r.send_w.at[0], r.recv_w.at[0])
    shard_out = LineGather(w, r.full_out, r.send_w.at[1], r.recv_w.at[1])
    shard_z = LineGather(w, r.full_z, r.send_w.at[2], r.recv_w.at[2])
    row_n = RowGather(w, r.row_normed, r.send_r.at[0], r.recv_r.at[0])
    row_c = RowGather(w, r.row_cot, r.send_r.at[1], r.recv_r.at[1])
    sums = SumExchange(w, r.parts, r.send_s, r.recv_s)
    block = r.x_in.shape[0]
    start = pl.multiple_of(w.tp * block, block)
    greet(w)
    shard_x.relay(0)
    norm_rows(r.x_in, r.pre_gain, r.row_normed, start)
    row_n.start()
    r.row_cot[pl.ds(start, block), :] = r.cot[...]
    r.state[...] = jnp.zeros_like(r.state)
    shard_x.relay(1)
    row_n.hand_on()
    row_c.start()
    shard_x.relay(2)
    shard_x.relay(3)
    shard_out.relay(0)
    row_n.finish()
    shard_x.finish()
    shard_out.relay(1)

    def project_x(rows):
        out = dot_nn(r.row_normed[rows, :], r.full_x[...])
        r.xr[rows, :] = out[:, :width]
        r.bc[rows, :] = out[:, width : width + 2 * NSTATE]
        r.dtr[rows, :] = out[:, width + 2 * NSTATE :]

    by_rows(tokens, 256, project_x)
    shard_out.relay(2)

    def body(c, carry):
        prepare_steps(c, r)
        scan_chunk(c, r)

        @pl.when(c == 1)
        def _():
            shard_out.relay(3)
            shard_z.relay(0)

        @pl.when(c == 3)
        def _():
            shard_z.relay(1)
            row_c.hand_on()

        @pl.when(c == 5)
        def _():
            shard_z.relay(2)

        return carry

    lax.fori_loop(0, chunks, body, 0)
    shard_z.relay(3)
    row_c.finish()
    shard_out.finish()

    def mix_back(rows):
        r.d_mixed[rows, :] = dot_nn(r.row_cot[rows, :], r.full_out[...])

    by_rows(tokens, 256, mix_back)
    shard_z.finish()

    def project_z(rows):
        r.z[rows, :] = dot_nn(r.row_normed[rows, :], r.full_z[...])

    by_rows(tokens, 256, project_z)

    def gate(c, carry):
        gate_chunk(c, r)
        return carry

    lax.fori_loop(0, chunks, gate, 0)
    sums.start()
    for item in (shard_x, shard_out, shard_z, row_n, row_c):
        item.drain()
    sums.finish()


ONE_IN = ("x_in", "pre_gain", "w_z", "w_x", "w_bc", "w_dt", "w_out", "gain", "cot") + SMALL_IN
ONE_OUT = lambda tokens, features, width: dict(
    row_normed=((tokens, features), BF16),
    row_cot=((tokens, features), BF16),
    full_x=((features, width + 2 * NSTATE + LANES), BF16),
    full_z=((features, width), BF16),
    full_out=((features, width), BF16),
    z=((tokens, width), F32),
    xr=((tokens, width), F32),
    bc=((tokens, 2 * NSTATE), F32),
    dtr=((tokens, LANES), F32),
    y=((tokens, width), F32),
    pre_x=((tokens, width), F32),
    pre_bc=((tokens, 2 * NSTATE), F32),
    maps=((tokens, 2 * NSTATE), BF16),
    states=((tokens, width), BF16),
    step=((tokens, LANES), F32),
    total=((tokens, LANES), F32),
    total_t=((tokens // CHUNK * 16, LANES), F32),
    d_mixed=((tokens, width), F32),
    parts=((4, 2 * (tokens // CHUNK), LANES), F32),
)


def one_kernel(*refs, names, width):
    r = types.SimpleNamespace(**dict(zip(names, refs)))
    r.w = place()
    r.pairs = width // LANES
    r.xr_at = r.bc_at = r.dtr_at = 0
    phase_one(r)


def gather_forward(args, small, width):
    x_in, pre_gain, w_z, w_x, w_bc, w_dt, w_out, gate_gain, cotangent = args
    features = x_in.shape[1]
    tokens = x_in.shape[0] * 4
    outs = ONE_OUT(tokens, features, width)
    scratch = dict(state=((NSTATE, width), F32))
    names = ONE_IN + tuple(outs) + tuple(scratch)
    names = names + ("send_w", "recv_w", "send_r", "recv_r", "send_s", "recv_s")
    values = (
        x_in,
        pre_gain[None, :],
        w_z,
        w_x,
        w_bc,
        jnp.pad(w_dt, ((0, 0), (0, LANES - w_dt.shape[1]))),
        w_out.T,
        gate_gain[None, :],
        cotangent,
    )
    whole = pl.BlockSpec(memory_space=pltpu.VMEM)
    dma = pltpu.SemaphoreType.DMA
    out = pl.pallas_call(
        functools.partial(one_kernel, names=names, width=width),
        out_shape=tuple(jax.ShapeDtypeStruct(*spec) for spec in outs.values()),
        in_specs=[whole] * len(ONE_IN),
        out_specs=tuple([whole] * len(outs)),
        scratch_shapes=[pltpu.VMEM(*spec) for spec in scratch.values()]
        + [dma((3, 4, 4)), dma((3, 8)), dma((2, 4)), dma((2, 4)), dma((3,)), dma((3,))],
        compiler_params=pltpu.CompilerParams(
            vmem_limit_bytes=VMEM_LIMIT, collective_id=0, has_side_effects=True
        ),
        cost_estimate=pl.CostEstimate(
            flops=2 * 10**10, bytes_accessed=1 << 26, transcendentals=0
        ),
    )(*values, *small)
    return types.SimpleNamespace(**dict(zip(outs, out)))


def forward_plain(args, small, width):
    x_in, pre_gain, w_z, w_x, w_bc, w_dt, w_out, gate_gain, cotangent = args
    heads = w_dt.shape[1]
    at = layout_of(width)
    values = x_in.astype(F32)
    scale = lax.rsqrt(jnp.mean(values * values, axis=1) + EPS)
    normed = (values * scale[:, None] * pre_gain[None, :]).astype(BF16)
    row_normed = lax.all_gather(normed, "tensor", axis=0, tiled=True)
    mine = jnp.concatenate(
        (w_z, w_x, w_bc, jnp.pad(w_dt, ((0, 0), (0, LANES - heads)))), axis=1
    )
    stacked = lax.all_gather(mine, "dp", axis=0, tiled=True)
    full_out = lax.all_gather(w_out.T, "dp", axis=0, tiled=True)
    projected = jnp.dot(row_normed, stacked, preferred_element_type=F32)
    saved = mixer_forward(projected, small, width)
    row_cot = lax.all_gather(cotangent, "tensor", axis=0, tiled=True)
    y = saved[0]
    z_raw = projected[:, :width]
    gated = y * (z_raw * sigmoid(z_raw))
    d_mixed = dot_nn(row_cot, full_out)
    squares, cross = lax.psum(
        (
            jnp.sum(gated * gated, axis=1),
            jnp.sum(d_mixed * gate_gain[None, :] * gated, axis=1),
        ),
        "tensor",
    )
    return types.SimpleNamespace(
        row_normed=row_normed,
        row_cot=row_cot,
        full_z=stacked[:, :width],
        full_x=stacked[:, width:],
        full_out=full_out,
        z=z_raw,
        projected=(projected,),
        saved=saved,
        d_mixed=d_mixed,
        squares=squares,
        cross=cross,
    )


def on_device(
    x_in,
    segments,
    pre_gain,
    w_z,
    w_x,
    w_bc,
    w_dt,
    conv_x_w,
    conv_x_b,
    conv_bc_w,
    conv_bc_b,
    a_log,
    dt_bias,
    d_skip,
    gate_gain,
    w_out,
    cotangent,
):
    width = w_z.shape[1]
    heads = a_log.shape[0]
    at = layout_of(width)
    small = small_inputs(
        segments, conv_x_w, conv_x_b, conv_bc_w, conv_bc_b, a_log, dt_bias, d_skip
    )
    args = (x_in, pre_gain, w_z, w_x, w_bc, w_dt, w_out, gate_gain, cotangent)
    if lax.axis_size("dp") == 2 * (LAST_Z + 1) and lax.axis_size("tensor") == 4:
        f = gather_forward(args, small, width)
        f.projected = (f.xr, f.bc, f.dtr)
        f.saved = tuple(getattr(f, name) for name in SAVED)
        squares, cross = jnp.sum(f.parts, axis=0).reshape(2, -1)
    else:
        f = forward_plain(args, small, width)
        squares, cross = f.squares, f.cross
    y, z_raw, d_mixed = f.saved[0], f.z, f.d_mixed
    values = x_in.astype(F32)
    scale = lax.rsqrt(jnp.mean(values * values, axis=1) + EPS)
    gate = sigmoid(z_raw)
    gated = y * (z_raw * gate)
    inner_total = width * lax.axis_size("tensor")
    weighted = d_mixed * gate_gain[None, :]
    scale_two = lax.rsqrt(squares / inner_total + EPS)
    mixed = (gated * scale_two[:, None] * gate_gain[None, :]).astype(BF16)
    branch = lax.psum_scatter(
        dot_nt(mixed, f.full_out).astype(BF16), "tensor", scatter_dimension=0, tiled=True
    ).astype(F32)
    block_out = (values + branch).astype(BF16)
    grad_gate_part = jnp.sum(d_mixed * gated * scale_two[:, None], axis=0)
    d_gated = (
        scale_two[:, None] * weighted
        - gated * (scale_two * scale_two * scale_two * cross / inner_total)[:, None]
    )
    gy = (d_gated * (z_raw * gate)).astype(BF16)
    d_z = (d_gated * y * (gate * (1.0 + z_raw * (1.0 - gate)))).astype(BF16)
    d_rest, g_cxw, g_cxb, g_cbw, g_cbb, g_skip, g_alog, g_dtb = mixer_backward(
        f.projected, small, f.saved, gy, width
    )
    d_proj = jnp.concatenate((d_z, d_rest), axis=1)
    d_normed = lax.psum_scatter(
        (dot_nt(d_z, f.full_z) + dot_nt(d_rest, f.full_x)).astype(BF16),
        "tensor",
        scatter_dimension=0,
        tiled=True,
    ).astype(F32)
    proj_part = dot_tn(f.row_normed, d_proj)
    out_part = dot_tn(f.row_cot, mixed)
    owned = lax.psum_scatter(
        jnp.concatenate((proj_part, out_part), axis=1).astype(BF16),
        "dp",
        scatter_dimension=0,
        tiled=True,
    ).astype(F32)
    grad_w_bc = lax.psum(owned[:, at.bc : at.dt].astype(BF16), "tensor").astype(F32)
    pre_weighted = d_normed * pre_gain[None, :]
    grad_pre_part = jnp.sum(d_normed * values * scale[:, None], axis=0)
    feature_sum = jnp.sum(pre_weighted * values, axis=1)
    grad_x = (
        cotangent.astype(F32)
        + scale[:, None] * pre_weighted
        - values * (scale * scale * scale * feature_sum / values.shape[1])[:, None]
    ).astype(BF16)
    over_taps = lambda v: jnp.sum(v.reshape(4, 8, v.shape[1]), axis=1)
    over_rows = lambda v: jnp.sum(v, axis=0)
    grad_gate_gain, grad_cxw, grad_cxb, grad_alog, grad_dtb, grad_skip = lax.psum(
        (
            grad_gate_part,
            over_taps(g_cxw),
            over_rows(g_cxb),
            over_rows(g_alog)[:heads],
            over_rows(g_dtb)[:heads],
            jnp.sum(over_rows(g_skip).reshape(heads, HEADDIM), axis=1),
        ),
        "dp",
    )
    grad_pre_gain, grad_cbw, grad_cbb = lax.psum(
        (grad_pre_part, over_taps(g_cbw), over_rows(g_cbb)), ("dp", "tensor")
    )
    return (
        block_out,
        grad_x,
        grad_pre_gain,
        owned[:, :width],
        owned[:, width : at.bc],
        grad_w_bc,
        owned[:, at.dt : at.dt + heads],
        grad_cxw,
        grad_cxb,
        grad_cbw,
        grad_cbb,
        grad_alog,
        grad_dtb,
        grad_skip,
        grad_gate_gain,
        owned[:, at.all :].T,
    )


def solution(mesh):
    tokens = P(("dp", "tensor"), None)
    both = P("dp", "tensor")
    heads = P("tensor")
    return jax.shard_map(
        on_device,
        mesh=mesh,
        in_specs=(
            tokens,
            P("dp"),
            P(),
            both,
            both,
            P("dp", None),
            both,
            P(None, "tensor"),
            heads,
            P(),
            P(),
            heads,
            heads,
            heads,
            heads,
            P("tensor", "dp"),
            tokens,
        ),
        out_specs=(
            tokens,
            tokens,
            P(),
            both,
            both,
            P("dp", None),
            both,
            P(None, "tensor"),
            heads,
            P(),
            P(),
            heads,
            heads,
            heads,
            heads,
            P("tensor", "dp"),
        ),
        check_vma=False,
    )
```

```python
import functools
import types

import jax
import jax.numpy as jnp
from jax import lax
from jax.experimental import pallas as pl
from jax.experimental.pallas import tpu as pltpu
from jax.sharding import PartitionSpec as P

HEADDIM = 64
NSTATE = 128
CHUNK = 128
LANES = 128
EPS = 1e-05
LOG2E = 1.4426950408889634
F32 = jnp.float32
BF16 = jnp.bfloat16
VMEM_LIMIT = 62 * 1024 * 1024
exact = lax.Precision.HIGHEST


def dot_nn(a, b):
    return lax.dot_general(a, b, (((1,), (0,)), ((), ())), preferred_element_type=F32)


def dot_nt(a, b):
    return lax.dot_general(a, b, (((1,), (1,)), ((), ())), preferred_element_type=F32)


def dot_tn(a, b):
    return lax.dot_general(a, b, (((0,), (0,)), ((), ())), preferred_element_type=F32)


def sigmoid(v):
    return 1.0 / (1.0 + jnp.exp(-v))


def softplus(v):
    return jnp.maximum(v, 0.0) + jnp.log1p(jnp.exp(-jnp.abs(v)))


def fold_rows(v):
    return jnp.sum(v.reshape(v.shape[0] // 8, 8, v.shape[1]), axis=0)


def split_two(v):
    high = v.astype(BF16)
    return high, (v - high.astype(F32)).astype(BF16)


def tile_iotas():
    shape = (CHUNK, LANES)
    return lax.broadcasted_iota(jnp.int32, shape, 0), lax.broadcasted_iota(jnp.int32, shape, 1)


def chunk_rows(c, pad=0, extra=0):
    return pl.ds(pl.multiple_of(c * CHUNK + pad, 8), CHUNK + extra)


def prepare_steps(c, r):
    row, col = tile_iotas()
    rows = chunk_rows(c)
    lower = (row >= col).astype(F32)
    step = softplus(r.dtr[rows, r.dtr_at : r.dtr_at + LANES] + r.dt_bias[...])
    log_step = step * (-jnp.exp(r.a_log[...]) * LOG2E)
    total = jnp.dot(lower, log_step, precision=exact, preferred_element_type=F32)
    r.step[rows, :] = step
    r.total[rows, :] = total
    r.total_t[pl.ds(pl.multiple_of(c * 16, 16), 16), :] = total.T[:16]


def segment_parts(c, r):
    down = r.seg_down[chunk_rows(c, 8), :]
    across = r.seg_across[pl.ds(c, 1), :]
    before = r.seg_down[pl.ds(pl.multiple_of(c * CHUNK, 8), 8), :][7:8, :]
    last = down[CHUNK - 1 : CHUNK, :]
    carried = (down == before).astype(F32)
    to_end = (down == last).astype(F32)
    carry_on = (last == before).astype(F32)
    return down, across, carried, to_end, carry_on


def masks_back(c, r, down):
    window = r.seg_down[chunk_rows(c, 0, 8), :]
    return [
        (pltpu.roll(window, j, 0)[8 : 8 + CHUNK] == down).astype(F32) for j in range(1, 4)
    ]


def masks_ahead(c, r, down):
    window = r.seg_down[chunk_rows(c, 8, 8), :]
    full = CHUNK + 8
    return [(pltpu.roll(window, full - j, 0)[:CHUNK] == down).astype(F32) for j in range(1, 4)]


def conv_tile(c, ref, at, weight, bias, w_at, masks):
    lanes = slice(at, at + LANES)
    w_lanes = slice(w_at, w_at + LANES)
    here = ref[chunk_rows(c), lanes]
    ahead = ref[pl.ds(pl.multiple_of(jnp.maximum(c * CHUNK - 8, 0), 8), 8), lanes]
    window = jnp.concatenate([ahead, here], axis=0)
    out = here * weight[3:4, w_lanes] + bias[0:1, w_lanes]
    for j in range(1, 4):
        shifted = pltpu.roll(window, j, 0)[8 : 8 + CHUNK]
        out = out + (shifted * masks[j - 1]) * weight[3 - j : 4 - j, w_lanes]
    return out


def pair_columns(tile, p, first):
    left = jnp.broadcast_to(tile[:, 2 * p : 2 * p + 1], (CHUNK, LANES))
    right = jnp.broadcast_to(tile[:, 2 * p + 1 : 2 * p + 2], (CHUNK, LANES))
    return left, right, jnp.where(first, left, right)


def stack_heads(tile, first):
    zero = jnp.zeros_like(tile)
    return jnp.concatenate([jnp.where(first, tile, zero), jnp.where(first, zero, tile)], axis=0)


def scan_chunk(c, r):
    rows = chunk_rows(c)
    row, col = tile_iotas()
    down, across, carried, to_end, carry_on = segment_parts(c, r)
    masks = masks_back(c, r, down)
    maps = []
    for half in range(2):
        pre = conv_tile(c, r.bc, r.bc_at + half * LANES, r.cbw, r.cbb, half * LANES, masks)
        r.pre_bc[rows, half * LANES : (half + 1) * LANES] = pre
        maps.append((pre * sigmoid(pre)).astype(BF16))
    b_map, c_map = maps
    r.maps[rows, :LANES] = b_map
    r.maps[rows, LANES:] = c_map
    scores = jnp.where((down == across) & (row >= col), dot_nt(c_map, b_map), 0.0)
    b_turned = b_map.T
    total = r.total[rows, :]
    step = r.step[rows, :]
    first = col < HEADDIM
    for p in range(r.pairs):
        lanes = slice(p * LANES, (p + 1) * LANES)
        pre = conv_tile(c, r.xr, r.xr_at + p * LANES, r.cxw, r.cxb, p * LANES, masks)
        r.pre_x[rows, lanes] = pre
        chan = pre * sigmoid(pre)
        left, right, both = pair_columns(total, p, first)
        _, _, step_pair = pair_columns(step, p, first)
        fed = step_pair * chan
        stacked = stack_heads(fed.astype(BF16), first)
        mixing = []
        for k, mine in enumerate((left, right)):
            other = r.total_t[pl.ds(c * 16 + 2 * p + k, 1), :]
            mixing.append((scores * jnp.exp2(jnp.minimum(mine - other, 0.0))).astype(BF16))
        within = dot_nn(jnp.concatenate(mixing, axis=1), stacked)
        state = r.state[:, lanes]
        state_low = state.astype(BF16)
        r.states[rows, lanes] = state_low
        decay_in = jnp.exp2(both) * carried
        r.y[rows, lanes] = (
            within + decay_in * dot_nn(c_map, state_low) + r.skip[0:1, lanes] * chan
        )
        last = both[CHUNK - 1 : CHUNK, :]
        decay_out = jnp.exp2(last - both) * to_end
        r.state[:, lanes] = (jnp.exp2(last) * carry_on) * state + dot_nn(
            b_turned, (decay_out * fed).astype(BF16)
        )


def scan_chunk_back(c, r):
    rows = chunk_rows(c)
    row, col = tile_iotas()
    down, across, carried, to_end, carry_on = segment_parts(c, r)
    ahead = masks_ahead(c, r, down)
    b_map = r.maps[rows, :LANES]
    c_map = r.maps[rows, LANES:]
    visible = (down == across) & (row <= col)
    scores = jnp.where(visible, dot_nt(b_map, c_map), 0.0)
    c_turned = c_map.T
    total = r.total[rows, :]
    step = r.step[rows, :]
    first = col < HEADDIM
    d_scores = jnp.zeros((CHUNK, LANES), F32)
    width = r.pairs * LANES
    for p in range(r.pairs):
        lanes = slice(p * LANES, (p + 1) * LANES)
        lows = slice(width + p * LANES, width + (p + 1) * LANES)
        gy_low = r.gy[rows, lanes]
        gy = gy_low.astype(F32)
        pre = r.pre_x[rows, lanes]
        gate = sigmoid(pre)
        chan = pre * gate
        left, right, both = pair_columns(total, p, first)
        _, _, step_pair = pair_columns(step, p, first)
        fed = step_pair * chan
        fed_low = fed.astype(BF16)
        d_mixing = dot_nt(stack_heads(fed_low, first), gy_low)
        mixing = []
        for k, mine in enumerate((left, right)):
            other = r.total_t[pl.ds(c * 16 + 2 * p + k, 1), :]
            decay = jnp.exp2(jnp.minimum(other - mine, 0.0))
            mixing.append((scores * decay).astype(BF16))
            d_scores = d_scores + d_mixing[k * CHUNK : (k + 1) * CHUNK] * decay
        d_state = r.d_state[:, lanes]
        d_state_low = d_state.astype(BF16)
        last = both[CHUNK - 1 : CHUNK, :]
        decay_out = jnp.exp2(last - both) * to_end
        from_state = decay_out * dot_nn(b_map, d_state_low)
        d_fed = dot_nn(jnp.concatenate(mixing, axis=1), stack_heads(gy_low, first)) + from_state
        fed_held = fed_low.astype(F32)
        skip = r.skip[0:1, lanes]
        flow = gy * (r.y[rows, lanes] - skip * chan) - fed_held * d_fed
        direct = chan * d_fed
        for k, part in enumerate((flow, direct)):
            spot = slice(k * CHUNK, (k + 1) * CHUNK)
            r.sums[spot, lanes], r.sums[spot, lows] = split_two(part)
        keep = jnp.exp2(last) * carry_on
        through = jnp.sum(fed_held * from_state, axis=0, keepdims=True) + keep * jnp.sum(
            r.states[rows, lanes].astype(F32) * d_state, axis=0, keepdims=True
        )
        spot = slice(2 * CHUNK, 2 * CHUNK + 16)
        r.sums[spot, lanes], r.sums[spot, lows] = split_two(
            jnp.broadcast_to(through, (16, LANES))
        )
        grad_in = (jnp.exp2(both) * carried * gy).astype(BF16)
        r.grad_in[:, lanes] = grad_in
        r.fed_out[:, lanes] = (decay_out * fed).astype(BF16)
        r.d_state_low[:, lanes] = d_state_low
        r.d_state[:, lanes] = keep * d_state + dot_nn(c_turned, grad_in)
        d_chan = skip * gy + step_pair * d_fed
        r.g_skip[:, lanes] += fold_rows(gy * chan)
        d_pre = d_chan * (gate * (1.0 + pre * (1.0 - gate)))
        conv_back(c, r, d_pre, r.d_pre_x, r.xr, r.xr_at, r.cxw, p * LANES, ahead, r.dx_at, r.g_cxw, r.g_cxb)
    d_scores_low = jnp.where(visible, d_scores, 0.0).astype(BF16)
    d_b = dot_nn(d_scores_low, c_map) + dot_nt(r.fed_out[...], r.d_state_low[...])
    d_c = dot_tn(d_scores_low, b_map) + dot_nt(r.grad_in[...], r.states[rows, :])
    for half, d_map in enumerate((d_b, d_c)):
        pre = r.pre_bc[rows, half * LANES : (half + 1) * LANES]
        gate = sigmoid(pre)
        d_pre = d_map * (gate * (1.0 + pre * (1.0 - gate)))
        conv_back(
            c, r, d_pre, r.d_pre_bc, r.bc, r.bc_at, r.cbw, half * LANES, ahead, r.dbc_at, r.g_cbw, r.g_cbb
        )
    reduced = dot_nn(r.sums[...], r.head_sum[...])
    d_total = jnp.dot(
        (row <= col).astype(F32), reduced[:CHUNK], precision=exact, preferred_element_type=F32
    ) + reduced[2 * CHUNK : 2 * CHUNK + 1]
    a_neg = -jnp.exp(r.a_log[...])
    d_step = reduced[CHUNK : 2 * CHUNK] + a_neg * d_total
    r.g_alog[...] += fold_rows(step * d_total) * a_neg
    d_raw = d_step * sigmoid(r.dtr[rows, r.dtr_at : r.dtr_at + LANES] + r.dt_bias[...])
    r.g_dtb[...] += fold_rows(d_raw)
    r.d_proj[rows, r.ddt_at : r.ddt_at + LANES] = d_raw.astype(BF16)


def conv_back(c, r, d_pre, held, raw, raw_at, weight, at, ahead, out_at, g_w, g_b):
    lanes = slice(at, at + LANES)
    rows = chunk_rows(c)
    held[CHUNK : CHUNK + 8, lanes] = held[0:8, lanes]
    held[0:CHUNK, lanes] = d_pre
    window = held[:, lanes]
    values = raw[rows, raw_at + at : raw_at + at + LANES]
    g_b[:, lanes] += fold_rows(d_pre)
    g_w[24:32, lanes] += fold_rows(d_pre * values)
    d_raw = d_pre * weight[3:4, lanes]
    for j in range(1, 4):
        shifted = pltpu.roll(window, CHUNK + 8 - j, 0)[:CHUNK] * ahead[j - 1]
        d_raw = d_raw + shifted * weight[3 - j : 4 - j, lanes]
        g_w[(3 - j) * 8 : (4 - j) * 8, lanes] += fold_rows(shifted * values)
    r.d_proj[rows, out_at + at : out_at + at + LANES] = d_raw.astype(BF16)


def head_sum_matrix(width):
    shape = (2 * width, LANES)
    lane = lax.broadcasted_iota(jnp.int32, shape, 0)
    lane = jnp.where(lane >= width, lane - width, lane)
    return (lane // HEADDIM == lax.broadcasted_iota(jnp.int32, shape, 1)).astype(BF16)


def layout_of(width):
    return types.SimpleNamespace(
        x=width, bc=2 * width, dt=2 * width + 2 * NSTATE, all=2 * width + 2 * NSTATE + LANES
    )


SMALL_IN = ("seg_down", "seg_across", "cxw", "cxb", "cbw", "cbb", "a_log", "dt_bias", "skip")


def small_inputs(segments, cxw, cxb, cbw, cbb, a_log, dt_bias, d_skip):
    tokens = segments.shape[0]
    seg = segments.astype(F32)
    edge = jnp.full((8,), -1.0, F32)
    down = jnp.broadcast_to(jnp.concatenate([edge, seg, edge])[:, None], (tokens + 16, LANES))
    heads = a_log.shape[0]
    pad = lambda v: jnp.pad(v, (0, LANES - heads))[None, :]
    return (
        down,
        seg.reshape(tokens // CHUNK, CHUNK),
        cxw,
        cxb[None, :],
        cbw,
        cbb[None, :],
        pad(a_log),
        pad(dt_bias),
        jnp.repeat(d_skip, HEADDIM)[None, :],
    )


def take_projections(r, width):
    r.pairs = width // LANES
    if hasattr(r, "proj"):
        at = layout_of(width)
        r.xr = r.bc = r.dtr = r.proj
        r.xr_at, r.bc_at, r.dtr_at = at.x, at.bc, at.dt
    else:
        r.xr_at = r.bc_at = r.dtr_at = 0


def forward_kernel(*refs, names, width):
    r = types.SimpleNamespace(**dict(zip(names, refs)))
    take_projections(r, width)
    chunks = r.dtr.shape[0] // CHUNK
    r.state[...] = jnp.zeros_like(r.state)

    def body(c, carry):
        prepare_steps(c, r)
        scan_chunk(c, r)
        return carry

    lax.fori_loop(0, chunks, body, 0)


def backward_kernel(*refs, names, width):
    r = types.SimpleNamespace(**dict(zip(names, refs)))
    take_projections(r, width)
    r.dx_at, r.dbc_at, r.ddt_at = 0, width, width + 2 * NSTATE
    start_back(r)
    chunks = r.dtr.shape[0] // CHUNK

    def body(i, carry):
        scan_chunk_back(chunks - 1 - i, r)
        return carry

    lax.fori_loop(0, chunks, body, 0)


def start_back(r):
    for ref in (r.d_state, r.d_pre_x, r.d_pre_bc, r.g_cxw, r.g_cxb, r.g_cbw, r.g_cbb):
        ref[...] = jnp.zeros_like(ref)
    for ref in (r.g_skip, r.g_alog, r.g_dtb):
        ref[...] = jnp.zeros_like(ref)
    r.head_sum[...] = head_sum_matrix(r.pairs * LANES)


def call_local(kernel, width, ins, outs, scratch, values, flops):
    names = tuple(ins) + tuple(outs) + tuple(scratch)
    whole = pl.BlockSpec(memory_space=pltpu.VMEM)
    return pl.pallas_call(
        functools.partial(kernel, names=names, width=width),
        out_shape=tuple(jax.ShapeDtypeStruct(*spec) for spec in outs.values()),
        in_specs=[whole] * len(ins),
        out_specs=tuple([whole] * len(outs)),
        scratch_shapes=[pltpu.VMEM(*spec) for spec in scratch.values()],
        compiler_params=pltpu.CompilerParams(vmem_limit_bytes=VMEM_LIMIT),
        cost_estimate=pl.CostEstimate(flops=flops, bytes_accessed=1 << 24, transcendentals=0),
    )(*values)


def mixer_forward(projected, small, width):
    tokens = projected.shape[0]
    outs = dict(
        y=((tokens, width), F32),
        pre_x=((tokens, width), F32),
        pre_bc=((tokens, 2 * NSTATE), F32),
        maps=((tokens, 2 * NSTATE), BF16),
        states=((tokens, width), BF16),
        step=((tokens, LANES), F32),
        total=((tokens, LANES), F32),
        total_t=((tokens // CHUNK * 16, LANES), F32),
    )
    scratch = dict(state=((NSTATE, width), F32))
    return call_local(
        forward_kernel, width, ("proj",) + SMALL_IN, outs, scratch, (projected,) + small, 10**10
    )


BACK_SCRATCH = lambda width: dict(
    d_state=((NSTATE, width), F32),
    d_state_low=((NSTATE, width), BF16),
    grad_in=((CHUNK, width), BF16),
    fed_out=((CHUNK, width), BF16),
    sums=((2 * CHUNK + 16, 2 * width), BF16),
    head_sum=((2 * width, LANES), BF16),
    d_pre_x=((CHUNK + 8, width), F32),
    d_pre_bc=((CHUNK + 8, 2 * NSTATE), F32),
)
GRAD_OUT = lambda width: dict(
    g_cxw=((32, width), F32),
    g_cxb=((8, width), F32),
    g_cbw=((32, 2 * NSTATE), F32),
    g_cbb=((8, 2 * NSTATE), F32),
    g_skip=((8, width), F32),
    g_alog=((8, LANES), F32),
    g_dtb=((8, LANES), F32),
)


SAVED = ("y", "pre_x", "pre_bc", "maps", "states", "step", "total", "total_t")


def mixer_backward(projected, small, saved, gy, width):
    tokens = gy.shape[0]
    outs = dict(d_proj=((tokens, width + 2 * NSTATE + LANES), BF16), **GRAD_OUT(width))
    ins = (("proj",) if len(projected) == 1 else ("xr", "bc", "dtr")) + SMALL_IN
    ins = ins + SAVED + ("gy",)
    return call_local(
        backward_kernel,
        width,
        ins,
        outs,
        BACK_SCRATCH(width),
        tuple(projected) + small + tuple(saved) + (gy,),
        3 * 10**10,
    )


UP, DOWN, PAIR_LOW, PAIR_HIGH = range(4)
LAST_Z = 3


def place():
    dp = lax.axis_index("dp")
    tp = lax.axis_index("tensor")
    z = dp // 2
    core = dp - 2 * z
    y = tp // 2
    x = tp - 2 * y
    return types.SimpleNamespace(
        dp=dp,
        tp=tp,
        z=z,
        core=core,
        mate=dp + 1 - 2 * core,
        near_x=y * 2 + (1 - x),
        near_y=(1 - y) * 2 + x,
        across=(1 - y) * 2 + (1 - x),
    )


def device(w, dp=None, tp=None):
    return {"dp": w.dp if dp is None else dp, "tensor": w.tp if tp is None else tp}


def other_z(w, k):
    return lax.rem(w.z + k, LAST_Z + 1) * 2 + w.core


def peers(w):
    rows = [device(w, tp=t) for t in (w.near_x, w.near_y, w.across)]
    return rows + [device(w, dp=w.mate)] + [device(w, dp=other_z(w, k)) for k in (1, 2, 3)]


def tell(sem, where):
    pl.semaphore_signal(sem, inc=1, device_id=where, device_id_type=pl.DeviceIdType.MESH)


def greet(w):
    barrier = pltpu.get_barrier_semaphore()
    for where in peers(w):
        tell(barrier, where)
    pl.semaphore_wait(barrier, len(peers(w)))


def remote(src, dst, send, recv, where):
    return pltpu.make_async_remote_copy(
        src_ref=src,
        dst_ref=dst,
        send_sem=send,
        recv_sem=recv,
        device_id=where,
        device_id_type=pl.DeviceIdType.MESH,
    )


class LineGather:
    def __init__(self, w, ref, send, recv):
        self.w, self.ref, self.send, self.recv = w, ref, send, recv
        self.rows = ref.shape[0] // (2 * (LAST_Z + 1))

    def shard(self, z, core):
        start = pl.multiple_of((z * 2 + core) * self.rows, 16)
        return self.ref.at[pl.ds(start, self.rows)]

    def copy(self, z, step, kind):
        w = self.w
        part = self.shard(z, w.core)
        to = {UP: w.dp + 2, DOWN: w.dp - 2}.get(kind, w.mate)
        return remote(
            part,
            part,
            self.send.at[step, kind],
            self.recv.at[z * 2 + w.core],
            device(w, dp=to),
        )

    def arrived(self, z, core):
        part = self.shard(z, core)
        remote(
            part, part, self.send.at[0, 0], self.recv.at[z * 2 + core], device(self.w)
        ).wait_recv()

    def relay(self, step, act=None):
        w = self.w
        do = act or (lambda copy: copy.start())

        def low():
            z = w.z - step
            if act is None and step > 0:
                self.arrived(z, w.core)
            pl.when(w.z < LAST_Z)(lambda: do(self.copy(z, step, UP)))
            if step == 0:
                pl.when(w.z > 0)(lambda: do(self.copy(z, step, DOWN)))
            do(self.copy(z, step, PAIR_LOW))

        def high():
            z = w.z + step
            if act is None:
                self.arrived(z, w.core)
            pl.when(w.z > 0)(lambda: do(self.copy(z, step, DOWN)))
            do(self.copy(z, step, PAIR_HIGH))

        if step == 0:
            low()
        else:
            pl.when(w.z >= step)(low)
            pl.when(w.z <= LAST_Z - step)(high)

    def finish(self):
        for z in range(LAST_Z + 1):
            self.arrived(z, 1 - self.w.core)

    def drain(self):
        for step in range(LAST_Z + 1):
            self.relay(step, lambda copy: copy.wait_send())


class RowGather:
    def __init__(self, w, ref, send, recv):
        self.w, self.ref, self.send, self.recv = w, ref, send, recv
        self.rows = ref.shape[0] // 4

    def block(self, slot, half=None):
        return row_block(self.ref, self.rows, slot, half)

    def copy(self, i):
        w = self.w
        part, to = (
            (self.block(w.tp), w.near_x),
            (self.block(w.tp), w.near_y),
            (self.block(w.near_x, 0), w.near_y),
            (self.block(w.near_y, 1), w.near_x),
        )[i]
        return remote(part, part, self.send.at[i], self.recv.at[i], device(w, tp=to))

    def start(self):
        for i in range(2):
            self.copy(i).start()

    def hand_on(self):
        for i in range(2):
            self.copy(i).wait_recv()
            self.copy(i + 2).start()

    def finish(self):
        for i in range(2, 4):
            self.copy(i).wait_recv()

    def drain(self):
        for i in range(4):
            self.copy(i).wait_send()


def row_block(ref, rows, slot, half=None):
    start = slot * rows
    if half is not None:
        rows = rows // 2
        start = start + half * rows
    return ref.at[pl.ds(pl.multiple_of(start, 16), rows)]


def add_into(ref, other):
    rows = 64 if ref.shape[0] % 64 == 0 else ref.shape[0]

    def body(i, carry):
        here = pl.ds(pl.multiple_of(i * rows, rows), rows)
        ref[here, :] = (ref[here, :].astype(F32) + other[here, :].astype(F32)).astype(BF16)
        return carry

    lax.fori_loop(0, ref.shape[0] // rows, body, 0)


class RowScatter:
    def __init__(self, w, part, far, near, send, recv):
        self.w, self.part, self.far, self.near, self.send, self.recv = w, part, far, near, send, recv
        self.rows = part.shape[0] // 4

    def block(self, slot, half=None):
        return row_block(self.part, self.rows, slot, half)

    def copy(self, i):
        w = self.w
        half = lambda k, h: row_block(self.near.at[k], self.rows, 0, h)
        src, dst, to = (
            (lambda: self.block(w.across, 0), lambda: self.far.at[0], w.near_x),
            (lambda: self.block(w.across, 1), lambda: self.far.at[1], w.near_y),
            (lambda: self.block(w.near_x, 0), lambda: half(0, 0), w.near_x),
            (lambda: self.block(w.near_y, 1), lambda: half(1, 1), w.near_y),
            (lambda: self.block(w.near_x, 1), lambda: half(0, 1), w.near_x),
            (lambda: self.block(w.near_y, 0), lambda: half(1, 0), w.near_y),
        )[i]
        return remote(src(), dst(), self.send.at[i], self.recv.at[i], device(w, tp=to))

    def start(self, *which):
        for i in which:
            self.copy(i).start()

    def hand_on(self):
        w = self.w
        self.copy(1).wait_recv()
        add_into(self.block(w.near_x, 1), self.far.at[1])
        self.copy(4).start()
        self.copy(0).wait_recv()
        add_into(self.block(w.near_y, 0), self.far.at[0])
        self.copy(5).start()

    def finish(self):
        for i in range(2, 6):
            self.copy(i).wait_recv()

    def total(self, here, there):
        total = self.part[there, :].astype(F32)
        return total + self.near[0, here, :].astype(F32) + self.near[1, here, :].astype(F32)

    def drain(self):
        for i in range(6):
            self.copy(i).wait_send()


class LineScatter:
    def __init__(self, w, shard, pair, up, down, send, recv):
        self.w, self.shard, self.pair, self.up, self.down = w, shard, pair, up, down
        self.send, self.recv = send, recv
        self.rows = pair.shape[0] // (LAST_Z + 1)

    def slot(self, ref, i):
        return ref.at[pl.ds(pl.multiple_of(i * self.rows, 16), self.rows)]

    def pair_copy(self, z):
        w = self.w
        return remote(
            self.shard(z, 1 - w.core),
            self.slot(self.pair, z),
            self.send.at[z],
            self.recv.at[z],
            device(w, dp=w.mate),
        )

    def up_copy(self, z):
        return remote(
            self.shard(z, self.w.core),
            self.slot(self.up, z - 1),
            self.send.at[3 + z],
            self.recv.at[3 + z],
            device(self.w, dp=self.w.dp + 2),
        )

    def down_copy(self, z):
        return remote(
            self.shard(z, self.w.core),
            self.slot(self.down, z),
            self.send.at[7 + z],
            self.recv.at[7 + z],
            device(self.w, dp=self.w.dp - 2),
        )

    def pair_add(self):
        def body(z, carry):
            self.pair_copy(z).wait_recv()
            add_into(self.shard(z, self.w.core), self.slot(self.pair, z))
            return carry

        lax.fori_loop(0, LAST_Z + 1, body, 0)

    def launch(self):
        @pl.when(self.w.z == 0)
        def _():
            for z in (3, 2, 1):
                self.up_copy(z).start()

        @pl.when(self.w.z == LAST_Z)
        def _():
            for z in (0, 1, 2):
                self.down_copy(z).start()

    def pass_up(self, z):
        self.up_copy(z).wait_recv()
        add_into(self.shard(z, self.w.core), self.slot(self.up, z - 1))
        self.up_copy(z).start()

    def pass_down(self, z):
        self.down_copy(z).wait_recv()
        add_into(self.shard(z, self.w.core), self.slot(self.down, z))
        self.down_copy(z).start()

    def step(self, k):
        w = self.w
        if k == 0:
            pl.when(w.z == 1)(lambda: self.pass_up(3))
            pl.when(w.z == 2)(lambda: self.pass_down(0))
        else:

            @pl.when(w.z == 1)
            def _():
                self.pass_up(2)
                self.pass_down(0)

            @pl.when(w.z == 2)
            def _():
                self.pass_down(1)
                self.pass_up(3)

    def finish(self, out):
        w = self.w
        out[...] = self.shard(w.z, w.core)[...].astype(F32)

        @pl.when(w.z > 0)
        def _():
            self.up_copy(w.z).wait_recv()
            out[...] += self.slot(self.up, w.z - 1)[...].astype(F32)

        @pl.when(w.z < LAST_Z)
        def _():
            self.down_copy(w.z).wait_recv()
            out[...] += self.slot(self.down, w.z)[...].astype(F32)

    def drain(self):
        w = self.w

        def body(z, carry):
            self.pair_copy(z).wait_send()
            return carry

        lax.fori_loop(0, LAST_Z + 1, body, 0)
        for z in range(1, LAST_Z + 1):
            pl.when(w.z < z)(lambda z=z: self.up_copy(z).wait_send())
        for z in range(LAST_Z):
            pl.when(w.z > z)(lambda z=z: self.down_copy(z).wait_send())


class Exchange:
    def __init__(self, ref, mine, targets, send, recv):
        self.ref, self.mine, self.targets, self.send, self.recv = ref, mine, targets, send, recv

    def copy(self, i):
        part = self.ref.at[self.mine]
        return remote(part, part, self.send.at[i], self.recv.at[i], self.targets[i])

    def start(self):
        for i in range(len(self.targets)):
            self.copy(i).start()

    def finish(self):
        for i in range(len(self.targets)):
            self.copy(i).wait()

    def total(self):
        total = self.ref[0].astype(F32)
        for i in range(1, self.ref.shape[0]):
            total = total + self.ref[i].astype(F32)
        return total


def norm_rows(x_ref, gain, out_ref, start):
    rows = 64

    def body(i, carry):
        here = pl.ds(pl.multiple_of(i * rows, rows), rows)
        values = x_ref[here, :].astype(F32)
        scale = lax.rsqrt(jnp.mean(values * values, axis=1, keepdims=True) + EPS)
        there = pl.ds(pl.multiple_of(start + i * rows, 16), rows)
        out_ref[there, :] = (values * scale * gain).astype(BF16)
        return carry

    lax.fori_loop(0, x_ref.shape[0] // rows, body, 0)


def by_rows(total, rows, body):
    def step(i, carry):
        body(pl.ds(pl.multiple_of(i * rows, rows), rows))
        return carry

    lax.fori_loop(0, total // rows, step, 0)


def over_chunks(r, body):
    def step(c, carry):
        body(c)
        return carry

    lax.fori_loop(0, r.chunks, step, 0)


def turned(row):
    return jnp.broadcast_to(row, (CHUNK, LANES)).T


def gated_tile(c, r, p):
    rows, lanes = chunk_rows(c), slice(p * LANES, (p + 1) * LANES)
    z = r.z[rows, lanes]
    gate = sigmoid(z)
    return z, gate, r.y[rows, lanes]


def square_chunk(c, r):
    square = jnp.zeros((CHUNK, LANES), F32)
    for p in range(r.pairs):
        z, gate, y = gated_tile(c, r, p)
        gated = y * (z * gate)
        square = square + gated * gated
    r.squares.at[r.w.tp][pl.ds(c, 1), :] = jnp.sum(square.T, axis=0, keepdims=True)


def cross_chunk(c, r):
    rows = chunk_rows(c)
    cross = jnp.zeros((CHUNK, LANES), F32)
    for p in range(r.pairs):
        lanes = slice(p * LANES, (p + 1) * LANES)
        z, gate, y = gated_tile(c, r, p)
        cross = cross + r.d_mixed[rows, lanes] * r.gain[0:1, lanes] * (y * (z * gate))
    r.crosses.at[r.w.tp][pl.ds(c, 1), :] = jnp.sum(cross.T, axis=0, keepdims=True)


def slot_sum(ref, c):
    total = ref[0, pl.ds(c, 1), :]
    for i in range(1, 4):
        total = total + ref[i, pl.ds(c, 1), :]
    return total


def scale_two_row(c, r):
    return lax.rsqrt(slot_sum(r.squares, c) / (r.pairs * LANES * 4) + EPS)


def mix_chunk(c, r):
    rows = chunk_rows(c)
    scale = turned(scale_two_row(c, r))
    for p in range(r.pairs):
        lanes = slice(p * LANES, (p + 1) * LANES)
        z, gate, y = gated_tile(c, r, p)
        r.mixed[rows, lanes] = (y * (z * gate) * scale * r.gain[0:1, lanes]).astype(BF16)


def gate_back_chunk(c, r):
    rows = chunk_rows(c)
    row = scale_two_row(c, r)
    pull = turned(row * row * row * slot_sum(r.crosses, c) / (r.pairs * LANES * 4))
    scale = turned(row)
    for p in range(r.pairs):
        lanes = slice(p * LANES, (p + 1) * LANES)
        z, gate, y = gated_tile(c, r, p)
        silu = z * gate
        gated = y * silu
        scaled = r.d_mixed[rows, lanes] * scale
        r.g_gate[:, lanes] += fold_rows(scaled * gated)
        d_gated = scaled * r.gain[0:1, lanes] - gated * pull
        r.gy[rows, lanes] = (d_gated * silu).astype(BF16)
        r.d_z[rows, lanes] = (d_gated * y * (gate * (1.0 + z * (1.0 - gate)))).astype(BF16)


def ends_first(i):
    odd = lax.rem(i, 2)
    return (1 - odd) * (LAST_Z - i // 2) + odd * (i // 2)


def weight_parts(left, right, scatter, store):
    block = left.shape[1] // (LAST_Z + 1)

    def body(i, carry):
        z = ends_first(i)
        lanes = pl.ds(pl.multiple_of(z * block, LANES), block)
        store(z, dot_tn(left[:, lanes], right[...]).astype(BF16))
        scatter.pair_copy(z).start()
        return carry

    lax.fori_loop(0, LAST_Z + 1, body, 0)


def flat_shard(ref, rows):
    return lambda z, core: ref.at[pl.ds(pl.multiple_of((z * 2 + core) * rows, 16), rows)]


def flat_store(ref, rows):
    def store(z, value):
        ref[pl.ds(pl.multiple_of(z * 2 * rows, 16), 2 * rows), :] = value

    return store


def side_shard(ref, rows, width):
    return lambda z, core: ref.at[
        pl.ds(pl.multiple_of(z * rows, 16), rows),
        pl.ds(pl.multiple_of(core * width, LANES), width),
    ]


def side_store(ref, rows, width):
    def store(z, value):
        here = pl.ds(pl.multiple_of(z * rows, 16), rows)
        ref[here, :width] = value[:rows]
        ref[here, width : 2 * width] = value[rows:]

    return store


def prepare_inputs(r):
    w, width = r.w, r.pairs * LANES
    heads = r.a_log_in.shape[0]
    shard = r.w_x.shape[0]
    own = pl.ds(pl.multiple_of(w.dp * shard, 16), shard)
    r.full_x[own, :width] = r.w_x[...]
    r.full_x[own, width : width + 2 * NSTATE] = r.w_bc[...]
    r.turn[...] = jnp.zeros_like(r.turn)
    r.turn[0:heads, 0:shard] = r.w_dt[...]
    r.full_x[own, width + 2 * NSTATE :] = r.turn[...].T[:shard]


def prepare_small(r):
    heads = r.a_log_in.shape[0]
    w, width = r.w, r.pairs * LANES
    for ref in (r.a_log, r.dt_bias):
        ref[...] = jnp.zeros_like(ref)
    r.a_log[0:1, 0:heads] = r.a_log_in[...].reshape(1, heads)
    r.dt_bias[0:1, 0:heads] = r.dt_bias_in[...].reshape(1, heads)
    r.cxb[...] = r.cxb_in[...].reshape(1, width)
    r.cbb[...] = r.cbb_in[...].reshape(1, 2 * NSTATE)
    r.gain[...] = r.gain_in[...].reshape(1, width)
    skip = r.d_skip_in[...].reshape(1, heads)
    first = lax.broadcasted_iota(jnp.int32, (1, LANES), 1) < HEADDIM
    for p in range(r.pairs):
        pair = jnp.where(first, skip[:, 2 * p : 2 * p + 1], skip[:, 2 * p + 1 : 2 * p + 2])
        r.skip[:, p * LANES : (p + 1) * LANES] = pair
    r.seg_across[...] = r.segments[...].reshape(r.chunks, CHUNK).astype(F32)
    edge = jnp.full((8, LANES), -1.0, F32)
    r.seg_down[0:8, :] = edge
    r.seg_down[r.chunks * CHUNK + 8 :, :] = edge

    def body(c):
        r.seg_down[chunk_rows(c, 8), :] = turned(r.seg_across[pl.ds(c, 1), :])

    over_chunks(r, body)


def phase_one(r):
    w = r.w
    width = r.pairs * LANES
    tokens = r.row_normed.shape[0]
    block = r.x_in.shape[0]
    start = pl.multiple_of(w.tp * block, block)
    shard = r.w_x.shape[0]
    own = pl.ds(pl.multiple_of(w.dp * shard, 16), shard)
    prepare_inputs(r)
    greet(w)
    r.shard_x.relay(0)
    norm_rows(r.x_in, r.pre_gain[...].reshape(1, r.x_in.shape[1]), r.row_normed, start)
    r.row_n.start()
    moves = [
        pltpu.make_async_copy(src, dst.at[own], r.s_m.at[i])
        for i, (src, dst) in enumerate(((r.w_out, r.full_out), (r.w_z, r.full_z)))
    ]
    for move in moves:
        move.start()
    r.row_cot[pl.ds(start, block), :] = r.cot[...]
    r.state[...] = jnp.zeros_like(r.state)
    prepare_small(r)
    for move in moves:
        move.wait()
    r.shard_x.relay(1)
    r.row_n.hand_on()
    r.row_c.start()
    r.shard_x.relay(2)
    r.shard_x.relay(3)
    r.shard_z.relay(0)
    r.row_n.finish()
    r.shard_x.finish()
    r.shard_z.relay(1)

    def project_x(rows):
        out = dot_nn(r.row_normed[rows, :], r.full_x[...])
        r.xr[rows, :] = out[:, :width]
        r.bc[rows, :] = out[:, width : width + 2 * NSTATE]
        r.dtr[rows, :] = out[:, width + 2 * NSTATE :]

    by_rows(tokens, 256, project_x)
    r.shard_z.relay(2)

    def body(c):
        prepare_steps(c, r)
        scan_chunk(c, r)

        @pl.when(c == 1)
        def _():
            r.shard_z.relay(3)
            r.shard_out.relay(0)

        @pl.when(c == 3)
        def _():
            r.shard_out.relay(1)
            r.row_c.hand_on()

        @pl.when(c == 5)
        def _():
            r.shard_out.relay(2)

    over_chunks(r, body)


def phase_mid(r):
    w = r.w
    tokens = r.row_normed.shape[0]
    r.shard_z.finish()

    def project_z(rows):
        r.z[rows, :] = dot_nn(r.row_normed[rows, :], r.full_z[...])

    by_rows(tokens, 256, project_z)
    over_chunks(r, lambda c: square_chunk(c, r))
    r.ex_squares.start()
    r.shard_out.relay(3)
    r.row_c.finish()
    r.ex_squares.finish()
    over_chunks(r, lambda c: mix_chunk(c, r))
    weight_parts(r.row_cot, r.mixed, r.grad_out, flat_store(r.out_part, r.shard_rows))
    r.shard_out.finish()

    def mix_back(rows):
        r.d_mixed[rows, :] = dot_nn(r.row_cot[rows, :], r.full_out[...])

    by_rows(tokens, 256, mix_back)
    r.grad_out.pair_add()
    r.grad_out.launch()
    over_chunks(r, lambda c: cross_chunk(c, r))
    r.ex_crosses.start()
    block = r.x_in.shape[0]

    def share(slot):
        rows = pl.ds(pl.multiple_of(slot * block, block), block)
        tile = 512

        def body(n, carry):
            cols = pl.ds(pl.multiple_of(n * tile, tile), tile)
            r.part[rows, cols] = dot_nt(r.mixed[rows, :], r.full_out[cols, :]).astype(BF16)
            return carry

        lax.fori_loop(0, r.part.shape[1] // tile, body, 0)

    share(w.across)
    r.out_rows.start(0, 1)
    share(w.near_x)
    r.out_rows.start(2)
    share(w.near_y)
    r.out_rows.start(3)
    share(w.tp)
    r.ex_crosses.finish()
    for item in (r.shard_x, r.shard_z, r.shard_out, r.row_n, r.row_c):
        item.drain()
    r.g_gate[...] = jnp.zeros_like(r.g_gate)
    over_chunks(r, lambda c: gate_back_chunk(c, r))
    r.grad_out.step(0)
    r.out_rows.hand_on()
    tell(r.free_pair, device(w, dp=w.mate))
    pl.semaphore_wait(r.free_pair, 1)
    weight_parts(r.row_normed, r.d_z, r.grad_z, flat_store(r.full_out, r.shard_rows))


def phase_back(r):
    w = r.w
    block = r.x_in.shape[0]
    start_back(r)
    r.grad_z.pair_add()
    tell(r.free_pair, device(w, dp=w.mate))
    r.grad_z.launch()

    def body(i, carry):
        scan_chunk_back(r.chunks - 1 - i, r)

        @pl.when(i == 1)
        def _():
            r.grad_out.step(1)

        @pl.when(i == 3)
        def _():
            r.grad_out.finish(r.o_w_out)
            r.grad_out.drain()
            tell(r.free_line, device(w, dp=other_z(w, 1)))
            tell(r.free_line, device(w, dp=other_z(w, 3)))
            r.grad_z.step(0)

        @pl.when(i == 5)
        def _():
            r.out_rows.finish()
            step = 64

            def add(k, carry):
                here = pl.ds(pl.multiple_of(k * step, step), step)
                there = pl.ds(pl.multiple_of(w.tp * block + k * step, 16), step)
                total = r.x_in[here, :].astype(F32) + r.out_rows.total(here, there)
                r.o_block[here, :] = total.astype(BF16)
                return carry

            lax.fori_loop(0, block // step, add, 0)
            r.out_rows.drain()
            tell(r.free_row, device(w, tp=w.near_x))
            tell(r.free_row, device(w, tp=w.near_y))
            r.grad_z.step(1)

        return carry

    lax.fori_loop(0, r.chunks, body, 0)


def phase_last(r):
    w = r.w
    width = r.pairs * LANES
    block = r.x_in.shape[0]
    weight_parts(
        r.row_normed, r.d_rest.at[:, pl.ds(width, 2 * NSTATE + LANES)], r.grad_bc, flat_store(r.bc_part, r.shard_rows)
    )
    r.g_pre[...] = jnp.zeros_like(r.g_pre)
    pl.semaphore_wait(r.free_row, 2)

    def share(slot):
        rows = pl.ds(pl.multiple_of(slot * block, block), block)
        tile = 512

        def body(n, carry):
            cols = pl.ds(pl.multiple_of(n * tile, tile), tile)
            out = dot_nt(r.d_z[rows, :], r.full_z[cols, :]) + dot_nt(
                r.d_rest[rows, :], r.full_x[cols, :]
            )
            r.part[rows, cols] = out.astype(BF16)
            r.g_pre[:, cols] += fold_rows(out * r.row_normed[rows, cols].astype(F32))
            return carry

        lax.fori_loop(0, r.part.shape[1] // tile, body, 0)

    r.grad_bc.pair_add()
    r.grad_bc.launch()
    share(w.across)
    r.in_rows.start(0, 1)
    share(w.near_x)
    r.in_rows.start(2)
    r.grad_bc.step(0)
    share(w.near_y)
    r.in_rows.start(3)
    share(w.tp)
    pack_small(r)
    r.ex_pair.start()
    r.grad_bc.step(1)
    pl.semaphore_wait(r.free_pair, 1)
    weight_parts(
        r.row_normed,
        r.d_rest.at[:, pl.ds(0, width)],
        r.grad_x_part,
        side_store(r.row_cot, r.shard_rows, width),
    )
    r.grad_z.finish(r.o_w_z)
    r.in_rows.hand_on()
    r.ex_pair.finish()
    r.small_z.at[w.z][...] = r.ex_pair.total()
    r.ex_z.start()
    r.grad_x_part.pair_add()
    pl.semaphore_wait(r.free_line, 2)
    r.grad_x_part.launch()
    r.grad_bc.finish(r.bc_sum)
    r.o_w_dt[...] = r.bc_sum[:, 2 * NSTATE :]
    r.bc_slots.at[w.tp][...] = r.bc_sum[:, : 2 * NSTATE].astype(BF16)
    r.ex_bc.start()
    r.ex_z.finish()
    total = r.ex_z.total()
    r.o_small[...] = total[:SMALL_DP]
    r.small_t.at[w.tp][...] = total[SMALL_DP:]
    r.ex_t.start()
    r.grad_x_part.step(0)
    r.ex_bc.finish()
    r.o_w_bc[...] = r.ex_bc.total()
    r.ex_t.finish()
    r.o_shared[...] = r.ex_t.total()
    r.grad_x_part.step(1)
    r.in_rows.finish()
    gain = r.pre_gain[...].reshape(1, r.x_in.shape[1])
    step = 64

    def body(k, carry):
        here = pl.ds(pl.multiple_of(k * step, step), step)
        there = pl.ds(pl.multiple_of(w.tp * block + k * step, 16), step)
        values = r.x_in[here, :].astype(F32)
        scale = lax.rsqrt(jnp.mean(values * values, axis=1, keepdims=True) + EPS)
        weighted = r.in_rows.total(here, there) * gain
        along = jnp.mean(weighted * values, axis=1, keepdims=True)
        grad = r.cot[here, :].astype(F32) + scale * weighted
        r.o_grad_x[here, :] = (grad - values * (scale * scale * scale * along)).astype(BF16)
        return carry

    lax.fori_loop(0, block // step, body, 0)
    r.grad_x_part.finish(r.o_w_x)
    for item in (r.grad_z, r.grad_bc, r.grad_x_part, r.in_rows):
        item.drain()


SMALL_DP = 48
SMALL_ALL = 24


def pack_small(r):
    mine = r.small_pair.at[r.w.core]
    mine[...] = jnp.zeros_like(mine)

    def put(at, ref, first, count):
        for p in range(count):
            lanes = slice(p * LANES, (p + 1) * LANES)
            mine[at + p : at + p + 1, :] = jnp.sum(
                ref[first : first + 8, lanes], axis=0, keepdims=True
            )
        return at + count

    at = put(0, r.g_gate, 0, r.pairs)
    for k in range(4):
        at = put(at, r.g_cxw, 8 * k, r.pairs)
    at = put(at, r.g_cxb, 0, r.pairs)
    at = put(at, r.g_skip, 0, r.pairs)
    at = put(at, r.g_alog, 0, 1)
    at = put(at, r.g_dtb, 0, 1)
    at = put(SMALL_DP, r.g_pre, 0, r.g_pre.shape[1] // LANES)
    for k in range(4):
        at = put(at, r.g_cbw, 8 * k, 2)
    put(at, r.g_cbb, 0, 2)


RAW_IN = (
    "x_in",
    "segments",
    "pre_gain",
    "w_z",
    "w_x",
    "w_bc",
    "w_dt",
    "cxw",
    "cxb_in",
    "cbw",
    "cbb_in",
    "a_log_in",
    "dt_bias_in",
    "d_skip_in",
    "gain_in",
    "w_out",
    "cot",
)


def whole_kernel(*refs, names, width):
    r = types.SimpleNamespace(**dict(zip(names, refs)))
    r.w = w = place()
    r.pairs = width // LANES
    r.chunks = r.row_normed.shape[0] // CHUNK
    r.shard_rows = r.w_x.shape[0]
    r.xr_at = r.bc_at = r.dtr_at = 0
    r.dx_at, r.dbc_at, r.ddt_at = 0, width, width + 2 * NSTATE
    r.shard_x = LineGather(w, r.full_x, r.s_w.at[0], r.r_w.at[0])
    r.shard_z = LineGather(w, r.full_z, r.s_w.at[1], r.r_w.at[1])
    r.shard_out = LineGather(w, r.full_out, r.s_w.at[2], r.r_w.at[2])
    r.row_n = RowGather(w, r.row_normed, r.s_r.at[0], r.r_r.at[0])
    r.row_c = RowGather(w, r.row_cot, r.s_r.at[1], r.r_r.at[1])
    r.out_rows = RowScatter(w, r.part, r.far, r.near, r.s_q.at[0], r.r_q.at[0])
    r.in_rows = RowScatter(w, r.part, r.far, r.near, r.s_q.at[1], r.r_q.at[1])
    rows = r.shard_rows
    scatter = lambda i, shard, pair, up, down: LineScatter(
        w, shard, pair, up, down, r.s_l.at[i], r.r_l.at[i]
    )
    r.grad_out = scatter(0, flat_shard(r.out_part, rows), r.pair, r.up, r.down)
    r.grad_z = scatter(1, flat_shard(r.full_out, rows), r.pair, r.up_z, r.down_z)
    r.grad_x_part = scatter(3, side_shard(r.row_cot, rows, width), r.pair, r.up, r.down)
    in_row = [device(w, tp=t) for t in (w.near_x, w.near_y, w.across)]
    in_line = [device(w, dp=other_z(w, k)) for k in (1, 2, 3)]
    exchange = lambda i, ref, mine, targets: Exchange(ref, mine, targets, r.s_e.at[i], r.r_e.at[i])
    r.ex_squares = exchange(0, r.squares, w.tp, in_row)
    r.ex_crosses = exchange(1, r.crosses, w.tp, in_row)
    r.ex_pair = exchange(2, r.small_pair, w.core, [device(w, dp=w.mate)])
    r.ex_z = exchange(3, r.small_z, w.z, in_line)
    r.ex_t = exchange(4, r.small_t, w.tp, in_row)
    r.ex_bc = exchange(5, r.bc_slots, w.tp, in_row)
    tokens = r.chunks * CHUNK
    phase_one(r)

    def middle(z, d_mixed, mixed):
        r.z, r.d_mixed, r.mixed = z, d_mixed, mixed
        phase_mid(r)

    pl.run_scoped(
        middle,
        pltpu.VMEM((tokens, width), F32),
        pltpu.VMEM((tokens, width), F32),
        pltpu.VMEM((tokens, width), BF16),
    )
    later = dict(BACK_SCRATCH(width), bc_part=((r.full_x.shape[0], 2 * NSTATE + LANES), BF16))

    def rest(d_rest, *buffers):
        r.d_rest = r.d_proj = d_rest
        for name, buffer in zip(later, buffers):
            setattr(r, name, buffer)
        r.grad_bc = scatter(2, flat_shard(r.bc_part, rows), r.pair_bc, r.up_bc, r.down_bc)
        phase_back(r)
        phase_last(r)

    pl.run_scoped(
        rest,
        pltpu.VMEM((tokens, width + 2 * NSTATE + LANES), BF16),
        *[pltpu.VMEM(*spec) for spec in later.values()],
    )


def whole_call(args, width):
    x_in, w_x = args[0], args[4]
    features, block = x_in.shape[1], x_in.shape[0]
    tokens = block * 4
    shard = w_x.shape[0]
    rest = 2 * NSTATE + LANES
    chunks = tokens // CHUNK
    outs = dict(
        o_block=((block, features), BF16),
        o_grad_x=((block, features), BF16),
        o_w_z=((shard, width), F32),
        o_w_x=((shard, width), F32),
        o_w_bc=((shard, 2 * NSTATE), F32),
        o_w_dt=((shard, LANES), F32),
        o_w_out=((shard, width), F32),
        o_small=((SMALL_DP, LANES), F32),
        o_shared=((SMALL_ALL, LANES), F32),
    )
    scratch = dict(
        row_normed=((tokens, features), BF16),
        row_cot=((tokens, features), BF16),
        full_x=((features, width + rest), BF16),
        full_z=((features, width), BF16),
        full_out=((features, width), BF16),
        xr=((tokens, width), F32),
        bc=((tokens, 2 * NSTATE), F32),
        dtr=((tokens, LANES), F32),
        y=((tokens, width), F32),
        pre_x=((tokens, width), F32),
        pre_bc=((tokens, 2 * NSTATE), F32),
        maps=((tokens, 2 * NSTATE), BF16),
        states=((tokens, width), BF16),
        state=((NSTATE, width), F32),
        step=((tokens, LANES), F32),
        total=((tokens, LANES), F32),
        total_t=((chunks * 16, LANES), F32),
        seg_down=((tokens + 16, LANES), F32),
        seg_across=((chunks, LANES), F32),
        turn=((LANES, 2 * LANES), BF16),
        a_log=((1, LANES), F32),
        dt_bias=((1, LANES), F32),
        cxb=((1, width), F32),
        cbb=((1, 2 * NSTATE), F32),
        gain=((1, width), F32),
        skip=((1, width), F32),
        squares=((4, chunks, LANES), F32),
        crosses=((4, chunks, LANES), F32),
        gy=((tokens, width), BF16),
        d_z=((tokens, width), BF16),
        part=((tokens, features), BF16),
        far=((2, block // 2, features), BF16),
        near=((2, block, features), BF16),
        out_part=((features, width), BF16),
        pair=((4 * shard, width), BF16),
        pair_bc=((4 * shard, rest), BF16),
        up=((3 * shard, width), BF16),
        down=((3 * shard, width), BF16),
        up_z=((3 * shard, width), BF16),
        down_z=((3 * shard, width), BF16),
        up_bc=((3 * shard, rest), BF16),
        down_bc=((3 * shard, rest), BF16),
        bc_sum=((shard, rest), F32),
        bc_slots=((4, shard, 2 * NSTATE), BF16),
        small_pair=((2, SMALL_DP + SMALL_ALL, LANES), F32),
        small_z=((4, SMALL_DP + SMALL_ALL, LANES), F32),
        small_t=((4, SMALL_ALL, LANES), F32),
        g_gate=((8, width), F32),
        g_pre=((8, features), F32),
        **GRAD_OUT(width),
    )
    dma = pltpu.SemaphoreType.DMA
    signal = pltpu.SemaphoreType.REGULAR
    semaphores = dict(
        s_w=dma((3, 4, 4)),
        r_w=dma((3, 8)),
        s_r=dma((2, 4)),
        r_r=dma((2, 4)),
        s_q=dma((2, 6)),
        r_q=dma((2, 6)),
        s_l=dma((4, 10)),
        r_l=dma((4, 10)),
        s_e=dma((6, 3)),
        r_e=dma((6, 3)),
        s_m=dma((2,)),
        free_pair=signal,
        free_line=signal,
        free_row=signal,
    )
    names = RAW_IN + tuple(outs) + tuple(scratch) + tuple(semaphores)
    values = list(args)
    values[6] = values[6].T
    values[15] = values[15].T
    whole = pl.BlockSpec(memory_space=pltpu.VMEM)
    out = pl.pallas_call(
        functools.partial(whole_kernel, names=names, width=width),
        out_shape=tuple(jax.ShapeDtypeStruct(*spec) for spec in outs.values()),
        in_specs=[
            pl.BlockSpec(memory_space=pl.ANY) if name in ("w_z", "w_out") else whole
            for name in RAW_IN
        ],
        out_specs=tuple([whole] * len(outs)),
        scratch_shapes=[pltpu.VMEM(*spec) for spec in scratch.values()]
        + list(semaphores.values()),
        compiler_params=pltpu.CompilerParams(
            vmem_limit_bytes=VMEM_LIMIT, collective_id=0, has_side_effects=True
        ),
        cost_estimate=pl.CostEstimate(
            flops=5 * 10**10, bytes_accessed=1 << 26, transcendentals=0
        ),
    )(*values)
    return types.SimpleNamespace(**dict(zip(outs, out)))


def on_device_whole(*args):
    width = args[3].shape[1]
    heads = args[11].shape[0]
    features = args[0].shape[1]
    o = whole_call(args, width)
    pairs = width // LANES
    small = o.o_small
    rows = lambda at, count: small[at : at + count].reshape(count * LANES)
    taps = small[pairs : 5 * pairs].reshape(4, width)
    skip = jnp.sum(rows(6 * pairs, pairs).reshape(heads, HEADDIM), axis=1)
    shared = o.o_shared.reshape(-1)
    taps_bc = shared[features : features + 4 * 2 * NSTATE].reshape(4, 2 * NSTATE)
    at = features + 4 * 2 * NSTATE
    return (
        o.o_block,
        o.o_grad_x,
        shared[:features] / args[2],
        o.o_w_z,
        o.o_w_x,
        o.o_w_bc,
        o.o_w_dt[:, :heads],
        taps,
        rows(5 * pairs, pairs),
        taps_bc,
        shared[at : at + 2 * NSTATE],
        small[7 * pairs, :heads],
        small[7 * pairs + 1, :heads],
        skip,
        rows(0, pairs),
        o.o_w_out.T,
    )


def forward_plain(args, small, width):
    x_in, pre_gain, w_z, w_x, w_bc, w_dt, w_out, gate_gain, cotangent = args
    heads = w_dt.shape[1]
    at = layout_of(width)
    values = x_in.astype(F32)
    scale = lax.rsqrt(jnp.mean(values * values, axis=1) + EPS)
    normed = (values * scale[:, None] * pre_gain[None, :]).astype(BF16)
    row_normed = lax.all_gather(normed, "tensor", axis=0, tiled=True)
    mine = jnp.concatenate(
        (w_z, w_x, w_bc, jnp.pad(w_dt, ((0, 0), (0, LANES - heads)))), axis=1
    )
    stacked = lax.all_gather(mine, "dp", axis=0, tiled=True)
    full_out = lax.all_gather(w_out.T, "dp", axis=0, tiled=True)
    projected = jnp.dot(row_normed, stacked, preferred_element_type=F32)
    saved = mixer_forward(projected, small, width)
    row_cot = lax.all_gather(cotangent, "tensor", axis=0, tiled=True)
    y = saved[0]
    z_raw = projected[:, :width]
    gated = y * (z_raw * sigmoid(z_raw))
    d_mixed = dot_nn(row_cot, full_out)
    squares, cross = lax.psum(
        (
            jnp.sum(gated * gated, axis=1),
            jnp.sum(d_mixed * gate_gain[None, :] * gated, axis=1),
        ),
        "tensor",
    )
    return types.SimpleNamespace(
        row_normed=row_normed,
        row_cot=row_cot,
        full_z=stacked[:, :width],
        full_x=stacked[:, width:],
        full_out=full_out,
        z=z_raw,
        projected=(projected,),
        saved=saved,
        d_mixed=d_mixed,
        squares=squares,
        cross=cross,
    )


def on_device(
    x_in,
    segments,
    pre_gain,
    w_z,
    w_x,
    w_bc,
    w_dt,
    conv_x_w,
    conv_x_b,
    conv_bc_w,
    conv_bc_b,
    a_log,
    dt_bias,
    d_skip,
    gate_gain,
    w_out,
    cotangent,
):
    width = w_z.shape[1]
    heads = a_log.shape[0]
    at = layout_of(width)
    small = small_inputs(
        segments, conv_x_w, conv_x_b, conv_bc_w, conv_bc_b, a_log, dt_bias, d_skip
    )
    args = (x_in, pre_gain, w_z, w_x, w_bc, w_dt, w_out, gate_gain, cotangent)
    f = forward_plain(args, small, width)
    squares, cross = f.squares, f.cross
    y, z_raw, d_mixed = f.saved[0], f.z, f.d_mixed
    values = x_in.astype(F32)
    scale = lax.rsqrt(jnp.mean(values * values, axis=1) + EPS)
    gate = sigmoid(z_raw)
    gated = y * (z_raw * gate)
    inner_total = width * lax.axis_size("tensor")
    weighted = d_mixed * gate_gain[None, :]
    scale_two = lax.rsqrt(squares / inner_total + EPS)
    mixed = (gated * scale_two[:, None] * gate_gain[None, :]).astype(BF16)
    branch = lax.psum_scatter(
        dot_nt(mixed, f.full_out).astype(BF16), "tensor", scatter_dimension=0, tiled=True
    ).astype(F32)
    block_out = (values + branch).astype(BF16)
    grad_gate_part = jnp.sum(d_mixed * gated * scale_two[:, None], axis=0)
    d_gated = (
        scale_two[:, None] * weighted
        - gated * (scale_two * scale_two * scale_two * cross / inner_total)[:, None]
    )
    gy = (d_gated * (z_raw * gate)).astype(BF16)
    d_z = (d_gated * y * (gate * (1.0 + z_raw * (1.0 - gate)))).astype(BF16)
    d_rest, g_cxw, g_cxb, g_cbw, g_cbb, g_skip, g_alog, g_dtb = mixer_backward(
        f.projected, small, f.saved, gy, width
    )
    d_proj = jnp.concatenate((d_z, d_rest), axis=1)
    d_normed = lax.psum_scatter(
        (dot_nt(d_z, f.full_z) + dot_nt(d_rest, f.full_x)).astype(BF16),
        "tensor",
        scatter_dimension=0,
        tiled=True,
    ).astype(F32)
    proj_part = dot_tn(f.row_normed, d_proj)
    out_part = dot_tn(f.row_cot, mixed)
    owned = lax.psum_scatter(
        jnp.concatenate((proj_part, out_part), axis=1).astype(BF16),
        "dp",
        scatter_dimension=0,
        tiled=True,
    ).astype(F32)
    grad_w_bc = lax.psum(owned[:, at.bc : at.dt].astype(BF16), "tensor").astype(F32)
    pre_weighted = d_normed * pre_gain[None, :]
    grad_pre_part = jnp.sum(d_normed * values * scale[:, None], axis=0)
    feature_sum = jnp.sum(pre_weighted * values, axis=1)
    grad_x = (
        cotangent.astype(F32)
        + scale[:, None] * pre_weighted
        - values * (scale * scale * scale * feature_sum / values.shape[1])[:, None]
    ).astype(BF16)
    over_taps = lambda v: jnp.sum(v.reshape(4, 8, v.shape[1]), axis=1)
    over_rows = lambda v: jnp.sum(v, axis=0)
    grad_gate_gain, grad_cxw, grad_cxb, grad_alog, grad_dtb, grad_skip = lax.psum(
        (
            grad_gate_part,
            over_taps(g_cxw),
            over_rows(g_cxb),
            over_rows(g_alog)[:heads],
            over_rows(g_dtb)[:heads],
            jnp.sum(over_rows(g_skip).reshape(heads, HEADDIM), axis=1),
        ),
        "dp",
    )
    grad_pre_gain, grad_cbw, grad_cbb = lax.psum(
        (grad_pre_part, over_taps(g_cbw), over_rows(g_cbb)), ("dp", "tensor")
    )
    return (
        block_out,
        grad_x,
        grad_pre_gain,
        owned[:, :width],
        owned[:, width : at.bc],
        grad_w_bc,
        owned[:, at.dt : at.dt + heads],
        grad_cxw,
        grad_cxb,
        grad_cbw,
        grad_cbb,
        grad_alog,
        grad_dtb,
        grad_skip,
        grad_gate_gain,
        owned[:, at.all :].T,
    )


def solution(mesh):
    tokens = P(("dp", "tensor"), None)
    both = P("dp", "tensor")
    heads = P("tensor")
    line = mesh.shape["dp"] == 2 * (LAST_Z + 1) and mesh.shape["tensor"] == 4
    return jax.shard_map(
        on_device_whole if line else on_device,
        mesh=mesh,
        in_specs=(
            tokens,
            P("dp"),
            P(),
            both,
            both,
            P("dp", None),
            both,
            P(None, "tensor"),
            heads,
            P(),
            P(),
            heads,
            heads,
            heads,
            heads,
            P("tensor", "dp"),
            tokens,
        ),
        out_specs=(
            tokens,
            tokens,
            P(),
            both,
            both,
            P("dp", None),
            both,
            P(None, "tensor"),
            heads,
            P(),
            P(),
            heads,
            heads,
            heads,
            heads,
            P("tensor", "dp"),
        ),
        check_vma=False,
    )
```

```python
import functools
import types

import jax
import jax.numpy as jnp
from jax import lax
from jax.experimental import pallas as pl
from jax.experimental.pallas import tpu as pltpu
from jax.sharding import PartitionSpec as P

HEADDIM = 64
NSTATE = 128
CHUNK = 128
LANES = 128
EPS = 1e-05
LOG2E = 1.4426950408889634
F32 = jnp.float32
BF16 = jnp.bfloat16
VMEM_LIMIT = 62 * 1024 * 1024
exact = lax.Precision.HIGHEST


def dot_nn(a, b):
    return lax.dot_general(a, b, (((1,), (0,)), ((), ())), preferred_element_type=F32)


def dot_nt(a, b):
    return lax.dot_general(a, b, (((1,), (1,)), ((), ())), preferred_element_type=F32)


def dot_tn(a, b):
    return lax.dot_general(a, b, (((0,), (0,)), ((), ())), preferred_element_type=F32)


def sigmoid(v):
    return 1.0 / (1.0 + jnp.exp(-v))


def softplus(v):
    return jnp.maximum(v, 0.0) + jnp.log1p(jnp.exp(-jnp.abs(v)))


def fold_rows(v):
    return jnp.sum(v.reshape(v.shape[0] // 8, 8, v.shape[1]), axis=0)


def split_two(v):
    high = v.astype(BF16)
    return high, (v - high.astype(F32)).astype(BF16)


def tile_iotas():
    shape = (CHUNK, LANES)
    return lax.broadcasted_iota(jnp.int32, shape, 0), lax.broadcasted_iota(jnp.int32, shape, 1)


def chunk_rows(c, pad=0, extra=0):
    return pl.ds(pl.multiple_of(c * CHUNK + pad, 8), CHUNK + extra)


def prepare_steps(c, r):
    row, col = tile_iotas()
    rows = chunk_rows(c)
    lower = (row >= col).astype(F32)
    step = softplus(r.dtr[rows, r.dtr_at : r.dtr_at + LANES] + r.dt_bias[...])
    log_step = step * (-jnp.exp(r.a_log[...]) * LOG2E)
    total = jnp.dot(lower, log_step, precision=exact, preferred_element_type=F32)
    r.step[rows, :] = step
    r.total[rows, :] = total
    r.total_t[pl.ds(pl.multiple_of(c * 16, 16), 16), :] = total.T[:16]


def segment_parts(c, r):
    down = r.seg_down[chunk_rows(c, 8), :]
    across = r.seg_across[pl.ds(c, 1), :]
    before = r.seg_down[pl.ds(pl.multiple_of(c * CHUNK, 8), 8), :][7:8, :]
    last = down[CHUNK - 1 : CHUNK, :]
    carried = (down == before).astype(F32)
    to_end = (down == last).astype(F32)
    carry_on = (last == before).astype(F32)
    return down, across, carried, to_end, carry_on


def masks_back(c, r, down):
    window = r.seg_down[chunk_rows(c, 0, 8), :]
    return [
        (pltpu.roll(window, j, 0)[8 : 8 + CHUNK] == down).astype(F32) for j in range(1, 4)
    ]


def masks_ahead(c, r, down):
    window = r.seg_down[chunk_rows(c, 8, 8), :]
    full = CHUNK + 8
    return [(pltpu.roll(window, full - j, 0)[:CHUNK] == down).astype(F32) for j in range(1, 4)]


def conv_tile(c, ref, at, weight, bias, w_at, masks):
    lanes = slice(at, at + LANES)
    w_lanes = slice(w_at, w_at + LANES)
    here = ref[chunk_rows(c), lanes]
    ahead = ref[pl.ds(pl.multiple_of(jnp.maximum(c * CHUNK - 8, 0), 8), 8), lanes]
    window = jnp.concatenate([ahead, here], axis=0)
    out = here * weight[3:4, w_lanes] + bias[0:1, w_lanes]
    for j in range(1, 4):
        shifted = pltpu.roll(window, j, 0)[8 : 8 + CHUNK]
        out = out + (shifted * masks[j - 1]) * weight[3 - j : 4 - j, w_lanes]
    return out


def pair_columns(tile, p, first):
    left = jnp.broadcast_to(tile[:, 2 * p : 2 * p + 1], (CHUNK, LANES))
    right = jnp.broadcast_to(tile[:, 2 * p + 1 : 2 * p + 2], (CHUNK, LANES))
    return left, right, jnp.where(first, left, right)


def stack_heads(tile, first):
    zero = jnp.zeros_like(tile)
    return jnp.concatenate([jnp.where(first, tile, zero), jnp.where(first, zero, tile)], axis=0)


def scan_chunk(c, r):
    rows = chunk_rows(c)
    row, col = tile_iotas()
    down, across, carried, to_end, carry_on = segment_parts(c, r)
    masks = masks_back(c, r, down)
    maps = []
    for half in range(2):
        pre = conv_tile(c, r.bc, r.bc_at + half * LANES, r.cbw, r.cbb, half * LANES, masks)
        r.pre_bc[rows, half * LANES : (half + 1) * LANES] = pre
        maps.append((pre * sigmoid(pre)).astype(BF16))
    b_map, c_map = maps
    r.maps[rows, :LANES] = b_map
    r.maps[rows, LANES:] = c_map
    scores = jnp.where((down == across) & (row >= col), dot_nt(c_map, b_map), 0.0)
    b_turned = b_map.T
    total = r.total[rows, :]
    step = r.step[rows, :]
    first = col < HEADDIM
    for p in range(r.pairs):
        lanes = slice(p * LANES, (p + 1) * LANES)
        pre = conv_tile(c, r.xr, r.xr_at + p * LANES, r.cxw, r.cxb, p * LANES, masks)
        r.pre_x[rows, lanes] = pre
        chan = pre * sigmoid(pre)
        left, right, both = pair_columns(total, p, first)
        _, _, step_pair = pair_columns(step, p, first)
        fed = step_pair * chan
        stacked = stack_heads(fed.astype(BF16), first)
        mixing = []
        for k, mine in enumerate((left, right)):
            other = r.total_t[pl.ds(c * 16 + 2 * p + k, 1), :]
            mixing.append((scores * jnp.exp2(jnp.minimum(mine - other, 0.0))).astype(BF16))
        within = dot_nn(jnp.concatenate(mixing, axis=1), stacked)
        state = r.state[:, lanes]
        state_low = state.astype(BF16)
        r.states[rows, lanes] = state_low
        decay_in = jnp.exp2(both) * carried
        r.y[rows, lanes] = (
            within + decay_in * dot_nn(c_map, state_low) + r.skip[0:1, lanes] * chan
        )
        last = both[CHUNK - 1 : CHUNK, :]
        decay_out = jnp.exp2(last - both) * to_end
        r.state[:, lanes] = (jnp.exp2(last) * carry_on) * state + dot_nn(
            b_turned, (decay_out * fed).astype(BF16)
        )


def scan_chunk_back(c, r):
    rows = chunk_rows(c)
    row, col = tile_iotas()
    down, across, carried, to_end, carry_on = segment_parts(c, r)
    ahead = masks_ahead(c, r, down)
    b_map = r.maps[rows, :LANES]
    c_map = r.maps[rows, LANES:]
    visible = (down == across) & (row <= col)
    scores = jnp.where(visible, dot_nt(b_map, c_map), 0.0)
    c_turned = c_map.T
    total = r.total[rows, :]
    step = r.step[rows, :]
    first = col < HEADDIM
    d_scores = jnp.zeros((CHUNK, LANES), F32)
    width = r.pairs * LANES
    for p in range(r.pairs):
        lanes = slice(p * LANES, (p + 1) * LANES)
        lows = slice(width + p * LANES, width + (p + 1) * LANES)
        gy_low = r.gy[rows, lanes]
        gy = gy_low.astype(F32)
        pre = r.pre_x[rows, lanes]
        gate = sigmoid(pre)
        chan = pre * gate
        left, right, both = pair_columns(total, p, first)
        _, _, step_pair = pair_columns(step, p, first)
        fed = step_pair * chan
        fed_low = fed.astype(BF16)
        d_mixing = dot_nt(stack_heads(fed_low, first), gy_low)
        mixing = []
        for k, mine in enumerate((left, right)):
            other = r.total_t[pl.ds(c * 16 + 2 * p + k, 1), :]
            decay = jnp.exp2(jnp.minimum(other - mine, 0.0))
            mixing.append((scores * decay).astype(BF16))
            d_scores = d_scores + d_mixing[k * CHUNK : (k + 1) * CHUNK] * decay
        d_state = r.d_state[:, lanes]
        d_state_low = d_state.astype(BF16)
        last = both[CHUNK - 1 : CHUNK, :]
        decay_out = jnp.exp2(last - both) * to_end
        from_state = decay_out * dot_nn(b_map, d_state_low)
        d_fed = dot_nn(jnp.concatenate(mixing, axis=1), stack_heads(gy_low, first)) + from_state
        fed_held = fed_low.astype(F32)
        skip = r.skip[0:1, lanes]
        flow = gy * (r.y[rows, lanes] - skip * chan) - fed_held * d_fed
        direct = chan * d_fed
        for k, part in enumerate((flow, direct)):
            spot = slice(k * CHUNK, (k + 1) * CHUNK)
            r.sums[spot, lanes], r.sums[spot, lows] = split_two(part)
        keep = jnp.exp2(last) * carry_on
        through = jnp.sum(fed_held * from_state, axis=0, keepdims=True) + keep * jnp.sum(
            r.states[rows, lanes].astype(F32) * d_state, axis=0, keepdims=True
        )
        spot = slice(2 * CHUNK, 2 * CHUNK + 16)
        r.sums[spot, lanes], r.sums[spot, lows] = split_two(
            jnp.broadcast_to(through, (16, LANES))
        )
        grad_in = (jnp.exp2(both) * carried * gy).astype(BF16)
        r.grad_in[:, lanes] = grad_in
        r.fed_out[:, lanes] = (decay_out * fed).astype(BF16)
        r.d_state_low[:, lanes] = d_state_low
        r.d_state[:, lanes] = keep * d_state + dot_nn(c_turned, grad_in)
        d_chan = skip * gy + step_pair * d_fed
        r.g_skip[:, lanes] += fold_rows(gy * chan)
        d_pre = d_chan * (gate * (1.0 + pre * (1.0 - gate)))
        conv_back(c, r, d_pre, r.d_pre_x, r.xr, r.xr_at, r.cxw, p * LANES, ahead, r.dx_at, r.g_cxw, r.g_cxb)
    d_scores_low = jnp.where(visible, d_scores, 0.0).astype(BF16)
    d_b = dot_nn(d_scores_low, c_map) + dot_nt(r.fed_out[...], r.d_state_low[...])
    d_c = dot_tn(d_scores_low, b_map) + dot_nt(r.grad_in[...], r.states[rows, :])
    for half, d_map in enumerate((d_b, d_c)):
        pre = r.pre_bc[rows, half * LANES : (half + 1) * LANES]
        gate = sigmoid(pre)
        d_pre = d_map * (gate * (1.0 + pre * (1.0 - gate)))
        conv_back(
            c, r, d_pre, r.d_pre_bc, r.bc, r.bc_at, r.cbw, half * LANES, ahead, r.dbc_at, r.g_cbw, r.g_cbb
        )
    reduced = dot_nn(r.sums[...], r.head_sum[...])
    d_total = jnp.dot(
        (row <= col).astype(F32), reduced[:CHUNK], precision=exact, preferred_element_type=F32
    ) + reduced[2 * CHUNK : 2 * CHUNK + 1]
    a_neg = -jnp.exp(r.a_log[...])
    d_step = reduced[CHUNK : 2 * CHUNK] + a_neg * d_total
    r.g_alog[...] += fold_rows(step * d_total) * a_neg
    d_raw = d_step * sigmoid(r.dtr[rows, r.dtr_at : r.dtr_at + LANES] + r.dt_bias[...])
    r.g_dtb[...] += fold_rows(d_raw)
    r.d_proj[rows, r.ddt_at : r.ddt_at + LANES] = d_raw.astype(BF16)


def conv_back(c, r, d_pre, held, raw, raw_at, weight, at, ahead, out_at, g_w, g_b):
    lanes = slice(at, at + LANES)
    rows = chunk_rows(c)
    held[CHUNK : CHUNK + 8, lanes] = held[0:8, lanes]
    held[0:CHUNK, lanes] = d_pre
    window = held[:, lanes]
    values = raw[rows, raw_at + at : raw_at + at + LANES]
    g_b[:, lanes] += fold_rows(d_pre)
    g_w[24:32, lanes] += fold_rows(d_pre * values)
    d_raw = d_pre * weight[3:4, lanes]
    for j in range(1, 4):
        shifted = pltpu.roll(window, CHUNK + 8 - j, 0)[:CHUNK] * ahead[j - 1]
        d_raw = d_raw + shifted * weight[3 - j : 4 - j, lanes]
        g_w[(3 - j) * 8 : (4 - j) * 8, lanes] += fold_rows(shifted * values)
    r.d_proj[rows, out_at + at : out_at + at + LANES] = d_raw.astype(BF16)


def head_sum_matrix(width):
    shape = (2 * width, LANES)
    lane = lax.broadcasted_iota(jnp.int32, shape, 0)
    lane = jnp.where(lane >= width, lane - width, lane)
    return (lane // HEADDIM == lax.broadcasted_iota(jnp.int32, shape, 1)).astype(BF16)


def layout_of(width):
    return types.SimpleNamespace(
        x=width, bc=2 * width, dt=2 * width + 2 * NSTATE, all=2 * width + 2 * NSTATE + LANES
    )


SMALL_IN = ("seg_down", "seg_across", "cxw", "cxb", "cbw", "cbb", "a_log", "dt_bias", "skip")


def small_inputs(segments, cxw, cxb, cbw, cbb, a_log, dt_bias, d_skip):
    tokens = segments.shape[0]
    seg = segments.astype(F32)
    edge = jnp.full((8,), -1.0, F32)
    down = jnp.broadcast_to(jnp.concatenate([edge, seg, edge])[:, None], (tokens + 16, LANES))
    heads = a_log.shape[0]
    pad = lambda v: jnp.pad(v, (0, LANES - heads))[None, :]
    return (
        down,
        seg.reshape(tokens // CHUNK, CHUNK),
        cxw,
        cxb[None, :],
        cbw,
        cbb[None, :],
        pad(a_log),
        pad(dt_bias),
        jnp.repeat(d_skip, HEADDIM)[None, :],
    )


def take_projections(r, width):
    r.pairs = width // LANES
    if hasattr(r, "proj"):
        at = layout_of(width)
        r.xr = r.bc = r.dtr = r.proj
        r.xr_at, r.bc_at, r.dtr_at = at.x, at.bc, at.dt
    else:
        r.xr_at = r.bc_at = r.dtr_at = 0


def forward_kernel(*refs, names, width):
    r = types.SimpleNamespace(**dict(zip(names, refs)))
    take_projections(r, width)
    chunks = r.dtr.shape[0] // CHUNK
    r.state[...] = jnp.zeros_like(r.state)

    def body(c, carry):
        prepare_steps(c, r)
        scan_chunk(c, r)
        return carry

    lax.fori_loop(0, chunks, body, 0)


def backward_kernel(*refs, names, width):
    r = types.SimpleNamespace(**dict(zip(names, refs)))
    take_projections(r, width)
    r.dx_at, r.dbc_at, r.ddt_at = 0, width, width + 2 * NSTATE
    start_back(r)
    chunks = r.dtr.shape[0] // CHUNK

    def body(i, carry):
        scan_chunk_back(chunks - 1 - i, r)
        return carry

    lax.fori_loop(0, chunks, body, 0)


def start_back(r):
    for ref in (r.d_state, r.d_pre_x, r.d_pre_bc, r.g_cxw, r.g_cxb, r.g_cbw, r.g_cbb):
        ref[...] = jnp.zeros_like(ref)
    for ref in (r.g_skip, r.g_alog, r.g_dtb):
        ref[...] = jnp.zeros_like(ref)
    r.head_sum[...] = head_sum_matrix(r.pairs * LANES)


def call_local(kernel, width, ins, outs, scratch, values, flops):
    names = tuple(ins) + tuple(outs) + tuple(scratch)
    whole = pl.BlockSpec(memory_space=pltpu.VMEM)
    return pl.pallas_call(
        functools.partial(kernel, names=names, width=width),
        out_shape=tuple(jax.ShapeDtypeStruct(*spec) for spec in outs.values()),
        in_specs=[whole] * len(ins),
        out_specs=tuple([whole] * len(outs)),
        scratch_shapes=[pltpu.VMEM(*spec) for spec in scratch.values()],
        compiler_params=pltpu.CompilerParams(vmem_limit_bytes=VMEM_LIMIT),
        cost_estimate=pl.CostEstimate(flops=flops, bytes_accessed=1 << 24, transcendentals=0),
    )(*values)


def mixer_forward(projected, small, width):
    tokens = projected.shape[0]
    outs = dict(
        y=((tokens, width), F32),
        pre_x=((tokens, width), F32),
        pre_bc=((tokens, 2 * NSTATE), F32),
        maps=((tokens, 2 * NSTATE), BF16),
        states=((tokens, width), BF16),
        step=((tokens, LANES), F32),
        total=((tokens, LANES), F32),
        total_t=((tokens // CHUNK * 16, LANES), F32),
    )
    scratch = dict(state=((NSTATE, width), F32))
    return call_local(
        forward_kernel, width, ("proj",) + SMALL_IN, outs, scratch, (projected,) + small, 10**10
    )


BACK_SCRATCH = lambda width: dict(
    d_state=((NSTATE, width), F32),
    d_state_low=((NSTATE, width), BF16),
    grad_in=((CHUNK, width), BF16),
    fed_out=((CHUNK, width), BF16),
    sums=((2 * CHUNK + 16, 2 * width), BF16),
    head_sum=((2 * width, LANES), BF16),
    d_pre_x=((CHUNK + 8, width), F32),
    d_pre_bc=((CHUNK + 8, 2 * NSTATE), F32),
)
GRAD_OUT = lambda width: dict(
    g_cxw=((32, width), F32),
    g_cxb=((8, width), F32),
    g_cbw=((32, 2 * NSTATE), F32),
    g_cbb=((8, 2 * NSTATE), F32),
    g_skip=((8, width), F32),
    g_alog=((8, LANES), F32),
    g_dtb=((8, LANES), F32),
)


SAVED = ("y", "pre_x", "pre_bc", "maps", "states", "step", "total", "total_t")


def mixer_backward(projected, small, saved, gy, width):
    tokens = gy.shape[0]
    outs = dict(d_proj=((tokens, width + 2 * NSTATE + LANES), BF16), **GRAD_OUT(width))
    ins = (("proj",) if len(projected) == 1 else ("xr", "bc", "dtr")) + SMALL_IN
    ins = ins + SAVED + ("gy",)
    return call_local(
        backward_kernel,
        width,
        ins,
        outs,
        BACK_SCRATCH(width),
        tuple(projected) + small + tuple(saved) + (gy,),
        3 * 10**10,
    )


UP, DOWN, PAIR = range(3)
LAST_Z = 3
STEP_ROWS = 16
PARTS = 2


def place():
    dp = lax.axis_index("dp")
    tp = lax.axis_index("tensor")
    z = dp // 2
    core = dp - 2 * z
    y = tp // 2
    x = tp - 2 * y
    return types.SimpleNamespace(
        dp=dp,
        tp=tp,
        z=z,
        core=core,
        mate=dp + 1 - 2 * core,
        near_x=y * 2 + (1 - x),
        near_y=(1 - y) * 2 + x,
        across=(1 - y) * 2 + (1 - x),
    )


def device(w, dp=None, tp=None):
    return {"dp": w.dp if dp is None else dp, "tensor": w.tp if tp is None else tp}


def other_z(w, k):
    return lax.rem(w.z + k, LAST_Z + 1) * 2 + w.core


def peers(w):
    rows = [device(w, tp=t) for t in (w.near_x, w.near_y, w.across)]
    return rows + [device(w, dp=w.mate)] + [device(w, dp=other_z(w, k)) for k in (1, 2, 3)]


def tell(sem, where):
    pl.semaphore_signal(sem, inc=1, device_id=where, device_id_type=pl.DeviceIdType.MESH)


def greet(w):
    barrier = pltpu.get_barrier_semaphore()
    for where in peers(w):
        tell(barrier, where)
    pl.semaphore_wait(barrier, len(peers(w)))


def remote(src, dst, send, recv, where):
    return pltpu.make_async_remote_copy(
        src_ref=src,
        dst_ref=dst,
        send_sem=send,
        recv_sem=recv,
        device_id=where,
        device_id_type=pl.DeviceIdType.MESH,
    )


def settle(ref, send, recv, where, sent=True):
    copy = remote(ref, ref, send, recv, where)
    if sent:
        copy.wait_send()
    else:
        copy.wait_recv()


class LineGather:
    def __init__(self, w, ref, send, recv, parts):
        self.w, self.ref, self.send, self.recv, self.parts = w, ref, send, recv, parts
        self.rows = ref.shape[0] // (2 * (LAST_Z + 1))
        self.joint = recv.at[parts * (LAST_Z + 1)]

    def shard(self, z, core, part):
        rows = self.rows // self.parts
        start = pl.multiple_of((z * 2 + core) * self.rows + part * rows, 16)
        return self.ref.at[pl.ds(start, rows)]

    def copy(self, z, kind, part):
        w = self.w
        block = self.shard(z, w.core, part)
        to = {UP: w.dp + 2, DOWN: w.dp - 2}.get(kind, w.mate)
        recv = self.joint if kind == PAIR else self.recv.at[part * (LAST_Z + 1) + z]
        return remote(block, block, self.send.at[kind], recv, device(w, dp=to))

    def relay(self, step):
        for part in range(self.parts):
            self.relay_part(step, part)

    def relay_part(self, step, part):
        w = self.w

        def low():
            z = w.z - step
            if step > 0:
                self.copy(z, UP, part).wait_recv()
            pl.when(w.z < LAST_Z)(lambda: self.copy(z, UP, part).start())
            if step == 0:
                pl.when(w.z > 0)(lambda: self.copy(z, DOWN, part).start())
            self.copy(z, PAIR, part).start()

        def high():
            z = w.z + step
            self.copy(z, DOWN, part).wait_recv()
            pl.when(w.z > 0)(lambda: self.copy(z, DOWN, part).start())
            self.copy(z, PAIR, part).start()

        if step == 0:
            low()
        else:
            pl.when(w.z >= step)(low)
            pl.when(w.z <= LAST_Z - step)(high)

    def some(self, count):
        return self.ref.at[pl.ds(0, count * self.rows)]

    def finish(self):
        where = device(self.w, dp=self.w.mate)
        settle(self.some(LAST_Z + 1), self.send.at[PAIR], self.joint, where, sent=False)

    def drain(self):
        w = self.w
        settle(self.some(LAST_Z + 1), self.send.at[PAIR], self.joint, device(w, dp=w.mate))
        for z in range(LAST_Z):
            pl.when(w.z == z)(
                lambda z=z: settle(
                    self.some(z + 1), self.send.at[UP], self.joint, device(w, dp=w.mate)
                )
            )
            pl.when(w.z == LAST_Z - z)(
                lambda z=z: settle(
                    self.some(z + 1), self.send.at[DOWN], self.joint, device(w, dp=w.mate)
                )
            )


class RowGather:
    def __init__(self, w, ref, send, recv):
        self.w, self.ref, self.send, self.recv = w, ref, send, recv
        self.rows = ref.shape[0] // 4

    def copy(self, i):
        w = self.w
        slot, half, to = (
            (w.tp, 0, w.near_x),
            (w.tp, 1, w.near_y),
            (w.tp, 1, w.near_x),
            (w.tp, 0, w.near_y),
            (w.near_x, 0, w.near_y),
            (w.near_y, 1, w.near_x),
        )[i]
        block = row_block(self.ref, self.rows, slot, half)
        return remote(block, block, self.send, self.recv.at[min(i, 2)], device(w, tp=to))

    def start(self):
        for i in range(4):
            self.copy(i).start()

    def hand_on(self):
        for i in range(2):
            self.copy(i).wait_recv()
            self.copy(i + 4).start()

    def some(self, count):
        return self.ref.at[pl.ds(0, count * self.rows)]

    def finish(self):
        where = device(self.w, tp=self.w.near_x)
        settle(self.some(2), self.send, self.recv.at[2], where, sent=False)

    def drain(self):
        settle(self.some(3), self.send, self.recv.at[2], device(self.w, tp=self.w.near_x))


def row_block(ref, rows, slot, half=None):
    start = slot * rows
    if half is not None:
        rows = rows // 2
        start = start + half * rows
    return ref.at[pl.ds(pl.multiple_of(start, 16), rows)]


def add_into(ref, other):
    rows = 64 if ref.shape[0] % 64 == 0 else ref.shape[0]

    def body(i, carry):
        here = pl.ds(pl.multiple_of(i * rows, rows), rows)
        ref[here, :] = (ref[here, :].astype(F32) + other[here, :].astype(F32)).astype(ref.dtype)
        return carry

    lax.fori_loop(0, ref.shape[0] // rows, body, 0)


class RowScatter:
    def __init__(self, w, part, far, near, send, recv):
        self.w, self.part, self.far, self.near, self.send, self.recv = w, part, far, near, send, recv
        self.rows = part.shape[0] // 4

    def block(self, slot, half=None):
        return row_block(self.part, self.rows, slot, half)

    def copy(self, i):
        w = self.w
        half = lambda k, h: row_block(self.near.at[k], self.rows, 0, h)
        src, dst, to = (
            (lambda: self.block(w.across, 0), lambda: self.far.at[0], w.near_x),
            (lambda: self.block(w.across, 1), lambda: self.far.at[1], w.near_y),
            (lambda: self.block(w.near_x, 0), lambda: half(0, 0), w.near_x),
            (lambda: self.block(w.near_y, 1), lambda: half(1, 1), w.near_y),
            (lambda: self.block(w.near_x, 1), lambda: half(0, 1), w.near_x),
            (lambda: self.block(w.near_y, 0), lambda: half(1, 0), w.near_y),
        )[i]
        return remote(src(), dst(), self.send, self.recv.at[min(i, 2)], device(w, tp=to))

    def start(self, *which):
        for i in which:
            self.copy(i).start()

    def hand_on(self):
        w = self.w
        self.copy(1).wait_recv()
        add_into(self.block(w.near_x, 1), self.far.at[1])
        self.copy(4).start()
        self.copy(0).wait_recv()
        add_into(self.block(w.near_y, 0), self.far.at[0])
        self.copy(5).start()

    def some(self, count):
        return self.part.at[pl.ds(0, count * self.rows)]

    def finish(self):
        where = device(self.w, tp=self.w.near_x)
        settle(self.some(2), self.send, self.recv.at[2], where, sent=False)

    def total(self, here, there):
        total = self.part[there, :].astype(F32)
        return total + self.near[0, here, :].astype(F32) + self.near[1, here, :].astype(F32)

    def drain(self):
        settle(self.some(3), self.send, self.recv.at[2], device(self.w, tp=self.w.near_x))


class LineScatter:
    def __init__(self, w, shard, pair, up, down, pair_sem, line_sem, parts):
        self.w, self.shard, self.pair, self.up, self.down = w, shard, pair, up, down
        self.pair_sem, self.line_sem, self.parts = pair_sem, line_sem, parts
        self.rows = pair.shape[0] // (LAST_Z + 1)

    def slot(self, ref, i):
        return ref.at[pl.ds(pl.multiple_of(i * self.rows, 16), self.rows)]

    def piece(self, ref, part):
        rows = self.rows // self.parts
        return ref.at[pl.ds(part * rows, rows)]

    def pair_copy(self, z):
        w = self.w
        return remote(
            self.shard(z, 1 - w.core),
            self.slot(self.pair, z),
            self.pair_sem.at[LAST_Z + 1],
            self.pair_sem.at[z],
            device(w, dp=w.mate),
        )

    def up_copy(self, z, part):
        return remote(
            self.piece(self.shard(z, self.w.core), part),
            self.piece(self.slot(self.up, z - 1), part),
            self.line_sem.at[0],
            self.line_sem.at[2 + part * LAST_Z + z - 1],
            device(self.w, dp=self.w.dp + 2),
        )

    def down_copy(self, z, part):
        return remote(
            self.piece(self.shard(z, self.w.core), part),
            self.piece(self.slot(self.down, z), part),
            self.line_sem.at[1],
            self.line_sem.at[2 + (self.parts + part) * LAST_Z + z],
            device(self.w, dp=self.w.dp - 2),
        )

    def launch(self, z):
        w = self.w
        self.pair_copy(z).wait_recv()

        def every(send):
            for part in range(self.parts):
                add_into(self.piece(self.shard(z, w.core), part), self.piece(self.slot(self.pair, z), part))
                if send is not None:
                    send(z, part).start()

        low = (w.z == 0) & (z > 0)
        high = (w.z == LAST_Z) & (z < LAST_Z)
        pl.when(low)(lambda: every(self.up_copy))
        pl.when(high)(lambda: every(self.down_copy))
        pl.when(jnp.logical_not(low | high))(lambda: every(None))

    def pass_up(self, z):
        for part in range(self.parts):
            self.up_copy(z, part).wait_recv()
            add_into(
                self.piece(self.shard(z, self.w.core), part),
                self.piece(self.slot(self.up, z - 1), part),
            )
            self.up_copy(z, part).start()

    def pass_down(self, z):
        for part in range(self.parts):
            self.down_copy(z, part).wait_recv()
            add_into(
                self.piece(self.shard(z, self.w.core), part),
                self.piece(self.slot(self.down, z), part),
            )
            self.down_copy(z, part).start()

    def step(self, k):
        w = self.w
        if k == 0:
            pl.when(w.z == 1)(lambda: self.pass_up(3))
            pl.when(w.z == 2)(lambda: self.pass_down(0))
        else:

            @pl.when(w.z == 1)
            def _():
                self.pass_up(2)
                self.pass_down(0)

            @pl.when(w.z == 2)
            def _():
                self.pass_down(1)
                self.pass_up(3)

    def finish(self, out):
        w = self.w
        own = self.shard(w.z, w.core)
        rows = self.rows // self.parts

        def add(part, copy, slot):
            here = pl.ds(part * rows, rows)
            copy(w.z, part).wait_recv()
            out[here, :] += self.piece(slot, part)[...].astype(F32)

        out[...] = own[...].astype(F32)
        for part in range(self.parts):
            pl.when(w.z > 0)(
                lambda part=part: add(part, self.up_copy, self.slot(self.up, w.z - 1))
            )
            pl.when(w.z < LAST_Z)(
                lambda part=part: add(part, self.down_copy, self.slot(self.down, w.z))
            )

    def drain_pair(self):
        where = device(self.w, dp=self.w.mate)
        settle(self.pair, self.pair_sem.at[LAST_Z + 1], self.pair_sem.at[0], where)

    def drain(self):
        w = self.w
        where = device(w, dp=w.mate)
        for z in range(LAST_Z):
            sent = self.up.at[pl.ds(0, (LAST_Z - z) * self.rows)]
            pl.when(w.z == z)(
                lambda sent=sent: settle(sent, self.line_sem.at[0], self.line_sem.at[2], where)
            )
            pl.when(w.z == LAST_Z - z)(
                lambda sent=sent: settle(sent, self.line_sem.at[1], self.line_sem.at[2], where)
            )


class Exchange:
    def __init__(self, ref, mine, targets, sems):
        self.ref, self.mine, self.targets, self.sems = ref, mine, targets, sems

    def start(self):
        part = self.ref.at[self.mine]
        for target in self.targets:
            remote(part, part, self.sems.at[0], self.sems.at[1], target).start()

    def finish(self):
        count = len(self.targets)
        some = self.ref.at[pl.ds(0, count)]
        for sent in (False, True):
            settle(some, self.sems.at[0], self.sems.at[1], self.targets[0], sent=sent)

    def total(self):
        total = self.ref[0].astype(F32)
        for i in range(1, self.ref.shape[0]):
            total = total + self.ref[i].astype(F32)
        return total


def norm_rows(x_ref, gain, out_ref, start):
    rows = 64

    def body(i, carry):
        here = pl.ds(pl.multiple_of(i * rows, rows), rows)
        values = x_ref[here, :].astype(F32)
        scale = lax.rsqrt(jnp.mean(values * values, axis=1, keepdims=True) + EPS)
        there = pl.ds(pl.multiple_of(start + i * rows, 16), rows)
        out_ref[there, :] = (values * scale * gain).astype(BF16)
        return carry

    lax.fori_loop(0, x_ref.shape[0] // rows, body, 0)


def by_rows(total, rows, body):
    def step(i, carry):
        body(pl.ds(pl.multiple_of(i * rows, rows), rows))
        return carry

    lax.fori_loop(0, total // rows, step, 0)


def over_chunks(r, body):
    def step(c, carry):
        body(c)
        return carry

    lax.fori_loop(0, r.chunks, step, 0)


def turned(row):
    return jnp.broadcast_to(row, (CHUNK, LANES)).T


def gated_tile(c, r, p):
    rows, lanes = chunk_rows(c), slice(p * LANES, (p + 1) * LANES)
    z = r.z[rows, lanes]
    gate = sigmoid(z)
    return z, gate, r.y[rows, lanes]


def square_chunk(c, r):
    square = jnp.zeros((CHUNK, LANES), F32)
    for p in range(r.pairs):
        z, gate, y = gated_tile(c, r, p)
        gated = y * (z * gate)
        square = square + gated * gated
    r.squares.at[r.w.tp][pl.ds(c, 1), :] = jnp.sum(square.T, axis=0, keepdims=True)


def cross_chunk(c, r):
    rows = chunk_rows(c)
    cross = jnp.zeros((CHUNK, LANES), F32)
    for p in range(r.pairs):
        lanes = slice(p * LANES, (p + 1) * LANES)
        z, gate, y = gated_tile(c, r, p)
        cross = cross + r.d_mixed[rows, lanes] * r.gain[0:1, lanes] * (y * (z * gate))
    r.crosses.at[r.w.tp][pl.ds(c, 1), :] = jnp.sum(cross.T, axis=0, keepdims=True)


def slot_sum(ref, c):
    total = ref[0, pl.ds(c, 1), :]
    for i in range(1, 4):
        total = total + ref[i, pl.ds(c, 1), :]
    return total


def scale_two_row(c, r):
    return lax.rsqrt(slot_sum(r.squares, c) / (r.pairs * LANES * 4) + EPS)


def mix_chunk(c, r):
    rows = chunk_rows(c)
    scale = turned(scale_two_row(c, r))
    for p in range(r.pairs):
        lanes = slice(p * LANES, (p + 1) * LANES)
        z, gate, y = gated_tile(c, r, p)
        r.mixed[rows, lanes] = (y * (z * gate) * scale * r.gain[0:1, lanes]).astype(BF16)


def gate_back_chunk(c, r):
    rows = chunk_rows(c)
    row = scale_two_row(c, r)
    pull = turned(row * row * row * slot_sum(r.crosses, c) / (r.pairs * LANES * 4))
    scale = turned(row)
    for p in range(r.pairs):
        lanes = slice(p * LANES, (p + 1) * LANES)
        z, gate, y = gated_tile(c, r, p)
        silu = z * gate
        gated = y * silu
        scaled = r.d_mixed[rows, lanes] * scale
        r.g_gate[:, lanes] += fold_rows(scaled * gated)
        d_gated = scaled * r.gain[0:1, lanes] - gated * pull
        r.gy[rows, lanes] = (d_gated * silu).astype(BF16)
        r.d_z[rows, lanes] = (d_gated * y * (gate * (1.0 + z * (1.0 - gate)))).astype(BF16)


def ends_first(i):
    odd = lax.rem(i, 2)
    return (1 - odd) * (LAST_Z - i // 2) + odd * (i // 2)


def weight_parts(make, scatter):
    def body(i, carry):
        z = ends_first(i)
        make(z)
        scatter.pair_copy(z).start()
        pl.when(i > 0)(lambda: scatter.launch(ends_first(i - 1)))
        return carry

    lax.fori_loop(0, LAST_Z + 1, body, 0)
    scatter.launch(ends_first(LAST_Z))
    scatter.drain_pair()


def product_maker(left, right, store):
    block = left.shape[1] // (LAST_Z + 1)

    def make(z):
        lanes = pl.ds(pl.multiple_of(z * block, LANES), block)
        store(z, dot_tn(left[:, lanes], right[...]).astype(BF16))

    return make


def flat_shard(ref, rows):
    return lambda z, core: ref.at[pl.ds(pl.multiple_of((z * 2 + core) * rows, 16), rows)]


def flat_store(ref, rows):
    def store(z, value):
        ref[pl.ds(pl.multiple_of(z * 2 * rows, 16), 2 * rows), :] = value

    return store


def side_shard(ref, rows, width):
    return lambda z, core: ref.at[
        pl.ds(pl.multiple_of(z * rows, 16), rows),
        pl.ds(pl.multiple_of(core * width, LANES), width),
    ]


def side_store(ref, rows, width):
    def store(z, value):
        here = pl.ds(pl.multiple_of(z * rows, 16), rows)
        ref[here, :width] = value[:rows]
        ref[here, width : 2 * width] = value[rows:]

    return store


def own_rows(r):
    shard = r.w_x.shape[0]
    return pl.ds(pl.multiple_of(r.w.dp * shard, 16), shard)


def input_moves(r):
    width = r.pairs * LANES
    own = own_rows(r)
    block = r.cot.shape[0]
    mine = pl.ds(pl.multiple_of(r.w.tp * block, block), block)
    moves = (
        (r.w_x, r.full_x.at[own, pl.ds(0, width)]),
        (r.w_bc, r.full_x.at[own, pl.ds(width, 2 * NSTATE)]),
        (r.x_in, r.x_held),
        (r.w_z, r.full_z.at[own]),
        (r.w_out, r.full_out.at[own]),
        (r.cot, r.row_cot.at[mine]),
    )
    return [pltpu.make_async_copy(src, dst, r.s_m.at[i]) for i, (src, dst) in enumerate(moves)]


def place_steps(r):
    heads, shard = r.w_dt.shape
    mine = r.steps_t.at[pl.ds(pl.multiple_of(r.w.dp * STEP_ROWS, STEP_ROWS), STEP_ROWS)]
    r.turn[...] = jnp.zeros_like(r.turn)
    r.turn[0:heads, 0:shard] = r.w_dt[...]
    mine[...] = r.turn[0:STEP_ROWS, :]


def turn_steps(r):
    shard = r.w_x.shape[0]

    def body(d, carry):
        r.turn[0:STEP_ROWS, :] = r.steps_t[
            pl.ds(pl.multiple_of(d * STEP_ROWS, STEP_ROWS), STEP_ROWS), :
        ]
        r.full_dt[pl.ds(pl.multiple_of(d * shard, 16), shard), :] = r.turn[...].T[:shard]
        return carry

    lax.fori_loop(0, 2 * (LAST_Z + 1), body, 0)


def prepare_small(r):
    heads = r.a_log_in.shape[0]
    w, width = r.w, r.pairs * LANES
    for ref in (r.a_log, r.dt_bias):
        ref[...] = jnp.zeros_like(ref)
    r.a_log[0:1, 0:heads] = r.a_log_in[...].reshape(1, heads)
    r.dt_bias[0:1, 0:heads] = r.dt_bias_in[...].reshape(1, heads)
    r.cxb[...] = r.cxb_in[...].reshape(1, width)
    r.cbb[...] = r.cbb_in[...].reshape(1, 2 * NSTATE)
    r.gain[...] = r.gain_in[...].reshape(1, width)
    skip = r.d_skip_in[...].reshape(1, heads)
    first = lax.broadcasted_iota(jnp.int32, (1, LANES), 1) < HEADDIM
    for p in range(r.pairs):
        pair = jnp.where(first, skip[:, 2 * p : 2 * p + 1], skip[:, 2 * p + 1 : 2 * p + 2])
        r.skip[:, p * LANES : (p + 1) * LANES] = pair
    r.seg_across[...] = r.segments[...].reshape(r.chunks, CHUNK).astype(F32)
    edge = jnp.full((8, LANES), -1.0, F32)
    r.seg_down[0:8, :] = edge
    r.seg_down[r.chunks * CHUNK + 8 :, :] = edge

    def body(c):
        r.seg_down[chunk_rows(c, 8), :] = turned(r.seg_across[pl.ds(c, 1), :])

    over_chunks(r, body)


def phase_one(r):
    w = r.w
    width = r.pairs * LANES
    tokens = r.row_normed.shape[0]
    block = r.x_held.shape[0]
    start = pl.multiple_of(w.tp * block, block)
    moves = input_moves(r)
    for move in moves:
        move.start()
    place_steps(r)
    greet(w)
    moves[0].wait()
    moves[1].wait()
    r.shard_x.relay(0)
    r.shard_dt.relay(0)
    moves[2].wait()
    norm_rows(r.x_held, r.pre_gain[...].reshape(1, r.x_held.shape[1]), r.row_normed, start)
    r.row_n.start()
    r.state[...] = jnp.zeros_like(r.state)
    prepare_small(r)
    for move in moves[3:]:
        move.wait()
    r.shard_x.relay(1)
    r.shard_dt.relay(1)
    r.shard_x.relay(2)
    r.shard_dt.relay(2)
    r.row_n.hand_on()
    r.row_c.start()
    r.shard_x.relay(3)
    r.shard_dt.relay(3)
    r.shard_z.relay(0)
    r.shard_dt.finish()
    turn_steps(r)
    r.row_n.finish()
    r.shard_x.finish()

    def project_x(rows):
        normed = r.row_normed[rows, :]
        out = dot_nn(normed, r.full_x[...])
        r.xr[rows, :] = out[:, :width]
        r.bc[rows, :] = out[:, width:]
        r.dtr[rows, :] = dot_nn(normed, r.full_dt[...])

    by_rows(tokens, 256, project_x)

    def body(c):
        prepare_steps(c, r)
        scan_chunk(c, r)

        @pl.when(c == 1)
        def _():
            r.shard_z.relay(1)
            r.row_c.hand_on()

        pl.when(c == 5)(lambda: r.shard_z.relay(2))

    over_chunks(r, body)


def phase_mid(r):
    w = r.w
    tokens = r.row_normed.shape[0]
    block = r.x_held.shape[0]
    r.shard_z.relay(3)
    r.shard_out.relay(0)
    r.shard_z.finish()

    def project_z(rows):
        r.z[rows, :] = dot_nn(r.row_normed[rows, :], r.full_z[...])

    by_rows(tokens, 256, project_z)
    over_chunks(r, lambda c: square_chunk(c, r))
    r.ex_squares.start()
    r.row_c.finish()
    r.ex_squares.finish()
    over_chunks(r, lambda c: mix_chunk(c, r))
    r.shard_out.relay(1)
    weight_parts(
        product_maker(r.row_cot, r.mixed, flat_store(r.out_part, r.shard_rows)), r.grad_out
    )
    tell(r.free_pair, device(w, dp=w.mate))
    r.shard_out.relay(2)
    r.grad_out.step(0)
    r.shard_out.relay(3)
    r.shard_out.finish()

    def mix_back(rows):
        r.d_mixed[rows, :] = dot_nn(r.row_cot[rows, :], r.full_out[...])

    by_rows(tokens, 256, mix_back)
    over_chunks(r, lambda c: cross_chunk(c, r))
    r.ex_crosses.start()
    r.grad_out.step(1)

    def share(slot):
        rows = pl.ds(pl.multiple_of(slot * block, block), block)
        tile = 512

        def body(n, carry):
            cols = pl.ds(pl.multiple_of(n * tile, tile), tile)
            r.part[rows, cols] = dot_nt(r.mixed[rows, :], r.full_out[cols, :]).astype(BF16)
            return carry

        lax.fori_loop(0, r.part.shape[1] // tile, body, 0)

    share(w.across)
    r.out_rows.start(0, 1)
    share(w.near_x)
    r.out_rows.start(2)
    share(w.near_y)
    r.out_rows.start(3)
    share(w.tp)
    for item in (r.shard_x, r.shard_dt, r.shard_z, r.shard_out, r.row_n, r.row_c):
        item.drain()
    r.ex_crosses.finish()
    r.g_gate[...] = jnp.zeros_like(r.g_gate)
    over_chunks(r, lambda c: gate_back_chunk(c, r))
    pl.semaphore_wait(r.free_pair, 1)
    weight_parts(
        product_maker(r.row_normed, r.d_z, flat_store(r.full_out, r.shard_rows)), r.grad_z
    )
    tell(r.free_pair, device(w, dp=w.mate))


def phase_back(r):
    w = r.w
    block = r.x_held.shape[0]
    start_back(r)

    def body(i, carry):
        scan_chunk_back(r.chunks - 1 - i, r)

        @pl.when(i == 0)
        def _():
            r.grad_out.finish(r.v_w_out)
            r.put(r.v_w_out, r.o_w_out, 0).start()
            r.grad_out.drain()
            tell(r.free_line, device(w, dp=other_z(w, 1)))
            tell(r.free_line, device(w, dp=other_z(w, 3)))

        @pl.when(i == 2)
        def _():
            r.out_rows.hand_on()
            r.grad_z.step(0)

        pl.when(i == 5)(lambda: r.grad_z.step(1))
        return carry

    lax.fori_loop(0, r.chunks, body, 0)


def finish_block(r):
    w = r.w
    block = r.x_held.shape[0]
    step = 64
    r.out_rows.finish()

    def add(k, carry):
        here = pl.ds(pl.multiple_of(k * step, step), step)
        there = pl.ds(pl.multiple_of(w.tp * block + k * step, 16), step)
        total = r.x_held[here, :].astype(F32) + r.out_rows.total(here, there)
        r.v_block[here, :] = total.astype(BF16)
        return carry

    lax.fori_loop(0, block // step, add, 0)
    r.put(r.v_block, r.o_block, 1).start()
    r.out_rows.drain()
    tell(r.free_row, device(w, tp=w.near_x))
    tell(r.free_row, device(w, tp=w.near_y))


def step_parts(r, at):
    shard = r.shard_rows
    out = dot_tn(r.d_rest[:, at : at + LANES], r.row_normed[...])[:STEP_ROWS]
    for d in range(2 * (LAST_Z + 1)):
        here = slice(d * STEP_ROWS, (d + 1) * STEP_ROWS)
        r.dt_part[here, 0:shard] = out[:, d * shard : (d + 1) * shard]


def phase_last(r):
    w = r.w
    width = r.pairs * LANES
    block = r.x_held.shape[0]
    edge = width + 2 * NSTATE
    weight_parts(
        product_maker(
            r.row_normed,
            r.d_rest.at[:, pl.ds(width, 2 * NSTATE)],
            flat_store(r.bc_part, r.shard_rows),
        ),
        r.grad_bc,
    )
    step_parts(r, edge)
    for z in range(LAST_Z + 1):
        r.grad_dt.pair_copy(z).start()
    finish_block(r)
    r.g_pre[...] = jnp.zeros_like(r.g_pre)
    pl.semaphore_wait(r.free_row, 2)

    def share(slot):
        rows = pl.ds(pl.multiple_of(slot * block, block), block)
        tile = 512

        def body(n, carry):
            cols = pl.ds(pl.multiple_of(n * tile, tile), tile)
            out = dot_nt(r.d_z[rows, :], r.full_z[cols, :])
            out = out + dot_nt(r.d_rest[rows, :edge], r.full_x[cols, :])
            out = out + dot_nt(r.d_rest[rows, edge:], r.full_dt[cols, :])
            r.part[rows, cols] = out.astype(BF16)
            r.g_pre[:, cols] += fold_rows(out * r.row_normed[rows, cols].astype(F32))
            return carry

        lax.fori_loop(0, r.part.shape[1] // tile, body, 0)

    share(w.across)
    r.in_rows.start(0, 1)
    for z in (3, 0, 2, 1):
        r.grad_dt.launch(z)
    r.grad_dt.drain_pair()
    pl.semaphore_wait(r.free_pair, 1)
    pl.semaphore_wait(r.free_line, 2)
    weight_parts(
        product_maker(
            r.row_normed,
            r.d_rest.at[:, pl.ds(0, width)],
            side_store(r.row_cot, r.shard_rows, width),
        ),
        r.grad_x_part,
    )
    r.grad_bc.step(0)
    r.grad_dt.step(0)
    share(w.near_x)
    r.in_rows.start(2)
    share(w.near_y)
    r.in_rows.start(3)
    r.grad_bc.step(1)
    r.grad_dt.step(1)
    share(w.tp)
    pack_small(r)
    r.ex_pair.start()
    r.grad_z.finish(r.v_w_z)
    r.put(r.v_w_z, r.o_w_z, 2).start()
    r.grad_x_part.step(0)
    r.in_rows.hand_on()
    again = [
        pltpu.make_async_copy(r.cot.at[pl.ds(k * (block // 2), block // 2)], r.far.at[k], r.s_m.at[k])
        for k in range(2)
    ]
    for copy in again:
        copy.start()
    r.ex_pair.finish()
    r.small_z.at[w.z][...] = r.ex_pair.total()
    r.ex_z.start()
    r.grad_bc.finish(r.bc_sum)
    r.grad_dt.finish(r.v_w_dt)
    r.put(r.v_w_dt, r.o_w_dt, 3).start()
    r.bc_slots.at[w.tp][...] = r.bc_sum[...].astype(BF16)
    r.ex_bc.start()
    r.ex_z.finish()
    total = r.ex_z.total()
    r.v_small[...] = total[:SMALL_DP]
    r.put(r.v_small, r.o_small, 4).start()
    r.small_t.at[w.tp][...] = total[SMALL_DP:]
    r.ex_t.start()
    r.grad_x_part.step(1)
    r.ex_bc.finish()
    r.v_w_bc[...] = r.ex_bc.total()
    r.put(r.v_w_bc, r.o_w_bc, 5).start()
    r.ex_t.finish()
    shared = r.ex_t.total()
    gain = r.pre_gain[...].reshape(1, r.x_held.shape[1])
    count = gain.shape[1] // LANES
    r.v_shared[...] = shared
    for p in range(count):
        r.v_shared[p : p + 1, :] = shared[p : p + 1, :] / gain[:, p * LANES : (p + 1) * LANES]
    r.put(r.v_shared, r.o_shared, 6).start()
    for copy in again:
        copy.wait()
    r.in_rows.finish()
    step = 64

    def body(k, carry):
        here = pl.ds(pl.multiple_of(k * step, step), step)
        there = pl.ds(pl.multiple_of(w.tp * block + k * step, 16), step)
        half = k // (block // 2 // step)
        inner = pl.ds(pl.multiple_of(k * step - half * (block // 2), step), step)
        values = r.x_held[here, :].astype(F32)
        scale = lax.rsqrt(jnp.mean(values * values, axis=1, keepdims=True) + EPS)
        weighted = r.in_rows.total(here, there) * gain
        along = jnp.mean(weighted * values, axis=1, keepdims=True)
        grad = r.far[half, inner, :].astype(F32) + scale * weighted
        r.v_grad_x[here, :] = (grad - values * (scale * scale * scale * along)).astype(BF16)
        return carry

    lax.fori_loop(0, block // step, body, 0)
    r.put(r.v_grad_x, r.o_grad_x, 7).start()
    for item in (r.grad_z, r.grad_bc, r.grad_dt, r.in_rows):
        item.drain()
    r.grad_x_part.finish(r.v_w_x)
    r.put(r.v_w_x, r.o_w_x, 8).start()
    r.grad_x_part.drain()
    ends = ("w_out", "block", "w_z", "w_dt", "small", "w_bc", "shared", "grad_x", "w_x")
    for i, name in enumerate(ends):
        r.put(getattr(r, "v_" + name), getattr(r, "o_" + name), i).wait()


SMALL_DP = 40
SMALL_ALL = 24


def head_row(r):
    lane = lax.broadcasted_iota(jnp.int32, (1, LANES), 1)
    out = jnp.zeros((1, LANES), F32)
    for p in range(r.pairs):
        tile = jnp.sum(r.g_skip[:, p * LANES : (p + 1) * LANES], axis=0, keepdims=True)
        for k, part in enumerate((lane < HEADDIM, lane >= HEADDIM)):
            head = jnp.sum(jnp.where(part, tile, 0.0), axis=1, keepdims=True)
            out = jnp.where(lane == 2 * p + k, head, out)
    return out


def pack_small(r):
    mine = r.small_pair.at[r.w.core]
    mine[...] = jnp.zeros_like(mine)

    def put(at, ref, first, count):
        for p in range(count):
            lanes = slice(p * LANES, (p + 1) * LANES)
            mine[at + p : at + p + 1, :] = jnp.sum(
                ref[first : first + 8, lanes], axis=0, keepdims=True
            )
        return at + count

    at = put(0, r.g_gate, 0, r.pairs)
    for k in range(4):
        at = put(at, r.g_cxw, 8 * k, r.pairs)
    at = put(at, r.g_cxb, 0, r.pairs)
    mine[at : at + 1, :] = head_row(r)
    at = at + 1
    at = put(at, r.g_alog, 0, 1)
    at = put(at, r.g_dtb, 0, 1)
    at = put(SMALL_DP, r.g_pre, 0, r.g_pre.shape[1] // LANES)
    for k in range(4):
        at = put(at, r.g_cbw, 8 * k, 2)
    put(at, r.g_cbb, 0, 2)


RAW_IN = (
    "x_in",
    "segments",
    "pre_gain",
    "w_z",
    "w_x",
    "w_bc",
    "w_dt",
    "cxw",
    "cxb_in",
    "cbw",
    "cbb_in",
    "a_log_in",
    "dt_bias_in",
    "d_skip_in",
    "gain_in",
    "w_out",
    "cot",
)


def whole_kernel(*refs, names, width):
    r = types.SimpleNamespace(**dict(zip(names, refs)))
    r.w = w = place()
    r.pairs = width // LANES
    r.chunks = r.row_normed.shape[0] // CHUNK
    r.shard_rows = r.w_x.shape[0]
    r.xr_at = r.bc_at = r.dtr_at = 0
    r.dx_at, r.dbc_at, r.ddt_at = 0, width, width + 2 * NSTATE
    gather = lambda i, ref: LineGather(w, ref, r.s_w.at[i], r.r_w.at[i], PARTS)
    r.shard_x = gather(0, r.full_x)
    r.shard_z = gather(1, r.full_z)
    r.shard_out = gather(2, r.full_out)
    r.shard_dt = LineGather(w, r.steps_t, r.s_d, r.r_d, 1)
    r.row_n = RowGather(w, r.row_normed, r.s_r.at[0], r.r_r.at[0])
    r.row_c = RowGather(w, r.row_cot, r.s_r.at[1], r.r_r.at[1])
    r.out_rows = r.in_rows = RowScatter(w, r.part, r.far, r.near, r.s_q.at[0], r.r_q)
    rows = r.shard_rows
    held = (r.pair, r.up, r.down, r.p_main, r.l_main, PARTS)
    r.grad_out = LineScatter(w, flat_shard(r.out_part, rows), *held)
    r.grad_x_part = LineScatter(w, side_shard(r.row_cot, rows, width), *held)
    r.grad_z = LineScatter(
        w, flat_shard(r.full_out, rows), r.pair, r.up_z, r.down_z, r.p_main, r.l_z, PARTS
    )
    held_dt = (r.pair_dt, r.up_dt, r.down_dt, r.p_dt, r.l_dt, 1)
    r.grad_dt = LineScatter(w, flat_shard(r.dt_part, STEP_ROWS), *held_dt)
    in_row = [device(w, tp=t) for t in (w.near_x, w.near_y, w.across)]
    in_line = [device(w, dp=other_z(w, k)) for k in (1, 2, 3)]
    exchange = lambda i, ref, mine, targets: Exchange(ref, mine, targets, r.s_e.at[i])
    r.ex_squares = exchange(0, r.squares, w.tp, in_row)
    r.ex_crosses = exchange(1, r.crosses, w.tp, in_row)
    r.ex_pair = exchange(2, r.small_pair, w.core, [device(w, dp=w.mate)])
    r.ex_z = exchange(3, r.small_z, w.z, in_line)
    r.ex_t = exchange(4, r.small_t, w.tp, in_row)
    r.ex_bc = exchange(5, r.bc_slots, w.tp, in_row)
    r.put = lambda src, dst, i: pltpu.make_async_copy(src, dst, r.s_o.at[i])
    tokens = r.chunks * CHUNK
    phase_one(r)

    def middle(z, d_mixed, mixed):
        r.z, r.d_mixed, r.mixed = z, d_mixed, mixed
        phase_mid(r)

    pl.run_scoped(
        middle,
        pltpu.VMEM((tokens, width), F32),
        pltpu.VMEM((tokens, width), F32),
        pltpu.VMEM((tokens, width), BF16),
    )
    later = dict(BACK_SCRATCH(width), bc_part=((r.full_x.shape[0], 2 * NSTATE), BF16))

    def rest(d_rest, *buffers):
        r.d_rest = r.d_proj = d_rest
        for name, buffer in zip(later, buffers):
            setattr(r, name, buffer)
        held_bc = (r.pair_bc, r.up_bc, r.down_bc, r.p_bc, r.l_bc, 1)
        r.grad_bc = LineScatter(w, flat_shard(r.bc_part, rows), *held_bc)
        phase_back(r)
        phase_last(r)

    pl.run_scoped(
        rest,
        pltpu.VMEM((tokens, width + 2 * NSTATE + LANES), BF16),
        *[pltpu.VMEM(*spec) for spec in later.values()],
    )


def whole_call(args, width):
    x_in, w_x = args[0], args[4]
    features, block = x_in.shape[1], x_in.shape[0]
    tokens = block * 4
    shard = w_x.shape[0]
    maps = 2 * NSTATE
    chunks = tokens // CHUNK
    turned_step = (STEP_ROWS, 2 * LANES)
    outs = dict(
        block=((block, features), BF16),
        grad_x=((block, features), BF16),
        w_z=((shard, width), F32),
        w_x=((shard, width), F32),
        w_bc=((shard, maps), F32),
        w_dt=(turned_step, F32),
        w_out=((shard, width), F32),
        small=((SMALL_DP, LANES), F32),
        shared=((SMALL_ALL, LANES), F32),
    )
    scratch = dict(
        x_held=((block, features), BF16),
        row_normed=((tokens, features), BF16),
        row_cot=((tokens, features), BF16),
        full_x=((features, width + maps), BF16),
        full_z=((features, width), BF16),
        full_out=((features, width), BF16),
        full_dt=((features, LANES), BF16),
        steps_t=((8 * STEP_ROWS, 2 * LANES), BF16),
        xr=((tokens, width), F32),
        bc=((tokens, maps), F32),
        dtr=((tokens, LANES), F32),
        y=((tokens, width), F32),
        pre_x=((tokens, width), F32),
        pre_bc=((tokens, maps), F32),
        maps=((tokens, maps), BF16),
        states=((tokens, width), BF16),
        state=((NSTATE, width), F32),
        step=((tokens, LANES), F32),
        total=((tokens, LANES), F32),
        total_t=((chunks * 16, LANES), F32),
        seg_down=((tokens + 16, LANES), F32),
        seg_across=((chunks, LANES), F32),
        turn=((LANES, 2 * LANES), BF16),
        a_log=((1, LANES), F32),
        dt_bias=((1, LANES), F32),
        cxb=((1, width), F32),
        cbb=((1, maps), F32),
        gain=((1, width), F32),
        skip=((1, width), F32),
        squares=((4, chunks, LANES), F32),
        crosses=((4, chunks, LANES), F32),
        gy=((tokens, width), BF16),
        d_z=((tokens, width), BF16),
        part=((tokens, features), BF16),
        far=((2, block // 2, features), BF16),
        near=((2, block, features), BF16),
        out_part=((features, width), BF16),
        dt_part=((8 * STEP_ROWS, 2 * LANES), F32),
        pair=((4 * shard, width), BF16),
        pair_bc=((4 * shard, maps), BF16),
        pair_dt=((4 * STEP_ROWS, 2 * LANES), F32),
        up=((3 * shard, width), BF16),
        down=((3 * shard, width), BF16),
        up_z=((3 * shard, width), BF16),
        down_z=((3 * shard, width), BF16),
        up_bc=((3 * shard, maps), BF16),
        down_bc=((3 * shard, maps), BF16),
        up_dt=((3 * STEP_ROWS, 2 * LANES), F32),
        down_dt=((3 * STEP_ROWS, 2 * LANES), F32),
        bc_sum=((shard, maps), F32),
        bc_slots=((4, shard, maps), BF16),
        small_pair=((2, SMALL_DP + SMALL_ALL, LANES), F32),
        small_z=((4, SMALL_DP + SMALL_ALL, LANES), F32),
        small_t=((4, SMALL_ALL, LANES), F32),
        g_gate=((8, width), F32),
        g_pre=((8, features), F32),
        **GRAD_OUT(width),
        **{"v_" + name: spec for name, spec in outs.items()},
    )
    dma = pltpu.SemaphoreType.DMA
    signal = pltpu.SemaphoreType.REGULAR
    semaphores = dict(
        s_w=dma((3, 3)),
        r_w=dma((3, 4 * PARTS + 1)),
        s_d=dma((3,)),
        r_d=dma((5,)),
        s_r=dma((2,)),
        r_r=dma((2, 3)),
        s_q=dma((1,)),
        r_q=dma((3,)),
        p_main=dma((5,)),
        p_bc=dma((5,)),
        p_dt=dma((5,)),
        l_main=dma((2 + 6 * PARTS,)),
        l_z=dma((2 + 6 * PARTS,)),
        l_bc=dma((8,)),
        l_dt=dma((8,)),
        s_e=dma((6, 2)),
        s_m=dma((6,)),
        s_o=dma((len(outs),)),
        free_pair=signal,
        free_line=signal,
        free_row=signal,
    )
    names = RAW_IN + tuple("o_" + name for name in outs) + tuple(scratch) + tuple(semaphores)
    values = list(args)
    values[6] = values[6].T
    values[15] = values[15].T
    whole = pl.BlockSpec(memory_space=pltpu.VMEM)
    apart = pl.BlockSpec(memory_space=pl.ANY)
    moved = ("x_in", "w_z", "w_x", "w_bc", "w_out", "cot")
    out = pl.pallas_call(
        functools.partial(whole_kernel, names=names, width=width),
        out_shape=tuple(jax.ShapeDtypeStruct(*spec) for spec in outs.values()),
        in_specs=[apart if name in moved else whole for name in RAW_IN],
        out_specs=tuple([apart] * len(outs)),
        scratch_shapes=[pltpu.VMEM(*spec) for spec in scratch.values()]
        + list(semaphores.values()),
        compiler_params=pltpu.CompilerParams(
            vmem_limit_bytes=VMEM_LIMIT, collective_id=0, has_side_effects=True
        ),
        cost_estimate=pl.CostEstimate(
            flops=5 * 10**10, bytes_accessed=1 << 26, transcendentals=0
        ),
    )(*values)
    return dict(zip(outs, out))


LARGE = ("block", "grad_x", "w_z", "w_x", "w_bc", "w_out")
FINAL = ("pre", "dt", "cxw", "cxb", "cbw", "cbb", "alog", "dtb", "skip", "gate")


def publish_kernel(*refs):
    count = len(LARGE)
    large_in, (steps, small, shared) = refs[:count], refs[count : count + 3]
    large_out = refs[count + 3 : 2 * count + 3]
    o = types.SimpleNamespace(**dict(zip(FINAL, refs[2 * count + 3 : -1])))
    sem = refs[-1]
    moves = [
        pltpu.make_async_copy(src, dst, sem.at[i])
        for i, (src, dst) in enumerate(zip(large_in, large_out))
    ]
    for move in moves:
        move.start()
    heads = o.alog.shape[0]

    def line(out, src, at):
        for p in range(out.shape[0] // LANES):
            out[p * LANES : (p + 1) * LANES] = src[at + p : at + p + 1, :].reshape(LANES)
        return at + out.shape[0] // LANES

    def taps(out, src, at):
        count = out.shape[1] // LANES
        for k in range(4):
            for p in range(count):
                out[k : k + 1, p * LANES : (p + 1) * LANES] = src[at + p : at + p + 1, :]
            at = at + count
        return at

    at = line(o.gate, small, 0)
    at = taps(o.cxw, small, at)
    at = line(o.cxb, small, at)
    for out in (o.skip, o.alog, o.dtb):
        out[...] = small[at : at + 1, 0:heads].reshape(heads)
        at = at + 1
    at = line(o.pre, shared, 0)
    at = taps(o.cbw, shared, at)
    line(o.cbb, shared, at)
    o.dt[...] = steps[0:heads, 0 : o.dt.shape[1]]
    for move in moves:
        move.wait()


def publish(o, width, heads):
    features = o["block"].shape[1]
    shard = o["w_z"].shape[0]
    shapes = dict(
        pre=(features,),
        dt=(heads, shard),
        cxw=(4, width),
        cxb=(width,),
        cbw=(4, 2 * NSTATE),
        cbb=(2 * NSTATE,),
        alog=(heads,),
        dtb=(heads,),
        skip=(heads,),
        gate=(width,),
    )
    whole = pl.BlockSpec(memory_space=pltpu.VMEM)
    apart = pl.BlockSpec(memory_space=pl.ANY)
    large = [o[name] for name in LARGE]
    out = pl.pallas_call(
        publish_kernel,
        out_shape=tuple(
            [jax.ShapeDtypeStruct(v.shape, v.dtype) for v in large]
            + [jax.ShapeDtypeStruct(shapes[name], F32) for name in FINAL]
        ),
        in_specs=[apart] * len(large) + [whole] * 3,
        out_specs=tuple([whole] * (len(large) + len(FINAL))),
        scratch_shapes=[pltpu.SemaphoreType.DMA((len(large),))],
    )(*large, o["w_dt"], o["small"], o["shared"])
    return types.SimpleNamespace(**dict(zip(LARGE + FINAL, out)))


def on_device_whole(*args):
    width = args[3].shape[1]
    heads = args[11].shape[0]
    p = publish(whole_call(args, width), width, heads)
    return (
        p.block,
        p.grad_x,
        p.pre,
        p.w_z,
        p.w_x,
        p.w_bc,
        p.dt.T,
        p.cxw,
        p.cxb,
        p.cbw,
        p.cbb,
        p.alog,
        p.dtb,
        p.skip,
        p.gate,
        p.w_out.T,
    )


def forward_plain(args, small, width):
    x_in, pre_gain, w_z, w_x, w_bc, w_dt, w_out, gate_gain, cotangent = args
    heads = w_dt.shape[1]
    at = layout_of(width)
    values = x_in.astype(F32)
    scale = lax.rsqrt(jnp.mean(values * values, axis=1) + EPS)
    normed = (values * scale[:, None] * pre_gain[None, :]).astype(BF16)
    row_normed = lax.all_gather(normed, "tensor", axis=0, tiled=True)
    mine = jnp.concatenate(
        (w_z, w_x, w_bc, jnp.pad(w_dt, ((0, 0), (0, LANES - heads)))), axis=1
    )
    stacked = lax.all_gather(mine, "dp", axis=0, tiled=True)
    full_out = lax.all_gather(w_out.T, "dp", axis=0, tiled=True)
    projected = jnp.dot(row_normed, stacked, preferred_element_type=F32)
    saved = mixer_forward(projected, small, width)
    row_cot = lax.all_gather(cotangent, "tensor", axis=0, tiled=True)
    y = saved[0]
    z_raw = projected[:, :width]
    gated = y * (z_raw * sigmoid(z_raw))
    d_mixed = dot_nn(row_cot, full_out)
    squares, cross = lax.psum(
        (
            jnp.sum(gated * gated, axis=1),
            jnp.sum(d_mixed * gate_gain[None, :] * gated, axis=1),
        ),
        "tensor",
    )
    return types.SimpleNamespace(
        row_normed=row_normed,
        row_cot=row_cot,
        full_z=stacked[:, :width],
        full_x=stacked[:, width:],
        full_out=full_out,
        z=z_raw,
        projected=(projected,),
        saved=saved,
        d_mixed=d_mixed,
        squares=squares,
        cross=cross,
    )


def on_device(
    x_in,
    segments,
    pre_gain,
    w_z,
    w_x,
    w_bc,
    w_dt,
    conv_x_w,
    conv_x_b,
    conv_bc_w,
    conv_bc_b,
    a_log,
    dt_bias,
    d_skip,
    gate_gain,
    w_out,
    cotangent,
):
    width = w_z.shape[1]
    heads = a_log.shape[0]
    at = layout_of(width)
    small = small_inputs(
        segments, conv_x_w, conv_x_b, conv_bc_w, conv_bc_b, a_log, dt_bias, d_skip
    )
    args = (x_in, pre_gain, w_z, w_x, w_bc, w_dt, w_out, gate_gain, cotangent)
    f = forward_plain(args, small, width)
    squares, cross = f.squares, f.cross
    y, z_raw, d_mixed = f.saved[0], f.z, f.d_mixed
    values = x_in.astype(F32)
    scale = lax.rsqrt(jnp.mean(values * values, axis=1) + EPS)
    gate = sigmoid(z_raw)
    gated = y * (z_raw * gate)
    inner_total = width * lax.axis_size("tensor")
    weighted = d_mixed * gate_gain[None, :]
    scale_two = lax.rsqrt(squares / inner_total + EPS)
    mixed = (gated * scale_two[:, None] * gate_gain[None, :]).astype(BF16)
    branch = lax.psum_scatter(
        dot_nt(mixed, f.full_out).astype(BF16), "tensor", scatter_dimension=0, tiled=True
    ).astype(F32)
    block_out = (values + branch).astype(BF16)
    grad_gate_part = jnp.sum(d_mixed * gated * scale_two[:, None], axis=0)
    d_gated = (
        scale_two[:, None] * weighted
        - gated * (scale_two * scale_two * scale_two * cross / inner_total)[:, None]
    )
    gy = (d_gated * (z_raw * gate)).astype(BF16)
    d_z = (d_gated * y * (gate * (1.0 + z_raw * (1.0 - gate)))).astype(BF16)
    d_rest, g_cxw, g_cxb, g_cbw, g_cbb, g_skip, g_alog, g_dtb = mixer_backward(
        f.projected, small, f.saved, gy, width
    )
    d_proj = jnp.concatenate((d_z, d_rest), axis=1)
    d_normed = lax.psum_scatter(
        (dot_nt(d_z, f.full_z) + dot_nt(d_rest, f.full_x)).astype(BF16),
        "tensor",
        scatter_dimension=0,
        tiled=True,
    ).astype(F32)
    proj_part = dot_tn(f.row_normed, d_proj)
    out_part = dot_tn(f.row_cot, mixed)
    owned = lax.psum_scatter(
        jnp.concatenate((proj_part, out_part), axis=1).astype(BF16),
        "dp",
        scatter_dimension=0,
        tiled=True,
    ).astype(F32)
    grad_w_bc = lax.psum(owned[:, at.bc : at.dt].astype(BF16), "tensor").astype(F32)
    pre_weighted = d_normed * pre_gain[None, :]
    grad_pre_part = jnp.sum(d_normed * values * scale[:, None], axis=0)
    feature_sum = jnp.sum(pre_weighted * values, axis=1)
    grad_x = (
        cotangent.astype(F32)
        + scale[:, None] * pre_weighted
        - values * (scale * scale * scale * feature_sum / values.shape[1])[:, None]
    ).astype(BF16)
    over_taps = lambda v: jnp.sum(v.reshape(4, 8, v.shape[1]), axis=1)
    over_rows = lambda v: jnp.sum(v, axis=0)
    grad_gate_gain, grad_cxw, grad_cxb, grad_alog, grad_dtb, grad_skip = lax.psum(
        (
            grad_gate_part,
            over_taps(g_cxw),
            over_rows(g_cxb),
            over_rows(g_alog)[:heads],
            over_rows(g_dtb)[:heads],
            jnp.sum(over_rows(g_skip).reshape(heads, HEADDIM), axis=1),
        ),
        "dp",
    )
    grad_pre_gain, grad_cbw, grad_cbb = lax.psum(
        (grad_pre_part, over_taps(g_cbw), over_rows(g_cbb)), ("dp", "tensor")
    )
    return (
        block_out,
        grad_x,
        grad_pre_gain,
        owned[:, :width],
        owned[:, width : at.bc],
        grad_w_bc,
        owned[:, at.dt : at.dt + heads],
        grad_cxw,
        grad_cxb,
        grad_cbw,
        grad_cbb,
        grad_alog,
        grad_dtb,
        grad_skip,
        grad_gate_gain,
        owned[:, at.all :].T,
    )


def solution(mesh):
    tokens = P(("dp", "tensor"), None)
    both = P("dp", "tensor")
    heads = P("tensor")
    line = mesh.shape["dp"] == 2 * (LAST_Z + 1) and mesh.shape["tensor"] == 4
    return jax.shard_map(
        on_device_whole if line else on_device,
        mesh=mesh,
        in_specs=(
            tokens,
            P("dp"),
            P(),
            both,
            both,
            P("dp", None),
            both,
            P(None, "tensor"),
            heads,
            P(),
            P(),
            heads,
            heads,
            heads,
            heads,
            P("tensor", "dp"),
            tokens,
        ),
        out_specs=(
            tokens,
            tokens,
            P(),
            both,
            both,
            P("dp", None),
            both,
            P(None, "tensor"),
            heads,
            P(),
            P(),
            heads,
            heads,
            heads,
            heads,
            P("tensor", "dp"),
        ),
        check_vma=False,
    )
```

```python
import functools
import types

import jax
import jax.numpy as jnp
from jax import lax
from jax.experimental import pallas as pl
from jax.experimental.pallas import tpu as pltpu
from jax.sharding import PartitionSpec as P

HEADDIM = 64
NSTATE = 128
CHUNK = 128
LANES = 128
EPS = 1e-05
LOG2E = 1.4426950408889634
F32 = jnp.float32
BF16 = jnp.bfloat16
VMEM_LIMIT = 62 * 1024 * 1024
exact = lax.Precision.HIGHEST


def dot_nn(a, b):
    return lax.dot_general(a, b, (((1,), (0,)), ((), ())), preferred_element_type=F32)


def dot_nt(a, b):
    return lax.dot_general(a, b, (((1,), (1,)), ((), ())), preferred_element_type=F32)


def dot_tn(a, b):
    return lax.dot_general(a, b, (((0,), (0,)), ((), ())), preferred_element_type=F32)


def sigmoid(v):
    return 1.0 / (1.0 + jnp.exp(-v))


def softplus(v):
    return jnp.maximum(v, 0.0) + jnp.log1p(jnp.exp(-jnp.abs(v)))


def fold_rows(v):
    return jnp.sum(v.reshape(v.shape[0] // 8, 8, v.shape[1]), axis=0)


def split_two(v):
    high = v.astype(BF16)
    return high, (v - high.astype(F32)).astype(BF16)


def tile_iotas():
    shape = (CHUNK, LANES)
    return lax.broadcasted_iota(jnp.int32, shape, 0), lax.broadcasted_iota(jnp.int32, shape, 1)


def chunk_rows(c, pad=0, extra=0):
    return pl.ds(pl.multiple_of(c * CHUNK + pad, 8), CHUNK + extra)


def prepare_steps(c, r):
    row, col = tile_iotas()
    rows = chunk_rows(c)
    lower = (row >= col).astype(F32)
    step = softplus(r.dtr[rows, r.dtr_at : r.dtr_at + LANES] + r.dt_bias[...])
    log_step = step * (-jnp.exp(r.a_log[...]) * LOG2E)
    total = jnp.dot(lower, log_step, precision=exact, preferred_element_type=F32)
    r.step[rows, :] = step
    r.total[rows, :] = total
    r.total_t[pl.ds(pl.multiple_of(c * 16, 16), 16), :] = total.T[:16]


def segment_parts(c, r):
    down = r.seg_down[chunk_rows(c, 8), :]
    across = r.seg_across[pl.ds(c, 1), :]
    before = r.seg_down[pl.ds(pl.multiple_of(c * CHUNK, 8), 8), :][7:8, :]
    last = down[CHUNK - 1 : CHUNK, :]
    carried = (down == before).astype(F32)
    to_end = (down == last).astype(F32)
    carry_on = (last == before).astype(F32)
    return down, across, carried, to_end, carry_on


def masks_back(c, r, down):
    window = r.seg_down[chunk_rows(c, 0, 8), :]
    return [
        (pltpu.roll(window, j, 0)[8 : 8 + CHUNK] == down).astype(F32) for j in range(1, 4)
    ]


def masks_ahead(c, r, down):
    window = r.seg_down[chunk_rows(c, 8, 8), :]
    full = CHUNK + 8
    return [(pltpu.roll(window, full - j, 0)[:CHUNK] == down).astype(F32) for j in range(1, 4)]


def conv_tile(c, ref, at, weight, bias, w_at, masks):
    lanes = slice(at, at + LANES)
    w_lanes = slice(w_at, w_at + LANES)
    here = ref[chunk_rows(c), lanes]
    ahead = ref[pl.ds(pl.multiple_of(jnp.maximum(c * CHUNK - 8, 0), 8), 8), lanes]
    window = jnp.concatenate([ahead, here], axis=0)
    out = here * weight[3:4, w_lanes] + bias[0:1, w_lanes]
    for j in range(1, 4):
        shifted = pltpu.roll(window, j, 0)[8 : 8 + CHUNK]
        out = out + (shifted * masks[j - 1]) * weight[3 - j : 4 - j, w_lanes]
    return out


def pair_columns(tile, p, first):
    left = jnp.broadcast_to(tile[:, 2 * p : 2 * p + 1], (CHUNK, LANES))
    right = jnp.broadcast_to(tile[:, 2 * p + 1 : 2 * p + 2], (CHUNK, LANES))
    return left, right, jnp.where(first, left, right)


def stack_heads(tile, first):
    zero = jnp.zeros_like(tile)
    return jnp.concatenate([jnp.where(first, tile, zero), jnp.where(first, zero, tile)], axis=0)


def scan_chunk(c, r):
    rows = chunk_rows(c)
    row, col = tile_iotas()
    down, across, carried, to_end, carry_on = segment_parts(c, r)
    masks = masks_back(c, r, down)
    maps = []
    for half in range(2):
        pre = conv_tile(c, r.bc, r.bc_at + half * LANES, r.cbw, r.cbb, half * LANES, masks)
        r.pre_bc[rows, half * LANES : (half + 1) * LANES] = pre
        maps.append((pre * sigmoid(pre)).astype(BF16))
    b_map, c_map = maps
    r.maps[rows, :LANES] = b_map
    r.maps[rows, LANES:] = c_map
    scores = jnp.where((down == across) & (row >= col), dot_nt(c_map, b_map), 0.0)
    b_turned = b_map.T
    total = r.total[rows, :]
    step = r.step[rows, :]
    first = col < HEADDIM
    for p in range(r.pairs):
        lanes = slice(p * LANES, (p + 1) * LANES)
        pre = conv_tile(c, r.xr, r.xr_at + p * LANES, r.cxw, r.cxb, p * LANES, masks)
        r.pre_x[rows, lanes] = pre
        chan = pre * sigmoid(pre)
        left, right, both = pair_columns(total, p, first)
        _, _, step_pair = pair_columns(step, p, first)
        fed = step_pair * chan
        stacked = stack_heads(fed.astype(BF16), first)
        mixing = []
        for k, mine in enumerate((left, right)):
            other = r.total_t[pl.ds(c * 16 + 2 * p + k, 1), :]
            mixing.append((scores * jnp.exp2(jnp.minimum(mine - other, 0.0))).astype(BF16))
        within = dot_nn(jnp.concatenate(mixing, axis=1), stacked)
        state = r.state[:, lanes]
        state_low = state.astype(BF16)
        r.states[rows, lanes] = state_low
        decay_in = jnp.exp2(both) * carried
        r.y[rows, lanes] = (
            within + decay_in * dot_nn(c_map, state_low) + r.skip[0:1, lanes] * chan
        )
        last = both[CHUNK - 1 : CHUNK, :]
        decay_out = jnp.exp2(last - both) * to_end
        r.state[:, lanes] = (jnp.exp2(last) * carry_on) * state + dot_nn(
            b_turned, (decay_out * fed).astype(BF16)
        )


def scan_chunk_back(c, r):
    rows = chunk_rows(c)
    row, col = tile_iotas()
    down, across, carried, to_end, carry_on = segment_parts(c, r)
    ahead = masks_ahead(c, r, down)
    b_map = r.maps[rows, :LANES]
    c_map = r.maps[rows, LANES:]
    visible = (down == across) & (row <= col)
    scores = jnp.where(visible, dot_nt(b_map, c_map), 0.0)
    c_turned = c_map.T
    total = r.total[rows, :]
    step = r.step[rows, :]
    first = col < HEADDIM
    d_scores = jnp.zeros((CHUNK, LANES), F32)
    width = r.pairs * LANES
    for p in range(r.pairs):
        lanes = slice(p * LANES, (p + 1) * LANES)
        lows = slice(width + p * LANES, width + (p + 1) * LANES)
        gy_low = r.gy[rows, lanes]
        gy = gy_low.astype(F32)
        pre = r.pre_x[rows, lanes]
        gate = sigmoid(pre)
        chan = pre * gate
        left, right, both = pair_columns(total, p, first)
        _, _, step_pair = pair_columns(step, p, first)
        fed = step_pair * chan
        fed_low = fed.astype(BF16)
        d_mixing = dot_nt(stack_heads(fed_low, first), gy_low)
        mixing = []
        for k, mine in enumerate((left, right)):
            other = r.total_t[pl.ds(c * 16 + 2 * p + k, 1), :]
            decay = jnp.exp2(jnp.minimum(other - mine, 0.0))
            mixing.append((scores * decay).astype(BF16))
            d_scores = d_scores + d_mixing[k * CHUNK : (k + 1) * CHUNK] * decay
        d_state = r.d_state[:, lanes]
        d_state_low = d_state.astype(BF16)
        last = both[CHUNK - 1 : CHUNK, :]
        decay_out = jnp.exp2(last - both) * to_end
        from_state = decay_out * dot_nn(b_map, d_state_low)
        d_fed = dot_nn(jnp.concatenate(mixing, axis=1), stack_heads(gy_low, first)) + from_state
        fed_held = fed_low.astype(F32)
        skip = r.skip[0:1, lanes]
        flow = gy * (r.y[rows, lanes] - skip * chan) - fed_held * d_fed
        direct = chan * d_fed
        for k, part in enumerate((flow, direct)):
            spot = slice(k * CHUNK, (k + 1) * CHUNK)
            r.sums[spot, lanes], r.sums[spot, lows] = split_two(part)
        keep = jnp.exp2(last) * carry_on
        through = jnp.sum(fed_held * from_state, axis=0, keepdims=True) + keep * jnp.sum(
            r.states[rows, lanes].astype(F32) * d_state, axis=0, keepdims=True
        )
        spot = slice(2 * CHUNK, 2 * CHUNK + 16)
        r.sums[spot, lanes], r.sums[spot, lows] = split_two(
            jnp.broadcast_to(through, (16, LANES))
        )
        grad_in = (jnp.exp2(both) * carried * gy).astype(BF16)
        r.grad_in[:, lanes] = grad_in
        r.fed_out[:, lanes] = (decay_out * fed).astype(BF16)
        r.d_state_low[:, lanes] = d_state_low
        r.d_state[:, lanes] = keep * d_state + dot_nn(c_turned, grad_in)
        d_chan = skip * gy + step_pair * d_fed
        r.g_skip[:, lanes] += fold_rows(gy * chan)
        d_pre = d_chan * (gate * (1.0 + pre * (1.0 - gate)))
        conv_back(c, r, d_pre, r.d_pre_x, r.xr, r.xr_at, r.cxw, p * LANES, ahead, r.dx_at, r.g_cxw, r.g_cxb)
    d_scores_low = jnp.where(visible, d_scores, 0.0).astype(BF16)
    d_b = dot_nn(d_scores_low, c_map) + dot_nt(r.fed_out[...], r.d_state_low[...])
    d_c = dot_tn(d_scores_low, b_map) + dot_nt(r.grad_in[...], r.states[rows, :])
    for half, d_map in enumerate((d_b, d_c)):
        pre = r.pre_bc[rows, half * LANES : (half + 1) * LANES]
        gate = sigmoid(pre)
        d_pre = d_map * (gate * (1.0 + pre * (1.0 - gate)))
        conv_back(
            c, r, d_pre, r.d_pre_bc, r.bc, r.bc_at, r.cbw, half * LANES, ahead, r.dbc_at, r.g_cbw, r.g_cbb
        )
    reduced = dot_nn(r.sums[...], r.head_sum[...])
    d_total = jnp.dot(
        (row <= col).astype(F32), reduced[:CHUNK], precision=exact, preferred_element_type=F32
    ) + reduced[2 * CHUNK : 2 * CHUNK + 1]
    a_neg = -jnp.exp(r.a_log[...])
    d_step = reduced[CHUNK : 2 * CHUNK] + a_neg * d_total
    r.g_alog[...] += fold_rows(step * d_total) * a_neg
    d_raw = d_step * sigmoid(r.dtr[rows, r.dtr_at : r.dtr_at + LANES] + r.dt_bias[...])
    r.g_dtb[...] += fold_rows(d_raw)
    r.d_proj[rows, r.ddt_at : r.ddt_at + LANES] = d_raw.astype(BF16)


def conv_back(c, r, d_pre, held, raw, raw_at, weight, at, ahead, out_at, g_w, g_b):
    lanes = slice(at, at + LANES)
    rows = chunk_rows(c)
    held[CHUNK : CHUNK + 8, lanes] = held[0:8, lanes]
    held[0:CHUNK, lanes] = d_pre
    window = held[:, lanes]
    values = raw[rows, raw_at + at : raw_at + at + LANES]
    g_b[:, lanes] += fold_rows(d_pre)
    g_w[24:32, lanes] += fold_rows(d_pre * values)
    d_raw = d_pre * weight[3:4, lanes]
    for j in range(1, 4):
        shifted = pltpu.roll(window, CHUNK + 8 - j, 0)[:CHUNK] * ahead[j - 1]
        d_raw = d_raw + shifted * weight[3 - j : 4 - j, lanes]
        g_w[(3 - j) * 8 : (4 - j) * 8, lanes] += fold_rows(shifted * values)
    r.d_proj[rows, out_at + at : out_at + at + LANES] = d_raw.astype(BF16)


def head_sum_matrix(width):
    shape = (2 * width, LANES)
    lane = lax.broadcasted_iota(jnp.int32, shape, 0)
    lane = jnp.where(lane >= width, lane - width, lane)
    return (lane // HEADDIM == lax.broadcasted_iota(jnp.int32, shape, 1)).astype(BF16)


def layout_of(width):
    return types.SimpleNamespace(
        x=width, bc=2 * width, dt=2 * width + 2 * NSTATE, all=2 * width + 2 * NSTATE + LANES
    )


SMALL_IN = ("seg_down", "seg_across", "cxw", "cxb", "cbw", "cbb", "a_log", "dt_bias", "skip")


def small_inputs(segments, cxw, cxb, cbw, cbb, a_log, dt_bias, d_skip):
    tokens = segments.shape[0]
    seg = segments.astype(F32)
    edge = jnp.full((8,), -1.0, F32)
    down = jnp.broadcast_to(jnp.concatenate([edge, seg, edge])[:, None], (tokens + 16, LANES))
    heads = a_log.shape[0]
    pad = lambda v: jnp.pad(v, (0, LANES - heads))[None, :]
    return (
        down,
        seg.reshape(tokens // CHUNK, CHUNK),
        cxw,
        cxb[None, :],
        cbw,
        cbb[None, :],
        pad(a_log),
        pad(dt_bias),
        jnp.repeat(d_skip, HEADDIM)[None, :],
    )


def take_projections(r, width):
    r.pairs = width // LANES
    if hasattr(r, "proj"):
        at = layout_of(width)
        r.xr = r.bc = r.dtr = r.proj
        r.xr_at, r.bc_at, r.dtr_at = at.x, at.bc, at.dt
    else:
        r.xr_at = r.bc_at = r.dtr_at = 0


def forward_kernel(*refs, names, width):
    r = types.SimpleNamespace(**dict(zip(names, refs)))
    take_projections(r, width)
    chunks = r.dtr.shape[0] // CHUNK
    r.state[...] = jnp.zeros_like(r.state)

    def body(c, carry):
        prepare_steps(c, r)
        scan_chunk(c, r)
        return carry

    lax.fori_loop(0, chunks, body, 0)


def backward_kernel(*refs, names, width):
    r = types.SimpleNamespace(**dict(zip(names, refs)))
    take_projections(r, width)
    r.dx_at, r.dbc_at, r.ddt_at = 0, width, width + 2 * NSTATE
    start_back(r)
    chunks = r.dtr.shape[0] // CHUNK

    def body(i, carry):
        scan_chunk_back(chunks - 1 - i, r)
        return carry

    lax.fori_loop(0, chunks, body, 0)


def start_back(r):
    for ref in (r.d_state, r.d_pre_x, r.d_pre_bc, r.g_cxw, r.g_cxb, r.g_cbw, r.g_cbb):
        ref[...] = jnp.zeros_like(ref)
    for ref in (r.g_skip, r.g_alog, r.g_dtb):
        ref[...] = jnp.zeros_like(ref)
    r.head_sum[...] = head_sum_matrix(r.pairs * LANES)


def call_local(kernel, width, ins, outs, scratch, values, flops):
    names = tuple(ins) + tuple(outs) + tuple(scratch)
    whole = pl.BlockSpec(memory_space=pltpu.VMEM)
    return pl.pallas_call(
        functools.partial(kernel, names=names, width=width),
        out_shape=tuple(jax.ShapeDtypeStruct(*spec) for spec in outs.values()),
        in_specs=[whole] * len(ins),
        out_specs=tuple([whole] * len(outs)),
        scratch_shapes=[pltpu.VMEM(*spec) for spec in scratch.values()],
        compiler_params=pltpu.CompilerParams(vmem_limit_bytes=VMEM_LIMIT),
        cost_estimate=pl.CostEstimate(flops=flops, bytes_accessed=1 << 24, transcendentals=0),
    )(*values)


def mixer_forward(projected, small, width):
    tokens = projected.shape[0]
    outs = dict(
        y=((tokens, width), F32),
        pre_x=((tokens, width), F32),
        pre_bc=((tokens, 2 * NSTATE), F32),
        maps=((tokens, 2 * NSTATE), BF16),
        states=((tokens, width), BF16),
        step=((tokens, LANES), F32),
        total=((tokens, LANES), F32),
        total_t=((tokens // CHUNK * 16, LANES), F32),
    )
    scratch = dict(state=((NSTATE, width), F32))
    return call_local(
        forward_kernel, width, ("proj",) + SMALL_IN, outs, scratch, (projected,) + small, 10**10
    )


BACK_SCRATCH = lambda width: dict(
    d_state=((NSTATE, width), F32),
    d_state_low=((NSTATE, width), BF16),
    grad_in=((CHUNK, width), BF16),
    fed_out=((CHUNK, width), BF16),
    sums=((2 * CHUNK + 16, 2 * width), BF16),
    head_sum=((2 * width, LANES), BF16),
    d_pre_x=((CHUNK + 8, width), F32),
    d_pre_bc=((CHUNK + 8, 2 * NSTATE), F32),
)
GRAD_OUT = lambda width: dict(
    g_cxw=((32, width), F32),
    g_cxb=((8, width), F32),
    g_cbw=((32, 2 * NSTATE), F32),
    g_cbb=((8, 2 * NSTATE), F32),
    g_skip=((8, width), F32),
    g_alog=((8, LANES), F32),
    g_dtb=((8, LANES), F32),
)


SAVED = ("y", "pre_x", "pre_bc", "maps", "states", "step", "total", "total_t")


def mixer_backward(projected, small, saved, gy, width):
    tokens = gy.shape[0]
    outs = dict(d_proj=((tokens, width + 2 * NSTATE + LANES), BF16), **GRAD_OUT(width))
    ins = (("proj",) if len(projected) == 1 else ("xr", "bc", "dtr")) + SMALL_IN
    ins = ins + SAVED + ("gy",)
    return call_local(
        backward_kernel,
        width,
        ins,
        outs,
        BACK_SCRATCH(width),
        tuple(projected) + small + tuple(saved) + (gy,),
        3 * 10**10,
    )


UP, DOWN, PAIR = range(3)
LAST_Z = 3
STEP_ROWS = 16
PARTS = 2


def place():
    dp = lax.axis_index("dp")
    tp = lax.axis_index("tensor")
    z = dp // 2
    core = dp - 2 * z
    y = tp // 2
    x = tp - 2 * y
    return types.SimpleNamespace(
        dp=dp,
        tp=tp,
        z=z,
        core=core,
        mate=dp + 1 - 2 * core,
        near_x=y * 2 + (1 - x),
        near_y=(1 - y) * 2 + x,
        across=(1 - y) * 2 + (1 - x),
    )


def device(w, dp=None, tp=None):
    return {"dp": w.dp if dp is None else dp, "tensor": w.tp if tp is None else tp}


def other_z(w, k):
    return lax.rem(w.z + k, LAST_Z + 1) * 2 + w.core


def peers(w):
    rows = [device(w, tp=t) for t in (w.near_x, w.near_y, w.across)]
    return rows + [device(w, dp=w.mate)] + [device(w, dp=other_z(w, k)) for k in (1, 2, 3)]


def tell(sem, where):
    pl.semaphore_signal(sem, inc=1, device_id=where, device_id_type=pl.DeviceIdType.MESH)


def greet(w):
    barrier = pltpu.get_barrier_semaphore()
    for where in peers(w):
        tell(barrier, where)
    pl.semaphore_wait(barrier, len(peers(w)))


def remote(src, dst, send, recv, where):
    return pltpu.make_async_remote_copy(
        src_ref=src,
        dst_ref=dst,
        send_sem=send,
        recv_sem=recv,
        device_id=where,
        device_id_type=pl.DeviceIdType.MESH,
    )


def settle(ref, send, recv, where, sent=True):
    copy = remote(ref, ref, send, recv, where)
    if sent:
        copy.wait_send()
    else:
        copy.wait_recv()


class LineGather:
    def __init__(self, w, ref, send, recv, parts):
        self.w, self.ref, self.send, self.recv, self.parts = w, ref, send, recv, parts
        self.rows = ref.shape[0] // (2 * (LAST_Z + 1))

    def shard(self, z, core, part):
        rows = self.rows // self.parts
        start = pl.multiple_of((z * 2 + core) * self.rows + part * rows, 16)
        return self.ref.at[pl.ds(start, rows)]

    def copy(self, z, kind, part):
        w = self.w
        block = self.shard(z, w.core, part)
        to = {UP: w.dp + 2, DOWN: w.dp - 2}.get(kind, w.mate)
        first = (self.parts if kind == PAIR else part) * (LAST_Z + 1)
        return remote(block, block, self.send.at[kind], self.recv.at[first + z], device(w, dp=to))

    def relay(self, step):
        for part in range(self.parts):
            self.relay_part(step, part)

    def relay_part(self, step, part):
        w = self.w

        def low():
            z = w.z - step
            if step > 0:
                self.copy(z, UP, part).wait_recv()
            pl.when(w.z < LAST_Z)(lambda: self.copy(z, UP, part).start())
            if step == 0:
                pl.when(w.z > 0)(lambda: self.copy(z, DOWN, part).start())
            self.copy(z, PAIR, part).start()

        def high():
            z = w.z + step
            self.copy(z, DOWN, part).wait_recv()
            pl.when(w.z > 0)(lambda: self.copy(z, DOWN, part).start())
            self.copy(z, PAIR, part).start()

        if step == 0:
            low()
        else:
            pl.when(w.z >= step)(low)
            pl.when(w.z <= LAST_Z - step)(high)

    def some(self, count):
        return self.ref.at[pl.ds(0, count * self.rows)]

    def from_mate(self, z):
        block = self.some(1)
        recv = self.recv.at[self.parts * (LAST_Z + 1) + z]
        settle(block, self.send.at[PAIR], recv, device(self.w, dp=self.w.mate), sent=False)

    def finish(self):
        for z in range(LAST_Z + 1):
            self.from_mate(z)

    def drain(self):
        w = self.w
        where = device(w, dp=w.mate)
        wait = lambda count, kind: settle(
            self.some(count), self.send.at[kind], self.recv.at[0], where
        )
        wait(LAST_Z + 1, PAIR)
        for z in range(LAST_Z):
            pl.when(w.z == z)(lambda z=z: wait(z + 1, UP))
            pl.when(w.z == LAST_Z - z)(lambda z=z: wait(z + 1, DOWN))


class RowGather:
    def __init__(self, w, ref, send, recv):
        self.w, self.ref, self.send, self.recv = w, ref, send, recv
        self.rows = ref.shape[0] // 4

    def copy(self, i):
        w = self.w
        slot, half, to = (
            (w.tp, 0, w.near_x),
            (w.tp, 1, w.near_y),
            (w.tp, 1, w.near_x),
            (w.tp, 0, w.near_y),
            (w.near_x, 0, w.near_y),
            (w.near_y, 1, w.near_x),
        )[i]
        block = row_block(self.ref, self.rows, slot, half)
        return remote(block, block, self.send, self.recv.at[min(i, 2)], device(w, tp=to))

    def start(self):
        for i in range(4):
            self.copy(i).start()

    def hand_on(self):
        for i in range(2):
            self.copy(i).wait_recv()
            self.copy(i + 4).start()

    def some(self, count):
        return self.ref.at[pl.ds(0, count * self.rows)]

    def finish(self):
        where = device(self.w, tp=self.w.near_x)
        settle(self.some(2), self.send, self.recv.at[2], where, sent=False)

    def drain(self):
        settle(self.some(3), self.send, self.recv.at[2], device(self.w, tp=self.w.near_x))


def row_block(ref, rows, slot, half=None):
    start = slot * rows
    if half is not None:
        rows = rows // 2
        start = start + half * rows
    return ref.at[pl.ds(pl.multiple_of(start, 16), rows)]


def add_into(ref, other):
    rows = 64 if ref.shape[0] % 64 == 0 else ref.shape[0]

    def body(i, carry):
        here = pl.ds(pl.multiple_of(i * rows, rows), rows)
        ref[here, :] = (ref[here, :].astype(F32) + other[here, :].astype(F32)).astype(ref.dtype)
        return carry

    lax.fori_loop(0, ref.shape[0] // rows, body, 0)


class RowScatter:
    def __init__(self, w, part, far, near, send, recv):
        self.w, self.part, self.far, self.near, self.send, self.recv = w, part, far, near, send, recv
        self.rows = part.shape[0] // 4

    def block(self, slot, half=None):
        return row_block(self.part, self.rows, slot, half)

    def copy(self, i):
        w = self.w
        half = lambda k, h: row_block(self.near.at[k], self.rows, 0, h)
        src, dst, to = (
            (lambda: self.block(w.across, 0), lambda: self.far.at[0], w.near_x),
            (lambda: self.block(w.across, 1), lambda: self.far.at[1], w.near_y),
            (lambda: self.block(w.near_x, 0), lambda: half(0, 0), w.near_x),
            (lambda: self.block(w.near_y, 1), lambda: half(1, 1), w.near_y),
            (lambda: self.block(w.near_x, 1), lambda: half(0, 1), w.near_x),
            (lambda: self.block(w.near_y, 0), lambda: half(1, 0), w.near_y),
        )[i]
        return remote(src(), dst(), self.send, self.recv.at[min(i, 2)], device(w, tp=to))

    def start(self, *which):
        for i in which:
            self.copy(i).start()

    def hand_on(self):
        w = self.w
        self.copy(1).wait_recv()
        add_into(self.block(w.near_x, 1), self.far.at[1])
        self.copy(4).start()
        self.copy(0).wait_recv()
        add_into(self.block(w.near_y, 0), self.far.at[0])
        self.copy(5).start()

    def some(self, count):
        return self.part.at[pl.ds(0, count * self.rows)]

    def finish(self):
        where = device(self.w, tp=self.w.near_x)
        settle(self.some(2), self.send, self.recv.at[2], where, sent=False)

    def total(self, here, there):
        total = self.part[there, :].astype(F32)
        return total + self.near[0, here, :].astype(F32) + self.near[1, here, :].astype(F32)

    def drain(self):
        settle(self.some(3), self.send, self.recv.at[2], device(self.w, tp=self.w.near_x))


class LineScatter:
    def __init__(self, w, shard, pair, up, down, pair_sem, line_sem, parts):
        self.w, self.shard, self.pair, self.up, self.down = w, shard, pair, up, down
        self.pair_sem, self.line_sem, self.parts = pair_sem, line_sem, parts
        self.rows = pair.shape[0] // (LAST_Z + 1)

    def slot(self, ref, i):
        return ref.at[pl.ds(pl.multiple_of(i * self.rows, 16), self.rows)]

    def piece(self, ref, part):
        rows = self.rows // self.parts
        return ref.at[pl.ds(part * rows, rows)]

    def pair_copy(self, z):
        w = self.w
        return remote(
            self.shard(z, 1 - w.core),
            self.slot(self.pair, z),
            self.pair_sem.at[LAST_Z + 1],
            self.pair_sem.at[z],
            device(w, dp=w.mate),
        )

    def up_copy(self, z, part):
        return remote(
            self.piece(self.shard(z, self.w.core), part),
            self.piece(self.slot(self.up, z - 1), part),
            self.line_sem.at[0],
            self.line_sem.at[2 + part * LAST_Z + z - 1],
            device(self.w, dp=self.w.dp + 2),
        )

    def down_copy(self, z, part):
        return remote(
            self.piece(self.shard(z, self.w.core), part),
            self.piece(self.slot(self.down, z), part),
            self.line_sem.at[1],
            self.line_sem.at[2 + (self.parts + part) * LAST_Z + z],
            device(self.w, dp=self.w.dp - 2),
        )

    def launch(self, z):
        w = self.w
        self.pair_copy(z).wait_recv()

        def every(send):
            for part in range(self.parts):
                add_into(self.piece(self.shard(z, w.core), part), self.piece(self.slot(self.pair, z), part))
                if send is not None:
                    send(z, part).start()

        low = (w.z == 0) & (z > 0)
        high = (w.z == LAST_Z) & (z < LAST_Z)
        pl.when(low)(lambda: every(self.up_copy))
        pl.when(high)(lambda: every(self.down_copy))
        pl.when(jnp.logical_not(low | high))(lambda: every(None))

    def pass_up(self, z):
        for part in range(self.parts):
            self.up_copy(z, part).wait_recv()
            add_into(
                self.piece(self.shard(z, self.w.core), part),
                self.piece(self.slot(self.up, z - 1), part),
            )
            self.up_copy(z, part).start()

    def pass_down(self, z):
        for part in range(self.parts):
            self.down_copy(z, part).wait_recv()
            add_into(
                self.piece(self.shard(z, self.w.core), part),
                self.piece(self.slot(self.down, z), part),
            )
            self.down_copy(z, part).start()

    def step(self, k):
        w = self.w
        if k == 0:
            pl.when(w.z == 1)(lambda: self.pass_up(3))
            pl.when(w.z == 2)(lambda: self.pass_down(0))
        else:

            @pl.when(w.z == 1)
            def _():
                self.pass_up(2)
                self.pass_down(0)

            @pl.when(w.z == 2)
            def _():
                self.pass_down(1)
                self.pass_up(3)

    def finish(self, out):
        w = self.w
        own = self.shard(w.z, w.core)
        rows = self.rows // self.parts

        def add(part, copy, slot):
            here = pl.ds(part * rows, rows)
            copy(w.z, part).wait_recv()
            out[here, :] += self.piece(slot, part)[...].astype(F32)

        out[...] = own[...].astype(F32)
        for part in range(self.parts):
            pl.when(w.z > 0)(
                lambda part=part: add(part, self.up_copy, self.slot(self.up, w.z - 1))
            )
            pl.when(w.z < LAST_Z)(
                lambda part=part: add(part, self.down_copy, self.slot(self.down, w.z))
            )

    def drain_pair(self):
        where = device(self.w, dp=self.w.mate)
        settle(self.pair, self.pair_sem.at[LAST_Z + 1], self.pair_sem.at[0], where)

    def drain(self):
        w = self.w
        where = device(w, dp=w.mate)
        for z in range(LAST_Z):
            sent = self.up.at[pl.ds(0, (LAST_Z - z) * self.rows)]
            pl.when(w.z == z)(
                lambda sent=sent: settle(sent, self.line_sem.at[0], self.line_sem.at[2], where)
            )
            pl.when(w.z == LAST_Z - z)(
                lambda sent=sent: settle(sent, self.line_sem.at[1], self.line_sem.at[2], where)
            )


class Exchange:
    def __init__(self, ref, mine, targets, sems):
        self.ref, self.mine, self.targets, self.sems = ref, mine, targets, sems

    def start(self):
        part = self.ref.at[self.mine]
        for target in self.targets:
            remote(part, part, self.sems.at[0], self.sems.at[1], target).start()

    def finish(self):
        count = len(self.targets)
        some = self.ref.at[pl.ds(0, count)]
        for sent in (False, True):
            settle(some, self.sems.at[0], self.sems.at[1], self.targets[0], sent=sent)

    def total(self):
        total = self.ref[0].astype(F32)
        for i in range(1, self.ref.shape[0]):
            total = total + self.ref[i].astype(F32)
        return total


def norm_rows(x_ref, gain, out_ref, start):
    rows = 64

    def body(i, carry):
        here = pl.ds(pl.multiple_of(i * rows, rows), rows)
        values = x_ref[here, :].astype(F32)
        scale = lax.rsqrt(jnp.mean(values * values, axis=1, keepdims=True) + EPS)
        there = pl.ds(pl.multiple_of(start + i * rows, 16), rows)
        out_ref[there, :] = (values * scale * gain).astype(BF16)
        return carry

    lax.fori_loop(0, x_ref.shape[0] // rows, body, 0)


def by_rows(total, rows, body):
    def step(i, carry):
        body(pl.ds(pl.multiple_of(i * rows, rows), rows))
        return carry

    lax.fori_loop(0, total // rows, step, 0)


def over_chunks(r, body):
    def step(c, carry):
        body(c)
        return carry

    lax.fori_loop(0, r.chunks, step, 0)


def turned(row):
    return jnp.broadcast_to(row, (CHUNK, LANES)).T


def gated_tile(c, r, p):
    rows, lanes = chunk_rows(c), slice(p * LANES, (p + 1) * LANES)
    z = r.z[rows, lanes]
    gate = sigmoid(z)
    return z, gate, r.y[rows, lanes]


def square_chunk(c, r):
    square = jnp.zeros((CHUNK, LANES), F32)
    for p in range(r.pairs):
        z, gate, y = gated_tile(c, r, p)
        gated = y * (z * gate)
        square = square + gated * gated
    r.squares.at[r.w.tp][pl.ds(c, 1), :] = jnp.sum(square.T, axis=0, keepdims=True)


def cross_chunk(c, r):
    rows = chunk_rows(c)
    cross = jnp.zeros((CHUNK, LANES), F32)
    for p in range(r.pairs):
        lanes = slice(p * LANES, (p + 1) * LANES)
        z, gate, y = gated_tile(c, r, p)
        cross = cross + r.d_mixed[rows, lanes] * r.gain[0:1, lanes] * (y * (z * gate))
    r.crosses.at[r.w.tp][pl.ds(c, 1), :] = jnp.sum(cross.T, axis=0, keepdims=True)


def slot_sum(ref, c):
    total = ref[0, pl.ds(c, 1), :]
    for i in range(1, 4):
        total = total + ref[i, pl.ds(c, 1), :]
    return total


def scale_two_row(c, r):
    return lax.rsqrt(slot_sum(r.squares, c) / (r.pairs * LANES * 4) + EPS)


def mix_chunk(c, r):
    rows = chunk_rows(c)
    scale = turned(scale_two_row(c, r))
    for p in range(r.pairs):
        lanes = slice(p * LANES, (p + 1) * LANES)
        z, gate, y = gated_tile(c, r, p)
        r.mixed[rows, lanes] = (y * (z * gate) * scale * r.gain[0:1, lanes]).astype(BF16)


def gate_back_chunk(c, r):
    rows = chunk_rows(c)
    row = scale_two_row(c, r)
    pull = turned(row * row * row * slot_sum(r.crosses, c) / (r.pairs * LANES * 4))
    scale = turned(row)
    for p in range(r.pairs):
        lanes = slice(p * LANES, (p + 1) * LANES)
        z, gate, y = gated_tile(c, r, p)
        silu = z * gate
        gated = y * silu
        scaled = r.d_mixed[rows, lanes] * scale
        r.g_gate[:, lanes] += fold_rows(scaled * gated)
        d_gated = scaled * r.gain[0:1, lanes] - gated * pull
        r.gy[rows, lanes] = (d_gated * silu).astype(BF16)
        r.d_z[rows, lanes] = (d_gated * y * (gate * (1.0 + z * (1.0 - gate)))).astype(BF16)


def by_distance(z, i):
    upper = z // 2
    low = z + upper * (LAST_Z - 2 * z)
    chip = low + i * (1 - 2 * low) if i < 2 else i
    return chip + upper * (LAST_Z - 2 * chip)


def chip_rows(r, z):
    count = 2 * r.shard_rows
    return pl.ds(pl.multiple_of(z * count, LANES), count)


def accumulate(ref, rows, value, first):
    if first:
        ref[rows, :] = value
    else:
        ref[rows, :] += value


def project_z(r, i):
    z = by_distance(r.w.z, i)
    r.shard_z.from_mate(z)
    here = chip_rows(r, z)

    def body(rows):
        accumulate(r.z, rows, dot_nn(r.row_normed[rows, here], r.full_z[here, :]), i == 0)

    by_rows(r.row_normed.shape[0], 256, body)


def output_back(r, i):
    z = by_distance(r.w.z, i)
    r.shard_out.from_mate(z)
    here = chip_rows(r, z)

    def body(rows):
        accumulate(r.d_mixed, rows, dot_nn(r.row_cot[rows, here], r.full_out[here, :]), i == 0)

    by_rows(r.row_normed.shape[0], 256, body)


def output_share(r, slot):
    block = r.x_held.shape[0]
    rows = pl.ds(pl.multiple_of(slot * block, block), block)
    tile = 512

    def body(n, carry):
        cols = pl.ds(pl.multiple_of(n * tile, tile), tile)
        r.part[rows, cols] = dot_nt(r.mixed[rows, :], r.full_out[cols, :]).astype(BF16)
        return carry

    lax.fori_loop(0, r.part.shape[1] // tile, body, 0)


def far_first(w, i):
    upper = w.z // 2
    return (1 - upper) * (LAST_Z - i) + upper * i


def weight_parts(make, scatter):
    def body(i, carry):
        z = far_first(scatter.w, i)
        make(z)
        scatter.pair_copy(z).start()
        pl.when(i > 0)(lambda: scatter.launch(far_first(scatter.w, i - 1)))
        return carry

    lax.fori_loop(0, LAST_Z + 1, body, 0)
    scatter.launch(far_first(scatter.w, LAST_Z))
    scatter.drain_pair()


def product_maker(left, right, store):
    block = left.shape[1] // (LAST_Z + 1)

    def make(z):
        lanes = pl.ds(pl.multiple_of(z * block, LANES), block)
        store(z, dot_tn(left[:, lanes], right[...]).astype(BF16))

    return make


def flat_shard(ref, rows):
    return lambda z, core: ref.at[pl.ds(pl.multiple_of((z * 2 + core) * rows, 16), rows)]


def flat_store(ref, rows):
    def store(z, value):
        ref[pl.ds(pl.multiple_of(z * 2 * rows, 16), 2 * rows), :] = value

    return store


def side_shard(ref, rows, width):
    return lambda z, core: ref.at[
        pl.ds(pl.multiple_of(z * rows, 16), rows),
        pl.ds(pl.multiple_of(core * width, LANES), width),
    ]


def side_store(ref, rows, width):
    def store(z, value):
        here = pl.ds(pl.multiple_of(z * rows, 16), rows)
        ref[here, :width] = value[:rows]
        ref[here, width : 2 * width] = value[rows:]

    return store


def own_rows(r):
    shard = r.w_x.shape[0]
    return pl.ds(pl.multiple_of(r.w.dp * shard, 16), shard)


def input_moves(r):
    width = r.pairs * LANES
    own = own_rows(r)
    block = r.cot.shape[0]
    mine = pl.ds(pl.multiple_of(r.w.tp * block, block), block)
    moves = (
        (r.w_x, r.full_x.at[own, pl.ds(0, width)]),
        (r.w_bc, r.full_x.at[own, pl.ds(width, 2 * NSTATE)]),
        (r.x_in, r.x_held),
        (r.w_z, r.full_z.at[own]),
        (r.w_out, r.full_out.at[own]),
        (r.cot, r.row_cot.at[mine]),
    )
    return [pltpu.make_async_copy(src, dst, r.s_m.at[i]) for i, (src, dst) in enumerate(moves)]


def place_steps(r):
    heads, shard = r.w_dt.shape
    mine = r.steps_t.at[pl.ds(pl.multiple_of(r.w.dp * STEP_ROWS, STEP_ROWS), STEP_ROWS)]
    r.turn[...] = jnp.zeros_like(r.turn)
    r.turn[0:heads, 0:shard] = r.w_dt[...]
    mine[...] = r.turn[0:STEP_ROWS, :]


def turn_steps(r):
    shard = r.w_x.shape[0]

    def body(d, carry):
        r.turn[0:STEP_ROWS, :] = r.steps_t[
            pl.ds(pl.multiple_of(d * STEP_ROWS, STEP_ROWS), STEP_ROWS), :
        ]
        r.full_dt[pl.ds(pl.multiple_of(d * shard, 16), shard), :] = r.turn[...].T[:shard]
        return carry

    lax.fori_loop(0, 2 * (LAST_Z + 1), body, 0)


def prepare_small(r):
    heads = r.a_log_in.shape[0]
    w, width = r.w, r.pairs * LANES
    for ref in (r.a_log, r.dt_bias):
        ref[...] = jnp.zeros_like(ref)
    r.a_log[0:1, 0:heads] = r.a_log_in[...].reshape(1, heads)
    r.dt_bias[0:1, 0:heads] = r.dt_bias_in[...].reshape(1, heads)
    r.cxb[...] = r.cxb_in[...].reshape(1, width)
    r.cbb[...] = r.cbb_in[...].reshape(1, 2 * NSTATE)
    r.gain[...] = r.gain_in[...].reshape(1, width)
    skip = r.d_skip_in[...].reshape(1, heads)
    first = lax.broadcasted_iota(jnp.int32, (1, LANES), 1) < HEADDIM
    for p in range(r.pairs):
        pair = jnp.where(first, skip[:, 2 * p : 2 * p + 1], skip[:, 2 * p + 1 : 2 * p + 2])
        r.skip[:, p * LANES : (p + 1) * LANES] = pair
    r.seg_across[...] = r.segments[...].reshape(r.chunks, CHUNK).astype(F32)
    edge = jnp.full((8, LANES), -1.0, F32)
    r.seg_down[0:8, :] = edge
    r.seg_down[r.chunks * CHUNK + 8 :, :] = edge

    def body(c):
        r.seg_down[chunk_rows(c, 8), :] = turned(r.seg_across[pl.ds(c, 1), :])

    over_chunks(r, body)


def phase_one(r):
    w = r.w
    width = r.pairs * LANES
    tokens = r.row_normed.shape[0]
    block = r.x_held.shape[0]
    start = pl.multiple_of(w.tp * block, block)
    moves = input_moves(r)
    for move in moves:
        move.start()
    place_steps(r)
    greet(w)
    moves[0].wait()
    moves[1].wait()
    r.shard_x.relay(0)
    r.shard_dt.relay(0)
    moves[2].wait()
    norm_rows(r.x_held, r.pre_gain[...].reshape(1, r.x_held.shape[1]), r.row_normed, start)
    r.row_n.start()
    r.state[...] = jnp.zeros_like(r.state)
    prepare_small(r)
    for move in moves[3:]:
        move.wait()
    r.shard_x.relay(1)
    r.shard_dt.relay(1)
    r.shard_x.relay(2)
    r.shard_dt.relay(2)
    r.row_n.hand_on()
    r.row_c.start()
    r.shard_x.relay(3)
    r.shard_dt.relay(3)
    r.shard_z.relay(0)
    r.shard_dt.finish()
    turn_steps(r)
    r.row_n.finish()
    r.shard_x.finish()

    def project_x(rows):
        normed = r.row_normed[rows, :]
        out = dot_nn(normed, r.full_x[...])
        r.xr[rows, :] = out[:, :width]
        r.bc[rows, :] = out[:, width:]
        r.dtr[rows, :] = dot_nn(normed, r.full_dt[...])

    by_rows(tokens, 256, project_x)

    def body(c):
        prepare_steps(c, r)
        scan_chunk(c, r)

        @pl.when(c == 1)
        def _():
            r.shard_z.relay(1)
            r.shard_out.relay(0)
            project_z(r, 0)

        @pl.when(c == 3)
        def _():
            r.row_c.hand_on()
            project_z(r, 1)

        @pl.when(c == 5)
        def _():
            r.shard_z.relay(2)
            project_z(r, 2)

    over_chunks(r, body)


def phase_mid(r):
    w = r.w
    r.shard_out.relay(1)
    r.shard_z.relay(3)
    project_z(r, 3)
    over_chunks(r, lambda c: square_chunk(c, r))
    r.ex_squares.start()
    r.shard_out.relay(2)
    r.row_c.finish()
    r.ex_squares.finish()
    over_chunks(r, lambda c: mix_chunk(c, r))
    weight_parts(
        product_maker(r.row_cot, r.mixed, flat_store(r.out_part, r.shard_rows)), r.grad_out
    )
    tell(r.free_pair, device(w, dp=w.mate))
    output_back(r, 0)
    output_back(r, 1)
    r.shard_out.relay(3)
    output_back(r, 2)
    output_back(r, 3)
    over_chunks(r, lambda c: cross_chunk(c, r))
    r.ex_crosses.start()
    r.grad_out.step(0)
    output_share(r, w.across)
    r.out_rows.start(0, 1)
    r.g_gate[...] = jnp.zeros_like(r.g_gate)
    r.ex_crosses.finish()
    over_chunks(r, lambda c: gate_back_chunk(c, r))
    for item in (r.shard_x, r.shard_dt, r.shard_z, r.shard_out, r.row_n, r.row_c):
        item.drain()
    pl.semaphore_wait(r.free_pair, 1)
    weight_parts(
        product_maker(
            r.row_normed, r.d_z, side_store(r.row_cot, r.shard_rows, r.pairs * LANES)
        ),
        r.grad_z,
    )
    tell(r.free_pair, device(w, dp=w.mate))
    r.grad_out.step(1)
    for slot, copy in ((w.near_x, 2), (w.near_y, 3)):
        output_share(r, slot)
        r.out_rows.start(copy)
    output_share(r, w.tp)
    r.out_rows.hand_on()
    tell(r.free_far, device(w, tp=w.near_x))
    tell(r.free_far, device(w, tp=w.near_y))


def phase_back(r):
    w = r.w
    block = r.x_held.shape[0]
    start_back(r)

    def body(i, carry):
        scan_chunk_back(r.chunks - 1 - i, r)

        @pl.when(i == 0)
        def _():
            r.grad_out.finish(r.v_w_out)
            r.put(r.v_w_out, r.o_w_out, 0).start()
            r.grad_out.drain()
            tell(r.free_line, device(w, dp=other_z(w, 1)))
            tell(r.free_line, device(w, dp=other_z(w, 3)))

        @pl.when(i == 2)
        def _():
            r.grad_z.step(0)

        pl.when(i == 5)(lambda: r.grad_z.step(1))
        return carry

    lax.fori_loop(0, r.chunks, body, 0)


def finish_block(r):
    w = r.w
    block = r.x_held.shape[0]
    step = 64
    r.out_rows.finish()

    def add(k, carry):
        here = pl.ds(pl.multiple_of(k * step, step), step)
        there = pl.ds(pl.multiple_of(w.tp * block + k * step, 16), step)
        total = r.x_held[here, :].astype(F32) + r.out_rows.total(here, there)
        r.v_block[here, :] = total.astype(BF16)
        return carry

    lax.fori_loop(0, block // step, add, 0)
    r.put(r.v_block, r.o_block, 1).start()
    tell(r.free_row, device(w, tp=w.near_x))
    tell(r.free_row, device(w, tp=w.near_y))


def step_parts(r, at):
    shard = r.shard_rows
    out = dot_tn(r.d_rest[:, at : at + LANES], r.row_normed[...])[:STEP_ROWS]
    for d in range(2 * (LAST_Z + 1)):
        here = slice(d * STEP_ROWS, (d + 1) * STEP_ROWS)
        r.dt_part[here, 0:shard] = out[:, d * shard : (d + 1) * shard]


def phase_last(r):
    w = r.w
    width = r.pairs * LANES
    block = r.x_held.shape[0]
    edge = width + 2 * NSTATE
    weight_parts(
        product_maker(
            r.row_normed,
            r.d_rest.at[:, pl.ds(width, 2 * NSTATE)],
            flat_store(r.bc_part, r.shard_rows),
        ),
        r.grad_bc,
    )
    r.out_rows.drain()
    r.g_pre[...] = jnp.zeros_like(r.g_pre)

    def share(slot):
        rows = pl.ds(pl.multiple_of(slot * block, block), block)
        tile = 512

        def body(n, carry):
            cols = pl.ds(pl.multiple_of(n * tile, tile), tile)
            out = dot_nt(r.d_z[rows, :], r.full_z[cols, :])
            out = out + dot_nt(r.d_rest[rows, :edge], r.full_x[cols, :])
            out = out + dot_nt(r.d_rest[rows, edge:], r.full_dt[cols, :])
            r.part[rows, cols] = out.astype(BF16)
            r.g_pre[:, cols] += fold_rows(out * r.row_normed[rows, cols].astype(F32))
            return carry

        lax.fori_loop(0, r.part.shape[1] // tile, body, 0)

    share(w.across)
    pl.semaphore_wait(r.free_far, 2)
    r.in_rows.start(0, 1)
    pl.semaphore_wait(r.free_pair, 1)
    pl.semaphore_wait(r.free_line, 2)
    weight_parts(
        product_maker(
            r.row_normed,
            r.d_rest.at[:, pl.ds(0, width)],
            flat_store(r.full_out, r.shard_rows),
        ),
        r.grad_x_part,
    )
    r.grad_bc.step(0)
    finish_block(r)
    share(w.near_x)
    pl.semaphore_wait(r.free_row, 2)
    r.in_rows.start(2)
    r.grad_bc.step(1)
    share(w.near_y)
    r.in_rows.start(3)
    share(w.tp)
    r.in_rows.hand_on()
    r.grad_x_part.step(0)
    step_parts(r, edge)
    for z in range(LAST_Z + 1):
        r.grad_dt.pair_copy(z).start()
    pack_small(r)
    r.ex_pair.start()
    r.grad_z.finish(r.v_w_z)
    r.put(r.v_w_z, r.o_w_z, 2).start()
    r.grad_bc.finish(r.bc_sum)
    r.bc_slots.at[w.tp][...] = r.bc_sum[...].astype(BF16)
    r.ex_bc.start()
    again = [
        pltpu.make_async_copy(r.cot.at[pl.ds(k * (block // 2), block // 2)], r.far.at[k], r.s_m.at[k])
        for k in range(2)
    ]
    for copy in again:
        copy.start()
    for z in (3, 0, 2, 1):
        r.grad_dt.launch(z)
    r.grad_dt.drain_pair()
    r.ex_pair.finish()
    r.small_z.at[w.z][...] = r.ex_pair.total()
    r.ex_z.start()
    r.grad_x_part.step(1)
    r.grad_dt.step(0)
    r.ex_z.finish()
    total = r.ex_z.total()
    r.v_small[...] = total[:SMALL_DP]
    r.put(r.v_small, r.o_small, 4).start()
    r.small_t.at[w.tp][...] = total[SMALL_DP:]
    r.ex_t.start()
    r.grad_dt.step(1)
    r.ex_bc.finish()
    r.v_w_bc[...] = r.ex_bc.total()
    r.put(r.v_w_bc, r.o_w_bc, 5).start()
    for item in (r.grad_z, r.grad_bc):
        item.drain()
    r.ex_t.finish()
    shared = r.ex_t.total()
    gain = r.pre_gain[...].reshape(1, r.x_held.shape[1])
    count = gain.shape[1] // LANES
    r.v_shared[...] = shared
    for p in range(count):
        r.v_shared[p : p + 1, :] = shared[p : p + 1, :] / gain[:, p * LANES : (p + 1) * LANES]
    r.put(r.v_shared, r.o_shared, 6).start()
    r.grad_dt.finish(r.v_w_dt)
    r.put(r.v_w_dt, r.o_w_dt, 3).start()
    r.grad_dt.drain()
    for copy in again:
        copy.wait()
    r.in_rows.finish()
    step = 64

    def body(k, carry):
        here = pl.ds(pl.multiple_of(k * step, step), step)
        there = pl.ds(pl.multiple_of(w.tp * block + k * step, 16), step)
        half = k // (block // 2 // step)
        inner = pl.ds(pl.multiple_of(k * step - half * (block // 2), step), step)
        values = r.x_held[here, :].astype(F32)
        scale = lax.rsqrt(jnp.mean(values * values, axis=1, keepdims=True) + EPS)
        weighted = r.in_rows.total(here, there) * gain
        along = jnp.mean(weighted * values, axis=1, keepdims=True)
        grad = r.far[half, inner, :].astype(F32) + scale * weighted
        r.v_grad_x[here, :] = (grad - values * (scale * scale * scale * along)).astype(BF16)
        return carry

    lax.fori_loop(0, block // step, body, 0)
    r.put(r.v_grad_x, r.o_grad_x, 7).start()
    r.in_rows.drain()
    r.grad_x_part.finish(r.v_w_x)
    r.put(r.v_w_x, r.o_w_x, 8).start()
    r.grad_x_part.drain()
    ends = ("w_out", "block", "w_z", "w_dt", "small", "w_bc", "shared", "grad_x", "w_x")
    for i, name in enumerate(ends):
        r.put(getattr(r, "v_" + name), getattr(r, "o_" + name), i).wait()


SMALL_DP = 40
SMALL_ALL = 24


def head_row(r):
    lane = lax.broadcasted_iota(jnp.int32, (1, LANES), 1)
    out = jnp.zeros((1, LANES), F32)
    for p in range(r.pairs):
        tile = jnp.sum(r.g_skip[:, p * LANES : (p + 1) * LANES], axis=0, keepdims=True)
        for k, part in enumerate((lane < HEADDIM, lane >= HEADDIM)):
            head = jnp.sum(jnp.where(part, tile, 0.0), axis=1, keepdims=True)
            out = jnp.where(lane == 2 * p + k, head, out)
    return out


def pack_small(r):
    mine = r.small_pair.at[r.w.core]
    mine[...] = jnp.zeros_like(mine)

    def put(at, ref, first, count):
        for p in range(count):
            lanes = slice(p * LANES, (p + 1) * LANES)
            mine[at + p : at + p + 1, :] = jnp.sum(
                ref[first : first + 8, lanes], axis=0, keepdims=True
            )
        return at + count

    at = put(0, r.g_gate, 0, r.pairs)
    for k in range(4):
        at = put(at, r.g_cxw, 8 * k, r.pairs)
    at = put(at, r.g_cxb, 0, r.pairs)
    mine[at : at + 1, :] = head_row(r)
    at = at + 1
    at = put(at, r.g_alog, 0, 1)
    at = put(at, r.g_dtb, 0, 1)
    at = put(SMALL_DP, r.g_pre, 0, r.g_pre.shape[1] // LANES)
    for k in range(4):
        at = put(at, r.g_cbw, 8 * k, 2)
    put(at, r.g_cbb, 0, 2)


RAW_IN = (
    "x_in",
    "segments",
    "pre_gain",
    "w_z",
    "w_x",
    "w_bc",
    "w_dt",
    "cxw",
    "cxb_in",
    "cbw",
    "cbb_in",
    "a_log_in",
    "dt_bias_in",
    "d_skip_in",
    "gain_in",
    "w_out",
    "cot",
)


def whole_kernel(*refs, names, width):
    r = types.SimpleNamespace(**dict(zip(names, refs)))
    r.w = w = place()
    r.pairs = width // LANES
    r.chunks = r.row_normed.shape[0] // CHUNK
    r.shard_rows = r.w_x.shape[0]
    r.xr_at = r.bc_at = r.dtr_at = 0
    r.dx_at, r.dbc_at, r.ddt_at = 0, width, width + 2 * NSTATE
    gather = lambda i, ref: LineGather(w, ref, r.s_w.at[i], r.r_w.at[i], PARTS)
    r.shard_x = gather(0, r.full_x)
    r.shard_z = gather(1, r.full_z)
    r.shard_out = gather(2, r.full_out)
    r.shard_dt = LineGather(w, r.steps_t, r.s_d, r.r_d, 1)
    r.row_n = RowGather(w, r.row_normed, r.s_r.at[0], r.r_r.at[0])
    r.row_c = RowGather(w, r.row_cot, r.s_r.at[1], r.r_r.at[1])
    r.out_rows = r.in_rows = RowScatter(w, r.part, r.far, r.near, r.s_q.at[0], r.r_q)
    rows = r.shard_rows
    held = (r.pair, r.up, r.down, r.p_main, r.l_main, PARTS)
    r.grad_out = LineScatter(w, flat_shard(r.out_part, rows), *held)
    r.grad_x_part = LineScatter(w, flat_shard(r.full_out, rows), *held)
    side = side_shard(r.row_cot, rows, width)
    r.grad_z = LineScatter(w, side, r.pair, r.up_z, r.down_z, r.p_main, r.l_z, PARTS)
    held_dt = (r.pair_dt, r.up_dt, r.down_dt, r.p_dt, r.l_dt, 1)
    r.grad_dt = LineScatter(w, flat_shard(r.dt_part, STEP_ROWS), *held_dt)
    in_row = [device(w, tp=t) for t in (w.near_x, w.near_y, w.across)]
    in_line = [device(w, dp=other_z(w, k)) for k in (1, 2, 3)]
    exchange = lambda i, ref, mine, targets: Exchange(ref, mine, targets, r.s_e.at[i])
    r.ex_squares = exchange(0, r.squares, w.tp, in_row)
    r.ex_crosses = exchange(1, r.crosses, w.tp, in_row)
    r.ex_pair = exchange(2, r.small_pair, w.core, [device(w, dp=w.mate)])
    r.ex_z = exchange(3, r.small_z, w.z, in_line)
    r.ex_t = exchange(4, r.small_t, w.tp, in_row)
    r.ex_bc = exchange(5, r.bc_slots, w.tp, in_row)
    r.put = lambda src, dst, i: pltpu.make_async_copy(src, dst, r.s_o.at[i])
    tokens = r.chunks * CHUNK

    def middle(z, d_mixed, mixed):
        r.z, r.d_mixed, r.mixed = z, d_mixed, mixed
        phase_one(r)
        phase_mid(r)

    pl.run_scoped(
        middle,
        pltpu.VMEM((tokens, width), F32),
        pltpu.VMEM((tokens, width), F32),
        pltpu.VMEM((tokens, width), BF16),
    )
    later = dict(BACK_SCRATCH(width), bc_part=((r.full_x.shape[0], 2 * NSTATE), BF16))

    def rest(d_rest, *buffers):
        r.d_rest = r.d_proj = d_rest
        for name, buffer in zip(later, buffers):
            setattr(r, name, buffer)
        held_bc = (r.pair_bc, r.up_bc, r.down_bc, r.p_bc, r.l_bc, 1)
        r.grad_bc = LineScatter(w, flat_shard(r.bc_part, rows), *held_bc)
        phase_back(r)
        phase_last(r)

    pl.run_scoped(
        rest,
        pltpu.VMEM((tokens, width + 2 * NSTATE + LANES), BF16),
        *[pltpu.VMEM(*spec) for spec in later.values()],
    )


def whole_call(args, width):
    x_in, w_x = args[0], args[4]
    features, block = x_in.shape[1], x_in.shape[0]
    tokens = block * 4
    shard = w_x.shape[0]
    maps = 2 * NSTATE
    chunks = tokens // CHUNK
    turned_step = (STEP_ROWS, 2 * LANES)
    outs = dict(
        block=((block, features), BF16),
        grad_x=((block, features), BF16),
        w_z=((shard, width), F32),
        w_x=((shard, width), F32),
        w_bc=((shard, maps), F32),
        w_dt=(turned_step, F32),
        w_out=((shard, width), F32),
        small=((SMALL_DP, LANES), F32),
        shared=((SMALL_ALL, LANES), F32),
    )
    scratch = dict(
        x_held=((block, features), BF16),
        row_normed=((tokens, features), BF16),
        row_cot=((tokens, features), BF16),
        full_x=((features, width + maps), BF16),
        full_z=((features, width), BF16),
        full_out=((features, width), BF16),
        full_dt=((features, LANES), BF16),
        steps_t=((8 * STEP_ROWS, 2 * LANES), BF16),
        xr=((tokens, width), F32),
        bc=((tokens, maps), F32),
        dtr=((tokens, LANES), F32),
        y=((tokens, width), F32),
        pre_x=((tokens, width), F32),
        pre_bc=((tokens, maps), F32),
        maps=((tokens, maps), BF16),
        states=((tokens, width), BF16),
        state=((NSTATE, width), F32),
        step=((tokens, LANES), F32),
        total=((tokens, LANES), F32),
        total_t=((chunks * 16, LANES), F32),
        seg_down=((tokens + 16, LANES), F32),
        seg_across=((chunks, LANES), F32),
        turn=((LANES, 2 * LANES), BF16),
        a_log=((1, LANES), F32),
        dt_bias=((1, LANES), F32),
        cxb=((1, width), F32),
        cbb=((1, maps), F32),
        gain=((1, width), F32),
        skip=((1, width), F32),
        squares=((4, chunks, LANES), F32),
        crosses=((4, chunks, LANES), F32),
        gy=((tokens, width), BF16),
        d_z=((tokens, width), BF16),
        part=((tokens, features), BF16),
        far=((2, block // 2, features), BF16),
        near=((2, block, features), BF16),
        out_part=((features, width), BF16),
        dt_part=((8 * STEP_ROWS, 2 * LANES), F32),
        pair=((4 * shard, width), BF16),
        pair_bc=((4 * shard, maps), BF16),
        pair_dt=((4 * STEP_ROWS, 2 * LANES), F32),
        up=((3 * shard, width), BF16),
        down=((3 * shard, width), BF16),
        up_z=((3 * shard, width), BF16),
        down_z=((3 * shard, width), BF16),
        up_bc=((3 * shard, maps), BF16),
        down_bc=((3 * shard, maps), BF16),
        up_dt=((3 * STEP_ROWS, 2 * LANES), F32),
        down_dt=((3 * STEP_ROWS, 2 * LANES), F32),
        bc_sum=((shard, maps), F32),
        bc_slots=((4, shard, maps), BF16),
        small_pair=((2, SMALL_DP + SMALL_ALL, LANES), F32),
        small_z=((4, SMALL_DP + SMALL_ALL, LANES), F32),
        small_t=((4, SMALL_ALL, LANES), F32),
        g_gate=((8, width), F32),
        g_pre=((8, features), F32),
        **GRAD_OUT(width),
        **{"v_" + name: spec for name, spec in outs.items()},
    )
    dma = pltpu.SemaphoreType.DMA
    signal = pltpu.SemaphoreType.REGULAR
    semaphores = dict(
        s_w=dma((3, 3)),
        r_w=dma((3, 4 * PARTS + 4)),
        s_d=dma((3,)),
        r_d=dma((8,)),
        s_r=dma((2,)),
        r_r=dma((2, 3)),
        s_q=dma((1,)),
        r_q=dma((3,)),
        p_main=dma((5,)),
        p_bc=dma((5,)),
        p_dt=dma((5,)),
        l_main=dma((2 + 6 * PARTS,)),
        l_z=dma((2 + 6 * PARTS,)),
        l_bc=dma((8,)),
        l_dt=dma((8,)),
        s_e=dma((6, 2)),
        s_m=dma((6,)),
        s_o=dma((len(outs),)),
        free_pair=signal,
        free_line=signal,
        free_row=signal,
        free_far=signal,
    )
    names = RAW_IN + tuple("o_" + name for name in outs) + tuple(scratch) + tuple(semaphores)
    values = list(args)
    values[6] = values[6].T
    values[15] = values[15].T
    whole = pl.BlockSpec(memory_space=pltpu.VMEM)
    apart = pl.BlockSpec(memory_space=pl.ANY)
    moved = ("x_in", "w_z", "w_x", "w_bc", "w_out", "cot")
    out = pl.pallas_call(
        functools.partial(whole_kernel, names=names, width=width),
        out_shape=tuple(jax.ShapeDtypeStruct(*spec) for spec in outs.values()),
        in_specs=[apart if name in moved else whole for name in RAW_IN],
        out_specs=tuple([apart] * len(outs)),
        scratch_shapes=[pltpu.VMEM(*spec) for spec in scratch.values()]
        + list(semaphores.values()),
        compiler_params=pltpu.CompilerParams(
            vmem_limit_bytes=VMEM_LIMIT, collective_id=0, has_side_effects=True
        ),
        cost_estimate=pl.CostEstimate(
            flops=5 * 10**10, bytes_accessed=1 << 26, transcendentals=0
        ),
    )(*values)
    return dict(zip(outs, out))


LARGE = ("block", "grad_x", "w_z", "w_x", "w_bc", "w_out")
FINAL = ("pre", "dt", "cxw", "cxb", "cbw", "cbb", "alog", "dtb", "skip", "gate")


def publish_kernel(*refs):
    count = len(LARGE)
    large_in, (steps, small, shared) = refs[:count], refs[count : count + 3]
    large_out = refs[count + 3 : 2 * count + 3]
    o = types.SimpleNamespace(**dict(zip(FINAL, refs[2 * count + 3 : -1])))
    sem = refs[-1]
    moves = [
        pltpu.make_async_copy(src, dst, sem.at[i])
        for i, (src, dst) in enumerate(zip(large_in, large_out))
    ]
    for move in moves:
        move.start()
    heads = o.alog.shape[0]

    def line(out, src, at):
        for p in range(out.shape[0] // LANES):
            out[p * LANES : (p + 1) * LANES] = src[at + p : at + p + 1, :].reshape(LANES)
        return at + out.shape[0] // LANES

    def taps(out, src, at):
        count = out.shape[1] // LANES
        for k in range(4):
            for p in range(count):
                out[k : k + 1, p * LANES : (p + 1) * LANES] = src[at + p : at + p + 1, :]
            at = at + count
        return at

    at = line(o.gate, small, 0)
    at = taps(o.cxw, small, at)
    at = line(o.cxb, small, at)
    for out in (o.skip, o.alog, o.dtb):
        out[...] = small[at : at + 1, 0:heads].reshape(heads)
        at = at + 1
    at = line(o.pre, shared, 0)
    at = taps(o.cbw, shared, at)
    line(o.cbb, shared, at)
    o.dt[...] = steps[0:heads, 0 : o.dt.shape[1]]
    for move in moves:
        move.wait()


def publish(o, width, heads):
    features = o["block"].shape[1]
    shard = o["w_z"].shape[0]
    shapes = dict(
        pre=(features,),
        dt=(heads, shard),
        cxw=(4, width),
        cxb=(width,),
        cbw=(4, 2 * NSTATE),
        cbb=(2 * NSTATE,),
        alog=(heads,),
        dtb=(heads,),
        skip=(heads,),
        gate=(width,),
    )
    whole = pl.BlockSpec(memory_space=pltpu.VMEM)
    apart = pl.BlockSpec(memory_space=pl.ANY)
    large = [o[name] for name in LARGE]
    out = pl.pallas_call(
        publish_kernel,
        out_shape=tuple(
            [jax.ShapeDtypeStruct(v.shape, v.dtype) for v in large]
            + [jax.ShapeDtypeStruct(shapes[name], F32) for name in FINAL]
        ),
        in_specs=[apart] * len(large) + [whole] * 3,
        out_specs=tuple([whole] * (len(large) + len(FINAL))),
        scratch_shapes=[pltpu.SemaphoreType.DMA((len(large),))],
    )(*large, o["w_dt"], o["small"], o["shared"])
    return types.SimpleNamespace(**dict(zip(LARGE + FINAL, out)))


def on_device_whole(*args):
    width = args[3].shape[1]
    heads = args[11].shape[0]
    p = publish(whole_call(args, width), width, heads)
    return (
        p.block,
        p.grad_x,
        p.pre,
        p.w_z,
        p.w_x,
        p.w_bc,
        p.dt.T,
        p.cxw,
        p.cxb,
        p.cbw,
        p.cbb,
        p.alog,
        p.dtb,
        p.skip,
        p.gate,
        p.w_out.T,
    )


def forward_plain(args, small, width):
    x_in, pre_gain, w_z, w_x, w_bc, w_dt, w_out, gate_gain, cotangent = args
    heads = w_dt.shape[1]
    at = layout_of(width)
    values = x_in.astype(F32)
    scale = lax.rsqrt(jnp.mean(values * values, axis=1) + EPS)
    normed = (values * scale[:, None] * pre_gain[None, :]).astype(BF16)
    row_normed = lax.all_gather(normed, "tensor", axis=0, tiled=True)
    mine = jnp.concatenate(
        (w_z, w_x, w_bc, jnp.pad(w_dt, ((0, 0), (0, LANES - heads)))), axis=1
    )
    stacked = lax.all_gather(mine, "dp", axis=0, tiled=True)
    full_out = lax.all_gather(w_out.T, "dp", axis=0, tiled=True)
    projected = jnp.dot(row_normed, stacked, preferred_element_type=F32)
    saved = mixer_forward(projected, small, width)
    row_cot = lax.all_gather(cotangent, "tensor", axis=0, tiled=True)
    y = saved[0]
    z_raw = projected[:, :width]
    gated = y * (z_raw * sigmoid(z_raw))
    d_mixed = dot_nn(row_cot, full_out)
    squares, cross = lax.psum(
        (
            jnp.sum(gated * gated, axis=1),
            jnp.sum(d_mixed * gate_gain[None, :] * gated, axis=1),
        ),
        "tensor",
    )
    return types.SimpleNamespace(
        row_normed=row_normed,
        row_cot=row_cot,
        full_z=stacked[:, :width],
        full_x=stacked[:, width:],
        full_out=full_out,
        z=z_raw,
        projected=(projected,),
        saved=saved,
        d_mixed=d_mixed,
        squares=squares,
        cross=cross,
    )


def on_device(
    x_in,
    segments,
    pre_gain,
    w_z,
    w_x,
    w_bc,
    w_dt,
    conv_x_w,
    conv_x_b,
    conv_bc_w,
    conv_bc_b,
    a_log,
    dt_bias,
    d_skip,
    gate_gain,
    w_out,
    cotangent,
):
    width = w_z.shape[1]
    heads = a_log.shape[0]
    at = layout_of(width)
    small = small_inputs(
        segments, conv_x_w, conv_x_b, conv_bc_w, conv_bc_b, a_log, dt_bias, d_skip
    )
    args = (x_in, pre_gain, w_z, w_x, w_bc, w_dt, w_out, gate_gain, cotangent)
    f = forward_plain(args, small, width)
    squares, cross = f.squares, f.cross
    y, z_raw, d_mixed = f.saved[0], f.z, f.d_mixed
    values = x_in.astype(F32)
    scale = lax.rsqrt(jnp.mean(values * values, axis=1) + EPS)
    gate = sigmoid(z_raw)
    gated = y * (z_raw * gate)
    inner_total = width * lax.axis_size("tensor")
    weighted = d_mixed * gate_gain[None, :]
    scale_two = lax.rsqrt(squares / inner_total + EPS)
    mixed = (gated * scale_two[:, None] * gate_gain[None, :]).astype(BF16)
    branch = lax.psum_scatter(
        dot_nt(mixed, f.full_out).astype(BF16), "tensor", scatter_dimension=0, tiled=True
    ).astype(F32)
    block_out = (values + branch).astype(BF16)
    grad_gate_part = jnp.sum(d_mixed * gated * scale_two[:, None], axis=0)
    d_gated = (
        scale_two[:, None] * weighted
        - gated * (scale_two * scale_two * scale_two * cross / inner_total)[:, None]
    )
    gy = (d_gated * (z_raw * gate)).astype(BF16)
    d_z = (d_gated * y * (gate * (1.0 + z_raw * (1.0 - gate)))).astype(BF16)
    d_rest, g_cxw, g_cxb, g_cbw, g_cbb, g_skip, g_alog, g_dtb = mixer_backward(
        f.projected, small, f.saved, gy, width
    )
    d_proj = jnp.concatenate((d_z, d_rest), axis=1)
    d_normed = lax.psum_scatter(
        (dot_nt(d_z, f.full_z) + dot_nt(d_rest, f.full_x)).astype(BF16),
        "tensor",
        scatter_dimension=0,
        tiled=True,
    ).astype(F32)
    proj_part = dot_tn(f.row_normed, d_proj)
    out_part = dot_tn(f.row_cot, mixed)
    owned = lax.psum_scatter(
        jnp.concatenate((proj_part, out_part), axis=1).astype(BF16),
        "dp",
        scatter_dimension=0,
        tiled=True,
    ).astype(F32)
    grad_w_bc = lax.psum(owned[:, at.bc : at.dt].astype(BF16), "tensor").astype(F32)
    pre_weighted = d_normed * pre_gain[None, :]
    grad_pre_part = jnp.sum(d_normed * values * scale[:, None], axis=0)
    feature_sum = jnp.sum(pre_weighted * values, axis=1)
    grad_x = (
        cotangent.astype(F32)
        + scale[:, None] * pre_weighted
        - values * (scale * scale * scale * feature_sum / values.shape[1])[:, None]
    ).astype(BF16)
    over_taps = lambda v: jnp.sum(v.reshape(4, 8, v.shape[1]), axis=1)
    over_rows = lambda v: jnp.sum(v, axis=0)
    grad_gate_gain, grad_cxw, grad_cxb, grad_alog, grad_dtb, grad_skip = lax.psum(
        (
            grad_gate_part,
            over_taps(g_cxw),
            over_rows(g_cxb),
            over_rows(g_alog)[:heads],
            over_rows(g_dtb)[:heads],
            jnp.sum(over_rows(g_skip).reshape(heads, HEADDIM), axis=1),
        ),
        "dp",
    )
    grad_pre_gain, grad_cbw, grad_cbb = lax.psum(
        (grad_pre_part, over_taps(g_cbw), over_rows(g_cbb)), ("dp", "tensor")
    )
    return (
        block_out,
        grad_x,
        grad_pre_gain,
        owned[:, :width],
        owned[:, width : at.bc],
        grad_w_bc,
        owned[:, at.dt : at.dt + heads],
        grad_cxw,
        grad_cxb,
        grad_cbw,
        grad_cbb,
        grad_alog,
        grad_dtb,
        grad_skip,
        grad_gate_gain,
        owned[:, at.all :].T,
    )


def solution(mesh):
    tokens = P(("dp", "tensor"), None)
    both = P("dp", "tensor")
    heads = P("tensor")
    line = mesh.shape["dp"] == 2 * (LAST_Z + 1) and mesh.shape["tensor"] == 4
    return jax.shard_map(
        on_device_whole if line else on_device,
        mesh=mesh,
        in_specs=(
            tokens,
            P("dp"),
            P(),
            both,
            both,
            P("dp", None),
            both,
            P(None, "tensor"),
            heads,
            P(),
            P(),
            heads,
            heads,
            heads,
            heads,
            P("tensor", "dp"),
            tokens,
        ),
        out_specs=(
            tokens,
            tokens,
            P(),
            both,
            both,
            P("dp", None),
            both,
            P(None, "tensor"),
            heads,
            P(),
            P(),
            heads,
            heads,
            heads,
            heads,
            P("tensor", "dp"),
        ),
        check_vma=False,
    )
```

```python
import functools
import types

import jax
import jax.numpy as jnp
from jax import lax
from jax.experimental import pallas as pl
from jax.experimental.pallas import tpu as pltpu
from jax.sharding import PartitionSpec as P

HEADDIM = 64
NSTATE = 128
CHUNK = 128
LANES = 128
EPS = 1e-05
LOG2E = 1.4426950408889634
F32 = jnp.float32
BF16 = jnp.bfloat16
VMEM_LIMIT = 62 * 1024 * 1024
exact = lax.Precision.HIGHEST


def dot_nn(a, b):
    return lax.dot_general(a, b, (((1,), (0,)), ((), ())), preferred_element_type=F32)


def dot_nt(a, b):
    return lax.dot_general(a, b, (((1,), (1,)), ((), ())), preferred_element_type=F32)


def dot_tn(a, b):
    return lax.dot_general(a, b, (((0,), (0,)), ((), ())), preferred_element_type=F32)


def sigmoid(v):
    return 1.0 / (1.0 + jnp.exp(-v))


def softplus(v):
    return jnp.maximum(v, 0.0) + jnp.log1p(jnp.exp(-jnp.abs(v)))


def fold_rows(v):
    return jnp.sum(v.reshape(v.shape[0] // 8, 8, v.shape[1]), axis=0)


def split_two(v):
    high = v.astype(BF16)
    return high, (v - high.astype(F32)).astype(BF16)


def tile_iotas():
    shape = (CHUNK, LANES)
    return lax.broadcasted_iota(jnp.int32, shape, 0), lax.broadcasted_iota(jnp.int32, shape, 1)


def chunk_rows(c, pad=0, extra=0):
    return pl.ds(pl.multiple_of(c * CHUNK + pad, 8), CHUNK + extra)


def prepare_steps(c, r):
    row, col = tile_iotas()
    rows = chunk_rows(c)
    lower = (row >= col).astype(F32)
    step = softplus(r.dtr[rows, r.dtr_at : r.dtr_at + LANES] + r.dt_bias[...])
    log_step = step * (-jnp.exp(r.a_log[...]) * LOG2E)
    total = jnp.dot(lower, log_step, precision=exact, preferred_element_type=F32)
    r.step[rows, :] = step
    r.total[rows, :] = total
    r.total_t[pl.ds(pl.multiple_of(c * 16, 16), 16), :] = total.T[:16]


def segment_parts(c, r):
    down = r.seg_down[chunk_rows(c, 8), :]
    across = r.seg_across[pl.ds(c, 1), :]
    before = r.seg_down[pl.ds(pl.multiple_of(c * CHUNK, 8), 8), :][7:8, :]
    last = down[CHUNK - 1 : CHUNK, :]
    carried = (down == before).astype(F32)
    to_end = (down == last).astype(F32)
    carry_on = (last == before).astype(F32)
    return down, across, carried, to_end, carry_on


def masks_back(c, r, down):
    window = r.seg_down[chunk_rows(c, 0, 8), :]
    return [
        (pltpu.roll(window, j, 0)[8 : 8 + CHUNK] == down).astype(F32) for j in range(1, 4)
    ]


def masks_ahead(c, r, down):
    window = r.seg_down[chunk_rows(c, 8, 8), :]
    full = CHUNK + 8
    return [(pltpu.roll(window, full - j, 0)[:CHUNK] == down).astype(F32) for j in range(1, 4)]


def conv_tile(c, ref, at, weight, bias, w_at, masks):
    lanes = slice(at, at + LANES)
    w_lanes = slice(w_at, w_at + LANES)
    here = ref[chunk_rows(c), lanes]
    ahead = ref[pl.ds(pl.multiple_of(jnp.maximum(c * CHUNK - 8, 0), 8), 8), lanes]
    window = jnp.concatenate([ahead, here], axis=0)
    out = here * weight[3:4, w_lanes] + bias[0:1, w_lanes]
    for j in range(1, 4):
        shifted = pltpu.roll(window, j, 0)[8 : 8 + CHUNK]
        out = out + (shifted * masks[j - 1]) * weight[3 - j : 4 - j, w_lanes]
    return out


def pair_columns(tile, p, first):
    left = jnp.broadcast_to(tile[:, 2 * p : 2 * p + 1], (CHUNK, LANES))
    right = jnp.broadcast_to(tile[:, 2 * p + 1 : 2 * p + 2], (CHUNK, LANES))
    return left, right, jnp.where(first, left, right)


def stack_heads(tile, first):
    zero = jnp.zeros_like(tile)
    return jnp.concatenate([jnp.where(first, tile, zero), jnp.where(first, zero, tile)], axis=0)


def scan_chunk(c, r):
    rows = chunk_rows(c)
    row, col = tile_iotas()
    down, across, carried, to_end, carry_on = segment_parts(c, r)
    masks = masks_back(c, r, down)
    maps = []
    for half in range(2):
        pre = conv_tile(c, r.bc, r.bc_at + half * LANES, r.cbw, r.cbb, half * LANES, masks)
        r.pre_bc[rows, half * LANES : (half + 1) * LANES] = pre
        maps.append((pre * sigmoid(pre)).astype(BF16))
    b_map, c_map = maps
    r.maps[rows, :LANES] = b_map
    r.maps[rows, LANES:] = c_map
    scores = jnp.where((down == across) & (row >= col), dot_nt(c_map, b_map), 0.0)
    b_turned = b_map.T
    total = r.total[rows, :]
    step = r.step[rows, :]
    first = col < HEADDIM
    for p in range(r.pairs):
        lanes = slice(p * LANES, (p + 1) * LANES)
        pre = conv_tile(c, r.xr, r.xr_at + p * LANES, r.cxw, r.cxb, p * LANES, masks)
        r.pre_x[rows, lanes] = pre
        chan = pre * sigmoid(pre)
        left, right, both = pair_columns(total, p, first)
        _, _, step_pair = pair_columns(step, p, first)
        fed = step_pair * chan
        stacked = stack_heads(fed.astype(BF16), first)
        mixing = []
        for k, mine in enumerate((left, right)):
            other = r.total_t[pl.ds(c * 16 + 2 * p + k, 1), :]
            mixing.append((scores * jnp.exp2(jnp.minimum(mine - other, 0.0))).astype(BF16))
        within = dot_nn(jnp.concatenate(mixing, axis=1), stacked)
        state = r.state[:, lanes]
        state_low = state.astype(BF16)
        r.states[rows, lanes] = state_low
        decay_in = jnp.exp2(both) * carried
        r.y[rows, lanes] = (
            within + decay_in * dot_nn(c_map, state_low) + r.skip[0:1, lanes] * chan
        )
        last = both[CHUNK - 1 : CHUNK, :]
        decay_out = jnp.exp2(last - both) * to_end
        r.state[:, lanes] = (jnp.exp2(last) * carry_on) * state + dot_nn(
            b_turned, (decay_out * fed).astype(BF16)
        )


def scan_chunk_back(c, r):
    rows = chunk_rows(c)
    row, col = tile_iotas()
    down, across, carried, to_end, carry_on = segment_parts(c, r)
    ahead = masks_ahead(c, r, down)
    b_map = r.maps[rows, :LANES]
    c_map = r.maps[rows, LANES:]
    visible = (down == across) & (row <= col)
    scores = jnp.where(visible, dot_nt(b_map, c_map), 0.0)
    c_turned = c_map.T
    total = r.total[rows, :]
    step = r.step[rows, :]
    first = col < HEADDIM
    d_scores = jnp.zeros((CHUNK, LANES), F32)
    width = r.pairs * LANES
    for p in range(r.pairs):
        lanes = slice(p * LANES, (p + 1) * LANES)
        lows = slice(width + p * LANES, width + (p + 1) * LANES)
        gy_low = r.gy[rows, lanes]
        gy = gy_low.astype(F32)
        pre = r.pre_x[rows, lanes]
        gate = sigmoid(pre)
        chan = pre * gate
        left, right, both = pair_columns(total, p, first)
        _, _, step_pair = pair_columns(step, p, first)
        fed = step_pair * chan
        fed_low = fed.astype(BF16)
        d_mixing = dot_nt(stack_heads(fed_low, first), gy_low)
        mixing = []
        for k, mine in enumerate((left, right)):
            other = r.total_t[pl.ds(c * 16 + 2 * p + k, 1), :]
            decay = jnp.exp2(jnp.minimum(other - mine, 0.0))
            mixing.append((scores * decay).astype(BF16))
            d_scores = d_scores + d_mixing[k * CHUNK : (k + 1) * CHUNK] * decay
        d_state = r.d_state[:, lanes]
        d_state_low = d_state.astype(BF16)
        last = both[CHUNK - 1 : CHUNK, :]
        decay_out = jnp.exp2(last - both) * to_end
        from_state = decay_out * dot_nn(b_map, d_state_low)
        d_fed = dot_nn(jnp.concatenate(mixing, axis=1), stack_heads(gy_low, first)) + from_state
        fed_held = fed_low.astype(F32)
        skip = r.skip[0:1, lanes]
        flow = gy * (r.y[rows, lanes] - skip * chan) - fed_held * d_fed
        direct = chan * d_fed
        for k, part in enumerate((flow, direct)):
            spot = slice(k * CHUNK, (k + 1) * CHUNK)
            r.sums[spot, lanes], r.sums[spot, lows] = split_two(part)
        keep = jnp.exp2(last) * carry_on
        through = jnp.sum(fed_held * from_state, axis=0, keepdims=True) + keep * jnp.sum(
            r.states[rows, lanes].astype(F32) * d_state, axis=0, keepdims=True
        )
        spot = slice(2 * CHUNK, 2 * CHUNK + 16)
        r.sums[spot, lanes], r.sums[spot, lows] = split_two(
            jnp.broadcast_to(through, (16, LANES))
        )
        grad_in = (jnp.exp2(both) * carried * gy).astype(BF16)
        r.grad_in[:, lanes] = grad_in
        r.fed_out[:, lanes] = (decay_out * fed).astype(BF16)
        r.d_state_low[:, lanes] = d_state_low
        r.d_state[:, lanes] = keep * d_state + dot_nn(c_turned, grad_in)
        d_chan = skip * gy + step_pair * d_fed
        r.g_skip[:, lanes] += fold_rows(gy * chan)
        d_pre = d_chan * (gate * (1.0 + pre * (1.0 - gate)))
        conv_back(c, r, d_pre, r.d_pre_x, r.xr, r.xr_at, r.cxw, p * LANES, ahead, r.dx_at, r.g_cxw, r.g_cxb)
    d_scores_low = jnp.where(visible, d_scores, 0.0).astype(BF16)
    d_b = dot_nn(d_scores_low, c_map) + dot_nt(r.fed_out[...], r.d_state_low[...])
    d_c = dot_tn(d_scores_low, b_map) + dot_nt(r.grad_in[...], r.states[rows, :])
    for half, d_map in enumerate((d_b, d_c)):
        pre = r.pre_bc[rows, half * LANES : (half + 1) * LANES]
        gate = sigmoid(pre)
        d_pre = d_map * (gate * (1.0 + pre * (1.0 - gate)))
        conv_back(
            c, r, d_pre, r.d_pre_bc, r.bc, r.bc_at, r.cbw, half * LANES, ahead, r.dbc_at, r.g_cbw, r.g_cbb
        )
    reduced = dot_nn(r.sums[...], r.head_sum[...])
    d_total = jnp.dot(
        (row <= col).astype(F32), reduced[:CHUNK], precision=exact, preferred_element_type=F32
    ) + reduced[2 * CHUNK : 2 * CHUNK + 1]
    a_neg = -jnp.exp(r.a_log[...])
    d_step = reduced[CHUNK : 2 * CHUNK] + a_neg * d_total
    r.g_alog[...] += fold_rows(step * d_total) * a_neg
    d_raw = d_step * sigmoid(r.dtr[rows, r.dtr_at : r.dtr_at + LANES] + r.dt_bias[...])
    r.g_dtb[...] += fold_rows(d_raw)
    r.d_proj[rows, r.ddt_at : r.ddt_at + LANES] = d_raw.astype(BF16)


def conv_back(c, r, d_pre, held, raw, raw_at, weight, at, ahead, out_at, g_w, g_b):
    lanes = slice(at, at + LANES)
    rows = chunk_rows(c)
    held[CHUNK : CHUNK + 8, lanes] = held[0:8, lanes]
    held[0:CHUNK, lanes] = d_pre
    window = held[:, lanes]
    values = raw[rows, raw_at + at : raw_at + at + LANES]
    g_b[:, lanes] += fold_rows(d_pre)
    g_w[24:32, lanes] += fold_rows(d_pre * values)
    d_raw = d_pre * weight[3:4, lanes]
    for j in range(1, 4):
        shifted = pltpu.roll(window, CHUNK + 8 - j, 0)[:CHUNK] * ahead[j - 1]
        d_raw = d_raw + shifted * weight[3 - j : 4 - j, lanes]
        g_w[(3 - j) * 8 : (4 - j) * 8, lanes] += fold_rows(shifted * values)
    r.d_proj[rows, out_at + at : out_at + at + LANES] = d_raw.astype(BF16)


def head_sum_matrix(width):
    shape = (2 * width, LANES)
    lane = lax.broadcasted_iota(jnp.int32, shape, 0)
    lane = jnp.where(lane >= width, lane - width, lane)
    return (lane // HEADDIM == lax.broadcasted_iota(jnp.int32, shape, 1)).astype(BF16)


def layout_of(width):
    return types.SimpleNamespace(
        x=width, bc=2 * width, dt=2 * width + 2 * NSTATE, all=2 * width + 2 * NSTATE + LANES
    )


SMALL_IN = ("seg_down", "seg_across", "cxw", "cxb", "cbw", "cbb", "a_log", "dt_bias", "skip")


def small_inputs(segments, cxw, cxb, cbw, cbb, a_log, dt_bias, d_skip):
    tokens = segments.shape[0]
    seg = segments.astype(F32)
    edge = jnp.full((8,), -1.0, F32)
    down = jnp.broadcast_to(jnp.concatenate([edge, seg, edge])[:, None], (tokens + 16, LANES))
    heads = a_log.shape[0]
    pad = lambda v: jnp.pad(v, (0, LANES - heads))[None, :]
    return (
        down,
        seg.reshape(tokens // CHUNK, CHUNK),
        cxw,
        cxb[None, :],
        cbw,
        cbb[None, :],
        pad(a_log),
        pad(dt_bias),
        jnp.repeat(d_skip, HEADDIM)[None, :],
    )


def take_projections(r, width):
    r.pairs = width // LANES
    if hasattr(r, "proj"):
        at = layout_of(width)
        r.xr = r.bc = r.dtr = r.proj
        r.xr_at, r.bc_at, r.dtr_at = at.x, at.bc, at.dt
    else:
        r.xr_at = r.bc_at = r.dtr_at = 0


def forward_kernel(*refs, names, width):
    r = types.SimpleNamespace(**dict(zip(names, refs)))
    take_projections(r, width)
    chunks = r.dtr.shape[0] // CHUNK
    r.state[...] = jnp.zeros_like(r.state)

    def body(c, carry):
        prepare_steps(c, r)
        scan_chunk(c, r)
        return carry

    lax.fori_loop(0, chunks, body, 0)


def backward_kernel(*refs, names, width):
    r = types.SimpleNamespace(**dict(zip(names, refs)))
    take_projections(r, width)
    r.dx_at, r.dbc_at, r.ddt_at = 0, width, width + 2 * NSTATE
    start_back(r)
    chunks = r.dtr.shape[0] // CHUNK

    def body(i, carry):
        scan_chunk_back(chunks - 1 - i, r)
        return carry

    lax.fori_loop(0, chunks, body, 0)


def start_back(r):
    for ref in (r.d_state, r.d_pre_x, r.d_pre_bc, r.g_cxw, r.g_cxb, r.g_cbw, r.g_cbb):
        ref[...] = jnp.zeros_like(ref)
    for ref in (r.g_skip, r.g_alog, r.g_dtb):
        ref[...] = jnp.zeros_like(ref)
    r.head_sum[...] = head_sum_matrix(r.pairs * LANES)


def call_local(kernel, width, ins, outs, scratch, values, flops):
    names = tuple(ins) + tuple(outs) + tuple(scratch)
    whole = pl.BlockSpec(memory_space=pltpu.VMEM)
    return pl.pallas_call(
        functools.partial(kernel, names=names, width=width),
        out_shape=tuple(jax.ShapeDtypeStruct(*spec) for spec in outs.values()),
        in_specs=[whole] * len(ins),
        out_specs=tuple([whole] * len(outs)),
        scratch_shapes=[pltpu.VMEM(*spec) for spec in scratch.values()],
        compiler_params=pltpu.CompilerParams(vmem_limit_bytes=VMEM_LIMIT),
        cost_estimate=pl.CostEstimate(flops=flops, bytes_accessed=1 << 24, transcendentals=0),
    )(*values)


def mixer_forward(projected, small, width):
    tokens = projected.shape[0]
    outs = dict(
        y=((tokens, width), F32),
        pre_x=((tokens, width), F32),
        pre_bc=((tokens, 2 * NSTATE), F32),
        maps=((tokens, 2 * NSTATE), BF16),
        states=((tokens, width), BF16),
        step=((tokens, LANES), F32),
        total=((tokens, LANES), F32),
        total_t=((tokens // CHUNK * 16, LANES), F32),
    )
    scratch = dict(state=((NSTATE, width), F32))
    return call_local(
        forward_kernel, width, ("proj",) + SMALL_IN, outs, scratch, (projected,) + small, 10**10
    )


BACK_SCRATCH = lambda width: dict(
    d_state=((NSTATE, width), F32),
    d_state_low=((NSTATE, width), BF16),
    grad_in=((CHUNK, width), BF16),
    fed_out=((CHUNK, width), BF16),
    sums=((2 * CHUNK + 16, 2 * width), BF16),
    head_sum=((2 * width, LANES), BF16),
    d_pre_x=((CHUNK + 8, width), F32),
    d_pre_bc=((CHUNK + 8, 2 * NSTATE), F32),
)
GRAD_OUT = lambda width: dict(
    g_cxw=((32, width), F32),
    g_cxb=((8, width), F32),
    g_cbw=((32, 2 * NSTATE), F32),
    g_cbb=((8, 2 * NSTATE), F32),
    g_skip=((8, width), F32),
    g_alog=((8, LANES), F32),
    g_dtb=((8, LANES), F32),
)


SAVED = ("y", "pre_x", "pre_bc", "maps", "states", "step", "total", "total_t")


def mixer_backward(projected, small, saved, gy, width):
    tokens = gy.shape[0]
    outs = dict(d_proj=((tokens, width + 2 * NSTATE + LANES), BF16), **GRAD_OUT(width))
    ins = (("proj",) if len(projected) == 1 else ("xr", "bc", "dtr")) + SMALL_IN
    ins = ins + SAVED + ("gy",)
    return call_local(
        backward_kernel,
        width,
        ins,
        outs,
        BACK_SCRATCH(width),
        tuple(projected) + small + tuple(saved) + (gy,),
        3 * 10**10,
    )


UP, DOWN, PAIR = range(3)
LAST_Z = 3
STEP_ROWS = 16
PARTS = 2


def place():
    dp = lax.axis_index("dp")
    tp = lax.axis_index("tensor")
    z = dp // 2
    core = dp - 2 * z
    y = tp // 2
    x = tp - 2 * y
    return types.SimpleNamespace(
        dp=dp,
        tp=tp,
        z=z,
        core=core,
        mate=dp + 1 - 2 * core,
        near_x=y * 2 + (1 - x),
        near_y=(1 - y) * 2 + x,
        across=(1 - y) * 2 + (1 - x),
    )


def device(w, dp=None, tp=None):
    return {"dp": w.dp if dp is None else dp, "tensor": w.tp if tp is None else tp}


def other_z(w, k):
    return lax.rem(w.z + k, LAST_Z + 1) * 2 + w.core


def peers(w):
    rows = [device(w, tp=t) for t in (w.near_x, w.near_y, w.across)]
    return rows + [device(w, dp=w.mate)] + [device(w, dp=other_z(w, k)) for k in (1, 2, 3)]


def tell(sem, where):
    pl.semaphore_signal(sem, inc=1, device_id=where, device_id_type=pl.DeviceIdType.MESH)


def greet(w):
    barrier = pltpu.get_barrier_semaphore()
    for where in peers(w):
        tell(barrier, where)
    pl.semaphore_wait(barrier, len(peers(w)))


def remote(src, dst, send, recv, where):
    return pltpu.make_async_remote_copy(
        src_ref=src,
        dst_ref=dst,
        send_sem=send,
        recv_sem=recv,
        device_id=where,
        device_id_type=pl.DeviceIdType.MESH,
    )


def settle(ref, send, recv, where, sent=True):
    copy = remote(ref, ref, send, recv, where)
    if sent:
        copy.wait_send()
    else:
        copy.wait_recv()


class LineGather:
    def __init__(self, w, ref, send, recv, parts):
        self.w, self.ref, self.send, self.recv, self.parts = w, ref, send, recv, parts
        self.rows = ref.shape[0] // (2 * (LAST_Z + 1))

    def shard(self, z, core, part):
        rows = self.rows // self.parts
        start = pl.multiple_of((z * 2 + core) * self.rows + part * rows, 16)
        return self.ref.at[pl.ds(start, rows)]

    def copy(self, z, kind, part):
        w = self.w
        block = self.shard(z, w.core, part)
        to = {UP: w.dp + 2, DOWN: w.dp - 2}.get(kind, w.mate)
        first = (self.parts if kind == PAIR else part) * (LAST_Z + 1)
        return remote(block, block, self.send.at[kind], self.recv.at[first + z], device(w, dp=to))

    def relay(self, step):
        for part in range(self.parts):
            self.relay_part(step, part)

    def relay_part(self, step, part):
        w = self.w

        def low():
            z = w.z - step
            if step > 0:
                self.copy(z, UP, part).wait_recv()
            pl.when(w.z < LAST_Z)(lambda: self.copy(z, UP, part).start())
            if step == 0:
                pl.when(w.z > 0)(lambda: self.copy(z, DOWN, part).start())
            self.copy(z, PAIR, part).start()

        def high():
            z = w.z + step
            self.copy(z, DOWN, part).wait_recv()
            pl.when(w.z > 0)(lambda: self.copy(z, DOWN, part).start())
            self.copy(z, PAIR, part).start()

        if step == 0:
            low()
        else:
            pl.when(w.z >= step)(low)
            pl.when(w.z <= LAST_Z - step)(high)

    def some(self, count):
        return self.ref.at[pl.ds(0, count * self.rows)]

    def from_mate(self, z):
        block = self.some(1)
        recv = self.recv.at[self.parts * (LAST_Z + 1) + z]
        settle(block, self.send.at[PAIR], recv, device(self.w, dp=self.w.mate), sent=False)

    def finish(self):
        for z in range(LAST_Z + 1):
            self.from_mate(z)

    def drain(self):
        w = self.w
        where = device(w, dp=w.mate)
        wait = lambda count, kind: settle(
            self.some(count), self.send.at[kind], self.recv.at[0], where
        )
        wait(LAST_Z + 1, PAIR)
        for z in range(LAST_Z):
            pl.when(w.z == z)(lambda z=z: wait(z + 1, UP))
            pl.when(w.z == LAST_Z - z)(lambda z=z: wait(z + 1, DOWN))


class RowGather:
    def __init__(self, w, ref, send, recv):
        self.w, self.ref, self.send, self.recv = w, ref, send, recv
        self.rows = ref.shape[0] // 4

    def copy(self, i):
        w = self.w
        slot, half, to = (
            (w.tp, 0, w.near_x),
            (w.tp, 1, w.near_y),
            (w.tp, 1, w.near_x),
            (w.tp, 0, w.near_y),
            (w.near_x, 0, w.near_y),
            (w.near_y, 1, w.near_x),
        )[i]
        block = row_block(self.ref, self.rows, slot, half)
        return remote(block, block, self.send, self.recv.at[min(i, 2)], device(w, tp=to))

    def start(self):
        for i in range(4):
            self.copy(i).start()

    def hand_on(self):
        for i in range(2):
            self.copy(i).wait_recv()
            self.copy(i + 4).start()

    def some(self, count):
        return self.ref.at[pl.ds(0, count * self.rows)]

    def finish(self):
        where = device(self.w, tp=self.w.near_x)
        settle(self.some(2), self.send, self.recv.at[2], where, sent=False)

    def drain(self):
        settle(self.some(3), self.send, self.recv.at[2], device(self.w, tp=self.w.near_x))


def row_block(ref, rows, slot, half=None):
    start = slot * rows
    if half is not None:
        rows = rows // 2
        start = start + half * rows
    return ref.at[pl.ds(pl.multiple_of(start, 16), rows)]


def add_into(ref, other):
    rows = 64 if ref.shape[0] % 64 == 0 else ref.shape[0]

    def body(i, carry):
        here = pl.ds(pl.multiple_of(i * rows, rows), rows)
        ref[here, :] = (ref[here, :].astype(F32) + other[here, :].astype(F32)).astype(ref.dtype)
        return carry

    lax.fori_loop(0, ref.shape[0] // rows, body, 0)


class RowScatter:
    def __init__(self, w, part, far, near, send, recv):
        self.w, self.part, self.far, self.near, self.send, self.recv = w, part, far, near, send, recv
        self.rows = part.shape[0] // 4

    def block(self, slot, half=None):
        return row_block(self.part, self.rows, slot, half)

    def copy(self, i):
        w = self.w
        half = lambda k, h: row_block(self.near.at[k], self.rows, 0, h)
        src, dst, to = (
            (lambda: self.block(w.across, 0), lambda: self.far.at[0], w.near_x),
            (lambda: self.block(w.across, 1), lambda: self.far.at[1], w.near_y),
            (lambda: self.block(w.near_x, 0), lambda: half(0, 0), w.near_x),
            (lambda: self.block(w.near_y, 1), lambda: half(1, 1), w.near_y),
            (lambda: self.block(w.near_x, 1), lambda: half(0, 1), w.near_x),
            (lambda: self.block(w.near_y, 0), lambda: half(1, 0), w.near_y),
        )[i]
        return remote(src(), dst(), self.send, self.recv.at[min(i, 2)], device(w, tp=to))

    def start(self, *which):
        for i in which:
            self.copy(i).start()

    def hand_on(self):
        w = self.w
        self.copy(1).wait_recv()
        add_into(self.block(w.near_x, 1), self.far.at[1])
        self.copy(4).start()
        self.copy(0).wait_recv()
        add_into(self.block(w.near_y, 0), self.far.at[0])
        self.copy(5).start()

    def some(self, count):
        return self.part.at[pl.ds(0, count * self.rows)]

    def finish(self):
        where = device(self.w, tp=self.w.near_x)
        settle(self.some(2), self.send, self.recv.at[2], where, sent=False)

    def total(self, here, there):
        total = self.part[there, :].astype(F32)
        return total + self.near[0, here, :].astype(F32) + self.near[1, here, :].astype(F32)

    def drain(self):
        settle(self.some(3), self.send, self.recv.at[2], device(self.w, tp=self.w.near_x))


class LineScatter:
    def __init__(self, w, shard, pair, up, down, pair_sem, line_sem, parts, hold=False):
        self.w, self.shard, self.pair, self.up, self.down = w, shard, pair, up, down
        self.hold = hold
        self.pair_sem, self.line_sem, self.parts = pair_sem, line_sem, parts
        self.rows = pair.shape[0] // (LAST_Z + 1)

    def slot(self, ref, i):
        return ref.at[pl.ds(pl.multiple_of(i * self.rows, 16), self.rows)]

    def piece(self, ref, part):
        rows = self.rows // self.parts
        return ref.at[pl.ds(part * rows, rows)]

    def pair_copy(self, z):
        w = self.w
        return remote(
            self.shard(z, 1 - w.core),
            self.slot(self.pair, z),
            self.pair_sem.at[LAST_Z + 1],
            self.pair_sem.at[z],
            device(w, dp=w.mate),
        )

    def up_copy(self, z, part):
        return remote(
            self.piece(self.shard(z, self.w.core), part),
            self.piece(self.slot(self.up, z - 1), part),
            self.line_sem.at[0],
            self.line_sem.at[2 + part * LAST_Z + z - 1],
            device(self.w, dp=self.w.dp + 2),
        )

    def down_copy(self, z, part):
        return remote(
            self.piece(self.shard(z, self.w.core), part),
            self.piece(self.slot(self.down, z), part),
            self.line_sem.at[1],
            self.line_sem.at[2 + (self.parts + part) * LAST_Z + z],
            device(self.w, dp=self.w.dp - 2),
        )

    def launch(self, z):
        w = self.w
        self.pair_copy(z).wait_recv()

        def every(send):
            for part in range(self.parts):
                add_into(self.piece(self.shard(z, w.core), part), self.piece(self.slot(self.pair, z), part))
                if send is not None:
                    send(z, part).start()

        held = 1 if self.hold else 0
        low = (w.z == 0) & (z > held)
        high = (w.z == LAST_Z) & (z < LAST_Z - held)
        pl.when(low)(lambda: every(self.up_copy))
        pl.when(high)(lambda: every(self.down_copy))
        pl.when(jnp.logical_not(low | high))(lambda: every(None))

    def launch_last(self):
        for part in range(self.parts):
            pl.when(self.w.z == 0)(lambda part=part: self.up_copy(1, part).start())
            pl.when(self.w.z == LAST_Z)(lambda part=part: self.down_copy(LAST_Z - 1, part).start())

    def pass_up(self, z, part):
        self.up_copy(z, part).wait_recv()
        add_into(
            self.piece(self.shard(z, self.w.core), part),
            self.piece(self.slot(self.up, z - 1), part),
        )
        self.up_copy(z, part).start()

    def pass_down(self, z, part):
        self.down_copy(z, part).wait_recv()
        add_into(
            self.piece(self.shard(z, self.w.core), part),
            self.piece(self.slot(self.down, z), part),
        )
        self.down_copy(z, part).start()

    def step(self, k, part=None):
        w = self.w
        if part is None:
            for part in range(self.parts):
                self.step(k, part)
        elif k == 0:
            pl.when(w.z == 1)(lambda: self.pass_up(3, part))
            pl.when(w.z == 2)(lambda: self.pass_down(0, part))
        else:

            @pl.when(w.z == 1)
            def _():
                self.pass_up(2, part)
                self.pass_down(0, part)

            @pl.when(w.z == 2)
            def _():
                self.pass_down(1, part)
                self.pass_up(3, part)

    def finish(self, out):
        w = self.w
        own = self.shard(w.z, w.core)
        rows = self.rows // self.parts

        def add(part, copy, slot):
            here = pl.ds(part * rows, rows)
            copy(w.z, part).wait_recv()
            out[here, :] += self.piece(slot, part)[...].astype(F32)

        out[...] = own[...].astype(F32)
        for part in range(self.parts):
            pl.when(w.z > 0)(
                lambda part=part: add(part, self.up_copy, self.slot(self.up, w.z - 1))
            )
            pl.when(w.z < LAST_Z)(
                lambda part=part: add(part, self.down_copy, self.slot(self.down, w.z))
            )

    def drain_pair(self):
        where = device(self.w, dp=self.w.mate)
        settle(self.pair, self.pair_sem.at[LAST_Z + 1], self.pair_sem.at[0], where)

    def drain(self):
        w = self.w
        where = device(w, dp=w.mate)
        for z in range(LAST_Z):
            sent = self.up.at[pl.ds(0, (LAST_Z - z) * self.rows)]
            pl.when(w.z == z)(
                lambda sent=sent: settle(sent, self.line_sem.at[0], self.line_sem.at[2], where)
            )
            pl.when(w.z == LAST_Z - z)(
                lambda sent=sent: settle(sent, self.line_sem.at[1], self.line_sem.at[2], where)
            )


class Exchange:
    def __init__(self, ref, mine, targets, sems):
        self.ref, self.mine, self.targets, self.sems = ref, mine, targets, sems

    def start(self):
        part = self.ref.at[self.mine]
        for target in self.targets:
            remote(part, part, self.sems.at[0], self.sems.at[1], target).start()

    def finish(self):
        count = len(self.targets)
        some = self.ref.at[pl.ds(0, count)]
        for sent in (False, True):
            settle(some, self.sems.at[0], self.sems.at[1], self.targets[0], sent=sent)

    def total(self):
        total = self.ref[0].astype(F32)
        for i in range(1, self.ref.shape[0]):
            total = total + self.ref[i].astype(F32)
        return total


def norm_rows(x_ref, gain, out_ref, start):
    rows = 64

    def body(i, carry):
        here = pl.ds(pl.multiple_of(i * rows, rows), rows)
        values = x_ref[here, :].astype(F32)
        scale = lax.rsqrt(jnp.mean(values * values, axis=1, keepdims=True) + EPS)
        there = pl.ds(pl.multiple_of(start + i * rows, 16), rows)
        out_ref[there, :] = (values * scale * gain).astype(BF16)
        return carry

    lax.fori_loop(0, x_ref.shape[0] // rows, body, 0)


def by_rows(total, rows, body):
    def step(i, carry):
        body(pl.ds(pl.multiple_of(i * rows, rows), rows))
        return carry

    lax.fori_loop(0, total // rows, step, 0)


def over_chunks(r, body):
    def step(c, carry):
        body(c)
        return carry

    lax.fori_loop(0, r.chunks, step, 0)


def turned(row):
    return jnp.broadcast_to(row, (CHUNK, LANES)).T


def gated_tile(c, r, p):
    rows, lanes = chunk_rows(c), slice(p * LANES, (p + 1) * LANES)
    z = r.z[rows, lanes]
    gate = sigmoid(z)
    return z, gate, r.y[rows, lanes]


def square_chunk(c, r):
    square = jnp.zeros((CHUNK, LANES), F32)
    for p in range(r.pairs):
        z, gate, y = gated_tile(c, r, p)
        gated = y * (z * gate)
        square = square + gated * gated
    r.squares.at[r.w.tp][pl.ds(c, 1), :] = jnp.sum(square.T, axis=0, keepdims=True)


def cross_chunk(c, r):
    rows = chunk_rows(c)
    cross = jnp.zeros((CHUNK, LANES), F32)
    for p in range(r.pairs):
        lanes = slice(p * LANES, (p + 1) * LANES)
        z, gate, y = gated_tile(c, r, p)
        cross = cross + r.d_mixed[rows, lanes] * r.gain[0:1, lanes] * (y * (z * gate))
    r.crosses.at[r.w.tp][pl.ds(c, 1), :] = jnp.sum(cross.T, axis=0, keepdims=True)


def slot_sum(ref, c):
    total = ref[0, pl.ds(c, 1), :]
    for i in range(1, 4):
        total = total + ref[i, pl.ds(c, 1), :]
    return total


def scale_two_row(c, r):
    return lax.rsqrt(slot_sum(r.squares, c) / (r.pairs * LANES * 4) + EPS)


def mix_chunk(c, r):
    rows = chunk_rows(c)
    scale = turned(scale_two_row(c, r))
    for p in range(r.pairs):
        lanes = slice(p * LANES, (p + 1) * LANES)
        z, gate, y = gated_tile(c, r, p)
        r.mixed[rows, lanes] = (y * (z * gate) * scale * r.gain[0:1, lanes]).astype(BF16)


def gate_back_chunk(c, r):
    rows = chunk_rows(c)
    row = scale_two_row(c, r)
    pull = turned(row * row * row * slot_sum(r.crosses, c) / (r.pairs * LANES * 4))
    scale = turned(row)
    for p in range(r.pairs):
        lanes = slice(p * LANES, (p + 1) * LANES)
        z, gate, y = gated_tile(c, r, p)
        silu = z * gate
        gated = y * silu
        scaled = r.d_mixed[rows, lanes] * scale
        r.g_gate[:, lanes] += fold_rows(scaled * gated)
        d_gated = scaled * r.gain[0:1, lanes] - gated * pull
        r.gy[rows, lanes] = (d_gated * silu).astype(BF16)
        r.d_z[rows, lanes] = (d_gated * y * (gate * (1.0 + z * (1.0 - gate)))).astype(BF16)


def by_distance(z, i):
    upper = z // 2
    low = z + upper * (LAST_Z - 2 * z)
    chip = low + i * (1 - 2 * low) if i < 2 else i
    return chip + upper * (LAST_Z - 2 * chip)


def chip_rows(r, z):
    count = 2 * r.shard_rows
    return pl.ds(pl.multiple_of(z * count, LANES), count)


def accumulate(ref, rows, value, first):
    if first:
        ref[rows, :] = value
    else:
        ref[rows, :] += value


def project_z(r, i):
    z = by_distance(r.w.z, i)
    r.shard_z.from_mate(z)
    here = chip_rows(r, z)

    def body(rows):
        accumulate(r.z, rows, dot_nn(r.row_normed[rows, here], r.full_z[here, :]), i == 0)

    by_rows(r.row_normed.shape[0], 256, body)


def output_back(r, i):
    z = by_distance(r.w.z, i)
    r.shard_out.from_mate(z)
    here = chip_rows(r, z)

    def body(rows):
        accumulate(r.d_mixed, rows, dot_nn(r.row_cot[rows, here], r.full_out[here, :]), i == 0)

    by_rows(r.row_normed.shape[0], 256, body)


def output_share(r, slot):
    block = r.x_held.shape[0]
    rows = pl.ds(pl.multiple_of(slot * block, block), block)
    tile = 512

    def body(n, carry):
        cols = pl.ds(pl.multiple_of(n * tile, tile), tile)
        r.part[rows, cols] = dot_nt(r.mixed[rows, :], r.full_out[cols, :]).astype(BF16)
        return carry

    lax.fori_loop(0, r.part.shape[1] // tile, body, 0)


def far_first(w, i):
    upper = w.z // 2
    return (1 - upper) * (LAST_Z - i) + upper * i


def weight_parts(make, scatter):
    def body(i, carry):
        z = far_first(scatter.w, i)
        make(z)
        scatter.pair_copy(z).start()
        pl.when(i > 0)(lambda: scatter.launch(far_first(scatter.w, i - 1)))
        return carry

    lax.fori_loop(0, LAST_Z + 1, body, 0)
    scatter.launch(far_first(scatter.w, LAST_Z))
    scatter.drain_pair()


def product_maker(left, right, store):
    block = left.shape[1] // (LAST_Z + 1)

    def make(z):
        lanes = pl.ds(pl.multiple_of(z * block, LANES), block)
        store(z, dot_tn(left[:, lanes], right[...]).astype(BF16))

    return make


def flat_shard(ref, rows):
    return lambda z, core: ref.at[pl.ds(pl.multiple_of((z * 2 + core) * rows, 16), rows)]


def flat_store(ref, rows):
    def store(z, value):
        ref[pl.ds(pl.multiple_of(z * 2 * rows, 16), 2 * rows), :] = value

    return store


def side_shard(ref, rows, width):
    return lambda z, core: ref.at[
        pl.ds(pl.multiple_of(z * rows, 16), rows),
        pl.ds(pl.multiple_of(core * width, LANES), width),
    ]


def side_store(ref, rows, width):
    def store(z, value):
        here = pl.ds(pl.multiple_of(z * rows, 16), rows)
        ref[here, :width] = value[:rows]
        ref[here, width : 2 * width] = value[rows:]

    return store


def own_rows(r):
    shard = r.w_x.shape[0]
    return pl.ds(pl.multiple_of(r.w.dp * shard, 16), shard)


def input_moves(r):
    width = r.pairs * LANES
    own = own_rows(r)
    block = r.cot.shape[0]
    mine = pl.ds(pl.multiple_of(r.w.tp * block, block), block)
    moves = (
        (r.w_x, r.full_x.at[own, pl.ds(0, width)]),
        (r.w_bc, r.full_x.at[own, pl.ds(width, 2 * NSTATE)]),
        (r.x_in, r.x_held),
        (r.w_z, r.full_z.at[own]),
        (r.w_out, r.full_out.at[own]),
        (r.cot, r.row_cot.at[mine]),
    )
    return [pltpu.make_async_copy(src, dst, r.s_m.at[i]) for i, (src, dst) in enumerate(moves)]


def place_steps(r):
    heads, shard = r.w_dt.shape
    mine = r.steps_t.at[pl.ds(pl.multiple_of(r.w.dp * STEP_ROWS, STEP_ROWS), STEP_ROWS)]
    r.turn[...] = jnp.zeros_like(r.turn)
    r.turn[0:heads, 0:shard] = r.w_dt[...]
    mine[...] = r.turn[0:STEP_ROWS, :]


def turn_steps(r):
    shard = r.w_x.shape[0]

    def body(d, carry):
        r.turn[0:STEP_ROWS, :] = r.steps_t[
            pl.ds(pl.multiple_of(d * STEP_ROWS, STEP_ROWS), STEP_ROWS), :
        ]
        r.full_dt[pl.ds(pl.multiple_of(d * shard, 16), shard), :] = r.turn[...].T[:shard]
        return carry

    lax.fori_loop(0, 2 * (LAST_Z + 1), body, 0)


def prepare_small(r):
    heads = r.a_log_in.shape[0]
    w, width = r.w, r.pairs * LANES
    for ref in (r.a_log, r.dt_bias):
        ref[...] = jnp.zeros_like(ref)
    r.a_log[0:1, 0:heads] = r.a_log_in[...].reshape(1, heads)
    r.dt_bias[0:1, 0:heads] = r.dt_bias_in[...].reshape(1, heads)
    r.cxb[...] = r.cxb_in[...].reshape(1, width)
    r.cbb[...] = r.cbb_in[...].reshape(1, 2 * NSTATE)
    r.gain[...] = r.gain_in[...].reshape(1, width)
    skip = r.d_skip_in[...].reshape(1, heads)
    first = lax.broadcasted_iota(jnp.int32, (1, LANES), 1) < HEADDIM
    for p in range(r.pairs):
        pair = jnp.where(first, skip[:, 2 * p : 2 * p + 1], skip[:, 2 * p + 1 : 2 * p + 2])
        r.skip[:, p * LANES : (p + 1) * LANES] = pair
    r.seg_across[...] = r.segments[...].reshape(r.chunks, CHUNK).astype(F32)
    edge = jnp.full((8, LANES), -1.0, F32)
    r.seg_down[0:8, :] = edge
    r.seg_down[r.chunks * CHUNK + 8 :, :] = edge

    def body(c):
        r.seg_down[chunk_rows(c, 8), :] = turned(r.seg_across[pl.ds(c, 1), :])

    over_chunks(r, body)


def phase_one(r):
    w = r.w
    width = r.pairs * LANES
    tokens = r.row_normed.shape[0]
    block = r.x_held.shape[0]
    start = pl.multiple_of(w.tp * block, block)
    moves = input_moves(r)
    for move in moves:
        move.start()
    place_steps(r)
    greet(w)
    moves[0].wait()
    moves[1].wait()
    r.shard_x.relay(0)
    r.shard_dt.relay(0)
    moves[2].wait()
    norm_rows(r.x_held, r.pre_gain[...].reshape(1, r.x_held.shape[1]), r.row_normed, start)
    r.row_n.start()
    r.state[...] = jnp.zeros_like(r.state)
    prepare_small(r)
    for move in moves[3:]:
        move.wait()
    r.shard_x.relay(1)
    r.shard_dt.relay(1)
    r.shard_x.relay(2)
    r.shard_dt.relay(2)
    r.row_n.hand_on()
    r.row_c.start()
    r.shard_x.relay(3)
    r.shard_dt.relay(3)
    r.shard_z.relay(0)
    r.shard_dt.finish()
    turn_steps(r)
    r.row_n.finish()
    r.shard_x.finish()

    def project_x(rows):
        normed = r.row_normed[rows, :]
        out = dot_nn(normed, r.full_x[...])
        r.xr[rows, :] = out[:, :width]
        r.bc[rows, :] = out[:, width:]
        r.dtr[rows, :] = dot_nn(normed, r.full_dt[...])

    by_rows(tokens, 256, project_x)

    def body(c):
        prepare_steps(c, r)
        scan_chunk(c, r)

        @pl.when(c == 1)
        def _():
            r.shard_z.relay(1)
            r.shard_out.relay(0)
            project_z(r, 0)

        @pl.when(c == 3)
        def _():
            r.row_c.hand_on()
            project_z(r, 1)

        @pl.when(c == 5)
        def _():
            r.shard_z.relay(2)
            project_z(r, 2)

    over_chunks(r, body)


def phase_mid(r):
    w = r.w
    r.shard_out.relay(1)
    r.shard_z.relay(3)
    project_z(r, 3)
    over_chunks(r, lambda c: square_chunk(c, r))
    r.ex_squares.start()
    r.shard_out.relay(2)
    r.row_c.finish()
    r.ex_squares.finish()
    over_chunks(r, lambda c: mix_chunk(c, r))
    weight_parts(
        product_maker(r.row_cot, r.mixed, flat_store(r.out_part, r.shard_rows)), r.grad_out
    )
    tell(r.free_pair, device(w, dp=w.mate))
    output_back(r, 0)
    output_back(r, 1)
    r.shard_out.relay(3)
    output_back(r, 2)
    output_back(r, 3)
    over_chunks(r, lambda c: cross_chunk(c, r))
    r.ex_crosses.start()
    r.grad_out.step(0)
    output_share(r, w.across)
    r.out_rows.start(0, 1)
    r.g_gate[...] = jnp.zeros_like(r.g_gate)
    r.ex_crosses.finish()
    over_chunks(r, lambda c: gate_back_chunk(c, r))
    for item in (r.shard_x, r.shard_dt, r.shard_z, r.shard_out, r.row_n, r.row_c):
        item.drain()
    pl.semaphore_wait(r.free_pair, 1)
    weight_parts(
        product_maker(
            r.row_normed, r.d_z, side_store(r.row_cot, r.shard_rows, r.pairs * LANES)
        ),
        r.grad_z,
    )
    tell(r.free_pair, device(w, dp=w.mate))
    r.grad_out.step(1)
    for slot, copy in ((w.near_x, 2), (w.near_y, 3)):
        output_share(r, slot)
        r.out_rows.start(copy)
    output_share(r, w.tp)
    r.out_rows.hand_on()
    tell(r.free_far, device(w, tp=w.near_x))
    tell(r.free_far, device(w, tp=w.near_y))


def phase_back(r):
    w = r.w
    block = r.x_held.shape[0]
    start_back(r)

    def body(i, carry):
        scan_chunk_back(r.chunks - 1 - i, r)

        @pl.when(i == 0)
        def _():
            r.grad_out.finish(r.v_w_out)
            r.put(r.v_w_out, r.o_w_out, 0).start()
            r.grad_out.drain()
            tell(r.free_line, device(w, dp=other_z(w, 1)))
            tell(r.free_line, device(w, dp=other_z(w, 3)))

        for at, k, part in ((1, 0, 0), (2, 0, 1), (4, 1, 0), (5, 1, 1)):
            pl.when(i == at)(lambda k=k, part=part: r.grad_z.step(k, part))

        return carry

    lax.fori_loop(0, r.chunks, body, 0)


def finish_block(r):
    w = r.w
    block = r.x_held.shape[0]
    step = 64
    r.out_rows.finish()

    def add(k, carry):
        here = pl.ds(pl.multiple_of(k * step, step), step)
        there = pl.ds(pl.multiple_of(w.tp * block + k * step, 16), step)
        total = r.x_held[here, :].astype(F32) + r.out_rows.total(here, there)
        r.v_block[here, :] = total.astype(BF16)
        return carry

    lax.fori_loop(0, block // step, add, 0)
    r.put(r.v_block, r.o_block, 1).start()
    tell(r.free_row, device(w, tp=w.near_x))
    tell(r.free_row, device(w, tp=w.near_y))


def step_parts(r, at):
    shard = r.shard_rows
    out = dot_tn(r.d_rest[:, at : at + LANES], r.row_normed[...])[:STEP_ROWS]
    for d in range(2 * (LAST_Z + 1)):
        here = slice(d * STEP_ROWS, (d + 1) * STEP_ROWS)
        r.dt_part[here, 0:shard] = out[:, d * shard : (d + 1) * shard]


def phase_last(r):
    w = r.w
    width = r.pairs * LANES
    block = r.x_held.shape[0]
    edge = width + 2 * NSTATE
    r.out_rows.drain()
    r.g_pre[...] = jnp.zeros_like(r.g_pre)

    def share(slot):
        rows = pl.ds(pl.multiple_of(slot * block, block), block)
        tile = 512

        def body(n, carry):
            cols = pl.ds(pl.multiple_of(n * tile, tile), tile)
            out = dot_nt(r.d_z[rows, :], r.full_z[cols, :])
            out = out + dot_nt(r.d_rest[rows, :edge], r.full_x[cols, :])
            out = out + dot_nt(r.d_rest[rows, edge:], r.full_dt[cols, :])
            r.part[rows, cols] = out.astype(BF16)
            r.g_pre[:, cols] += fold_rows(out * r.row_normed[rows, cols].astype(F32))
            return carry

        lax.fori_loop(0, r.part.shape[1] // tile, body, 0)

    share(w.across)
    pl.semaphore_wait(r.free_far, 2)
    r.in_rows.start(0, 1)
    weight_parts(
        product_maker(
            r.row_normed,
            r.d_rest.at[:, pl.ds(width, 2 * NSTATE)],
            flat_store(r.bc_part, r.shard_rows),
        ),
        r.grad_bc,
    )
    step_parts(r, edge)
    for z in range(LAST_Z + 1):
        r.grad_dt.pair_copy(z).start()
    finish_block(r)
    share(w.near_x)
    pl.semaphore_wait(r.free_row, 2)
    r.in_rows.start(2)
    r.grad_bc.step(0)
    for i in range(LAST_Z + 1):
        r.grad_dt.launch(far_first(w, i))
    r.grad_dt.drain_pair()
    share(w.near_y)
    r.in_rows.start(3)
    pl.semaphore_wait(r.free_pair, 1)
    pl.semaphore_wait(r.free_line, 2)
    weight_parts(
        product_maker(
            r.row_normed,
            r.d_rest.at[:, pl.ds(0, width)],
            flat_store(r.full_out, r.shard_rows),
        ),
        r.grad_x_part,
    )
    r.grad_bc.step(1)
    r.grad_dt.step(0)
    share(w.tp)
    r.in_rows.hand_on()
    again = [
        pltpu.make_async_copy(r.cot.at[pl.ds(k * (block // 2), block // 2)], r.far.at[k], r.s_m.at[k])
        for k in range(2)
    ]
    for copy in again:
        copy.start()
    r.grad_dt.step(1)
    pack_small(r)
    r.ex_pair.start()
    r.grad_x_part.step(0, 0)
    r.grad_bc.finish(r.bc_sum)
    r.bc_slots.at[w.tp][...] = r.bc_sum[...].astype(BF16)
    r.ex_bc.start()
    r.ex_pair.finish()
    r.small_z.at[w.z][...] = r.ex_pair.total()
    r.ex_z.start()
    r.grad_x_part.launch_last()
    r.grad_x_part.step(0, 1)
    r.grad_dt.finish(r.v_w_dt)
    r.put(r.v_w_dt, r.o_w_dt, 3).start()
    r.grad_z.finish(r.v_w_z)
    r.put(r.v_w_z, r.o_w_z, 2).start()
    r.grad_x_part.step(1, 0)
    r.grad_x_part.step(1, 1)
    r.ex_z.finish()
    total = r.ex_z.total()
    r.small_t.at[w.tp][...] = total[SMALL_DP:]
    r.ex_t.start()
    r.v_small[...] = total[:SMALL_DP]
    r.put(r.v_small, r.o_small, 4).start()
    for item in (r.grad_z, r.grad_bc, r.grad_dt):
        item.drain()
    gain = r.pre_gain[...].reshape(1, r.x_held.shape[1])
    for copy in again:
        copy.wait()
    r.in_rows.finish()
    step = 64

    def body(k, carry):
        here = pl.ds(pl.multiple_of(k * step, step), step)
        there = pl.ds(pl.multiple_of(w.tp * block + k * step, 16), step)
        half = k // (block // 2 // step)
        inner = pl.ds(pl.multiple_of(k * step - half * (block // 2), step), step)
        values = r.x_held[here, :].astype(F32)
        scale = lax.rsqrt(jnp.mean(values * values, axis=1, keepdims=True) + EPS)
        weighted = r.in_rows.total(here, there) * gain
        along = jnp.mean(weighted * values, axis=1, keepdims=True)
        grad = r.far[half, inner, :].astype(F32) + scale * weighted
        r.v_grad_x[here, :] = (grad - values * (scale * scale * scale * along)).astype(BF16)
        return carry

    lax.fori_loop(0, block // step, body, 0)
    r.put(r.v_grad_x, r.o_grad_x, 7).start()
    r.in_rows.drain()
    r.ex_bc.finish()
    r.v_w_bc[...] = r.ex_bc.total()
    r.put(r.v_w_bc, r.o_w_bc, 5).start()
    r.grad_x_part.finish(r.v_w_x)
    r.put(r.v_w_x, r.o_w_x, 8).start()
    r.grad_x_part.drain()
    r.ex_t.finish()
    shared = r.ex_t.total()
    count = gain.shape[1] // LANES
    r.v_shared[...] = shared
    for p in range(count):
        r.v_shared[p : p + 1, :] = shared[p : p + 1, :] / gain[:, p * LANES : (p + 1) * LANES]
    r.put(r.v_shared, r.o_shared, 6).start()
    ends = ("w_out", "block", "w_z", "w_dt", "small", "w_bc", "shared", "grad_x", "w_x")
    for i, name in enumerate(ends):
        r.put(getattr(r, "v_" + name), getattr(r, "o_" + name), i).wait()


SMALL_DP = 40
SMALL_ALL = 24


def head_row(r):
    lane = lax.broadcasted_iota(jnp.int32, (1, LANES), 1)
    out = jnp.zeros((1, LANES), F32)
    for p in range(r.pairs):
        tile = jnp.sum(r.g_skip[:, p * LANES : (p + 1) * LANES], axis=0, keepdims=True)
        for k, part in enumerate((lane < HEADDIM, lane >= HEADDIM)):
            head = jnp.sum(jnp.where(part, tile, 0.0), axis=1, keepdims=True)
            out = jnp.where(lane == 2 * p + k, head, out)
    return out


def pack_small(r):
    mine = r.small_pair.at[r.w.core]
    mine[...] = jnp.zeros_like(mine)

    def put(at, ref, first, count):
        for p in range(count):
            lanes = slice(p * LANES, (p + 1) * LANES)
            mine[at + p : at + p + 1, :] = jnp.sum(
                ref[first : first + 8, lanes], axis=0, keepdims=True
            )
        return at + count

    at = put(0, r.g_gate, 0, r.pairs)
    for k in range(4):
        at = put(at, r.g_cxw, 8 * k, r.pairs)
    at = put(at, r.g_cxb, 0, r.pairs)
    mine[at : at + 1, :] = head_row(r)
    at = at + 1
    at = put(at, r.g_alog, 0, 1)
    at = put(at, r.g_dtb, 0, 1)
    at = put(SMALL_DP, r.g_pre, 0, r.g_pre.shape[1] // LANES)
    for k in range(4):
        at = put(at, r.g_cbw, 8 * k, 2)
    put(at, r.g_cbb, 0, 2)


RAW_IN = (
    "x_in",
    "segments",
    "pre_gain",
    "w_z",
    "w_x",
    "w_bc",
    "w_dt",
    "cxw",
    "cxb_in",
    "cbw",
    "cbb_in",
    "a_log_in",
    "dt_bias_in",
    "d_skip_in",
    "gain_in",
    "w_out",
    "cot",
)


def whole_kernel(*refs, names, width):
    r = types.SimpleNamespace(**dict(zip(names, refs)))
    r.w = w = place()
    r.pairs = width // LANES
    r.chunks = r.row_normed.shape[0] // CHUNK
    r.shard_rows = r.w_x.shape[0]
    r.xr_at = r.bc_at = r.dtr_at = 0
    r.dx_at, r.dbc_at, r.ddt_at = 0, width, width + 2 * NSTATE
    gather = lambda i, ref: LineGather(w, ref, r.s_w.at[i], r.r_w.at[i], PARTS)
    r.shard_x = gather(0, r.full_x)
    r.shard_z = gather(1, r.full_z)
    r.shard_out = gather(2, r.full_out)
    r.shard_dt = LineGather(w, r.steps_t, r.s_d, r.r_d, 1)
    r.row_n = RowGather(w, r.row_normed, r.s_r.at[0], r.r_r.at[0])
    r.row_c = RowGather(w, r.row_cot, r.s_r.at[1], r.r_r.at[1])
    r.out_rows = r.in_rows = RowScatter(w, r.part, r.far, r.near, r.s_q.at[0], r.r_q)
    rows = r.shard_rows
    held = (r.pair, r.up, r.down, r.p_main, r.l_main, PARTS)
    r.grad_out = LineScatter(w, flat_shard(r.out_part, rows), *held)
    r.grad_x_part = LineScatter(w, flat_shard(r.full_out, rows), *held, hold=True)
    side = side_shard(r.row_cot, rows, width)
    r.grad_z = LineScatter(w, side, r.pair, r.up_z, r.down_z, r.p_main, r.l_z, PARTS)
    held_dt = (r.pair_dt, r.up_dt, r.down_dt, r.p_dt, r.l_dt, 1)
    r.grad_dt = LineScatter(w, flat_shard(r.dt_part, STEP_ROWS), *held_dt)
    in_row = [device(w, tp=t) for t in (w.near_x, w.near_y, w.across)]
    in_line = [device(w, dp=other_z(w, k)) for k in (1, 2, 3)]
    exchange = lambda i, ref, mine, targets: Exchange(ref, mine, targets, r.s_e.at[i])
    r.ex_squares = exchange(0, r.squares, w.tp, in_row)
    r.ex_crosses = exchange(1, r.crosses, w.tp, in_row)
    r.ex_pair = exchange(2, r.small_pair, w.core, [device(w, dp=w.mate)])
    r.ex_z = exchange(3, r.small_z, w.z, in_line)
    r.ex_t = exchange(4, r.small_t, w.tp, in_row)
    r.ex_bc = exchange(5, r.bc_slots, w.tp, in_row)
    r.put = lambda src, dst, i: pltpu.make_async_copy(src, dst, r.s_o.at[i])
    tokens = r.chunks * CHUNK

    def middle(z, d_mixed, mixed):
        r.z, r.d_mixed, r.mixed = z, d_mixed, mixed
        phase_one(r)
        phase_mid(r)

    pl.run_scoped(
        middle,
        pltpu.VMEM((tokens, width), F32),
        pltpu.VMEM((tokens, width), F32),
        pltpu.VMEM((tokens, width), BF16),
    )
    later = dict(BACK_SCRATCH(width), bc_part=((r.full_x.shape[0], 2 * NSTATE), BF16))

    def rest(d_rest, *buffers):
        r.d_rest = r.d_proj = d_rest
        for name, buffer in zip(later, buffers):
            setattr(r, name, buffer)
        held_bc = (r.pair_bc, r.up_bc, r.down_bc, r.p_bc, r.l_bc, 1)
        r.grad_bc = LineScatter(w, flat_shard(r.bc_part, rows), *held_bc)
        phase_back(r)
        phase_last(r)

    pl.run_scoped(
        rest,
        pltpu.VMEM((tokens, width + 2 * NSTATE + LANES), BF16),
        *[pltpu.VMEM(*spec) for spec in later.values()],
    )


def whole_call(args, width):
    x_in, w_x = args[0], args[4]
    features, block = x_in.shape[1], x_in.shape[0]
    tokens = block * 4
    shard = w_x.shape[0]
    maps = 2 * NSTATE
    chunks = tokens // CHUNK
    turned_step = (STEP_ROWS, 2 * LANES)
    outs = dict(
        block=((block, features), BF16),
        grad_x=((block, features), BF16),
        w_z=((shard, width), F32),
        w_x=((shard, width), F32),
        w_bc=((shard, maps), F32),
        w_dt=(turned_step, F32),
        w_out=((shard, width), F32),
        small=((SMALL_DP, LANES), F32),
        shared=((SMALL_ALL, LANES), F32),
    )
    scratch = dict(
        x_held=((block, features), BF16),
        row_normed=((tokens, features), BF16),
        row_cot=((tokens, features), BF16),
        full_x=((features, width + maps), BF16),
        full_z=((features, width), BF16),
        full_out=((features, width), BF16),
        full_dt=((features, LANES), BF16),
        steps_t=((8 * STEP_ROWS, 2 * LANES), BF16),
        xr=((tokens, width), F32),
        bc=((tokens, maps), F32),
        dtr=((tokens, LANES), F32),
        y=((tokens, width), F32),
        pre_x=((tokens, width), F32),
        pre_bc=((tokens, maps), F32),
        maps=((tokens, maps), BF16),
        states=((tokens, width), BF16),
        state=((NSTATE, width), F32),
        step=((tokens, LANES), F32),
        total=((tokens, LANES), F32),
        total_t=((chunks * 16, LANES), F32),
        seg_down=((tokens + 16, LANES), F32),
        seg_across=((chunks, LANES), F32),
        turn=((LANES, 2 * LANES), BF16),
        a_log=((1, LANES), F32),
        dt_bias=((1, LANES), F32),
        cxb=((1, width), F32),
        cbb=((1, maps), F32),
        gain=((1, width), F32),
        skip=((1, width), F32),
        squares=((4, chunks, LANES), F32),
        crosses=((4, chunks, LANES), F32),
        gy=((tokens, width), BF16),
        d_z=((tokens, width), BF16),
        part=((tokens, features), BF16),
        far=((2, block // 2, features), BF16),
        near=((2, block, features), BF16),
        out_part=((features, width), BF16),
        dt_part=((8 * STEP_ROWS, 2 * LANES), F32),
        pair=((4 * shard, width), BF16),
        pair_bc=((4 * shard, maps), BF16),
        pair_dt=((4 * STEP_ROWS, 2 * LANES), F32),
        up=((3 * shard, width), BF16),
        down=((3 * shard, width), BF16),
        up_z=((3 * shard, width), BF16),
        down_z=((3 * shard, width), BF16),
        up_bc=((3 * shard, maps), BF16),
        down_bc=((3 * shard, maps), BF16),
        up_dt=((3 * STEP_ROWS, 2 * LANES), F32),
        down_dt=((3 * STEP_ROWS, 2 * LANES), F32),
        bc_sum=((shard, maps), F32),
        bc_slots=((4, shard, maps), BF16),
        small_pair=((2, SMALL_DP + SMALL_ALL, LANES), F32),
        small_z=((4, SMALL_DP + SMALL_ALL, LANES), F32),
        small_t=((4, SMALL_ALL, LANES), F32),
        g_gate=((8, width), F32),
        g_pre=((8, features), F32),
        **GRAD_OUT(width),
        **{"v_" + name: spec for name, spec in outs.items()},
    )
    dma = pltpu.SemaphoreType.DMA
    signal = pltpu.SemaphoreType.REGULAR
    semaphores = dict(
        s_w=dma((3, 3)),
        r_w=dma((3, 4 * PARTS + 4)),
        s_d=dma((3,)),
        r_d=dma((8,)),
        s_r=dma((2,)),
        r_r=dma((2, 3)),
        s_q=dma((1,)),
        r_q=dma((3,)),
        p_main=dma((5,)),
        p_bc=dma((5,)),
        p_dt=dma((5,)),
        l_main=dma((2 + 6 * PARTS,)),
        l_z=dma((2 + 6 * PARTS,)),
        l_bc=dma((8,)),
        l_dt=dma((8,)),
        s_e=dma((6, 2)),
        s_m=dma((6,)),
        s_o=dma((len(outs),)),
        free_pair=signal,
        free_line=signal,
        free_row=signal,
        free_far=signal,
    )
    names = RAW_IN + tuple("o_" + name for name in outs) + tuple(scratch) + tuple(semaphores)
    values = list(args)
    values[6] = values[6].T
    values[15] = values[15].T
    whole = pl.BlockSpec(memory_space=pltpu.VMEM)
    apart = pl.BlockSpec(memory_space=pl.ANY)
    moved = ("x_in", "w_z", "w_x", "w_bc", "w_out", "cot")
    out = pl.pallas_call(
        functools.partial(whole_kernel, names=names, width=width),
        out_shape=tuple(jax.ShapeDtypeStruct(*spec) for spec in outs.values()),
        in_specs=[apart if name in moved else whole for name in RAW_IN],
        out_specs=tuple([apart] * len(outs)),
        scratch_shapes=[pltpu.VMEM(*spec) for spec in scratch.values()]
        + list(semaphores.values()),
        compiler_params=pltpu.CompilerParams(
            vmem_limit_bytes=VMEM_LIMIT, collective_id=0, has_side_effects=True
        ),
        cost_estimate=pl.CostEstimate(
            flops=5 * 10**10, bytes_accessed=1 << 26, transcendentals=0
        ),
    )(*values)
    return dict(zip(outs, out))


LARGE = ("block", "grad_x", "w_z", "w_x", "w_bc", "w_out")
FINAL = ("pre", "dt", "cxw", "cxb", "cbw", "cbb", "alog", "dtb", "skip", "gate")


def publish_kernel(*refs):
    count = len(LARGE)
    large_in, (steps, small, shared) = refs[:count], refs[count : count + 3]
    large_out = refs[count + 3 : 2 * count + 3]
    o = types.SimpleNamespace(**dict(zip(FINAL, refs[2 * count + 3 : -1])))
    sem = refs[-1]
    moves = [
        pltpu.make_async_copy(src, dst, sem.at[i])
        for i, (src, dst) in enumerate(zip(large_in, large_out))
    ]
    for move in moves:
        move.start()
    heads = o.alog.shape[0]

    def line(out, src, at):
        for p in range(out.shape[0] // LANES):
            out[p * LANES : (p + 1) * LANES] = src[at + p : at + p + 1, :].reshape(LANES)
        return at + out.shape[0] // LANES

    def taps(out, src, at):
        count = out.shape[1] // LANES
        for k in range(4):
            for p in range(count):
                out[k : k + 1, p * LANES : (p + 1) * LANES] = src[at + p : at + p + 1, :]
            at = at + count
        return at

    at = line(o.gate, small, 0)
    at = taps(o.cxw, small, at)
    at = line(o.cxb, small, at)
    for out in (o.skip, o.alog, o.dtb):
        out[...] = small[at : at + 1, 0:heads].reshape(heads)
        at = at + 1
    at = line(o.pre, shared, 0)
    at = taps(o.cbw, shared, at)
    line(o.cbb, shared, at)
    o.dt[...] = steps[0:heads, 0 : o.dt.shape[1]]
    for move in moves:
        move.wait()


def publish(o, width, heads):
    features = o["block"].shape[1]
    shard = o["w_z"].shape[0]
    shapes = dict(
        pre=(features,),
        dt=(heads, shard),
        cxw=(4, width),
        cxb=(width,),
        cbw=(4, 2 * NSTATE),
        cbb=(2 * NSTATE,),
        alog=(heads,),
        dtb=(heads,),
        skip=(heads,),
        gate=(width,),
    )
    whole = pl.BlockSpec(memory_space=pltpu.VMEM)
    apart = pl.BlockSpec(memory_space=pl.ANY)
    large = [o[name] for name in LARGE]
    out = pl.pallas_call(
        publish_kernel,
        out_shape=tuple(
            [jax.ShapeDtypeStruct(v.shape, v.dtype) for v in large]
            + [jax.ShapeDtypeStruct(shapes[name], F32) for name in FINAL]
        ),
        in_specs=[apart] * len(large) + [whole] * 3,
        out_specs=tuple([whole] * (len(large) + len(FINAL))),
        scratch_shapes=[pltpu.SemaphoreType.DMA((len(large),))],
    )(*large, o["w_dt"], o["small"], o["shared"])
    return types.SimpleNamespace(**dict(zip(LARGE + FINAL, out)))


def on_device_whole(*args):
    width = args[3].shape[1]
    heads = args[11].shape[0]
    p = publish(whole_call(args, width), width, heads)
    return (
        p.block,
        p.grad_x,
        p.pre,
        p.w_z,
        p.w_x,
        p.w_bc,
        p.dt.T,
        p.cxw,
        p.cxb,
        p.cbw,
        p.cbb,
        p.alog,
        p.dtb,
        p.skip,
        p.gate,
        p.w_out.T,
    )


def forward_plain(args, small, width):
    x_in, pre_gain, w_z, w_x, w_bc, w_dt, w_out, gate_gain, cotangent = args
    heads = w_dt.shape[1]
    at = layout_of(width)
    values = x_in.astype(F32)
    scale = lax.rsqrt(jnp.mean(values * values, axis=1) + EPS)
    normed = (values * scale[:, None] * pre_gain[None, :]).astype(BF16)
    row_normed = lax.all_gather(normed, "tensor", axis=0, tiled=True)
    mine = jnp.concatenate(
        (w_z, w_x, w_bc, jnp.pad(w_dt, ((0, 0), (0, LANES - heads)))), axis=1
    )
    stacked = lax.all_gather(mine, "dp", axis=0, tiled=True)
    full_out = lax.all_gather(w_out.T, "dp", axis=0, tiled=True)
    projected = jnp.dot(row_normed, stacked, preferred_element_type=F32)
    saved = mixer_forward(projected, small, width)
    row_cot = lax.all_gather(cotangent, "tensor", axis=0, tiled=True)
    y = saved[0]
    z_raw = projected[:, :width]
    gated = y * (z_raw * sigmoid(z_raw))
    d_mixed = dot_nn(row_cot, full_out)
    squares, cross = lax.psum(
        (
            jnp.sum(gated * gated, axis=1),
            jnp.sum(d_mixed * gate_gain[None, :] * gated, axis=1),
        ),
        "tensor",
    )
    return types.SimpleNamespace(
        row_normed=row_normed,
        row_cot=row_cot,
        full_z=stacked[:, :width],
        full_x=stacked[:, width:],
        full_out=full_out,
        z=z_raw,
        projected=(projected,),
        saved=saved,
        d_mixed=d_mixed,
        squares=squares,
        cross=cross,
    )


def on_device(
    x_in,
    segments,
    pre_gain,
    w_z,
    w_x,
    w_bc,
    w_dt,
    conv_x_w,
    conv_x_b,
    conv_bc_w,
    conv_bc_b,
    a_log,
    dt_bias,
    d_skip,
    gate_gain,
    w_out,
    cotangent,
):
    width = w_z.shape[1]
    heads = a_log.shape[0]
    at = layout_of(width)
    small = small_inputs(
        segments, conv_x_w, conv_x_b, conv_bc_w, conv_bc_b, a_log, dt_bias, d_skip
    )
    args = (x_in, pre_gain, w_z, w_x, w_bc, w_dt, w_out, gate_gain, cotangent)
    f = forward_plain(args, small, width)
    squares, cross = f.squares, f.cross
    y, z_raw, d_mixed = f.saved[0], f.z, f.d_mixed
    values = x_in.astype(F32)
    scale = lax.rsqrt(jnp.mean(values * values, axis=1) + EPS)
    gate = sigmoid(z_raw)
    gated = y * (z_raw * gate)
    inner_total = width * lax.axis_size("tensor")
    weighted = d_mixed * gate_gain[None, :]
    scale_two = lax.rsqrt(squares / inner_total + EPS)
    mixed = (gated * scale_two[:, None] * gate_gain[None, :]).astype(BF16)
    branch = lax.psum_scatter(
        dot_nt(mixed, f.full_out).astype(BF16), "tensor", scatter_dimension=0, tiled=True
    ).astype(F32)
    block_out = (values + branch).astype(BF16)
    grad_gate_part = jnp.sum(d_mixed * gated * scale_two[:, None], axis=0)
    d_gated = (
        scale_two[:, None] * weighted
        - gated * (scale_two * scale_two * scale_two * cross / inner_total)[:, None]
    )
    gy = (d_gated * (z_raw * gate)).astype(BF16)
    d_z = (d_gated * y * (gate * (1.0 + z_raw * (1.0 - gate)))).astype(BF16)
    d_rest, g_cxw, g_cxb, g_cbw, g_cbb, g_skip, g_alog, g_dtb = mixer_backward(
        f.projected, small, f.saved, gy, width
    )
    d_proj = jnp.concatenate((d_z, d_rest), axis=1)
    d_normed = lax.psum_scatter(
        (dot_nt(d_z, f.full_z) + dot_nt(d_rest, f.full_x)).astype(BF16),
        "tensor",
        scatter_dimension=0,
        tiled=True,
    ).astype(F32)
    proj_part = dot_tn(f.row_normed, d_proj)
    out_part = dot_tn(f.row_cot, mixed)
    owned = lax.psum_scatter(
        jnp.concatenate((proj_part, out_part), axis=1).astype(BF16),
        "dp",
        scatter_dimension=0,
        tiled=True,
    ).astype(F32)
    grad_w_bc = lax.psum(owned[:, at.bc : at.dt].astype(BF16), "tensor").astype(F32)
    pre_weighted = d_normed * pre_gain[None, :]
    grad_pre_part = jnp.sum(d_normed * values * scale[:, None], axis=0)
    feature_sum = jnp.sum(pre_weighted * values, axis=1)
    grad_x = (
        cotangent.astype(F32)
        + scale[:, None] * pre_weighted
        - values * (scale * scale * scale * feature_sum / values.shape[1])[:, None]
    ).astype(BF16)
    over_taps = lambda v: jnp.sum(v.reshape(4, 8, v.shape[1]), axis=1)
    over_rows = lambda v: jnp.sum(v, axis=0)
    grad_gate_gain, grad_cxw, grad_cxb, grad_alog, grad_dtb, grad_skip = lax.psum(
        (
            grad_gate_part,
            over_taps(g_cxw),
            over_rows(g_cxb),
            over_rows(g_alog)[:heads],
            over_rows(g_dtb)[:heads],
            jnp.sum(over_rows(g_skip).reshape(heads, HEADDIM), axis=1),
        ),
        "dp",
    )
    grad_pre_gain, grad_cbw, grad_cbb = lax.psum(
        (grad_pre_part, over_taps(g_cbw), over_rows(g_cbb)), ("dp", "tensor")
    )
    return (
        block_out,
        grad_x,
        grad_pre_gain,
        owned[:, :width],
        owned[:, width : at.bc],
        grad_w_bc,
        owned[:, at.dt : at.dt + heads],
        grad_cxw,
        grad_cxb,
        grad_cbw,
        grad_cbb,
        grad_alog,
        grad_dtb,
        grad_skip,
        grad_gate_gain,
        owned[:, at.all :].T,
    )


def solution(mesh):
    tokens = P(("dp", "tensor"), None)
    both = P("dp", "tensor")
    heads = P("tensor")
    line = mesh.shape["dp"] == 2 * (LAST_Z + 1) and mesh.shape["tensor"] == 4
    return jax.shard_map(
        on_device_whole if line else on_device,
        mesh=mesh,
        in_specs=(
            tokens,
            P("dp"),
            P(),
            both,
            both,
            P("dp", None),
            both,
            P(None, "tensor"),
            heads,
            P(),
            P(),
            heads,
            heads,
            heads,
            heads,
            P("tensor", "dp"),
            tokens,
        ),
        out_specs=(
            tokens,
            tokens,
            P(),
            both,
            both,
            P("dp", None),
            both,
            P(None, "tensor"),
            heads,
            P(),
            P(),
            heads,
            heads,
            heads,
            heads,
            P("tensor", "dp"),
        ),
        check_vma=False,
    )
```

```python
import functools
import types

import jax
import jax.numpy as jnp
from jax import lax
from jax.experimental import pallas as pl
from jax.experimental.pallas import tpu as pltpu
from jax.sharding import PartitionSpec as P

HEADDIM = 64
NSTATE = 128
CHUNK = 128
LANES = 128
EPS = 1e-05
LOG2E = 1.4426950408889634
F32 = jnp.float32
BF16 = jnp.bfloat16
VMEM_LIMIT = 62 * 1024 * 1024
exact = lax.Precision.HIGHEST


def dot_nn(a, b):
    return lax.dot_general(a, b, (((1,), (0,)), ((), ())), preferred_element_type=F32)


def dot_nt(a, b):
    return lax.dot_general(a, b, (((1,), (1,)), ((), ())), preferred_element_type=F32)


def dot_tn(a, b):
    return lax.dot_general(a, b, (((0,), (0,)), ((), ())), preferred_element_type=F32)


def sigmoid(v):
    return 1.0 / (1.0 + jnp.exp(-v))


def softplus(v):
    return jnp.maximum(v, 0.0) + jnp.log1p(jnp.exp(-jnp.abs(v)))


def fold_rows(v):
    return jnp.sum(v.reshape(v.shape[0] // 8, 8, v.shape[1]), axis=0)


def split_two(v):
    high = v.astype(BF16)
    return high, (v - high.astype(F32)).astype(BF16)


def tile_iotas():
    shape = (CHUNK, LANES)
    return lax.broadcasted_iota(jnp.int32, shape, 0), lax.broadcasted_iota(jnp.int32, shape, 1)


def chunk_rows(c, pad=0, extra=0):
    return pl.ds(pl.multiple_of(c * CHUNK + pad, 8), CHUNK + extra)


def prepare_steps(c, r):
    row, col = tile_iotas()
    rows = chunk_rows(c)
    lower = (row >= col).astype(F32)
    step = softplus(r.dtr[rows, r.dtr_at : r.dtr_at + LANES] + r.dt_bias[...])
    log_step = step * (-jnp.exp(r.a_log[...]) * LOG2E)
    total = jnp.dot(lower, log_step, precision=exact, preferred_element_type=F32)
    r.step[rows, :] = step
    r.total[rows, :] = total
    r.total_t[pl.ds(pl.multiple_of(c * 16, 16), 16), :] = total.T[:16]


def segment_parts(c, r):
    down = r.seg_down[chunk_rows(c, 8), :]
    across = r.seg_across[pl.ds(c, 1), :]
    before = r.seg_down[pl.ds(pl.multiple_of(c * CHUNK, 8), 8), :][7:8, :]
    last = down[CHUNK - 1 : CHUNK, :]
    carried = (down == before).astype(F32)
    to_end = (down == last).astype(F32)
    carry_on = (last == before).astype(F32)
    return down, across, carried, to_end, carry_on


def masks_back(c, r, down):
    window = r.seg_down[chunk_rows(c, 0, 8), :]
    return [
        (pltpu.roll(window, j, 0)[8 : 8 + CHUNK] == down).astype(F32) for j in range(1, 4)
    ]


def masks_ahead(c, r, down):
    window = r.seg_down[chunk_rows(c, 8, 8), :]
    full = CHUNK + 8
    return [(pltpu.roll(window, full - j, 0)[:CHUNK] == down).astype(F32) for j in range(1, 4)]


def conv_tile(c, ref, at, weight, bias, w_at, masks):
    lanes = slice(at, at + LANES)
    w_lanes = slice(w_at, w_at + LANES)
    here = ref[chunk_rows(c), lanes]
    ahead = ref[pl.ds(pl.multiple_of(jnp.maximum(c * CHUNK - 8, 0), 8), 8), lanes]
    window = jnp.concatenate([ahead, here], axis=0)
    out = here * weight[3:4, w_lanes] + bias[0:1, w_lanes]
    for j in range(1, 4):
        shifted = pltpu.roll(window, j, 0)[8 : 8 + CHUNK]
        out = out + (shifted * masks[j - 1]) * weight[3 - j : 4 - j, w_lanes]
    return out


def pair_columns(tile, p, first):
    left = jnp.broadcast_to(tile[:, 2 * p : 2 * p + 1], (CHUNK, LANES))
    right = jnp.broadcast_to(tile[:, 2 * p + 1 : 2 * p + 2], (CHUNK, LANES))
    return left, right, jnp.where(first, left, right)


def stack_heads(tile, first):
    zero = jnp.zeros_like(tile)
    return jnp.concatenate([jnp.where(first, tile, zero), jnp.where(first, zero, tile)], axis=0)


def scan_chunk(c, r):
    rows = chunk_rows(c)
    row, col = tile_iotas()
    down, across, carried, to_end, carry_on = segment_parts(c, r)
    masks = masks_back(c, r, down)
    maps = []
    for half in range(2):
        pre = conv_tile(c, r.bc, r.bc_at + half * LANES, r.cbw, r.cbb, half * LANES, masks)
        r.pre_bc[rows, half * LANES : (half + 1) * LANES] = pre
        maps.append((pre * sigmoid(pre)).astype(BF16))
    b_map, c_map = maps
    r.maps[rows, :LANES] = b_map
    r.maps[rows, LANES:] = c_map
    scores = jnp.where((down == across) & (row >= col), dot_nt(c_map, b_map), 0.0)
    b_turned = b_map.T
    total = r.total[rows, :]
    step = r.step[rows, :]
    first = col < HEADDIM
    for p in range(r.pairs):
        lanes = slice(p * LANES, (p + 1) * LANES)
        pre = conv_tile(c, r.xr, r.xr_at + p * LANES, r.cxw, r.cxb, p * LANES, masks)
        r.pre_x[rows, lanes] = pre
        chan = pre * sigmoid(pre)
        left, right, both = pair_columns(total, p, first)
        _, _, step_pair = pair_columns(step, p, first)
        fed = step_pair * chan
        stacked = stack_heads(fed.astype(BF16), first)
        mixing = []
        for k, mine in enumerate((left, right)):
            other = r.total_t[pl.ds(c * 16 + 2 * p + k, 1), :]
            mixing.append((scores * jnp.exp2(jnp.minimum(mine - other, 0.0))).astype(BF16))
        within = dot_nn(jnp.concatenate(mixing, axis=1), stacked)
        state = r.state[:, lanes]
        state_low = state.astype(BF16)
        r.states[rows, lanes] = state_low
        decay_in = jnp.exp2(both) * carried
        r.y[rows, lanes] = (
            within + decay_in * dot_nn(c_map, state_low) + r.skip[0:1, lanes] * chan
        )
        last = both[CHUNK - 1 : CHUNK, :]
        decay_out = jnp.exp2(last - both) * to_end
        r.state[:, lanes] = (jnp.exp2(last) * carry_on) * state + dot_nn(
            b_turned, (decay_out * fed).astype(BF16)
        )


def scan_chunk_back(c, r):
    rows = chunk_rows(c)
    row, col = tile_iotas()
    down, across, carried, to_end, carry_on = segment_parts(c, r)
    ahead = masks_ahead(c, r, down)
    b_map = r.maps[rows, :LANES]
    c_map = r.maps[rows, LANES:]
    visible = (down == across) & (row <= col)
    scores = jnp.where(visible, dot_nt(b_map, c_map), 0.0)
    c_turned = c_map.T
    total = r.total[rows, :]
    step = r.step[rows, :]
    first = col < HEADDIM
    d_scores = jnp.zeros((CHUNK, LANES), F32)
    width = r.pairs * LANES
    for p in range(r.pairs):
        lanes = slice(p * LANES, (p + 1) * LANES)
        lows = slice(width + p * LANES, width + (p + 1) * LANES)
        gy_low = r.gy[rows, lanes]
        gy = gy_low.astype(F32)
        pre = r.pre_x[rows, lanes]
        gate = sigmoid(pre)
        chan = pre * gate
        left, right, both = pair_columns(total, p, first)
        _, _, step_pair = pair_columns(step, p, first)
        fed = step_pair * chan
        fed_low = fed.astype(BF16)
        d_mixing = dot_nt(stack_heads(fed_low, first), gy_low)
        mixing = []
        for k, mine in enumerate((left, right)):
            other = r.total_t[pl.ds(c * 16 + 2 * p + k, 1), :]
            decay = jnp.exp2(jnp.minimum(other - mine, 0.0))
            mixing.append((scores * decay).astype(BF16))
            d_scores = d_scores + d_mixing[k * CHUNK : (k + 1) * CHUNK] * decay
        d_state = r.d_state[:, lanes]
        d_state_low = d_state.astype(BF16)
        last = both[CHUNK - 1 : CHUNK, :]
        decay_out = jnp.exp2(last - both) * to_end
        from_state = decay_out * dot_nn(b_map, d_state_low)
        d_fed = dot_nn(jnp.concatenate(mixing, axis=1), stack_heads(gy_low, first)) + from_state
        fed_held = fed_low.astype(F32)
        skip = r.skip[0:1, lanes]
        flow = gy * (r.y[rows, lanes] - skip * chan) - fed_held * d_fed
        direct = chan * d_fed
        for k, part in enumerate((flow, direct)):
            spot = slice(k * CHUNK, (k + 1) * CHUNK)
            r.sums[spot, lanes], r.sums[spot, lows] = split_two(part)
        keep = jnp.exp2(last) * carry_on
        through = jnp.sum(fed_held * from_state, axis=0, keepdims=True) + keep * jnp.sum(
            r.states[rows, lanes].astype(F32) * d_state, axis=0, keepdims=True
        )
        spot = slice(2 * CHUNK, 2 * CHUNK + 16)
        r.sums[spot, lanes], r.sums[spot, lows] = split_two(
            jnp.broadcast_to(through, (16, LANES))
        )
        grad_in = (jnp.exp2(both) * carried * gy).astype(BF16)
        r.grad_in[:, lanes] = grad_in
        r.fed_out[:, lanes] = (decay_out * fed).astype(BF16)
        r.d_state_low[:, lanes] = d_state_low
        r.d_state[:, lanes] = keep * d_state + dot_nn(c_turned, grad_in)
        d_chan = skip * gy + step_pair * d_fed
        r.g_skip[:, lanes] += fold_rows(gy * chan)
        d_pre = d_chan * (gate * (1.0 + pre * (1.0 - gate)))
        conv_back(c, r, d_pre, r.d_pre_x, r.xr, r.xr_at, r.cxw, p * LANES, ahead, r.dx_at, r.g_cxw, r.g_cxb)
    d_scores_low = jnp.where(visible, d_scores, 0.0).astype(BF16)
    d_b = dot_nn(d_scores_low, c_map) + dot_nt(r.fed_out[...], r.d_state_low[...])
    d_c = dot_tn(d_scores_low, b_map) + dot_nt(r.grad_in[...], r.states[rows, :])
    for half, d_map in enumerate((d_b, d_c)):
        pre = r.pre_bc[rows, half * LANES : (half + 1) * LANES]
        gate = sigmoid(pre)
        d_pre = d_map * (gate * (1.0 + pre * (1.0 - gate)))
        conv_back(
            c, r, d_pre, r.d_pre_bc, r.bc, r.bc_at, r.cbw, half * LANES, ahead, r.dbc_at, r.g_cbw, r.g_cbb
        )
    reduced = dot_nn(r.sums[...], r.head_sum[...])
    d_total = jnp.dot(
        (row <= col).astype(F32), reduced[:CHUNK], precision=exact, preferred_element_type=F32
    ) + reduced[2 * CHUNK : 2 * CHUNK + 1]
    a_neg = -jnp.exp(r.a_log[...])
    d_step = reduced[CHUNK : 2 * CHUNK] + a_neg * d_total
    r.g_alog[...] += fold_rows(step * d_total) * a_neg
    d_raw = d_step * sigmoid(r.dtr[rows, r.dtr_at : r.dtr_at + LANES] + r.dt_bias[...])
    r.g_dtb[...] += fold_rows(d_raw)
    r.d_proj[rows, r.ddt_at : r.ddt_at + LANES] = d_raw.astype(BF16)


def conv_back(c, r, d_pre, held, raw, raw_at, weight, at, ahead, out_at, g_w, g_b):
    lanes = slice(at, at + LANES)
    rows = chunk_rows(c)
    held[CHUNK : CHUNK + 8, lanes] = held[0:8, lanes]
    held[0:CHUNK, lanes] = d_pre
    window = held[:, lanes]
    values = raw[rows, raw_at + at : raw_at + at + LANES]
    g_b[:, lanes] += fold_rows(d_pre)
    g_w[24:32, lanes] += fold_rows(d_pre * values)
    d_raw = d_pre * weight[3:4, lanes]
    for j in range(1, 4):
        shifted = pltpu.roll(window, CHUNK + 8 - j, 0)[:CHUNK] * ahead[j - 1]
        d_raw = d_raw + shifted * weight[3 - j : 4 - j, lanes]
        g_w[(3 - j) * 8 : (4 - j) * 8, lanes] += fold_rows(shifted * values)
    r.d_proj[rows, out_at + at : out_at + at + LANES] = d_raw.astype(BF16)


def head_sum_matrix(width):
    shape = (2 * width, LANES)
    lane = lax.broadcasted_iota(jnp.int32, shape, 0)
    lane = jnp.where(lane >= width, lane - width, lane)
    return (lane // HEADDIM == lax.broadcasted_iota(jnp.int32, shape, 1)).astype(BF16)


def layout_of(width):
    return types.SimpleNamespace(
        x=width, bc=2 * width, dt=2 * width + 2 * NSTATE, all=2 * width + 2 * NSTATE + LANES
    )


SMALL_IN = ("seg_down", "seg_across", "cxw", "cxb", "cbw", "cbb", "a_log", "dt_bias", "skip")


def small_inputs(segments, cxw, cxb, cbw, cbb, a_log, dt_bias, d_skip):
    tokens = segments.shape[0]
    seg = segments.astype(F32)
    edge = jnp.full((8,), -1.0, F32)
    down = jnp.broadcast_to(jnp.concatenate([edge, seg, edge])[:, None], (tokens + 16, LANES))
    heads = a_log.shape[0]
    pad = lambda v: jnp.pad(v, (0, LANES - heads))[None, :]
    return (
        down,
        seg.reshape(tokens // CHUNK, CHUNK),
        cxw,
        cxb[None, :],
        cbw,
        cbb[None, :],
        pad(a_log),
        pad(dt_bias),
        jnp.repeat(d_skip, HEADDIM)[None, :],
    )


def take_projections(r, width):
    r.pairs = width // LANES
    if hasattr(r, "proj"):
        at = layout_of(width)
        r.xr = r.bc = r.dtr = r.proj
        r.xr_at, r.bc_at, r.dtr_at = at.x, at.bc, at.dt
    else:
        r.xr_at = r.bc_at = r.dtr_at = 0


def forward_kernel(*refs, names, width):
    r = types.SimpleNamespace(**dict(zip(names, refs)))
    take_projections(r, width)
    chunks = r.dtr.shape[0] // CHUNK
    r.state[...] = jnp.zeros_like(r.state)

    def body(c, carry):
        prepare_steps(c, r)
        scan_chunk(c, r)
        return carry

    lax.fori_loop(0, chunks, body, 0)


def backward_kernel(*refs, names, width):
    r = types.SimpleNamespace(**dict(zip(names, refs)))
    take_projections(r, width)
    r.dx_at, r.dbc_at, r.ddt_at = 0, width, width + 2 * NSTATE
    start_back(r)
    chunks = r.dtr.shape[0] // CHUNK

    def body(i, carry):
        scan_chunk_back(chunks - 1 - i, r)
        return carry

    lax.fori_loop(0, chunks, body, 0)


def start_back(r):
    for ref in (r.d_state, r.d_pre_x, r.d_pre_bc, r.g_cxw, r.g_cxb, r.g_cbw, r.g_cbb):
        ref[...] = jnp.zeros_like(ref)
    for ref in (r.g_skip, r.g_alog, r.g_dtb):
        ref[...] = jnp.zeros_like(ref)
    r.head_sum[...] = head_sum_matrix(r.pairs * LANES)


def call_local(kernel, width, ins, outs, scratch, values, flops):
    names = tuple(ins) + tuple(outs) + tuple(scratch)
    whole = pl.BlockSpec(memory_space=pltpu.VMEM)
    return pl.pallas_call(
        functools.partial(kernel, names=names, width=width),
        out_shape=tuple(jax.ShapeDtypeStruct(*spec) for spec in outs.values()),
        in_specs=[whole] * len(ins),
        out_specs=tuple([whole] * len(outs)),
        scratch_shapes=[pltpu.VMEM(*spec) for spec in scratch.values()],
        compiler_params=pltpu.CompilerParams(vmem_limit_bytes=VMEM_LIMIT),
        cost_estimate=pl.CostEstimate(flops=flops, bytes_accessed=1 << 24, transcendentals=0),
    )(*values)


def mixer_forward(projected, small, width):
    tokens = projected.shape[0]
    outs = dict(
        y=((tokens, width), F32),
        pre_x=((tokens, width), F32),
        pre_bc=((tokens, 2 * NSTATE), F32),
        maps=((tokens, 2 * NSTATE), BF16),
        states=((tokens, width), BF16),
        step=((tokens, LANES), F32),
        total=((tokens, LANES), F32),
        total_t=((tokens // CHUNK * 16, LANES), F32),
    )
    scratch = dict(state=((NSTATE, width), F32))
    return call_local(
        forward_kernel, width, ("proj",) + SMALL_IN, outs, scratch, (projected,) + small, 10**10
    )


BACK_SCRATCH = lambda width: dict(
    d_state=((NSTATE, width), F32),
    d_state_low=((NSTATE, width), BF16),
    grad_in=((CHUNK, width), BF16),
    fed_out=((CHUNK, width), BF16),
    sums=((2 * CHUNK + 16, 2 * width), BF16),
    head_sum=((2 * width, LANES), BF16),
    d_pre_x=((CHUNK + 8, width), F32),
    d_pre_bc=((CHUNK + 8, 2 * NSTATE), F32),
)
GRAD_OUT = lambda width: dict(
    g_cxw=((32, width), F32),
    g_cxb=((8, width), F32),
    g_cbw=((32, 2 * NSTATE), F32),
    g_cbb=((8, 2 * NSTATE), F32),
    g_skip=((8, width), F32),
    g_alog=((8, LANES), F32),
    g_dtb=((8, LANES), F32),
)


SAVED = ("y", "pre_x", "pre_bc", "maps", "states", "step", "total", "total_t")


def mixer_backward(projected, small, saved, gy, width):
    tokens = gy.shape[0]
    outs = dict(d_proj=((tokens, width + 2 * NSTATE + LANES), BF16), **GRAD_OUT(width))
    ins = (("proj",) if len(projected) == 1 else ("xr", "bc", "dtr")) + SMALL_IN
    ins = ins + SAVED + ("gy",)
    return call_local(
        backward_kernel,
        width,
        ins,
        outs,
        BACK_SCRATCH(width),
        tuple(projected) + small + tuple(saved) + (gy,),
        3 * 10**10,
    )


UP, DOWN, PAIR = range(3)
LAST_Z = 3
STEP_ROWS = 16
PARTS = 2


def place():
    dp = lax.axis_index("dp")
    tp = lax.axis_index("tensor")
    z = dp // 2
    core = dp - 2 * z
    y = tp // 2
    x = tp - 2 * y
    return types.SimpleNamespace(
        dp=dp,
        tp=tp,
        z=z,
        core=core,
        mate=dp + 1 - 2 * core,
        near_x=y * 2 + (1 - x),
        near_y=(1 - y) * 2 + x,
        across=(1 - y) * 2 + (1 - x),
    )


def device(w, dp=None, tp=None):
    return {"dp": w.dp if dp is None else dp, "tensor": w.tp if tp is None else tp}


def other_z(w, k):
    return lax.rem(w.z + k, LAST_Z + 1) * 2 + w.core


def peers(w):
    rows = [device(w, tp=t) for t in (w.near_x, w.near_y, w.across)]
    return rows + [device(w, dp=w.mate)] + [device(w, dp=other_z(w, k)) for k in (1, 2, 3)]


def tell(sem, where):
    pl.semaphore_signal(sem, inc=1, device_id=where, device_id_type=pl.DeviceIdType.MESH)


def greet(w):
    barrier = pltpu.get_barrier_semaphore()
    for where in peers(w):
        tell(barrier, where)
    pl.semaphore_wait(barrier, len(peers(w)))


def remote(src, dst, send, recv, where):
    return pltpu.make_async_remote_copy(
        src_ref=src,
        dst_ref=dst,
        send_sem=send,
        recv_sem=recv,
        device_id=where,
        device_id_type=pl.DeviceIdType.MESH,
    )


def settle(ref, send, recv, where, sent=True):
    copy = remote(ref, ref, send, recv, where)
    if sent:
        copy.wait_send()
    else:
        copy.wait_recv()


class LineGather:
    def __init__(self, w, ref, send, recv, parts):
        self.w, self.ref, self.send, self.recv, self.parts = w, ref, send, recv, parts
        self.rows = ref.shape[0] // (2 * (LAST_Z + 1))

    def shard(self, z, core, part):
        rows = self.rows // self.parts
        start = pl.multiple_of((z * 2 + core) * self.rows + part * rows, 16)
        return self.ref.at[pl.ds(start, rows)]

    def copy(self, z, kind, part):
        w = self.w
        block = self.shard(z, w.core, part)
        to = {UP: other_z(w, 1), DOWN: other_z(w, LAST_Z)}.get(kind, w.mate)
        first = (self.parts if kind == PAIR else part) * (LAST_Z + 1)
        return remote(block, block, self.send.at[kind], self.recv.at[first + z], device(w, dp=to))

    def relay(self, step):
        for part in range(self.parts):
            self.relay_part(step, part)

    def relay_part(self, step, part):
        w = self.w

        def low():
            z = w.z - step
            if step > 0:
                self.copy(z, UP, part).wait_recv()
            pl.when(w.z < LAST_Z)(lambda: self.copy(z, UP, part).start())
            if step == 0:
                pl.when(w.z > 0)(lambda: self.copy(z, DOWN, part).start())
            self.copy(z, PAIR, part).start()

        def high():
            z = w.z + step
            self.copy(z, DOWN, part).wait_recv()
            pl.when(w.z > 0)(lambda: self.copy(z, DOWN, part).start())
            self.copy(z, PAIR, part).start()

        if step == 0:
            low()
        else:
            pl.when(w.z >= step)(low)
            pl.when(w.z <= LAST_Z - step)(high)

    def some(self, count):
        return self.ref.at[pl.ds(0, count * self.rows)]

    def from_mate(self, z):
        block = self.some(1)
        recv = self.recv.at[self.parts * (LAST_Z + 1) + z]
        settle(block, self.send.at[PAIR], recv, device(self.w, dp=self.w.mate), sent=False)

    def finish(self):
        for z in range(LAST_Z + 1):
            self.from_mate(z)

    def drain(self):
        w = self.w
        where = device(w, dp=w.mate)
        wait = lambda count, kind: settle(
            self.some(count), self.send.at[kind], self.recv.at[0], where
        )
        wait(LAST_Z + 1, PAIR)
        for z in range(LAST_Z):
            pl.when(w.z == z)(lambda z=z: wait(z + 1, UP))
            pl.when(w.z == LAST_Z - z)(lambda z=z: wait(z + 1, DOWN))


class RowGather:
    def __init__(self, w, ref, send, recv):
        self.w, self.ref, self.send, self.recv = w, ref, send, recv
        self.rows = ref.shape[0] // 4

    def copy(self, i):
        w = self.w
        slot, half, to = (
            (w.tp, 0, w.near_x),
            (w.tp, 1, w.near_y),
            (w.tp, 1, w.near_x),
            (w.tp, 0, w.near_y),
            (w.near_x, 0, w.near_y),
            (w.near_y, 1, w.near_x),
        )[i]
        block = row_block(self.ref, self.rows, slot, half)
        return remote(block, block, self.send, self.recv.at[min(i, 2)], device(w, tp=to))

    def start(self):
        for i in range(4):
            self.copy(i).start()

    def hand_on(self):
        for i in range(2):
            self.copy(i).wait_recv()
            self.copy(i + 4).start()

    def some(self, count):
        return self.ref.at[pl.ds(0, count * self.rows)]

    def finish(self):
        where = device(self.w, tp=self.w.near_x)
        settle(self.some(2), self.send, self.recv.at[2], where, sent=False)

    def drain(self):
        settle(self.some(3), self.send, self.recv.at[2], device(self.w, tp=self.w.near_x))


def row_block(ref, rows, slot, half=None):
    start = slot * rows
    if half is not None:
        rows = rows // 2
        start = start + half * rows
    return ref.at[pl.ds(pl.multiple_of(start, 16), rows)]


def add_into(ref, other):
    rows = 64 if ref.shape[0] % 64 == 0 else ref.shape[0]

    def body(i, carry):
        here = pl.ds(pl.multiple_of(i * rows, rows), rows)
        ref[here, :] = (ref[here, :].astype(F32) + other[here, :].astype(F32)).astype(ref.dtype)
        return carry

    lax.fori_loop(0, ref.shape[0] // rows, body, 0)


class RowScatter:
    def __init__(self, w, part, far, near, send, recv):
        self.w, self.part, self.far, self.near, self.send, self.recv = w, part, far, near, send, recv
        self.rows = part.shape[0] // 4

    def block(self, slot, half=None):
        return row_block(self.part, self.rows, slot, half)

    def copy(self, i):
        w = self.w
        half = lambda k, h: row_block(self.near.at[k], self.rows, 0, h)
        src, dst, to = (
            (lambda: self.block(w.across, 0), lambda: self.far.at[0], w.near_x),
            (lambda: self.block(w.across, 1), lambda: self.far.at[1], w.near_y),
            (lambda: self.block(w.near_x, 0), lambda: half(0, 0), w.near_x),
            (lambda: self.block(w.near_y, 1), lambda: half(1, 1), w.near_y),
            (lambda: self.block(w.near_x, 1), lambda: half(0, 1), w.near_x),
            (lambda: self.block(w.near_y, 0), lambda: half(1, 0), w.near_y),
        )[i]
        return remote(src(), dst(), self.send, self.recv.at[min(i, 2)], device(w, tp=to))

    def start(self, *which):
        for i in which:
            self.copy(i).start()

    def hand_on(self):
        w = self.w
        self.copy(1).wait_recv()
        add_into(self.block(w.near_x, 1), self.far.at[1])
        self.copy(4).start()
        self.copy(0).wait_recv()
        add_into(self.block(w.near_y, 0), self.far.at[0])
        self.copy(5).start()

    def some(self, count):
        return self.part.at[pl.ds(0, count * self.rows)]

    def finish(self):
        where = device(self.w, tp=self.w.near_x)
        settle(self.some(2), self.send, self.recv.at[2], where, sent=False)

    def total(self, here, there):
        total = self.part[there, :].astype(F32)
        return total + self.near[0, here, :].astype(F32) + self.near[1, here, :].astype(F32)

    def drain(self):
        settle(self.some(3), self.send, self.recv.at[2], device(self.w, tp=self.w.near_x))


class LineScatter:
    def __init__(self, w, shard, pair, up, down, pair_sem, line_sem, parts, hold=False):
        self.w, self.shard, self.pair, self.up, self.down = w, shard, pair, up, down
        self.hold = hold
        self.pair_sem, self.line_sem, self.parts = pair_sem, line_sem, parts
        self.rows = pair.shape[0] // (LAST_Z + 1)

    def slot(self, ref, i):
        return ref.at[pl.ds(pl.multiple_of(i * self.rows, 16), self.rows)]

    def piece(self, ref, part):
        rows = self.rows // self.parts
        return ref.at[pl.ds(part * rows, rows)]

    def pair_copy(self, z):
        w = self.w
        return remote(
            self.shard(z, 1 - w.core),
            self.slot(self.pair, z),
            self.pair_sem.at[LAST_Z + 1],
            self.pair_sem.at[z],
            device(w, dp=w.mate),
        )

    def up_copy(self, z, part):
        return remote(
            self.piece(self.shard(z, self.w.core), part),
            self.piece(self.slot(self.up, z - 1), part),
            self.line_sem.at[0],
            self.line_sem.at[2 + part * LAST_Z + z - 1],
            device(self.w, dp=other_z(self.w, 1)),
        )

    def down_copy(self, z, part):
        return remote(
            self.piece(self.shard(z, self.w.core), part),
            self.piece(self.slot(self.down, z), part),
            self.line_sem.at[1],
            self.line_sem.at[2 + (self.parts + part) * LAST_Z + z],
            device(self.w, dp=other_z(self.w, LAST_Z)),
        )

    def launch(self, z):
        w = self.w
        self.pair_copy(z).wait_recv()

        def every(send):
            for part in range(self.parts):
                add_into(self.piece(self.shard(z, w.core), part), self.piece(self.slot(self.pair, z), part))
                if send is not None:
                    send(z, part).start()

        held = 1 if self.hold else 0
        low = (w.z == 0) & (z > held)
        high = (w.z == LAST_Z) & (z < LAST_Z - held)
        pl.when(low)(lambda: every(self.up_copy))
        pl.when(high)(lambda: every(self.down_copy))
        pl.when(jnp.logical_not(low | high))(lambda: every(None))

    def launch_last(self):
        for part in range(self.parts):
            pl.when(self.w.z == 0)(lambda part=part: self.up_copy(1, part).start())
            pl.when(self.w.z == LAST_Z)(lambda part=part: self.down_copy(LAST_Z - 1, part).start())

    def pass_up(self, z, part):
        self.up_copy(z, part).wait_recv()
        add_into(
            self.piece(self.shard(z, self.w.core), part),
            self.piece(self.slot(self.up, z - 1), part),
        )
        self.up_copy(z, part).start()

    def pass_down(self, z, part):
        self.down_copy(z, part).wait_recv()
        add_into(
            self.piece(self.shard(z, self.w.core), part),
            self.piece(self.slot(self.down, z), part),
        )
        self.down_copy(z, part).start()

    def step(self, k, part=None):
        w = self.w
        if part is None:
            for part in range(self.parts):
                self.step(k, part)
        elif k == 0:
            pl.when(w.z == 1)(lambda: self.pass_up(3, part))
            pl.when(w.z == 2)(lambda: self.pass_down(0, part))
        else:

            @pl.when(w.z == 1)
            def _():
                self.pass_up(2, part)
                self.pass_down(0, part)

            @pl.when(w.z == 2)
            def _():
                self.pass_down(1, part)
                self.pass_up(3, part)

    def finish(self, out):
        w = self.w
        own = self.shard(w.z, w.core)
        rows = self.rows // self.parts

        def add(part, copy, slot):
            here = pl.ds(part * rows, rows)
            copy(w.z, part).wait_recv()
            out[here, :] += self.piece(slot, part)[...].astype(F32)

        out[...] = own[...].astype(F32)
        for part in range(self.parts):
            pl.when(w.z > 0)(
                lambda part=part: add(part, self.up_copy, self.slot(self.up, w.z - 1))
            )
            pl.when(w.z < LAST_Z)(
                lambda part=part: add(part, self.down_copy, self.slot(self.down, w.z))
            )

    def drain_pair(self):
        where = device(self.w, dp=self.w.mate)
        settle(self.pair, self.pair_sem.at[LAST_Z + 1], self.pair_sem.at[0], where)

    def drain(self):
        w = self.w
        where = device(w, dp=w.mate)
        for z in range(LAST_Z):
            sent = self.up.at[pl.ds(0, (LAST_Z - z) * self.rows)]
            pl.when(w.z == z)(
                lambda sent=sent: settle(sent, self.line_sem.at[0], self.line_sem.at[2], where)
            )
            pl.when(w.z == LAST_Z - z)(
                lambda sent=sent: settle(sent, self.line_sem.at[1], self.line_sem.at[2], where)
            )


class Exchange:
    def __init__(self, ref, mine, targets, sems):
        self.ref, self.mine, self.targets, self.sems = ref, mine, targets, sems

    def start(self):
        part = self.ref.at[self.mine]
        for target in self.targets:
            remote(part, part, self.sems.at[0], self.sems.at[1], target).start()

    def finish(self):
        count = len(self.targets)
        some = self.ref.at[pl.ds(0, count)]
        for sent in (False, True):
            settle(some, self.sems.at[0], self.sems.at[1], self.targets[0], sent=sent)

    def total(self):
        total = self.ref[0].astype(F32)
        for i in range(1, self.ref.shape[0]):
            total = total + self.ref[i].astype(F32)
        return total


def norm_rows(x_ref, gain, out_ref, start):
    rows = 64

    def body(i, carry):
        here = pl.ds(pl.multiple_of(i * rows, rows), rows)
        values = x_ref[here, :].astype(F32)
        scale = lax.rsqrt(jnp.mean(values * values, axis=1, keepdims=True) + EPS)
        there = pl.ds(pl.multiple_of(start + i * rows, 16), rows)
        out_ref[there, :] = (values * scale * gain).astype(BF16)
        return carry

    lax.fori_loop(0, x_ref.shape[0] // rows, body, 0)


def by_rows(total, rows, body):
    def step(i, carry):
        body(pl.ds(pl.multiple_of(i * rows, rows), rows))
        return carry

    lax.fori_loop(0, total // rows, step, 0)


def over_chunks(r, body):
    def step(c, carry):
        body(c)
        return carry

    lax.fori_loop(0, r.chunks, step, 0)


def turned(row):
    return jnp.broadcast_to(row, (CHUNK, LANES)).T


def gated_tile(c, r, p):
    rows, lanes = chunk_rows(c), slice(p * LANES, (p + 1) * LANES)
    z = r.z[rows, lanes]
    gate = sigmoid(z)
    return z, gate, r.y[rows, lanes]


def square_chunk(c, r):
    square = jnp.zeros((CHUNK, LANES), F32)
    for p in range(r.pairs):
        z, gate, y = gated_tile(c, r, p)
        gated = y * (z * gate)
        square = square + gated * gated
    r.squares.at[r.w.tp][pl.ds(c, 1), :] = jnp.sum(square.T, axis=0, keepdims=True)


def cross_chunk(c, r):
    rows = chunk_rows(c)
    cross = jnp.zeros((CHUNK, LANES), F32)
    for p in range(r.pairs):
        lanes = slice(p * LANES, (p + 1) * LANES)
        z, gate, y = gated_tile(c, r, p)
        cross = cross + r.d_mixed[rows, lanes] * r.gain[0:1, lanes] * (y * (z * gate))
    r.crosses.at[r.w.tp][pl.ds(c, 1), :] = jnp.sum(cross.T, axis=0, keepdims=True)


def slot_sum(ref, c):
    total = ref[0, pl.ds(c, 1), :]
    for i in range(1, 4):
        total = total + ref[i, pl.ds(c, 1), :]
    return total


def scale_two_row(c, r):
    return lax.rsqrt(slot_sum(r.squares, c) / (r.pairs * LANES * 4) + EPS)


def mix_chunk(c, r):
    rows = chunk_rows(c)
    scale = turned(scale_two_row(c, r))
    for p in range(r.pairs):
        lanes = slice(p * LANES, (p + 1) * LANES)
        z, gate, y = gated_tile(c, r, p)
        r.mixed[rows, lanes] = (y * (z * gate) * scale * r.gain[0:1, lanes]).astype(BF16)


def gate_back_chunk(c, r):
    rows = chunk_rows(c)
    row = scale_two_row(c, r)
    pull = turned(row * row * row * slot_sum(r.crosses, c) / (r.pairs * LANES * 4))
    scale = turned(row)
    for p in range(r.pairs):
        lanes = slice(p * LANES, (p + 1) * LANES)
        z, gate, y = gated_tile(c, r, p)
        silu = z * gate
        gated = y * silu
        scaled = r.d_mixed[rows, lanes] * scale
        r.g_gate[:, lanes] += fold_rows(scaled * gated)
        d_gated = scaled * r.gain[0:1, lanes] - gated * pull
        r.gy[rows, lanes] = (d_gated * silu).astype(BF16)
        r.d_z[rows, lanes] = (d_gated * y * (gate * (1.0 + z * (1.0 - gate)))).astype(BF16)


def by_distance(z, i):
    upper = z // 2
    low = z + upper * (LAST_Z - 2 * z)
    chip = low + i * (1 - 2 * low) if i < 2 else i
    return chip + upper * (LAST_Z - 2 * chip)


def chip_rows(r, z):
    count = 2 * r.shard_rows
    return pl.ds(pl.multiple_of(z * count, LANES), count)


def accumulate(ref, rows, value, first):
    if first:
        ref[rows, :] = value
    else:
        ref[rows, :] += value


def project_z(r, i):
    z = by_distance(r.w.z, i)
    r.shard_z.from_mate(z)
    here = chip_rows(r, z)

    def body(rows):
        accumulate(r.z, rows, dot_nn(r.row_normed[rows, here], r.full_z[here, :]), i == 0)

    by_rows(r.row_normed.shape[0], 256, body)


def output_back(r, i):
    z = by_distance(r.w.z, i)
    r.shard_out.from_mate(z)
    here = chip_rows(r, z)

    def body(rows):
        accumulate(r.d_mixed, rows, dot_nn(r.row_cot[rows, here], r.full_out[here, :]), i == 0)

    by_rows(r.row_normed.shape[0], 256, body)


def output_share(r, slot):
    block = r.x_held.shape[0]
    rows = pl.ds(pl.multiple_of(slot * block, block), block)
    tile = 512

    def body(n, carry):
        cols = pl.ds(pl.multiple_of(n * tile, tile), tile)
        r.part[rows, cols] = dot_nt(r.mixed[rows, :], r.full_out[cols, :]).astype(BF16)
        return carry

    lax.fori_loop(0, r.part.shape[1] // tile, body, 0)


def far_first(w, i):
    upper = w.z // 2
    return (1 - upper) * (LAST_Z - i) + upper * i


def weight_parts(make, scatter):
    def body(i, carry):
        z = far_first(scatter.w, i)
        make(z)
        scatter.pair_copy(z).start()
        pl.when(i > 0)(lambda: scatter.launch(far_first(scatter.w, i - 1)))
        return carry

    lax.fori_loop(0, LAST_Z + 1, body, 0)
    scatter.launch(far_first(scatter.w, LAST_Z))
    scatter.drain_pair()


def product_maker(left, right, store):
    block = left.shape[1] // (LAST_Z + 1)

    def make(z):
        lanes = pl.ds(pl.multiple_of(z * block, LANES), block)
        store(z, dot_tn(left[:, lanes], right[...]).astype(BF16))

    return make


def flat_shard(ref, rows):
    return lambda z, core: ref.at[pl.ds(pl.multiple_of((z * 2 + core) * rows, 16), rows)]


def flat_store(ref, rows):
    def store(z, value):
        ref[pl.ds(pl.multiple_of(z * 2 * rows, 16), 2 * rows), :] = value

    return store


def side_shard(ref, rows, width):
    return lambda z, core: ref.at[
        pl.ds(pl.multiple_of(z * rows, 16), rows),
        pl.ds(pl.multiple_of(core * width, LANES), width),
    ]


def side_store(ref, rows, width):
    def store(z, value):
        here = pl.ds(pl.multiple_of(z * rows, 16), rows)
        ref[here, :width] = value[:rows]
        ref[here, width : 2 * width] = value[rows:]

    return store


def own_rows(r):
    shard = r.w_x.shape[0]
    return pl.ds(pl.multiple_of(r.w.dp * shard, 16), shard)


def input_moves(r):
    width = r.pairs * LANES
    own = own_rows(r)
    block = r.cot.shape[0]
    mine = pl.ds(pl.multiple_of(r.w.tp * block, block), block)
    moves = (
        (r.w_x, r.full_x.at[own, pl.ds(0, width)]),
        (r.w_bc, r.full_x.at[own, pl.ds(width, 2 * NSTATE)]),
        (r.x_in, r.x_held),
        (r.w_z, r.full_z.at[own]),
        (r.w_out, r.full_out.at[own]),
        (r.cot, r.row_cot.at[mine]),
    )
    return [pltpu.make_async_copy(src, dst, r.s_m.at[i]) for i, (src, dst) in enumerate(moves)]


def place_steps(r):
    heads, shard = r.w_dt.shape
    mine = r.steps_t.at[pl.ds(pl.multiple_of(r.w.dp * STEP_ROWS, STEP_ROWS), STEP_ROWS)]
    r.turn[...] = jnp.zeros_like(r.turn)
    r.turn[0:heads, 0:shard] = r.w_dt[...]
    mine[...] = r.turn[0:STEP_ROWS, :]


def turn_steps(r):
    shard = r.w_x.shape[0]

    def body(d, carry):
        r.turn[0:STEP_ROWS, :] = r.steps_t[
            pl.ds(pl.multiple_of(d * STEP_ROWS, STEP_ROWS), STEP_ROWS), :
        ]
        r.full_dt[pl.ds(pl.multiple_of(d * shard, 16), shard), :] = r.turn[...].T[:shard]
        return carry

    lax.fori_loop(0, 2 * (LAST_Z + 1), body, 0)


def prepare_small(r):
    heads = r.a_log_in.shape[0]
    w, width = r.w, r.pairs * LANES
    for ref in (r.a_log, r.dt_bias):
        ref[...] = jnp.zeros_like(ref)
    r.a_log[0:1, 0:heads] = r.a_log_in[...].reshape(1, heads)
    r.dt_bias[0:1, 0:heads] = r.dt_bias_in[...].reshape(1, heads)
    r.cxb[...] = r.cxb_in[...].reshape(1, width)
    r.cbb[...] = r.cbb_in[...].reshape(1, 2 * NSTATE)
    r.gain[...] = r.gain_in[...].reshape(1, width)
    skip = r.d_skip_in[...].reshape(1, heads)
    first = lax.broadcasted_iota(jnp.int32, (1, LANES), 1) < HEADDIM
    for p in range(r.pairs):
        pair = jnp.where(first, skip[:, 2 * p : 2 * p + 1], skip[:, 2 * p + 1 : 2 * p + 2])
        r.skip[:, p * LANES : (p + 1) * LANES] = pair
    r.seg_across[...] = r.segments[...].reshape(r.chunks, CHUNK).astype(F32)
    edge = jnp.full((8, LANES), -1.0, F32)
    r.seg_down[0:8, :] = edge
    r.seg_down[r.chunks * CHUNK + 8 :, :] = edge

    def body(c):
        r.seg_down[chunk_rows(c, 8), :] = turned(r.seg_across[pl.ds(c, 1), :])

    over_chunks(r, body)


def phase_one(r):
    w = r.w
    width = r.pairs * LANES
    tokens = r.row_normed.shape[0]
    block = r.x_held.shape[0]
    start = pl.multiple_of(w.tp * block, block)
    moves = input_moves(r)
    for move in moves:
        move.start()
    place_steps(r)
    greet(w)
    moves[0].wait()
    moves[1].wait()
    r.shard_x.relay(0)
    r.shard_dt.relay(0)
    moves[2].wait()
    norm_rows(r.x_held, r.pre_gain[...].reshape(1, r.x_held.shape[1]), r.row_normed, start)
    r.row_n.start()
    r.state[...] = jnp.zeros_like(r.state)
    prepare_small(r)
    for move in moves[3:]:
        move.wait()
    r.shard_x.relay(1)
    r.shard_dt.relay(1)
    r.shard_x.relay(2)
    r.shard_dt.relay(2)
    r.row_n.hand_on()
    r.row_c.start()
    r.shard_x.relay(3)
    r.shard_dt.relay(3)
    r.shard_z.relay(0)
    r.shard_dt.finish()
    turn_steps(r)
    r.row_n.finish()
    r.shard_x.finish()

    def project_x(rows):
        normed = r.row_normed[rows, :]
        out = dot_nn(normed, r.full_x[...])
        r.xr[rows, :] = out[:, :width]
        r.bc[rows, :] = out[:, width:]
        r.dtr[rows, :] = dot_nn(normed, r.full_dt[...])

    by_rows(tokens, 256, project_x)

    def body(c):
        prepare_steps(c, r)
        scan_chunk(c, r)

        @pl.when(c == 1)
        def _():
            r.shard_z.relay(1)
            project_z(r, 0)

        @pl.when(c == 3)
        def _():
            r.row_c.hand_on()
            project_z(r, 1)

        @pl.when(c == 5)
        def _():
            r.shard_z.relay(2)
            r.shard_out.relay(0)
            project_z(r, 2)

    over_chunks(r, body)


def phase_mid(r):
    w = r.w
    r.shard_z.relay(3)
    project_z(r, 3)
    over_chunks(r, lambda c: square_chunk(c, r))
    r.ex_squares.start()
    r.shard_out.relay(1)
    r.row_c.finish()
    r.ex_squares.finish()
    over_chunks(r, lambda c: mix_chunk(c, r))
    weight_parts(
        product_maker(r.row_cot, r.mixed, flat_store(r.out_part, r.shard_rows)), r.grad_out
    )
    tell(r.free_pair, device(w, dp=w.mate))
    output_back(r, 0)
    r.shard_out.relay(2)
    output_back(r, 1)
    r.shard_out.relay(3)
    output_back(r, 2)
    output_back(r, 3)
    over_chunks(r, lambda c: cross_chunk(c, r))
    r.ex_crosses.start()
    r.grad_out.step(0)
    output_share(r, w.across)
    r.out_rows.start(0, 1)
    r.g_gate[...] = jnp.zeros_like(r.g_gate)
    r.ex_crosses.finish()
    over_chunks(r, lambda c: gate_back_chunk(c, r))
    for item in (r.shard_x, r.shard_dt, r.shard_z, r.shard_out, r.row_n, r.row_c):
        item.drain()
    pl.semaphore_wait(r.free_pair, 1)
    weight_parts(
        product_maker(
            r.row_normed, r.d_z, side_store(r.row_cot, r.shard_rows, r.pairs * LANES)
        ),
        r.grad_z,
    )
    tell(r.free_pair, device(w, dp=w.mate))
    r.grad_out.step(1)
    for slot, copy in ((w.near_x, 2), (w.near_y, 3)):
        output_share(r, slot)
        r.out_rows.start(copy)
    output_share(r, w.tp)
    r.out_rows.hand_on()
    tell(r.free_far, device(w, tp=w.near_x))
    tell(r.free_far, device(w, tp=w.near_y))


def phase_back(r):
    w = r.w
    block = r.x_held.shape[0]
    start_back(r)

    def body(i, carry):
        scan_chunk_back(r.chunks - 1 - i, r)

        @pl.when(i == 0)
        def _():
            r.grad_out.finish(r.v_w_out)
            r.put(r.v_w_out, r.o_w_out, 0).start()
            r.grad_out.drain()
            tell(r.free_line, device(w, dp=other_z(w, 1)))
            tell(r.free_line, device(w, dp=other_z(w, 3)))

        for at, k, part in ((1, 0, 0), (2, 0, 1), (4, 1, 0), (5, 1, 1)):
            pl.when(i == at)(lambda k=k, part=part: r.grad_z.step(k, part))

        return carry

    lax.fori_loop(0, r.chunks, body, 0)


def finish_block(r):
    w = r.w
    block = r.x_held.shape[0]
    step = 64
    r.out_rows.finish()

    def add(k, carry):
        here = pl.ds(pl.multiple_of(k * step, step), step)
        there = pl.ds(pl.multiple_of(w.tp * block + k * step, 16), step)
        total = r.x_held[here, :].astype(F32) + r.out_rows.total(here, there)
        r.v_block[here, :] = total.astype(BF16)
        return carry

    lax.fori_loop(0, block // step, add, 0)
    r.put(r.v_block, r.o_block, 1).start()
    tell(r.free_row, device(w, tp=w.near_x))
    tell(r.free_row, device(w, tp=w.near_y))


def step_parts(r, at):
    shard = r.shard_rows
    out = dot_tn(r.d_rest[:, at : at + LANES], r.row_normed[...])[:STEP_ROWS]
    for d in range(2 * (LAST_Z + 1)):
        here = slice(d * STEP_ROWS, (d + 1) * STEP_ROWS)
        r.dt_part[here, 0:shard] = out[:, d * shard : (d + 1) * shard]


def phase_last(r):
    w = r.w
    width = r.pairs * LANES
    block = r.x_held.shape[0]
    edge = width + 2 * NSTATE
    r.out_rows.drain()
    r.g_pre[...] = jnp.zeros_like(r.g_pre)

    def share(slot):
        rows = pl.ds(pl.multiple_of(slot * block, block), block)
        tile = 512

        def body(n, carry):
            cols = pl.ds(pl.multiple_of(n * tile, tile), tile)
            out = dot_nt(r.d_z[rows, :], r.full_z[cols, :])
            out = out + dot_nt(r.d_rest[rows, :edge], r.full_x[cols, :])
            out = out + dot_nt(r.d_rest[rows, edge:], r.full_dt[cols, :])
            r.part[rows, cols] = out.astype(BF16)
            r.g_pre[:, cols] += fold_rows(out * r.row_normed[rows, cols].astype(F32))
            return carry

        lax.fori_loop(0, r.part.shape[1] // tile, body, 0)

    share(w.across)
    pl.semaphore_wait(r.free_far, 2)
    r.in_rows.start(0, 1)
    weight_parts(
        product_maker(
            r.row_normed,
            r.d_rest.at[:, pl.ds(width, 2 * NSTATE)],
            flat_store(r.bc_part, r.shard_rows),
        ),
        r.grad_bc,
    )
    step_parts(r, edge)
    for z in range(LAST_Z + 1):
        r.grad_dt.pair_copy(z).start()
    finish_block(r)
    share(w.near_x)
    pl.semaphore_wait(r.free_row, 2)
    r.in_rows.start(2)
    r.grad_bc.step(0)
    for i in range(LAST_Z + 1):
        r.grad_dt.launch(far_first(w, i))
    r.grad_dt.drain_pair()
    share(w.near_y)
    r.in_rows.start(3)
    pl.semaphore_wait(r.free_pair, 1)
    pl.semaphore_wait(r.free_line, 2)
    weight_parts(
        product_maker(
            r.row_normed,
            r.d_rest.at[:, pl.ds(0, width)],
            flat_store(r.full_out, r.shard_rows),
        ),
        r.grad_x_part,
    )
    r.grad_bc.step(1)
    r.grad_dt.step(0)
    share(w.tp)
    r.in_rows.hand_on()
    again = [
        pltpu.make_async_copy(r.cot.at[pl.ds(k * (block // 2), block // 2)], r.far.at[k], r.s_m.at[k])
        for k in range(2)
    ]
    for copy in again:
        copy.start()
    r.grad_dt.step(1)
    pack_small(r)
    r.ex_pair.start()
    r.grad_x_part.step(0, 0)
    r.grad_bc.finish(r.bc_sum)
    r.bc_slots.at[w.tp][...] = r.bc_sum[...].astype(BF16)
    r.ex_bc.start()
    r.ex_pair.finish()
    r.small_z.at[w.z][...] = r.ex_pair.total()
    r.ex_z.start()
    r.grad_x_part.launch_last()
    r.grad_x_part.step(0, 1)
    r.grad_dt.finish(r.v_w_dt)
    r.put(r.v_w_dt, r.o_w_dt, 3).start()
    r.grad_z.finish(r.v_w_z)
    r.put(r.v_w_z, r.o_w_z, 2).start()
    r.grad_x_part.step(1, 0)
    r.grad_x_part.step(1, 1)
    r.ex_z.finish()
    total = r.ex_z.total()
    r.small_t.at[w.tp][...] = total[SMALL_DP:]
    r.ex_t.start()
    r.v_small[...] = total[:SMALL_DP]
    r.put(r.v_small, r.o_small, 4).start()
    for item in (r.grad_z, r.grad_bc, r.grad_dt):
        item.drain()
    gain = r.pre_gain[...].reshape(1, r.x_held.shape[1])
    for copy in again:
        copy.wait()
    r.in_rows.finish()
    step = 64

    def body(k, carry):
        here = pl.ds(pl.multiple_of(k * step, step), step)
        there = pl.ds(pl.multiple_of(w.tp * block + k * step, 16), step)
        half = k // (block // 2 // step)
        inner = pl.ds(pl.multiple_of(k * step - half * (block // 2), step), step)
        values = r.x_held[here, :].astype(F32)
        scale = lax.rsqrt(jnp.mean(values * values, axis=1, keepdims=True) + EPS)
        weighted = r.in_rows.total(here, there) * gain
        along = jnp.mean(weighted * values, axis=1, keepdims=True)
        grad = r.far[half, inner, :].astype(F32) + scale * weighted
        r.v_grad_x[here, :] = (grad - values * (scale * scale * scale * along)).astype(BF16)
        return carry

    lax.fori_loop(0, block // step, body, 0)
    r.put(r.v_grad_x, r.o_grad_x, 7).start()
    r.in_rows.drain()
    r.ex_bc.finish()
    r.v_w_bc[...] = r.ex_bc.total()
    r.put(r.v_w_bc, r.o_w_bc, 5).start()
    r.grad_x_part.finish(r.v_w_x)
    r.put(r.v_w_x, r.o_w_x, 8).start()
    r.grad_x_part.drain()
    r.ex_t.finish()
    shared = r.ex_t.total()
    count = gain.shape[1] // LANES
    r.v_shared[...] = shared
    for p in range(count):
        r.v_shared[p : p + 1, :] = shared[p : p + 1, :] / gain[:, p * LANES : (p + 1) * LANES]
    r.put(r.v_shared, r.o_shared, 6).start()
    ends = ("w_out", "block", "w_z", "w_dt", "small", "w_bc", "shared", "grad_x", "w_x")
    for i, name in enumerate(ends):
        r.put(getattr(r, "v_" + name), getattr(r, "o_" + name), i).wait()


SMALL_DP = 40
SMALL_ALL = 24


def head_row(r):
    lane = lax.broadcasted_iota(jnp.int32, (1, LANES), 1)
    out = jnp.zeros((1, LANES), F32)
    for p in range(r.pairs):
        tile = jnp.sum(r.g_skip[:, p * LANES : (p + 1) * LANES], axis=0, keepdims=True)
        for k, part in enumerate((lane < HEADDIM, lane >= HEADDIM)):
            head = jnp.sum(jnp.where(part, tile, 0.0), axis=1, keepdims=True)
            out = jnp.where(lane == 2 * p + k, head, out)
    return out


def pack_small(r):
    mine = r.small_pair.at[r.w.core]
    mine[...] = jnp.zeros_like(mine)

    def put(at, ref, first, count):
        for p in range(count):
            lanes = slice(p * LANES, (p + 1) * LANES)
            mine[at + p : at + p + 1, :] = jnp.sum(
                ref[first : first + 8, lanes], axis=0, keepdims=True
            )
        return at + count

    at = put(0, r.g_gate, 0, r.pairs)
    for k in range(4):
        at = put(at, r.g_cxw, 8 * k, r.pairs)
    at = put(at, r.g_cxb, 0, r.pairs)
    mine[at : at + 1, :] = head_row(r)
    at = at + 1
    at = put(at, r.g_alog, 0, 1)
    at = put(at, r.g_dtb, 0, 1)
    at = put(SMALL_DP, r.g_pre, 0, r.g_pre.shape[1] // LANES)
    for k in range(4):
        at = put(at, r.g_cbw, 8 * k, 2)
    put(at, r.g_cbb, 0, 2)


RAW_IN = (
    "x_in",
    "segments",
    "pre_gain",
    "w_z",
    "w_x",
    "w_bc",
    "w_dt",
    "cxw",
    "cxb_in",
    "cbw",
    "cbb_in",
    "a_log_in",
    "dt_bias_in",
    "d_skip_in",
    "gain_in",
    "w_out",
    "cot",
)


def whole_kernel(*refs, names, width):
    r = types.SimpleNamespace(**dict(zip(names, refs)))
    r.w = w = place()
    r.pairs = width // LANES
    r.chunks = r.row_normed.shape[0] // CHUNK
    r.shard_rows = r.w_x.shape[0]
    r.xr_at = r.bc_at = r.dtr_at = 0
    r.dx_at, r.dbc_at, r.ddt_at = 0, width, width + 2 * NSTATE
    gather = lambda i, ref: LineGather(w, ref, r.s_w.at[i], r.r_w.at[i], PARTS)
    r.shard_x = gather(0, r.full_x)
    r.shard_z = gather(1, r.full_z)
    r.shard_out = gather(2, r.full_out)
    r.shard_dt = LineGather(w, r.steps_t, r.s_d, r.r_d, 1)
    r.row_n = RowGather(w, r.row_normed, r.s_r.at[0], r.r_r.at[0])
    r.row_c = RowGather(w, r.row_cot, r.s_r.at[1], r.r_r.at[1])
    r.out_rows = r.in_rows = RowScatter(w, r.part, r.far, r.near, r.s_q.at[0], r.r_q)
    rows = r.shard_rows
    held = (r.pair, r.up, r.down, r.p_main, r.l_main, PARTS)
    r.grad_out = LineScatter(w, flat_shard(r.out_part, rows), *held)
    r.grad_x_part = LineScatter(w, flat_shard(r.full_out, rows), *held, hold=True)
    side = side_shard(r.row_cot, rows, width)
    r.grad_z = LineScatter(w, side, r.pair, r.up_z, r.down_z, r.p_main, r.l_z, PARTS)
    held_dt = (r.pair_dt, r.up_dt, r.down_dt, r.p_dt, r.l_dt, 1)
    r.grad_dt = LineScatter(w, flat_shard(r.dt_part, STEP_ROWS), *held_dt)
    in_row = [device(w, tp=t) for t in (w.near_x, w.near_y, w.across)]
    in_line = [device(w, dp=other_z(w, k)) for k in (1, 2, 3)]
    exchange = lambda i, ref, mine, targets: Exchange(ref, mine, targets, r.s_e.at[i])
    r.ex_squares = exchange(0, r.squares, w.tp, in_row)
    r.ex_crosses = exchange(1, r.crosses, w.tp, in_row)
    r.ex_pair = exchange(2, r.small_pair, w.core, [device(w, dp=w.mate)])
    r.ex_z = exchange(3, r.small_z, w.z, in_line)
    r.ex_t = exchange(4, r.small_t, w.tp, in_row)
    r.ex_bc = exchange(5, r.bc_slots, w.tp, in_row)
    r.put = lambda src, dst, i: pltpu.make_async_copy(src, dst, r.s_o.at[i])
    tokens = r.chunks * CHUNK

    def middle(z, d_mixed, mixed):
        r.z, r.d_mixed, r.mixed = z, d_mixed, mixed
        phase_one(r)
        phase_mid(r)

    pl.run_scoped(
        middle,
        pltpu.VMEM((tokens, width), F32),
        pltpu.VMEM((tokens, width), F32),
        pltpu.VMEM((tokens, width), BF16),
    )
    later = dict(BACK_SCRATCH(width), bc_part=((r.full_x.shape[0], 2 * NSTATE), BF16))

    def rest(d_rest, *buffers):
        r.d_rest = r.d_proj = d_rest
        for name, buffer in zip(later, buffers):
            setattr(r, name, buffer)
        held_bc = (r.pair_bc, r.up_bc, r.down_bc, r.p_bc, r.l_bc, 1)
        r.grad_bc = LineScatter(w, flat_shard(r.bc_part, rows), *held_bc)
        phase_back(r)
        phase_last(r)

    pl.run_scoped(
        rest,
        pltpu.VMEM((tokens, width + 2 * NSTATE + LANES), BF16),
        *[pltpu.VMEM(*spec) for spec in later.values()],
    )


def whole_call(args, width):
    x_in, w_x = args[0], args[4]
    features, block = x_in.shape[1], x_in.shape[0]
    tokens = block * 4
    shard = w_x.shape[0]
    maps = 2 * NSTATE
    chunks = tokens // CHUNK
    turned_step = (STEP_ROWS, 2 * LANES)
    outs = dict(
        block=((block, features), BF16),
        grad_x=((block, features), BF16),
        w_z=((shard, width), F32),
        w_x=((shard, width), F32),
        w_bc=((shard, maps), F32),
        w_dt=(turned_step, F32),
        w_out=((shard, width), F32),
        small=((SMALL_DP, LANES), F32),
        shared=((SMALL_ALL, LANES), F32),
    )
    scratch = dict(
        x_held=((block, features), BF16),
        row_normed=((tokens, features), BF16),
        row_cot=((tokens, features), BF16),
        full_x=((features, width + maps), BF16),
        full_z=((features, width), BF16),
        full_out=((features, width), BF16),
        full_dt=((features, LANES), BF16),
        steps_t=((8 * STEP_ROWS, 2 * LANES), BF16),
        xr=((tokens, width), F32),
        bc=((tokens, maps), F32),
        dtr=((tokens, LANES), F32),
        y=((tokens, width), F32),
        pre_x=((tokens, width), F32),
        pre_bc=((tokens, maps), F32),
        maps=((tokens, maps), BF16),
        states=((tokens, width), BF16),
        state=((NSTATE, width), F32),
        step=((tokens, LANES), F32),
        total=((tokens, LANES), F32),
        total_t=((chunks * 16, LANES), F32),
        seg_down=((tokens + 16, LANES), F32),
        seg_across=((chunks, LANES), F32),
        turn=((LANES, 2 * LANES), BF16),
        a_log=((1, LANES), F32),
        dt_bias=((1, LANES), F32),
        cxb=((1, width), F32),
        cbb=((1, maps), F32),
        gain=((1, width), F32),
        skip=((1, width), F32),
        squares=((4, chunks, LANES), F32),
        crosses=((4, chunks, LANES), F32),
        gy=((tokens, width), BF16),
        d_z=((tokens, width), BF16),
        part=((tokens, features), BF16),
        far=((2, block // 2, features), BF16),
        near=((2, block, features), BF16),
        out_part=((features, width), BF16),
        dt_part=((8 * STEP_ROWS, 2 * LANES), F32),
        pair=((4 * shard, width), BF16),
        pair_bc=((4 * shard, maps), BF16),
        pair_dt=((4 * STEP_ROWS, 2 * LANES), F32),
        up=((3 * shard, width), BF16),
        down=((3 * shard, width), BF16),
        up_z=((3 * shard, width), BF16),
        down_z=((3 * shard, width), BF16),
        up_bc=((3 * shard, maps), BF16),
        down_bc=((3 * shard, maps), BF16),
        up_dt=((3 * STEP_ROWS, 2 * LANES), F32),
        down_dt=((3 * STEP_ROWS, 2 * LANES), F32),
        bc_sum=((shard, maps), F32),
        bc_slots=((4, shard, maps), BF16),
        small_pair=((2, SMALL_DP + SMALL_ALL, LANES), F32),
        small_z=((4, SMALL_DP + SMALL_ALL, LANES), F32),
        small_t=((4, SMALL_ALL, LANES), F32),
        g_gate=((8, width), F32),
        g_pre=((8, features), F32),
        **GRAD_OUT(width),
        **{"v_" + name: spec for name, spec in outs.items()},
    )
    dma = pltpu.SemaphoreType.DMA
    signal = pltpu.SemaphoreType.REGULAR
    semaphores = dict(
        s_w=dma((3, 3)),
        r_w=dma((3, 4 * PARTS + 4)),
        s_d=dma((3,)),
        r_d=dma((8,)),
        s_r=dma((2,)),
        r_r=dma((2, 3)),
        s_q=dma((1,)),
        r_q=dma((3,)),
        p_main=dma((5,)),
        p_bc=dma((5,)),
        p_dt=dma((5,)),
        l_main=dma((2 + 6 * PARTS,)),
        l_z=dma((2 + 6 * PARTS,)),
        l_bc=dma((8,)),
        l_dt=dma((8,)),
        s_e=dma((6, 2)),
        s_m=dma((6,)),
        s_o=dma((len(outs),)),
        free_pair=signal,
        free_line=signal,
        free_row=signal,
        free_far=signal,
    )
    names = RAW_IN + tuple("o_" + name for name in outs) + tuple(scratch) + tuple(semaphores)
    values = list(args)
    values[6] = values[6].T
    values[15] = values[15].T
    whole = pl.BlockSpec(memory_space=pltpu.VMEM)
    apart = pl.BlockSpec(memory_space=pl.ANY)
    moved = ("x_in", "w_z", "w_x", "w_bc", "w_out", "cot")
    out = pl.pallas_call(
        functools.partial(whole_kernel, names=names, width=width),
        out_shape=tuple(jax.ShapeDtypeStruct(*spec) for spec in outs.values()),
        in_specs=[apart if name in moved else whole for name in RAW_IN],
        out_specs=tuple([apart] * len(outs)),
        scratch_shapes=[pltpu.VMEM(*spec) for spec in scratch.values()]
        + list(semaphores.values()),
        compiler_params=pltpu.CompilerParams(
            vmem_limit_bytes=VMEM_LIMIT, collective_id=0, has_side_effects=True
        ),
        cost_estimate=pl.CostEstimate(
            flops=5 * 10**10, bytes_accessed=1 << 26, transcendentals=0
        ),
    )(*values)
    return dict(zip(outs, out))


LARGE = ("block", "grad_x", "w_z", "w_x", "w_bc", "w_out")
FINAL = ("pre", "dt", "cxw", "cxb", "cbw", "cbb", "alog", "dtb", "skip", "gate")


def publish_kernel(*refs):
    count = len(LARGE)
    large_in, (steps, small, shared) = refs[:count], refs[count : count + 3]
    large_out = refs[count + 3 : 2 * count + 3]
    o = types.SimpleNamespace(**dict(zip(FINAL, refs[2 * count + 3 : -1])))
    sem = refs[-1]
    moves = [
        pltpu.make_async_copy(src, dst, sem.at[i])
        for i, (src, dst) in enumerate(zip(large_in, large_out))
    ]
    for move in moves:
        move.start()
    heads = o.alog.shape[0]

    def line(out, src, at):
        for p in range(out.shape[0] // LANES):
            out[p * LANES : (p + 1) * LANES] = src[at + p : at + p + 1, :].reshape(LANES)
        return at + out.shape[0] // LANES

    def taps(out, src, at):
        count = out.shape[1] // LANES
        for k in range(4):
            for p in range(count):
                out[k : k + 1, p * LANES : (p + 1) * LANES] = src[at + p : at + p + 1, :]
            at = at + count
        return at

    at = line(o.gate, small, 0)
    at = taps(o.cxw, small, at)
    at = line(o.cxb, small, at)
    for out in (o.skip, o.alog, o.dtb):
        out[...] = small[at : at + 1, 0:heads].reshape(heads)
        at = at + 1
    at = line(o.pre, shared, 0)
    at = taps(o.cbw, shared, at)
    line(o.cbb, shared, at)
    o.dt[...] = steps[0:heads, 0 : o.dt.shape[1]]
    for move in moves:
        move.wait()


def publish(o, width, heads):
    features = o["block"].shape[1]
    shard = o["w_z"].shape[0]
    shapes = dict(
        pre=(features,),
        dt=(heads, shard),
        cxw=(4, width),
        cxb=(width,),
        cbw=(4, 2 * NSTATE),
        cbb=(2 * NSTATE,),
        alog=(heads,),
        dtb=(heads,),
        skip=(heads,),
        gate=(width,),
    )
    whole = pl.BlockSpec(memory_space=pltpu.VMEM)
    apart = pl.BlockSpec(memory_space=pl.ANY)
    large = [o[name] for name in LARGE]
    out = pl.pallas_call(
        publish_kernel,
        out_shape=tuple(
            [jax.ShapeDtypeStruct(v.shape, v.dtype) for v in large]
            + [jax.ShapeDtypeStruct(shapes[name], F32) for name in FINAL]
        ),
        in_specs=[apart] * len(large) + [whole] * 3,
        out_specs=tuple([whole] * (len(large) + len(FINAL))),
        scratch_shapes=[pltpu.SemaphoreType.DMA((len(large),))],
    )(*large, o["w_dt"], o["small"], o["shared"])
    return types.SimpleNamespace(**dict(zip(LARGE + FINAL, out)))


def on_device_whole(*args):
    width = args[3].shape[1]
    heads = args[11].shape[0]
    p = publish(whole_call(args, width), width, heads)
    return (
        p.block,
        p.grad_x,
        p.pre,
        p.w_z,
        p.w_x,
        p.w_bc,
        p.dt.T,
        p.cxw,
        p.cxb,
        p.cbw,
        p.cbb,
        p.alog,
        p.dtb,
        p.skip,
        p.gate,
        p.w_out.T,
    )


def forward_plain(args, small, width):
    x_in, pre_gain, w_z, w_x, w_bc, w_dt, w_out, gate_gain, cotangent = args
    heads = w_dt.shape[1]
    at = layout_of(width)
    values = x_in.astype(F32)
    scale = lax.rsqrt(jnp.mean(values * values, axis=1) + EPS)
    normed = (values * scale[:, None] * pre_gain[None, :]).astype(BF16)
    row_normed = lax.all_gather(normed, "tensor", axis=0, tiled=True)
    mine = jnp.concatenate(
        (w_z, w_x, w_bc, jnp.pad(w_dt, ((0, 0), (0, LANES - heads)))), axis=1
    )
    stacked = lax.all_gather(mine, "dp", axis=0, tiled=True)
    full_out = lax.all_gather(w_out.T, "dp", axis=0, tiled=True)
    projected = jnp.dot(row_normed, stacked, preferred_element_type=F32)
    saved = mixer_forward(projected, small, width)
    row_cot = lax.all_gather(cotangent, "tensor", axis=0, tiled=True)
    y = saved[0]
    z_raw = projected[:, :width]
    gated = y * (z_raw * sigmoid(z_raw))
    d_mixed = dot_nn(row_cot, full_out)
    squares, cross = lax.psum(
        (
            jnp.sum(gated * gated, axis=1),
            jnp.sum(d_mixed * gate_gain[None, :] * gated, axis=1),
        ),
        "tensor",
    )
    return types.SimpleNamespace(
        row_normed=row_normed,
        row_cot=row_cot,
        full_z=stacked[:, :width],
        full_x=stacked[:, width:],
        full_out=full_out,
        z=z_raw,
        projected=(projected,),
        saved=saved,
        d_mixed=d_mixed,
        squares=squares,
        cross=cross,
    )


def on_device(
    x_in,
    segments,
    pre_gain,
    w_z,
    w_x,
    w_bc,
    w_dt,
    conv_x_w,
    conv_x_b,
    conv_bc_w,
    conv_bc_b,
    a_log,
    dt_bias,
    d_skip,
    gate_gain,
    w_out,
    cotangent,
):
    width = w_z.shape[1]
    heads = a_log.shape[0]
    at = layout_of(width)
    small = small_inputs(
        segments, conv_x_w, conv_x_b, conv_bc_w, conv_bc_b, a_log, dt_bias, d_skip
    )
    args = (x_in, pre_gain, w_z, w_x, w_bc, w_dt, w_out, gate_gain, cotangent)
    f = forward_plain(args, small, width)
    squares, cross = f.squares, f.cross
    y, z_raw, d_mixed = f.saved[0], f.z, f.d_mixed
    values = x_in.astype(F32)
    scale = lax.rsqrt(jnp.mean(values * values, axis=1) + EPS)
    gate = sigmoid(z_raw)
    gated = y * (z_raw * gate)
    inner_total = width * lax.axis_size("tensor")
    weighted = d_mixed * gate_gain[None, :]
    scale_two = lax.rsqrt(squares / inner_total + EPS)
    mixed = (gated * scale_two[:, None] * gate_gain[None, :]).astype(BF16)
    branch = lax.psum_scatter(
        dot_nt(mixed, f.full_out).astype(BF16), "tensor", scatter_dimension=0, tiled=True
    ).astype(F32)
    block_out = (values + branch).astype(BF16)
    grad_gate_part = jnp.sum(d_mixed * gated * scale_two[:, None], axis=0)
    d_gated = (
        scale_two[:, None] * weighted
        - gated * (scale_two * scale_two * scale_two * cross / inner_total)[:, None]
    )
    gy = (d_gated * (z_raw * gate)).astype(BF16)
    d_z = (d_gated * y * (gate * (1.0 + z_raw * (1.0 - gate)))).astype(BF16)
    d_rest, g_cxw, g_cxb, g_cbw, g_cbb, g_skip, g_alog, g_dtb = mixer_backward(
        f.projected, small, f.saved, gy, width
    )
    d_proj = jnp.concatenate((d_z, d_rest), axis=1)
    d_normed = lax.psum_scatter(
        (dot_nt(d_z, f.full_z) + dot_nt(d_rest, f.full_x)).astype(BF16),
        "tensor",
        scatter_dimension=0,
        tiled=True,
    ).astype(F32)
    proj_part = dot_tn(f.row_normed, d_proj)
    out_part = dot_tn(f.row_cot, mixed)
    owned = lax.psum_scatter(
        jnp.concatenate((proj_part, out_part), axis=1).astype(BF16),
        "dp",
        scatter_dimension=0,
        tiled=True,
    ).astype(F32)
    grad_w_bc = lax.psum(owned[:, at.bc : at.dt].astype(BF16), "tensor").astype(F32)
    pre_weighted = d_normed * pre_gain[None, :]
    grad_pre_part = jnp.sum(d_normed * values * scale[:, None], axis=0)
    feature_sum = jnp.sum(pre_weighted * values, axis=1)
    grad_x = (
        cotangent.astype(F32)
        + scale[:, None] * pre_weighted
        - values * (scale * scale * scale * feature_sum / values.shape[1])[:, None]
    ).astype(BF16)
    over_taps = lambda v: jnp.sum(v.reshape(4, 8, v.shape[1]), axis=1)
    over_rows = lambda v: jnp.sum(v, axis=0)
    grad_gate_gain, grad_cxw, grad_cxb, grad_alog, grad_dtb, grad_skip = lax.psum(
        (
            grad_gate_part,
            over_taps(g_cxw),
            over_rows(g_cxb),
            over_rows(g_alog)[:heads],
            over_rows(g_dtb)[:heads],
            jnp.sum(over_rows(g_skip).reshape(heads, HEADDIM), axis=1),
        ),
        "dp",
    )
    grad_pre_gain, grad_cbw, grad_cbb = lax.psum(
        (grad_pre_part, over_taps(g_cbw), over_rows(g_cbb)), ("dp", "tensor")
    )
    return (
        block_out,
        grad_x,
        grad_pre_gain,
        owned[:, :width],
        owned[:, width : at.bc],
        grad_w_bc,
        owned[:, at.dt : at.dt + heads],
        grad_cxw,
        grad_cxb,
        grad_cbw,
        grad_cbb,
        grad_alog,
        grad_dtb,
        grad_skip,
        grad_gate_gain,
        owned[:, at.all :].T,
    )


def solution(mesh):
    tokens = P(("dp", "tensor"), None)
    both = P("dp", "tensor")
    heads = P("tensor")
    line = mesh.shape["dp"] == 2 * (LAST_Z + 1) and mesh.shape["tensor"] == 4
    return jax.shard_map(
        on_device_whole if line else on_device,
        mesh=mesh,
        in_specs=(
            tokens,
            P("dp"),
            P(),
            both,
            both,
            P("dp", None),
            both,
            P(None, "tensor"),
            heads,
            P(),
            P(),
            heads,
            heads,
            heads,
            heads,
            P("tensor", "dp"),
            tokens,
        ),
        out_specs=(
            tokens,
            tokens,
            P(),
            both,
            both,
            P("dp", None),
            both,
            P(None, "tensor"),
            heads,
            P(),
            P(),
            heads,
            heads,
            heads,
            heads,
            P("tensor", "dp"),
        ),
        check_vma=False,
    )
```
